32 devices in a mesh: dp: 4 (over y, x), ctx: 8 (over z, core).
Axes of the slice: x: 2, y: 2, z: 4, core: 2. Of those that a mesh axis runs over, the one named last changes fastest.
Arguments:
- hidden_in: bfloat16 [4, 1024, 2048], P('dp', 'ctx'), may hold values from -6 to 6
- out_grad: bfloat16 [4, 1024, 2048], P('dp', 'ctx'), may hold values from -6 to 6
- seg_ids: int32 [4, 1024], P('dp', 'ctx'), may hold values from 0 to 15, never falling along the last dimension, each value on 1 to 512 neighbouring positions
- valid_mask: int32 [4, 1024], P('dp', 'ctx'), may hold values 0 or 1
- w_query: float32 [2048, 2048], P(('dp', 'ctx')), may hold values from -0.1875 to 0.1875
- w_key: float32 [2048, 2048], P(('dp', 'ctx')), may hold values from -0.1875 to 0.1875
- w_value: float32 [2048, 2048], P(('dp', 'ctx')), may hold values from -0.125 to 0.125
- w_output: float32 [2048, 2048], P(('dp', 'ctx')), may hold values from -0.375 to 0.375
- w_gate: float32 [2048, 8192], P(('dp', 'ctx')), may hold values from -0.125 to 0.125
- w_up: float32 [2048, 8192], P(('dp', 'ctx')), may hold values from -0.125 to 0.125
- w_down: float32 [8192, 2048], P(('dp', 'ctx')), may hold values from -0.0625 to 0.0625
- gain_attn: float32 [2048], P(('dp', 'ctx')), may hold values from 0.5 to 1.5
- gain_mlp: float32 [2048], P(('dp', 'ctx')), may hold values from 0.5 to 1.5
Outputs:
- result: bfloat16 [4, 1024, 2048], P('dp', 'ctx')
- grad_input: bfloat16 [4, 1024, 2048], P('dp', 'ctx')
- grad_query: float32 [2048, 2048], P(('dp', 'ctx'))
- grad_key: float32 [2048, 2048], P(('dp', 'ctx'))
- grad_value: float32 [2048, 2048], P(('dp', 'ctx'))
- grad_output: float32 [2048, 2048], P(('dp', 'ctx'))
- grad_gate: float32 [2048, 8192], P(('dp', 'ctx'))
- grad_up: float32 [2048, 8192], P(('dp', 'ctx'))
- grad_down: float32 [8192, 2048], P(('dp', 'ctx'))
- grad_gain_attn: float32 [2048], P(('dp', 'ctx'))
- grad_gain_mlp: float32 [2048], P(('dp', 'ctx'))
- mass_mean: float32 [], replicated
The draws below stay inside these ranges and needn't reach their ends.
Inputs may be any that keep to these rules, and one draw needn't show every extreme that they name: `seg_ids`: within a slot ids never fall; each document has 1 to 512 tokens and one has exactly 512.
All inputs are finite; a program needn't handle non-finite values. No bound on the sum of `valid_mask` on one device may be relied on, other than what follows from the above.
Results may differ from the reference program's by a relative error of at most 0.015.
The reference program's roundings to bfloat16 on the way count: a program that leaves them out, or rounds other values in their place, can miss the bound.
Values may be sent and summed in bfloat16 or wider, within the bound.
A program may use at most 704 MiB of HBM per device.

```python
import math
import jax
import jax.numpy as jnp
import numpy as np
from jax import lax

D = 2048
HEADS = 16
HEAD_DIM = 128
FF = 8192
DOCS = 16
SEQ = 1024
BATCH = 4
DOC_MOST = 512


def with_ends(array, rng, least, largest):
    place = [jax.random.randint(jax.random.fold_in(rng, axis), (), 0, length) for axis, length in enumerate(array.shape)]
    longest = array.shape.index(max(array.shape))
    next_to = place[:longest] + [(place[longest] + 1) % array.shape[longest]] + place[longest + 1:]
    return array.at[tuple(place)].set(least).at[tuple(next_to)].set(largest)


def block_scale(own_key, extent, pieces, low, top_value):
    factor_of, own = 1.0, jax.random.fold_in(own_key, 6)
    for dim, shards_of in pieces:
        heights = jnp.exp(jax.random.uniform(jax.random.fold_in(own, dim), (shards_of,), jnp.float32, low / len(pieces), top_value / len(pieces)))
        factor_of = factor_of * jnp.repeat(heights, extent[dim] // shards_of).reshape([-1 if axis == dim else 1 for axis in range(len(extent))])
    return factor_of


def length_profile(count, total, most, slope):
    loads = [(1 << 20) // math.isqrt(rank ** slope) + 1 for rank in range(2, count + 1)]
    rest, holding = total - most - (count - 1), [1] * (count - 1)
    while rest > 0:
        free = [i for i in range(count - 1) if holding[i] < most]
        pool, budget = sum([loads[i] for i in free]), rest
        for i in free:
            more = min(most - holding[i], max(1, budget * loads[i] // pool), rest)
            holding[i] = holding[i] + more
            rest = rest - more
    return np.array([most] + holding)


def ragged_sizes(own_key, count, total, limit, lean):
    if count == 2:
        one = jax.random.randint(own_key, (), max(1, total - limit), min(limit, total - 1) + 1)
        return jnp.stack([one, total - one])
    lengths = jnp.asarray(length_profile(count, total, limit, lean), jnp.int32)
    couples = (count - 1) // 2
    donor, taker = lengths[1:1 + 2 * couples:2], lengths[2:2 + 2 * couples:2]
    room = jnp.minimum(donor - 1, limit - taker)
    passed = jax.random.randint(jax.random.fold_in(own_key, 1), (couples,), 0, 1 << 20) % (room + 1)
    lengths = lengths.at[1:1 + 2 * couples:2].set(donor - passed).at[2:2 + 2 * couples:2].set(taker + passed)
    return lengths[jax.random.permutation(jax.random.fold_in(own_key, 2), count)]


def gaussian(stream_key, extent, spread, bound, cuts=(), kind=jnp.bfloat16):
    entries = jax.random.normal(stream_key, extent, jnp.float32) * spread
    if len(cuts) > 0:
        entries = block_scale(stream_key, extent, cuts, -0.22, 0.18) * entries
    return jnp.clip(entries, min=-bound, max=bound).astype(kind)


def setup_inputs(seed: int = 0) -> dict:
    splits = jax.random.split(jax.random.key(seed), 14)
    return {
        "hidden_in": gaussian(splits[0], (BATCH, SEQ, D), 1.0, 6.0, ((0, 4), (1, 8))),
        "out_grad": gaussian(splits[1], (BATCH, SEQ, D), 1.0, 6.0, ((0, 4), (1, 8))),
        "seg_ids": jax.vmap(lambda own: jnp.searchsorted(jnp.cumsum(ragged_sizes(own, DOCS, SEQ, DOC_MOST, 2)), jnp.arange(SEQ), side="right"))(jax.random.split(splits[2], BATCH)).reshape((BATCH, SEQ)).astype(jnp.int32),
        "valid_mask": with_ends((jax.random.randint(splits[3], (BATCH, SEQ), 0, 8) < 7).astype(jnp.int32), jax.random.fold_in(splits[3], 1), 0, 1),
        "w_query": gaussian(splits[4], (D, D), (D // 2) ** -0.5, 0.1875, ((0, 32),), jnp.float32),
        "w_key": gaussian(splits[5], (D, D), (D // 2) ** -0.5, 0.1875, ((0, 32),), jnp.float32),
        "w_value": gaussian(splits[6], (D, D), D ** -0.5, 0.125, ((0, 32),), jnp.float32),
        "w_output": gaussian(splits[7], (D, D), (D // 8) ** -0.5, 0.375, ((0, 32),), jnp.float32),
        "w_gate": gaussian(splits[8], (D, FF), D ** -0.5, 0.125, ((0, 32),), jnp.float32),
        "w_up": gaussian(splits[9], (D, FF), D ** -0.5, 0.125, ((0, 32),), jnp.float32),
        "w_down": gaussian(splits[10], (FF, D), FF ** -0.5, 0.0625, ((0, 32),), jnp.float32),
        "gain_attn": jnp.clip(1.0 + 0.1 * jax.random.normal(splits[11], (D,), jnp.float32), 0.5, 1.5),
        "gain_mlp": jnp.clip(1.0 + 0.1 * jax.random.normal(splits[12], (D,), jnp.float32), 0.5, 1.5),
    }


@jax.custom_vjp
def low(v):
    return lax.optimization_barrier(v.astype(jnp.bfloat16)).astype(jnp.float32)

@jax.custom_vjp
def low_back(v):
    return v

def low_keep(v):
    return (low(v), None)

def low_pass(kept, grad):
    return (grad,)

def back_keep(v):
    return (v, None)

def back_low(kept, grad):
    return (low(grad),)
low.defvjp(low_keep, low_pass)
low_back.defvjp(back_keep, back_low)
norm_eps = 1e-05
rope_base = 10000.0
score_shift = math.log(4096.0)
highest = lax.Precision.HIGHEST

def rotate(values, cosines, sines):
    half_dim = values.shape[-1] // 2
    first = values[..., :half_dim]
    second = values[..., half_dim:]
    cos_b = cosines[:, None, :]
    sin_b = sines[:, None, :]
    return jnp.concatenate([first * cos_b - second * sin_b, second * cos_b + first * sin_b], axis=-1)

def normalized(values):
    return values * lax.rsqrt(lax.optimization_barrier(jnp.mean(values * values, axis=-1, keepdims=True)) + norm_eps)

def rope_tables(positions):
    half_dim = HEAD_DIM // 2
    inverse = jnp.exp(jnp.arange(half_dim, dtype=jnp.float32) * (-2.0 * math.log(rope_base) / HEAD_DIM))
    angles = positions[:, None] * inverse[None, :]
    return (jnp.cos(angles), jnp.sin(angles))

def slot_forward(weights, slot):
    w_query, w_key, w_value, w_output, w_gate, w_up, w_down, gain_attn, gain_mlp = weights
    inputs_f, seg_row, valid_row = slot
    seq_len = inputs_f.shape[0]
    token_index = jnp.arange(seq_len, dtype=jnp.int32)
    starts = lax.optimization_barrier(jnp.sum((seg_row[None, :] < seg_row[:, None]).astype(jnp.int32), axis=1))
    cosines, sines = rope_tables((token_index - starts).astype(jnp.float32))
    shape3 = (seq_len, HEADS, HEAD_DIM)
    attn_in = low(normalized(inputs_f) * low(gain_attn))
    queries = low(rotate(low_back(jnp.dot(attn_in, low(w_query), precision=highest)).reshape(shape3), cosines, sines))
    keys = low(rotate(low_back(jnp.dot(attn_in, low(w_key), precision=highest)).reshape(shape3), cosines, sines))
    values = low(low_back(jnp.dot(attn_in, low(w_value), precision=highest))).reshape(shape3)
    block_len = math.gcd(seq_len, 512)
    score_scale = 1.0 / math.sqrt(HEAD_DIM)

    def attend(block):
        start = block * block_len
        query_block = lax.dynamic_slice_in_dim(queries, start, block_len, 0)
        query_index = start + jnp.arange(block_len, dtype=jnp.int32)
        query_seg = lax.dynamic_slice_in_dim(seg_row, start, block_len, 0)
        allowed = (query_seg[:, None] == seg_row[None, :]) & (token_index[None, :] <= query_index[:, None]) & (valid_row[None, :] == 1)
        scores = jnp.einsum('qhd,khd->hqk', query_block, keys, precision=highest) * score_scale - score_shift
        probs = jax.nn.sigmoid(low_back(scores)) * allowed.astype(jnp.float32)[None]
        attended = jnp.einsum('hqk,khd->qhd', low(probs), values, precision=highest)
        return (attended, lax.optimization_barrier(jnp.sum(probs, axis=(0, 2))))
    attended, mass = lax.map(jax.checkpoint(attend), jnp.arange(seq_len // block_len, dtype=jnp.int32))
    attn_out = low(low_back(attended.reshape(seq_len, HEADS * HEAD_DIM)))
    middle = inputs_f + low_back(jnp.dot(attn_out, low(w_output), precision=highest))
    mlp_in = low(normalized(middle) * low(gain_mlp))
    gate = low_back(jnp.dot(mlp_in, low(w_gate), precision=highest))
    up_proj = low_back(jnp.dot(mlp_in, low(w_up), precision=highest))
    hidden = low(jax.nn.silu(gate) * up_proj)
    result = middle + low_back(jnp.dot(hidden, low(w_down), precision=highest))
    mass_sum = jnp.sum(valid_row.astype(jnp.float32) * mass.reshape(seq_len)) / HEADS
    return (result, mass_sum)

def reference(hidden_in, out_grad, seg_ids, valid_mask, w_query, w_key, w_value, w_output, w_gate, w_up, w_down, gain_attn, gain_mlp):
    inputs_f = hidden_in.astype(jnp.float32)
    grad_f = out_grad.astype(jnp.float32)

    def forward(inputs_all, *weights):

        def one_slot(slot):
            return slot_forward(weights, slot)
        results, masses = lax.map(jax.checkpoint(one_slot), (inputs_all, seg_ids, valid_mask))
        return (results, jnp.sum(masses) / (BATCH * SEQ))
    (result, mass_mean), pullback = jax.vjp(forward, inputs_f, w_query, w_key, w_value, w_output, w_gate, w_up, w_down, gain_attn, gain_mlp)
    grads = pullback((grad_f, jnp.zeros_like(mass_mean)))
    return (result.astype(jnp.bfloat16), grads[0].astype(jnp.bfloat16), grads[1], grads[2], grads[3], grads[4], grads[5], grads[6], grads[7], grads[8], grads[9], mass_mean)
```

```python
import math

import jax
import jax.numpy as jnp
from jax import lax
from jax.sharding import PartitionSpec as P

HEAD_DIM = 128
norm_eps = 1e-05
rope_base = 10000.0
score_shift = math.log(4096.0)
score_scale = 1.0 / math.sqrt(HEAD_DIM)
contract_rows = (((0,), (0,)), ((), ()))
contract_cols = (((1,), (1,)), ((), ()))
f32 = jnp.float32
bf16 = jnp.bfloat16


def dot(a, b, dims=(((1,), (0,)), ((), ()))):
    return lax.dot_general(a, b, dims, preferred_element_type=f32)


def rope_tables(positions):
    half_dim = HEAD_DIM // 2
    inverse = jnp.exp(
        jnp.arange(half_dim, dtype=f32) * (-2.0 * math.log(rope_base) / HEAD_DIM)
    )
    angles = positions[:, None] * inverse[None, :]
    return jnp.cos(angles), jnp.sin(angles)


def rotate(values, cosines, sines, sign):
    half = HEAD_DIM // 2
    parts = []
    for h in range(values.shape[1] // HEAD_DIM):
        a = values[:, h * HEAD_DIM : h * HEAD_DIM + half]
        b = values[:, h * HEAD_DIM + half : (h + 1) * HEAD_DIM]
        parts += [a * cosines - sign * b * sines, b * cosines + sign * a * sines]
    return jnp.concatenate(parts, axis=1)


def inverse_rms(values):
    return lax.rsqrt(jnp.mean(values * values, axis=-1, keepdims=True) + norm_eps)


def gather(v, axes, axis=0):
    return lax.all_gather(v, axes, axis=axis, tiled=True)


def scatter_sum(v, axes):
    return lax.psum_scatter(v, axes, scatter_dimension=0, tiled=True)


def swap(v, axes):
    return lax.all_to_all(v, axes, split_axis=0, concat_axis=0, tiled=True)


def shards(
    hidden_in,
    out_grad,
    seg_ids,
    valid_mask,
    w_query,
    w_key,
    w_value,
    w_output,
    w_gate,
    w_up,
    w_down,
    gain_attn,
    gain_mlp,
):
    dpn = lax.axis_size("dp")
    cn = lax.axis_size("ctx")
    x_local = hidden_in[0]
    rows, width = x_local.shape
    seq = rows * cn
    dr = w_query.shape[0]
    hw = width // cn
    heads = hw // HEAD_DIM
    ff_rows = w_down.shape[0]
    ff = ff_rows * dpn

    codes = gather(seg_ids[0] * 2 + valid_mask[0], "ctx")
    seg = codes // 2
    valid = codes % 2
    index = jnp.arange(seq, dtype=jnp.int32)
    starts = jnp.sum((seg[None, :] < seg[:, None]).astype(jnp.int32), axis=1)
    cosines, sines = rope_tables((index - starts).astype(f32))
    allowed = (
        (seg[:, None] == seg[None, :])
        & (index[None, :] <= index[:, None])
        & (valid[None, :] == 1)
    )

    gains = gather(jnp.stack([gain_attn, gain_mlp], axis=1).astype(bf16), ("dp", "ctx")).astype(f32)
    gain_one = gains[:, 0]
    gain_two = gains[:, 1]

    qkv = jnp.concatenate(
        [w.astype(bf16).reshape(dr, cn, hw) for w in (w_query, w_key, w_value)], axis=2
    ).transpose(1, 0, 2)
    out_cols = w_output.astype(bf16)
    qkv = gather(swap(qkv, "ctx").reshape(cn * dr, 3 * hw), "dp")
    owner = lax.axis_index("dp") * cn + lax.axis_index("ctx")
    wo_full = gather(out_cols, ("dp", "ctx"))
    wo = lax.dynamic_slice_in_dim(wo_full, lax.axis_index("ctx") * hw, hw, 0)
    gate_up = jnp.concatenate(
        [w.astype(bf16).reshape(dr, dpn, cn, ff_rows) for w in (w_gate, w_up)], axis=1
    ).transpose(2, 0, 1, 3).reshape(cn, dr, 2 * ff)
    gate_up = gather(swap(gate_up, "ctx").reshape(cn * dr, 2 * ff), "dp")
    down = gather(w_down.astype(bf16), "dp")

    xs = gather(x_local, "ctx").astype(f32)
    dy_local = out_grad[0]
    dys = gather(dy_local, "ctx")
    inv_all = inverse_rms(xs)
    xh_all = xs * inv_all
    an = (xh_all * gain_one).astype(bf16)
    proj = dot(an, qkv)
    q = rotate(proj[:, :hw], cosines, sines, 1.0).astype(bf16)
    k = rotate(proj[:, hw : 2 * hw], cosines, sines, 1.0).astype(bf16)
    v = proj[:, 2 * hw :].astype(bf16)

    def per_head(t, h):
        return t[:, h * HEAD_DIM : (h + 1) * HEAD_DIM]

    outs = []
    mass = jnp.zeros((seq,), f32)
    for h in range(heads):
        s = dot(per_head(q, h), per_head(k, h), contract_cols) * score_scale - score_shift
        p = jnp.where(allowed, jax.nn.sigmoid(s), 0.0)
        mass = mass + jnp.sum(p, axis=1)
        outs.append(dot(p.astype(bf16), per_head(v, h)))
    o = jnp.concatenate(outs, axis=1).astype(bf16)
    x_f = x_local.astype(f32)
    h1 = x_f + scatter_sum(dot(o, wo).astype(bf16), "ctx").astype(f32)
    r2 = inverse_rms(h1)
    xh2 = h1 * r2
    bn = gather((xh2 * gain_two).astype(bf16), "ctx")
    gu = dot(bn, gate_up)
    gate = gu[:, :ff]
    up = gu[:, ff:]
    sig = jax.nn.sigmoid(gate)
    silu = gate * sig
    hid = (silu * up).astype(bf16)
    result = h1 + scatter_sum(dot(hid, down).astype(bf16), "ctx").astype(f32)
    dhid = dot(dys, down, contract_cols)
    dgate = (dhid * up * sig * (1.0 + gate * (1.0 - sig))).astype(bf16)
    dup = (dhid * silu).astype(bf16)
    dgu = jnp.concatenate([dgate, dup], axis=1)
    dbn = scatter_sum(dot(dgu, gate_up, contract_cols).astype(bf16), "ctx").astype(f32)
    g_gu = scatter_sum(dot(bn, dgu, contract_rows).astype(bf16), "dp")
    g_down = scatter_sum(dot(hid, dys, contract_rows).astype(bf16), "dp")
    term_two = jnp.sum(dbn * xh2, axis=0)
    u2 = dbn * gain_two
    dh1 = dy_local.astype(f32) + r2 * (u2 - xh2 * jnp.mean(u2 * xh2, axis=-1, keepdims=True))
    dob = gather(dh1.astype(bf16), "ctx")
    do = dot(dob, wo, contract_cols).astype(bf16)
    dqs, dks, dvs = [], [], []
    for h in range(heads):
        qh, kh, vh, doh = (per_head(t, h) for t in (q, k, v, do))
        s = dot(qh, kh, contract_cols) * score_scale - score_shift
        sg = jnp.where(allowed, jax.nn.sigmoid(s), 0.0)
        pb = sg.astype(bf16)
        ds = (dot(doh, vh, contract_cols) * sg * (1.0 - sg)).astype(bf16)
        dqs.append(dot(ds, kh) * score_scale)
        dks.append(dot(ds, qh, contract_rows) * score_scale)
        dvs.append(dot(pb, doh, contract_rows))
    dq = rotate(jnp.concatenate(dqs, axis=1), cosines, sines, -1.0).astype(bf16)
    dk = rotate(jnp.concatenate(dks, axis=1), cosines, sines, -1.0).astype(bf16)
    dv = jnp.concatenate(dvs, axis=1).astype(bf16)
    dqkv = jnp.concatenate([dq, dk, dv], axis=1)
    dan_part = dot(dqkv, qkv, contract_cols)
    term_one = jnp.sum(dan_part * xh_all, axis=0)
    dan = scatter_sum(dan_part.astype(bf16), "ctx").astype(f32)
    inv_one = inverse_rms(x_f)
    xh1 = x_f * inv_one
    u1 = dan * gain_one
    grad_input = dh1 + inv_one * (u1 - xh1 * jnp.mean(u1 * xh1, axis=-1, keepdims=True))

    g_qkv = dot(an, dqkv, contract_rows).astype(bf16)
    g_out = dot(o, dob, contract_rows).astype(bf16)
    g_out_full = jnp.zeros((width, width), bf16)
    g_out_full = lax.dynamic_update_slice_in_dim(g_out_full, g_out, lax.axis_index("ctx") * hw, 0)
    g_out_own = scatter_sum(g_out_full, ("dp", "ctx")).astype(f32)
    g_qkv = swap(scatter_sum(g_qkv, "dp").reshape(cn, dr, 3 * hw), "ctx").astype(f32)
    g_q, g_k, g_v = (
        g_qkv[:, :, i * hw : (i + 1) * hw].transpose(1, 0, 2).reshape(dr, width) for i in range(3)
    )
    g_gu = swap(g_gu.reshape(cn, dr, 2 * ff), "ctx").astype(f32)
    g_gate, g_up = (
        g_gu[:, :, i * ff : (i + 1) * ff]
        .reshape(cn, dr, dpn, ff_rows)
        .transpose(1, 2, 0, 3)
        .reshape(dr, dpn * cn * ff_rows)
        for i in range(2)
    )
    totals = lax.psum(
        (term_one, term_two, jnp.sum(valid.astype(f32) * mass) / (heads * cn)), ("dp", "ctx")
    )
    grad_gain_attn = lax.dynamic_slice_in_dim(totals[0], owner * dr, dr)
    grad_gain_mlp = lax.dynamic_slice_in_dim(totals[1], owner * dr, dr)
    mass_mean = totals[2] / (dpn * seq)
    return (
        result.astype(bf16)[None],
        grad_input.astype(bf16)[None],
        g_q,
        g_k,
        g_v,
        g_out_own,
        g_gate,
        g_up,
        g_down.astype(f32),
        grad_gain_attn,
        grad_gain_mlp,
        mass_mean,
    )


def solution(mesh):
    tok = P("dp", "ctx", None)
    ids = P("dp", "ctx")
    mat = P(("dp", "ctx"), None)
    vec = P(("dp", "ctx"))
    return jax.shard_map(
        shards,
        mesh=mesh,
        in_specs=(tok, tok, ids, ids) + (mat,) * 7 + (vec, vec),
        out_specs=(tok, tok) + (mat,) * 7 + (vec, vec, P()),
        check_vma=False,
    )
```

```python
import functools
import math

import jax
import jax.numpy as jnp
from jax import lax
from jax.experimental import pallas as pl
from jax.experimental.pallas import tpu as pltpu
from jax.sharding import PartitionSpec as P

HEAD_DIM = 128
norm_eps = 1e-05
rope_base = 10000.0
score_shift = math.log(4096.0)
score_scale = 1.0 / math.sqrt(HEAD_DIM)
contract_rows = (((0,), (0,)), ((), ()))
contract_cols = (((1,), (1,)), ((), ()))
plain = (((1,), (0,)), ((), ()))
f32 = jnp.float32
bf16 = jnp.bfloat16
MESH = pl.DeviceIdType.MESH
ANY = pl.BlockSpec(memory_space=pl.ANY)
VMEM = pl.BlockSpec(memory_space=pltpu.VMEM)


def dot(a, b, dims=plain):
    return lax.dot_general(a, b, dims, preferred_element_type=f32)


def remote(src, dst, send, recv, target):
    return pltpu.make_async_remote_copy(
        src_ref=src,
        dst_ref=dst,
        send_sem=send,
        recv_sem=recv,
        device_id=target,
        device_id_type=MESH,
    )


def greet(target):
    pl.semaphore_signal(
        pltpu.get_barrier_semaphore(), inc=1, device_id=target, device_id_type=MESH
    )


def place(cn):
    c = lax.axis_index("ctx")
    j, k = c // 2, c % 2
    return c, j, k, cn // 2, 2 * j + 1 - k


def greet_line(cn):
    c, j, _, n, sib = place(cn)
    greet({"ctx": sib})

    @pl.when(j < n - 1)
    def _():
        greet({"ctx": c + 2})

    @pl.when(j > 0)
    def _():
        greet({"ctx": c - 2})

    inner = jnp.where(j > 0, 1, 0) + jnp.where(j < n - 1, 1, 0)
    pl.semaphore_wait(pltpu.get_barrier_semaphore(), 1 + inner)


def greet_ctx(cn):
    c = lax.axis_index("ctx")
    for s in range(1, cn):
        greet({"ctx": lax.rem(c + s, cn)})


class LineGather:
    def __init__(self, cn, own, full, sem):
        self.cn, self.own, self.full, self.sem = cn, own, full, sem

    def copy(self, src, origin, kind, target):
        _, _, k, _, _ = place(self.cn)
        sem = self.sem
        return remote(
            src,
            self.full.at[2 * origin + k],
            sem.at[kind, origin],
            sem.at[3 if kind < 2 else 4, origin],
            {"ctx": target},
        )

    def start(self):
        c, j, _, n, sib = place(self.cn)

        @pl.when(j < n - 1)
        def _():
            self.copy(self.own, j, 0, c + 2).start()

        @pl.when(j > 0)
        def _():
            self.copy(self.own, j, 1, c - 2).start()

        self.copy(self.own, j, 2, sib).start()

    def forward(self):
        c, j, k, n, sib = place(self.cn)
        for s in range(1, n):

            @pl.when(j - s >= 0)
            def _():
                o = j - s
                block = self.full.at[2 * o + k]
                self.copy(block, o, 0, sib).wait_recv()

                @pl.when(j < n - 1)
                def _():
                    self.copy(block, o, 0, c + 2).start()

                self.copy(block, o, 2, sib).start()

            @pl.when(j + s <= n - 1)
            def _():
                o = j + s
                block = self.full.at[2 * o + k]
                self.copy(block, o, 1, sib).wait_recv()

                @pl.when(j > 0)
                def _():
                    self.copy(block, o, 1, c - 2).start()

                self.copy(block, o, 2, sib).start()

    def finish(self):
        c, j, k, n, sib = place(self.cn)
        for o in range(n):
            block = self.full.at[2 * o + 1 - k]
            remote(
                block, block, self.sem.at[2, o], self.sem.at[4, o], {"ctx": sib}
            ).wait_recv()
        for o in range(n):
            block = self.full.at[2 * o + k]

            @pl.when((j < n - 1) & (o <= j))
            def _():
                self.copy(block, o, 0, sib).wait_send()

            @pl.when((j > 0) & (o >= j))
            def _():
                self.copy(block, o, 1, sib).wait_send()

            self.copy(block, o, 2, sib).wait_send()


class Swap:
    def __init__(self, cn, src, dst, sem, local):
        self.cn, self.src, self.dst, self.sem, self.local = cn, src, dst, sem, local

    def copy(self, s):
        c = lax.axis_index("ctx")
        peer = lax.rem(c + s, self.cn)
        return remote(
            self.src.at[peer],
            self.dst.at[c],
            self.sem.at[0, s],
            self.sem.at[1, s],
            {"ctx": peer},
        )

    def start(self):
        c = lax.axis_index("ctx")
        for s in range(1, self.cn):
            self.copy(s).start()
        pltpu.make_async_copy(self.src.at[c], self.dst.at[c], self.local).start()

    def finish(self):
        c = lax.axis_index("ctx")
        pltpu.make_async_copy(self.src.at[c], self.dst.at[c], self.local).wait()
        for s in range(1, self.cn):
            source = lax.rem(c - s + self.cn, self.cn)
            block = self.dst.at[source]
            remote(
                block, block, self.sem.at[0, s], self.sem.at[1, s], {"ctx": source}
            ).wait_recv()
            self.copy(s).wait_send()


class LineSum:
    def __init__(self, cn, compute, part, cross, cross_in, flow, arrived, sem):
        self.cn, self.compute, self.part = cn, compute, part
        self.cross, self.cross_in, self.flow = cross, cross_in, flow
        self.arrived, self.sem = arrived, sem

    def across(self, t):
        _, _, _, _, sib = place(self.cn)
        return remote(
            self.cross.at[t],
            self.cross_in.at[t],
            self.sem.at[0, t],
            self.sem.at[2, t],
            {"ctx": sib},
        )

    def along(self, t, slot, target):
        return remote(
            self.flow.at[t],
            self.arrived.at[slot],
            self.sem.at[1, t],
            self.sem.at[3, slot],
            {"ctx": target},
        )

    def produce(self, t, slot):
        _, _, k, _, _ = place(self.cn)
        part = self.part.at[slot]
        self.compute(t, part)
        self.cross[t] = part[1 - k].astype(bf16)
        self.across(t).start()

    def collect(self, t, slot):
        _, j, k, n, sib = place(self.cn)
        part = self.part.at[slot, k]
        self.across(t).wait_recv()
        part[...] += self.cross_in[t].astype(f32)

        @pl.when((j > 0) & (t >= j))
        def _():
            self.along(t, t, sib).wait_recv()
            part[...] += self.arrived[t].astype(f32)

        @pl.when((j < n - 1) & (t <= j))
        def _():
            slot_in = jnp.where(t == j, n, t)
            self.along(t, slot_in, sib).wait_recv()
            part[...] += self.arrived[slot_in].astype(f32)

    def send(self, t, slot, up):
        c, j, k, n, _ = place(self.cn)
        self.flow[t] = self.part[slot, k].astype(bf16)
        there = t if up else jnp.where(t == j - 1, n, t)
        self.along(t, there, c + 2 if up else c - 2).start()

    def drain(self):
        _, j, _, n, sib = place(self.cn)

        @pl.loop(0, n)
        def _(t):
            self.across(t).wait_send()

            @pl.when(t != j)
            def _():
                self.along(t, t, sib).wait_send()


def line_sums(cn, sums):
    _, j, _, n, _ = place(cn)

    @pl.loop(0, n - 1)
    def _(i):
        for total in sums:

            @pl.when(n - 1 - i > j)
            def _():
                total.produce(n - 1 - i, 0)

            @pl.when(i < j)
            def _():
                total.produce(i, 1)

        for total in sums:

            @pl.when(n - 1 - i > j)
            def _():
                total.collect(n - 1 - i, 0)
                total.send(n - 1 - i, 0, True)

            @pl.when(i < j)
            def _():
                total.collect(i, 1)
                total.send(i, 1, False)

    for total in sums:
        total.produce(j, 0)
    for total in sums:
        total.collect(j, 0)


def sum_scratch(cn, rows, width):
    n = cn // 2
    return [
        pltpu.VMEM((2, 2, rows, width), f32),
        pltpu.VMEM((n, rows, width), bf16),
        pltpu.VMEM((n, rows, width), bf16),
        pltpu.VMEM((n, rows, width), bf16),
        pltpu.VMEM((n + 1, rows, width), bf16),
        pltpu.SemaphoreType.DMA((4, n + 1)),
    ]


def product(a_ref, b_ref, dims, rows, width):
    tile = min(512, width)

    def compute(t, out):
        a = a_ref[pl.ds(pl.multiple_of(t * 2 * rows, 2 * rows), 2 * rows), :]

        @pl.loop(0, width // tile)
        def _(i):
            at = pl.ds(pl.multiple_of(i * tile, tile), tile)
            b = b_ref[:, at] if dims == plain else b_ref[at, :]
            out[:, :, at] = dot(a, b, dims).reshape(2, rows, tile)

    return compute


def rms(v):
    return lax.rsqrt(jnp.mean(v * v, axis=-1, keepdims=True) + norm_eps)


def front_kernel(cn, x, pack, x_all, pack_all, gsem, ssem, local):
    greet_ctx(cn)
    pl.semaphore_wait(pltpu.get_barrier_semaphore(), cn - 1)
    c = lax.axis_index("ctx")
    swap = Swap(cn, pack, pack_all, ssem, local.at[0])
    gather = LineGather(cn, x, x_all, gsem)
    swap.start()
    gather.start()
    keep = pltpu.make_async_copy(x, x_all.at[c], local.at[1])
    keep.start()
    gather.forward()
    keep.wait()
    swap.finish()
    gather.finish()


def spread_kernel(cn, dpn, pack, wo, pack_all, wo_all, ssem, osem, local):
    c, d = lax.axis_index("ctx"), lax.axis_index("dp")
    greet_ctx(cn)
    for r in range(dpn):
        g = c * dpn + r
        src_d, src_c = g // cn, lax.rem(g, cn)

        @pl.when((src_d != d) | (src_c != c))
        def _():
            greet({"dp": src_d, "ctx": src_c})

    mine = d * cn + c
    home, slot = mine // dpn, lax.rem(mine, dpn)
    outs = jnp.where(home == c, dpn - 1, dpn)
    pl.semaphore_wait(pltpu.get_barrier_semaphore(), cn - 1 + outs)
    swap = Swap(cn, pack, pack_all, ssem, local.at[0])
    swap.start()

    def copy(to):
        return remote(
            wo,
            wo_all.at[slot],
            osem.at[0, to],
            osem.at[1, slot],
            {"dp": to, "ctx": home},
        )

    def own():
        return pltpu.make_async_copy(wo, wo_all.at[slot], local.at[1])

    for to in range(dpn):
        self_target = (home == c) & (d == to)

        @pl.when(jnp.logical_not(self_target))
        def _():
            copy(to).start()

        @pl.when(self_target)
        def _():
            own().start()

    swap.finish()
    for r in range(dpn):
        g = c * dpn + r
        local_piece = g == mine

        @pl.when(jnp.logical_not(local_piece))
        def _():
            block = wo_all.at[r]
            remote(
                block, block, osem.at[0, r], osem.at[1, r], {"dp": d, "ctx": c}
            ).wait_recv()

        @pl.when(local_piece)
        def _():
            own().wait()

    for to in range(dpn):

        @pl.when(jnp.logical_not((home == c) & (d == to)))
        def _():
            copy(to).wait_send()


def middle_kernel(cn, o, wo, x, gain, h1, bn_all, own, gsem, lsem, *scratch):
    greet_line(cn)
    c, _, k, _, _ = place(cn)
    rows, width = x.shape
    total = LineSum(cn, product(o, wo, plain, rows, width), *scratch)
    line_sums(cn, [total])
    mid = x[...].astype(f32) + total.part[0, k]
    h1[...] = mid
    own[...] = (mid * rms(mid) * gain[...]).astype(bf16)
    gather = LineGather(cn, own, bn_all, gsem)
    gather.start()
    keep = pltpu.make_async_copy(own, bn_all.at[c], lsem)
    keep.start()
    gather.forward()
    keep.wait()
    gather.finish()
    total.drain()


def back_kernel(
    cn, dgu, w, h1, dy, gain, dh1, dob_all, term, own, gsem, lsem, *scratch
):
    greet_line(cn)
    c, _, k, _, _ = place(cn)
    rows, width = dy.shape
    total = LineSum(cn, product(dgu, w, contract_cols, rows, width), *scratch)
    line_sums(cn, [total])
    dbn = total.part[0, k]
    mid = h1[...]
    r2 = rms(mid)
    xh2 = mid * r2
    term[...] = jnp.sum(dbn * xh2, axis=0, keepdims=True)
    u2 = dbn * gain[...]
    grad = dy[...].astype(f32) + r2 * (u2 - xh2 * jnp.mean(u2 * xh2, axis=-1, keepdims=True))
    dh1[...] = grad
    own[...] = grad.astype(bf16)
    gather = LineGather(cn, own, dob_all, gsem)
    gather.start()
    keep = pltpu.make_async_copy(own, dob_all.at[c], lsem)
    keep.start()
    gather.forward()
    keep.wait()
    gather.finish()
    total.drain()


def last_kernel(
    cn, dqkv, w, dh1, x, gain, hid, down, h1, grad_in, result, term, *scratch
):
    greet_line(cn)
    _, _, k, _, _ = place(cn)
    rows, width = x.shape
    half = len(scratch) // 2
    dan_sum = LineSum(cn, product(dqkv, w, contract_cols, rows, width), *scratch[:half])
    res_sum = LineSum(cn, product(hid, down, plain, rows, width), *scratch[half:])
    line_sums(cn, [dan_sum, res_sum])
    result[...] = (h1[...] + res_sum.part[0, k]).astype(bf16)
    dan = dan_sum.part[0, k]
    xf = x[...].astype(f32)
    r1 = rms(xf)
    xh1 = xf * r1
    term[...] = jnp.sum(dan * xh1, axis=0, keepdims=True)
    u1 = dan * gain[...]
    grad = dh1[...] + r1 * (u1 - xh1 * jnp.mean(u1 * xh1, axis=-1, keepdims=True))
    grad_in[...] = grad.astype(bf16)
    dan_sum.drain()
    res_sum.drain()


def return_kernel(
    cn, dpn, qkv, gu, go, tot, qkv_all, gu_all, go_all, tot_out,
    tot_in, tot_sum, tot_last, qsem, usem, osem, tsem, dsem, local,
):
    c, d = lax.axis_index("ctx"), lax.axis_index("dp")
    mine = d * cn + c
    home, slot = mine // dpn, lax.rem(mine, dpn)
    greet_ctx(cn)
    for s in range(1, dpn):
        greet({"dp": lax.rem(d + s, dpn)})
    for s in range(dpn):

        @pl.when((home != c) | (d != s))
        def _():
            greet({"dp": s, "ctx": home})

    self_sends = jnp.where(home == c, dpn - 1, dpn)
    pl.semaphore_wait(pltpu.get_barrier_semaphore(), cn - 1 + dpn - 1 + self_sends)
    totals = Swap(cn, tot, tot_in, tsem, local.at[0])
    totals.start()
    first = Swap(cn, qkv, qkv_all, qsem, local.at[1])
    first.start()

    def copy(r):
        g = c * dpn + r
        return remote(
            go.at[r],
            go_all.at[d],
            osem.at[0, r],
            osem.at[1, d],
            {"dp": g // cn, "ctx": lax.rem(g, cn)},
        )

    def own(r):
        return pltpu.make_async_copy(go.at[r], go_all.at[d], local.at[2])

    for r in range(dpn):
        here = c * dpn + r == mine

        @pl.when(jnp.logical_not(here))
        def _():
            copy(r).start()

        @pl.when(here)
        def _():
            own(r).start()

    second = Swap(cn, gu, gu_all, usem, local.at[3])
    second.start()
    totals.finish()
    tot_sum[...] = jnp.sum(tot_in[...], axis=0)

    def share(s):
        peer = lax.rem(d + s, dpn)
        return remote(
            tot_sum.at[peer], tot_last.at[d], dsem.at[0, s], dsem.at[1, s], {"dp": peer}
        )

    for s in range(1, dpn):
        share(s).start()
    tot_last[d] = tot_sum[d]
    for s in range(1, dpn):
        source = lax.rem(d - s + dpn, dpn)
        block = tot_last.at[source]
        remote(
            block, block, dsem.at[0, s], dsem.at[1, s], {"dp": source}
        ).wait_recv()
    for s in range(1, dpn):
        share(s).wait_send()
    tot_out[...] = jnp.sum(tot_last[...], axis=0)
    for s in range(dpn):
        block = go_all.at[s]
        here = (home == c) & (d == s)

        @pl.when(jnp.logical_not(here))
        def _():
            remote(
                block, block, osem.at[0, s], osem.at[1, s], {"dp": s, "ctx": home}
            ).wait_recv()

        @pl.when(here)
        def _():
            own(slot).wait()

    for r in range(dpn):

        @pl.when(c * dpn + r != mine)
        def _():
            copy(r).wait_send()

    first.finish()
    second.finish()


def call(kernel, outs, ins, specs_in, specs_out, scratch, number, flops=0, moved=0):
    return pl.pallas_call(
        kernel,
        out_shape=outs,
        in_specs=specs_in,
        out_specs=specs_out,
        scratch_shapes=scratch,
        compiler_params=pltpu.CompilerParams(
            collective_id=number, has_side_effects=True, vmem_limit_bytes=60 * 2**20
        ),
        cost_estimate=pl.CostEstimate(flops=flops, bytes_accessed=moved, transcendentals=0),
    )(*ins)


def shape(dims, dtype=bf16):
    return jax.ShapeDtypeStruct(dims, dtype)


def rope_tables(positions):
    half_dim = HEAD_DIM // 2
    inverse = jnp.exp(
        jnp.arange(half_dim, dtype=f32) * (-2.0 * math.log(rope_base) / HEAD_DIM)
    )
    angles = positions[:, None] * inverse[None, :]
    return jnp.cos(angles), jnp.sin(angles)


def rotate(values, cosines, sines, sign):
    half = HEAD_DIM // 2
    parts = []
    for h in range(values.shape[1] // HEAD_DIM):
        a = values[:, h * HEAD_DIM : h * HEAD_DIM + half]
        b = values[:, h * HEAD_DIM + half : (h + 1) * HEAD_DIM]
        parts += [a * cosines - sign * b * sines, b * cosines + sign * a * sines]
    return jnp.concatenate(parts, axis=1)


def gather(v, axes, axis=0):
    return lax.all_gather(v, axes, axis=axis, tiled=True)


def scatter_sum(v, axes):
    return lax.psum_scatter(v, axes, scatter_dimension=0, tiled=True)


def shards(
    hidden_in,
    out_grad,
    seg_ids,
    valid_mask,
    w_query,
    w_key,
    w_value,
    w_output,
    w_gate,
    w_up,
    w_down,
    gain_attn,
    gain_mlp,
):
    dpn = lax.axis_size("dp")
    cn = lax.axis_size("ctx")
    n = cn // 2
    x_local = hidden_in[0]
    dy_local = out_grad[0]
    rows, width = x_local.shape
    seq = rows * cn
    dr = w_query.shape[0]
    hw = width // cn
    heads = hw // HEAD_DIM
    ff_rows = w_down.shape[0]
    ff = ff_rows * dpn
    dma = pltpu.SemaphoreType.DMA
    mib = 2**20

    code = (seg_ids[0] * 2 + valid_mask[0]).astype(bf16)
    x_ext = jnp.concatenate([x_local, jnp.broadcast_to(code[:, None], (rows, 128))], axis=1)
    lanes = jnp.arange(128)[None, :]
    gain_cols = jnp.where(lanes == 0, gain_attn[:, None], gain_mlp[:, None]).astype(bf16)
    qkv_pack = jnp.concatenate(
        [w.astype(bf16).reshape(dr, cn, hw) for w in (w_query, w_key, w_value)]
        + [jnp.broadcast_to(gain_cols[:, None, :], (dr, cn, 128))],
        axis=2,
    ).transpose(1, 0, 2)
    pw = 3 * hw + 128
    x_all, qkv_rows = call(
        functools.partial(front_kernel, cn),
        (shape((cn, rows, width + 128)), shape((cn, dr, pw))),
        (x_ext, qkv_pack),
        [ANY] * 2,
        (ANY, ANY),
        [dma((5, n)), dma((2, cn)), dma((2,))],
        1,
        moved=160 * mib,
    )
    down = gather(w_down.astype(bf16), "dp")
    dys = gather(dy_local, "ctx")
    qkv_full = gather(qkv_rows.reshape(cn * dr, pw), "dp")
    qkv = qkv_full[:, : 3 * hw]
    gain_one = qkv_full[:, 3 * hw].astype(f32)[None]
    gain_two = qkv_full[:, 3 * hw + 1].astype(f32)[None]

    gu_pack = (
        jnp.concatenate(
            [w.astype(bf16).reshape(dr, dpn, cn, ff_rows) for w in (w_gate, w_up)], axis=1
        )
        .transpose(2, 0, 1, 3)
        .reshape(cn, dr, 2 * ff)
    )
    gu_rows, wo = call(
        functools.partial(spread_kernel, cn, dpn),
        (shape((cn, dr, 2 * ff)), shape((dpn, dr, width))),
        (gu_pack, w_output.astype(bf16)),
        [ANY] * 2,
        (ANY, ANY),
        [dma((2, cn)), dma((2, dpn)), dma((2,))],
        2,
        moved=200 * mib,
    )
    gate_up = gather(gu_rows.reshape(cn * dr, 2 * ff), "dp")
    wo = wo.reshape(hw, width)

    all_codes = x_all[:, :, width].reshape(seq).astype(jnp.int32)
    seg = all_codes // 2
    valid = all_codes % 2
    index = jnp.arange(seq, dtype=jnp.int32)
    starts = jnp.sum((seg[None, :] < seg[:, None]).astype(jnp.int32), axis=1)
    cosines, sines = rope_tables((index - starts).astype(f32))
    allowed = (
        (seg[:, None] == seg[None, :])
        & (index[None, :] <= index[:, None])
        & (valid[None, :] == 1)
    )

    xs = x_all[:, :, :width].reshape(seq, width).astype(f32)
    an = (xs * rms(xs) * gain_one).astype(bf16)
    proj = dot(an, qkv)
    q = rotate(proj[:, :hw], cosines, sines, 1.0).astype(bf16)
    k = rotate(proj[:, hw : 2 * hw], cosines, sines, 1.0).astype(bf16)
    v = proj[:, 2 * hw :].astype(bf16)

    def per_head(t, h):
        return t[:, h * HEAD_DIM : (h + 1) * HEAD_DIM]

    outs = []
    mass = jnp.zeros((seq,), f32)
    for h in range(heads):
        s = dot(per_head(q, h), per_head(k, h), contract_cols) * score_scale - score_shift
        p = jnp.where(allowed, jax.nn.sigmoid(s), 0.0)
        mass = mass + jnp.sum(p, axis=1)
        outs.append(dot(p.astype(bf16), per_head(v, h)))
    o = jnp.concatenate(outs, axis=1).astype(bf16)

    line_scratch = sum_scratch(cn, rows, width)
    h1, bn = call(
        functools.partial(middle_kernel, cn),
        (shape((rows, width), f32), shape((cn, rows, width))),
        (o, wo, x_local, gain_two),
        [VMEM] * 4,
        (VMEM, ANY),
        [pltpu.VMEM((rows, width), bf16), dma((5, n)), dma] + line_scratch,
        3,
        moved=240 * mib,
    )
    bn = bn.reshape(seq, width)
    gu = dot(bn, gate_up)
    gate = gu[:, :ff]
    up = gu[:, ff:]
    sig = jax.nn.sigmoid(gate)
    silu = gate * sig
    hid = (silu * up).astype(bf16)
    dhid = dot(dys, down, contract_cols)
    dgate = (dhid * up * sig * (1.0 + gate * (1.0 - sig))).astype(bf16)
    dup = (dhid * silu).astype(bf16)
    dgu = jnp.concatenate([dgate, dup], axis=1)
    g_gu = scatter_sum(dot(bn, dgu, contract_rows).astype(bf16), "dp")
    g_down = scatter_sum(dot(hid, dys, contract_rows).astype(bf16), "dp")
    dh1, dob, term_two = call(
        functools.partial(back_kernel, cn),
        (shape((rows, width), f32), shape((cn, rows, width)), shape((1, width), f32)),
        (dgu, gate_up, h1, dy_local, gain_two),
        [VMEM] * 5,
        (VMEM, ANY, VMEM),
        [pltpu.VMEM((rows, width), bf16), dma((5, n)), dma] + line_scratch,
        4,
        moved=240 * mib,
    )
    dob = dob.reshape(seq, width)
    do = dot(dob, wo, contract_cols).astype(bf16)
    dqs, dks, dvs = [], [], []
    for h in range(heads):
        qh, kh, vh, doh = (per_head(t, h) for t in (q, k, v, do))
        s = dot(qh, kh, contract_cols) * score_scale - score_shift
        sg = jnp.where(allowed, jax.nn.sigmoid(s), 0.0)
        pb = sg.astype(bf16)
        ds = (dot(doh, vh, contract_cols) * sg * (1.0 - sg)).astype(bf16)
        dqs.append(dot(ds, kh) * score_scale)
        dks.append(dot(ds, qh, contract_rows) * score_scale)
        dvs.append(dot(pb, doh, contract_rows))
    dq = rotate(jnp.concatenate(dqs, axis=1), cosines, sines, -1.0).astype(bf16)
    dk = rotate(jnp.concatenate(dks, axis=1), cosines, sines, -1.0).astype(bf16)
    dv = jnp.concatenate(dvs, axis=1).astype(bf16)
    dqkv = jnp.concatenate([dq, dk, dv], axis=1)
    g_qkv = scatter_sum(dot(an, dqkv, contract_rows).astype(bf16), "dp")
    g_out = dot(o, dob, contract_rows).astype(bf16)
    grad_input, result, term_one = call(
        functools.partial(last_kernel, cn),
        (shape((rows, width)), shape((rows, width)), shape((1, width), f32)),
        (dqkv, qkv, dh1, x_local, gain_one, hid, down, h1),
        [VMEM] * 8,
        (VMEM, VMEM, VMEM),
        line_scratch + line_scratch,
        5,
        moved=240 * mib,
    )

    mass_part = jnp.sum(valid.astype(f32) * mass) / (heads * cn)
    pieces = [t.reshape(dpn, cn, dr).transpose(1, 0, 2) for t in (term_one, term_two)]
    pieces.append(jnp.broadcast_to(mass_part, (cn, dpn, dr)))
    tot = jnp.zeros((cn, dpn, 8, 128), f32).at[:, :, :3, :dr].set(jnp.stack(pieces, axis=2))
    q_all, u_all, o_all, totals = call(
        functools.partial(return_kernel, cn, dpn),
        (
            shape((cn, dr, 3 * hw)),
            shape((cn, dr, 2 * ff)),
            shape((dpn, dr, width)),
            shape((8, 128), f32),
        ),
        (
            g_qkv.reshape(cn, dr, 3 * hw),
            g_gu.reshape(cn, dr, 2 * ff),
            g_out.reshape(dpn, dr, width),
            tot,
        ),
        [ANY] * 3 + [VMEM],
        (ANY, ANY, ANY, VMEM),
        [
            pltpu.VMEM((cn, dpn, 8, 128), f32),
            pltpu.VMEM((dpn, 8, 128), f32),
            pltpu.VMEM((dpn, 8, 128), f32),
            dma((2, cn)),
            dma((2, cn)),
            dma((2, dpn)),
            dma((2, cn)),
            dma((2, dpn)),
            dma((4,)),
        ],
        6,
        moved=240 * mib,
    )
    q_all = q_all.astype(f32)
    u_all = u_all.astype(f32)
    g_q, g_k, g_v = (
        q_all[:, :, i * hw : (i + 1) * hw].transpose(1, 0, 2).reshape(dr, width) for i in range(3)
    )
    g_gate, g_up = (
        u_all[:, :, i * ff : (i + 1) * ff]
        .reshape(cn, dr, dpn, ff_rows)
        .transpose(1, 2, 0, 3)
        .reshape(dr, dpn * cn * ff_rows)
        for i in range(2)
    )
    mass_mean = totals[2, 0] / (dpn * seq)
    return (
        result[None],
        grad_input[None],
        g_q,
        g_k,
        g_v,
        jnp.sum(o_all.astype(f32), axis=0),
        g_gate,
        g_up,
        g_down.astype(f32),
        totals[0, :dr],
        totals[1, :dr],
        mass_mean,
    )


def solution(mesh):
    tok = P("dp", "ctx", None)
    ids = P("dp", "ctx")
    mat = P(("dp", "ctx"), None)
    vec = P(("dp", "ctx"))
    return jax.shard_map(
        shards,
        mesh=mesh,
        in_specs=(tok, tok, ids, ids) + (mat,) * 7 + (vec, vec),
        out_specs=(tok, tok) + (mat,) * 7 + (vec, vec, P()),
        check_vma=False,
    )
```

```python
import functools
import math

import jax
import jax.numpy as jnp
from jax import lax
from jax.experimental import pallas as pl
from jax.experimental.pallas import tpu as pltpu
from jax.sharding import PartitionSpec as P

HEAD_DIM = 128
norm_eps = 1e-05
rope_base = 10000.0
score_shift = math.log(4096.0)
score_scale = 1.0 / math.sqrt(HEAD_DIM)
contract_rows = (((0,), (0,)), ((), ()))
contract_cols = (((1,), (1,)), ((), ()))
plain = (((1,), (0,)), ((), ()))
f32 = jnp.float32
bf16 = jnp.bfloat16
MESH = pl.DeviceIdType.MESH
ANY = pl.BlockSpec(memory_space=pl.ANY)
VMEM = pl.BlockSpec(memory_space=pltpu.VMEM)


def dot(a, b, dims=plain):
    return lax.dot_general(a, b, dims, preferred_element_type=f32)


def remote(src, dst, send, recv, target):
    return pltpu.make_async_remote_copy(
        src_ref=src,
        dst_ref=dst,
        send_sem=send,
        recv_sem=recv,
        device_id=target,
        device_id_type=MESH,
    )


def greet(target):
    pl.semaphore_signal(
        pltpu.get_barrier_semaphore(), inc=1, device_id=target, device_id_type=MESH
    )


def place(cn):
    c = lax.axis_index("ctx")
    j, k = c // 2, c % 2
    return c, j, k, cn // 2, 2 * j + 1 - k


def greet_line(cn, ring):
    c, j, _, n, sib = place(cn)
    ring.greet()
    greet({"ctx": sib})

    @pl.when(j < n - 1)
    def _():
        greet({"ctx": c + 2})

    @pl.when(j > 0)
    def _():
        greet({"ctx": c - 2})

    inner = jnp.where(j > 0, 1, 0) + jnp.where(j < n - 1, 1, 0)
    pl.semaphore_wait(pltpu.get_barrier_semaphore(), 3 + inner)


def greet_ctx(cn):
    c = lax.axis_index("ctx")
    for s in range(1, cn):
        greet({"ctx": lax.rem(c + s, cn)})


class LineGather:
    def __init__(self, cn, own, full, sem):
        self.cn, self.own, self.full, self.sem = cn, own, full, sem

    def copy(self, src, origin, kind, target):
        _, _, k, _, _ = place(self.cn)
        sem = self.sem
        return remote(
            src,
            self.full.at[2 * origin + k],
            sem.at[kind, origin],
            sem.at[3 if kind < 2 else 4, origin],
            {"ctx": target},
        )

    def start(self):
        c, j, _, n, sib = place(self.cn)

        @pl.when(j < n - 1)
        def _():
            self.copy(self.own, j, 0, c + 2).start()

        @pl.when(j > 0)
        def _():
            self.copy(self.own, j, 1, c - 2).start()

        self.copy(self.own, j, 2, sib).start()

    def forward(self, first=1, last=None):
        c, j, k, n, sib = place(self.cn)
        for s in range(first, n if last is None else last + 1):

            @pl.when(j - s >= 0)
            def _():
                o = j - s
                block = self.full.at[2 * o + k]
                self.copy(block, o, 0, sib).wait_recv()

                @pl.when(j < n - 1)
                def _():
                    self.copy(block, o, 0, c + 2).start()

                self.copy(block, o, 2, sib).start()

            @pl.when(j + s <= n - 1)
            def _():
                o = j + s
                block = self.full.at[2 * o + k]
                self.copy(block, o, 1, sib).wait_recv()

                @pl.when(j > 0)
                def _():
                    self.copy(block, o, 1, c - 2).start()

                self.copy(block, o, 2, sib).start()

    def finish(self):
        c, j, k, n, sib = place(self.cn)
        for o in range(n):
            block = self.full.at[2 * o + 1 - k]
            remote(
                block, block, self.sem.at[2, o], self.sem.at[4, o], {"ctx": sib}
            ).wait_recv()
        for o in range(n):
            block = self.full.at[2 * o + k]

            @pl.when((j < n - 1) & (o <= j))
            def _():
                self.copy(block, o, 0, sib).wait_send()

            @pl.when((j > 0) & (o >= j))
            def _():
                self.copy(block, o, 1, sib).wait_send()

            self.copy(block, o, 2, sib).wait_send()


class Swap:
    def __init__(self, cn, src, dst, sem, local, pick=None):
        self.cn, self.sem, self.local = cn, sem, local
        self.src = pick or (lambda c: src.at[c])
        self.dst = dst if callable(dst) else lambda c: dst.at[c]

    def copy(self, s):
        c = lax.axis_index("ctx")
        peer = lax.rem(c + s, self.cn)
        return remote(
            self.src(peer),
            self.dst(c),
            self.sem.at[0, s],
            self.sem.at[1, s],
            {"ctx": peer},
        )

    def start(self):
        c = lax.axis_index("ctx")
        for s in range(1, self.cn):
            self.copy(s).start()
        pltpu.make_async_copy(self.src(c), self.dst(c), self.local).start()

    def finish(self):
        c = lax.axis_index("ctx")
        pltpu.make_async_copy(self.src(c), self.dst(c), self.local).wait()
        for s in range(1, self.cn):
            source = lax.rem(c - s + self.cn, self.cn)
            block = self.dst(source)
            remote(
                block, block, self.sem.at[0, s], self.sem.at[1, s], {"ctx": source}
            ).wait_recv()
            self.copy(s).wait_send()


class RingGather:
    def __init__(self, dpn, own, full, sem):
        self.dpn, self.own, self.full, self.sem = dpn, own, full, sem
        self.hops = dpn // 2
        d = lax.axis_index("dp")
        self.p = d // 2 * 2 + lax.rem(lax.rem(d, 2) + d // 2, 2)

    def member(self, step):
        p = lax.rem(self.p + step + self.dpn, self.dpn)
        return p // 2 * 2 + lax.rem(lax.rem(p, 2) + p // 2, 2)

    def half(self, ref, h, right):
        if h < self.hops:
            return ref
        m = self.full.shape[1] // 2
        return ref.at[pl.ds(0 if right else m, m)]

    def copy(self, h, right):
        way = 1 if right else -1
        origin = self.member(-way * (h - 1))
        src = self.own if h == 1 else self.full.at[origin]
        return remote(
            self.half(src, h, right),
            self.half(self.full.at[origin], h, right),
            self.sem.at[0 if right else 1, h],
            self.sem.at[2 if right else 3, h],
            {"dp": self.member(way)},
        )

    def arrival(self, h, right):
        way = 1 if right else -1
        block = self.half(self.full.at[self.member(-way * h)], h, right)
        return remote(
            block,
            block,
            self.sem.at[0 if right else 1, h],
            self.sem.at[2 if right else 3, h],
            {"dp": self.member(way)},
        )

    def greet(self):
        greet({"dp": self.member(1)})
        greet({"dp": self.member(-1)})

    def start(self):
        self.copy(1, True).start()
        self.copy(1, False).start()

    def forward(self):
        for h in range(1, self.hops):
            for right in (True, False):
                self.arrival(h, right).wait_recv()
                self.copy(h + 1, right).start()

    def finish(self):
        for right in (True, False):
            self.arrival(self.hops, right).wait_recv()
        for h in range(1, self.hops + 1):
            for right in (True, False):
                self.copy(h, right).wait_send()


class RingSum:
    def __init__(self, dpn, blocks, got, sem):
        self.dpn, self.blocks, self.got, self.sem = dpn, blocks, got, sem
        self.ring = RingGather(dpn, None, blocks, sem)
        self.hops = dpn // 2

    def part(self, s, right):
        m = self.blocks.shape[1] // 2
        if s > 1:
            return pl.ds(0, 2 * m)
        return pl.ds(0 if right else m, m)

    def copy(self, s, right):
        way = 1 if right else -1
        target = self.ring.member(way * (self.hops - s + 1))
        at = self.part(s, right)
        return remote(
            self.blocks.at[target, at],
            self.got.at[0 if right else 1, s - 1, at],
            self.sem.at[0 if right else 1, s],
            self.sem.at[2 if right else 3, s],
            {"dp": self.ring.member(way)},
        )

    def order(self):
        out = [self.ring.member(self.hops)]
        for s in range(self.hops - 1, 0, -1):
            out += [self.ring.member(s), self.ring.member(-s)]
        return out + [self.ring.member(0)]

    def start(self):
        self.copy(1, True).start()
        self.copy(1, False).start()

    def take(self, s, right, target):
        self.copy(s, right).wait_recv()
        at = self.part(s, right)
        side = 0 if right else 1
        block = self.blocks.at[target, at]
        block[...] = (block[...].astype(f32) + self.got[side, s - 1, at].astype(f32)).astype(bf16)

    def forward(self, s):
        for right in (True, False):
            way = 1 if right else -1
            self.take(s, right, self.ring.member(way * (self.hops - s)))
            self.copy(s + 1, right).start()

    def finish(self, out):
        for right in (True, False):
            self.copy(self.hops, right).wait_recv()
        mine = self.ring.member(0)
        if self.hops > 1:
            total = self.blocks[mine].astype(f32)
            for side in (0, 1):
                total = total + self.got[side, self.hops - 1].astype(f32)
            out[...] = total.reshape(out.shape).astype(out.dtype)
        for s in range(1, self.hops + 1):
            for right in (True, False):
                self.copy(s, right).wait_send()


def ring_scratch(dpn, m, width):
    return [
        pltpu.VMEM((dpn, m, width), bf16),
        pltpu.VMEM((2, dpn // 2, m, width), bf16),
        pltpu.SemaphoreType.DMA((4, dpn // 2 + 1)),
    ]


def outer(a_ref, b_ref, out, at, tile=512):
    a = a_ref[:, at]
    width = out.shape[-1]
    for lo in range(0, width, tile):
        to = slice(lo, min(lo + tile, width))
        out[:, to] = dot(a, b_ref[:, to], contract_rows).astype(bf16)


def outer_all(a_ref, b_ref, blocks, tile=512):
    count, m, width = blocks.shape
    many = max(1, 128 // m)
    for first in range(0, count, many):
        a = a_ref[:, first * m : (first + many) * m]
        for lo in range(0, width, tile):
            to = slice(lo, min(lo + tile, width))
            part = dot(a, b_ref[:, to], contract_rows).astype(bf16)
            for i in range(many):
                blocks[first + i, :, to] = part[i * m : (i + 1) * m]


class LineSum:
    def __init__(self, cn, compute, part, cross, cross_in, flow, arrived, sem):
        self.cn, self.compute, self.part = cn, compute, part
        self.cross, self.cross_in, self.flow = cross, cross_in, flow
        self.arrived, self.sem = arrived, sem

    def across(self, t):
        _, _, _, _, sib = place(self.cn)
        return remote(
            self.cross.at[t],
            self.cross_in.at[t],
            self.sem.at[0, t],
            self.sem.at[2, t],
            {"ctx": sib},
        )

    def along(self, t, slot, target):
        return remote(
            self.flow.at[t],
            self.arrived.at[slot],
            self.sem.at[1, t],
            self.sem.at[3, slot],
            {"ctx": target},
        )

    def produce(self, t, slot):
        _, _, k, _, _ = place(self.cn)
        part = self.part.at[slot]
        self.compute(t, part)
        self.cross[t] = part[1 - k].astype(bf16)
        self.across(t).start()

    def collect(self, t, slot):
        _, j, k, n, sib = place(self.cn)
        part = self.part.at[slot, k]
        self.across(t).wait_recv()
        part[...] += self.cross_in[t].astype(f32)

        @pl.when((j > 0) & (t >= j))
        def _():
            self.along(t, t, sib).wait_recv()
            part[...] += self.arrived[t].astype(f32)

        @pl.when((j < n - 1) & (t <= j))
        def _():
            slot_in = jnp.where(t == j, n, t)
            self.along(t, slot_in, sib).wait_recv()
            part[...] += self.arrived[slot_in].astype(f32)

    def send(self, t, slot, up):
        c, j, k, n, _ = place(self.cn)
        self.flow[t] = self.part[slot, k].astype(bf16)
        there = t if up else jnp.where(t == j - 1, n, t)
        self.along(t, there, c + 2 if up else c - 2).start()

    def drain(self):
        _, j, _, n, sib = place(self.cn)

        @pl.loop(0, n)
        def _(t):
            self.across(t).wait_send()

            @pl.when(t != j)
            def _():
                self.along(t, t, sib).wait_send()


def line_sums(cn, sums, between=None):
    _, j, _, n, _ = place(cn)

    @pl.loop(0, n - 1)
    def _(s):
        to_up, to_down = n - 1 - s + j, s - (n - 1 - j)
        for total in sums:

            @pl.when(s >= j)
            def _():
                total.produce(to_up, 0)

            @pl.when(s >= n - 1 - j)
            def _():
                total.produce(to_down, 1)

        for total in sums:

            @pl.when(s >= j)
            def _():
                total.collect(to_up, 0)
                total.send(to_up, 0, True)

            @pl.when(s >= n - 1 - j)
            def _():
                total.collect(to_down, 1)
                total.send(to_down, 1, False)

        if between is not None:
            between(s)

    for total in sums:
        total.produce(j, 0)
    for total in sums:
        total.collect(j, 0)


def sum_scratch(cn, rows, width):
    n = cn // 2
    return [
        pltpu.VMEM((2, 2, rows, width), f32),
        pltpu.VMEM((n, rows, width), bf16),
        pltpu.VMEM((n, rows, width), bf16),
        pltpu.VMEM((n, rows, width), bf16),
        pltpu.VMEM((n + 1, rows, width), bf16),
        pltpu.SemaphoreType.DMA((4, n + 1)),
    ]


def product(a_ref, b_ref, dims, rows, width):
    tile = min(512, width)

    def compute(t, out):
        a = a_ref[pl.ds(pl.multiple_of(t * 2 * rows, 2 * rows), 2 * rows), :]

        @pl.loop(0, width // tile)
        def _(i):
            at = pl.ds(pl.multiple_of(i * tile, tile), tile)
            b = b_ref[:, at] if dims == plain else b_ref[at, 0 : a_ref.shape[1]]
            out[:, :, at] = dot(a, b, dims).reshape(2, rows, tile)

    return compute


def rms(v):
    return lax.rsqrt(jnp.mean(v * v, axis=-1, keepdims=True) + norm_eps)


def front_kernel(
    cn, dpn, x, pack, down, x_all, pack_all, down_all, gsem, ssem, rsem, dsem, local
):
    c, d = lax.axis_index("ctx"), lax.axis_index("dp")
    mine = pack_all.at[d]
    swap = Swap(cn, pack, mine, ssem, local.at[0])
    gather = LineGather(cn, x, x_all, gsem)
    ring = RingGather(dpn, mine, pack_all, rsem)
    down_ring = RingGather(dpn, down, down_all, dsem)
    greet_ctx(cn)
    ring.greet()
    pl.semaphore_wait(pltpu.get_barrier_semaphore(), cn - 1 + 2)
    swap.start()
    gather.start()
    down_ring.start()
    keep = pltpu.make_async_copy(x, x_all.at[c], local.at[1])
    keep.start()
    keep_down = pltpu.make_async_copy(down, down_all.at[d], local.at[2])
    keep_down.start()
    gather.forward(1, 1)
    swap.finish()
    ring.start()
    down_ring.forward()
    gather.forward(2)
    ring.forward()
    keep.wait()
    keep_down.wait()
    gather.finish()
    ring.finish()
    down_ring.finish()


def project(x_all, w, gain, cosines, sines, an, qkv, hw, block):
    width = an.shape[1]
    per = block // x_all.shape[1]

    @pl.loop(0, an.shape[0] // block)
    def _(i):
        at = pl.ds(pl.multiple_of(i * block, block), block)
        x = x_all[pl.ds(i * per, per), :, 0:width].reshape(block, width).astype(f32)
        normed = (x * rms(x) * gain[...]).astype(bf16)
        an[at, :] = normed
        proj = dot(normed, w[:, 0 : 3 * hw])
        cos_b, sin_b = cosines[at, :], sines[at, :]
        for h in range(2 * hw // HEAD_DIM):
            lanes = slice(h * HEAD_DIM, (h + 1) * HEAD_DIM)
            v = proj[:, lanes]
            turned = v * cos_b + pltpu.roll(v, HEAD_DIM // 2, 1) * sin_b
            qkv[at, lanes] = turned.astype(bf16)
        qkv[at, 2 * hw :] = proj[:, 2 * hw :].astype(bf16)


def mask_block(q_seg, k_code, i, j, block):
    rows = lax.broadcasted_iota(jnp.int32, (block, block), 0) + i * block
    cols = lax.broadcasted_iota(jnp.int32, (block, block), 1) + j * block
    return (q_seg == k_code) & (cols <= rows)


def attend(qkv, q_info, k_code, out, mass, hw, block):
    mass[...] = jnp.zeros_like(mass)

    @pl.loop(0, qkv.shape[0] // block)
    def _(i):
        at = pl.ds(pl.multiple_of(i * block, block), block)
        q_seg, q_valid = q_info[at, 0:1], q_info[at, 1:2].astype(f32)
        for h in range(hw // HEAD_DIM):
            lane = [slice(t * hw + h * HEAD_DIM, t * hw + (h + 1) * HEAD_DIM) for t in range(3)]
            q = qkv[at, lane[0]]

            def step(j, acc):
                to = pl.ds(pl.multiple_of(j * block, block), block)
                s = dot(q, qkv[to, lane[1]], contract_cols) * score_scale - score_shift
                allowed = mask_block(q_seg, k_code[0:1, to], i, j, block)
                p = jnp.where(allowed, jax.nn.sigmoid(s), 0.0)
                mass[...] += jnp.sum(p * q_valid, axis=0, keepdims=True)
                return acc + dot(p.astype(bf16), qkv[to, lane[2]])

            acc = lax.fori_loop(0, i + 1, step, jnp.zeros((block, HEAD_DIM), f32))
            out[at, lane[0]] = acc.astype(bf16)


def attn_kernel(
    cn, dpn, x_all, w, gain, cosines, sines, q_info, k_code, gate, up, wo,
    an, qkv, o, mass, gate_all, up_own, wo_all, ssem, rsem, hsem, wsem, local,
):
    c, d = lax.axis_index("ctx"), lax.axis_index("dp")
    mine, wanted = d * cn + c, c * dpn + d
    stays = mine == wanted
    hop = remote(
        wo,
        wo_all.at[lax.rem(mine, dpn)],
        hsem.at[0],
        hsem.at[1],
        {"dp": lax.rem(mine, dpn), "ctx": mine // dpn},
    )
    keep = pltpu.make_async_copy(wo, wo_all.at[d], local.at[2])
    wo_ring = RingGather(dpn, wo_all.at[d], wo_all, wsem)
    rows = x_all.shape[1]
    hw = qkv.shape[1] // 3
    swap_gate = Swap(cn, gate, gate_all.at[d], ssem.at[0], local.at[0])
    swap_up = Swap(cn, up, up_own, ssem.at[1], local.at[1])
    ring = RingGather(dpn, gate_all.at[d], gate_all, rsem)
    greet_ctx(cn)
    ring.greet()

    @pl.when(jnp.logical_not(stays))
    def _():
        greet({"dp": wanted // cn, "ctx": lax.rem(wanted, cn)})

    pl.semaphore_wait(
        pltpu.get_barrier_semaphore(), cn - 1 + 2 + jnp.where(stays, 0, 1)
    )

    @pl.when(stays)
    def _():
        keep.start()
        keep.wait()

    @pl.when(jnp.logical_not(stays))
    def _():
        hop.start()

    swap_gate.start()
    swap_up.start()

    @pl.when(jnp.logical_not(stays))
    def _():
        arrived = wo_all.at[d]
        remote(arrived, arrived, hsem.at[0], hsem.at[1], {"dp": d, "ctx": c}).wait_recv()

    wo_ring.start()
    project(x_all, w, gain, cosines, sines, an, qkv, hw, 2 * rows)
    wo_ring.forward()
    swap_gate.finish()
    ring.start()
    attend(qkv, q_info, k_code, o, mass, hw, 2 * rows)
    ring.forward()
    swap_up.finish()
    wo_ring.finish()
    ring.finish()

    @pl.when(jnp.logical_not(stays))
    def _():
        hop.wait_send()


def middle_kernel(
    cn, dpn, o, wo, x, gain, up, h1, bn_all, up_all, own, gsem, rsem, local, *sum_refs
):
    c, d = lax.axis_index("ctx"), lax.axis_index("dp")
    _, _, k, n, _ = place(cn)
    rows, width = x.shape
    gather = LineGather(cn, own, bn_all, gsem)
    ring = RingGather(dpn, up, up_all, rsem)
    total = LineSum(cn, product(o, wo, plain, rows, width), *sum_refs)
    greet_line(cn, ring)
    ring.start()
    keep_up = pltpu.make_async_copy(up, up_all.at[d], local.at[0])
    keep_up.start()
    line_sums(cn, [total])
    mid = x[...].astype(f32) + total.part[0, k]
    h1[...] = mid
    own[...] = (mid * rms(mid) * gain[...]).astype(bf16)
    gather.start()
    keep = pltpu.make_async_copy(own, bn_all.at[c], local.at[1])
    keep.start()
    ring.forward()
    gather.forward()
    total.drain()
    keep.wait()
    keep_up.wait()
    gather.finish()
    ring.finish()


def back_kernel(
    cn, dpn, bn, dgu, wg, wu, h1, dy, gain, dh1, dob_all, term, g_own,
    own, gsem, lsem, *scratch,
):
    sum_refs, ring_refs = scratch[:-3], scratch[-3:]
    rows, width = dy.shape
    ff = wg.shape[1]
    tile = min(512, width)
    c, _, k, n, _ = place(cn)

    def compute(t, out):
        at = pl.ds(pl.multiple_of(t * 2 * rows, 2 * rows), 2 * rows)

        @pl.loop(0, width // tile)
        def _(i):
            to = pl.ds(pl.multiple_of(i * tile, tile), tile)
            part = dot(dgu[at, 0:ff], wg[to, :], contract_cols)
            part = part + dot(dgu[at, ff:], wu[to, :], contract_cols)
            out[:, :, to] = part.reshape(2, rows, tile)

    total = LineSum(cn, compute, *sum_refs)
    ring = RingSum(dpn, *ring_refs)
    blocks = ring_refs[0]
    m = blocks.shape[1]
    greet_line(cn, ring.ring)
    order = ring.order()

    def weight_grad(member):
        outer(bn, dgu, blocks.at[member], pl.ds(pl.multiple_of(member * m, m), m))

    weight_grad(order[0])
    ring.start()

    def between(s):
        for i in range(ring.hops - 1):

            @pl.when(s == min(i, n - 2))
            def _():
                weight_grad(order[1 + 2 * i])
                weight_grad(order[2 + 2 * i])

            @pl.when(s == min(i + 1, n - 2))
            def _():
                ring.forward(i + 1)

    line_sums(cn, [total], between)
    dbn = total.part[0, k]
    mid = h1[...]
    r2 = rms(mid)
    xh2 = mid * r2
    term[...] = jnp.sum(dbn * xh2, axis=0, keepdims=True)
    u2 = dbn * gain[...]
    grad = dy[...].astype(f32) + r2 * (u2 - xh2 * jnp.mean(u2 * xh2, axis=-1, keepdims=True))
    dh1[...] = grad
    own[...] = grad.astype(bf16)
    gather = LineGather(cn, own, dob_all, gsem)
    gather.start()
    keep = pltpu.make_async_copy(own, dob_all.at[c], lsem)
    keep.start()
    weight_grad(order[-1])
    gather.forward()
    total.drain()
    keep.wait()
    gather.finish()
    ring.finish(g_own)


def attend_back(qkv, do, cosines, sines, q_info, k_info, dq, dqkv, hw, block):
    count = qkv.shape[0] // block
    dq[...] = jnp.zeros_like(dq)

    def turn_back(g, at):
        return g * cosines[at, :] - pltpu.roll(g, HEAD_DIM // 2, 1) * sines[at, :]

    @pl.loop(0, count)
    def _(j):
        to = pl.ds(pl.multiple_of(j * block, block), block)
        k_code = k_info[to, :]
        for h in range(hw // HEAD_DIM):
            lane = [slice(t * hw + h * HEAD_DIM, t * hw + (h + 1) * HEAD_DIM) for t in range(3)]
            k, v = qkv[to, lane[1]], qkv[to, lane[2]]

            def step(i, carry):
                dk, dv = carry
                at = pl.ds(pl.multiple_of(i * block, block), block)
                q, do_i = qkv[at, lane[0]], do[at, lane[0]]
                s = dot(k, q, contract_cols) * score_scale - score_shift
                keys = lax.broadcasted_iota(jnp.int32, (block, block), 0) + j * block
                queries = lax.broadcasted_iota(jnp.int32, (block, block), 1) + i * block
                allowed = (k_code == q_info[0:1, at]) & (keys <= queries)
                sg = jnp.where(allowed, jax.nn.sigmoid(s), 0.0)
                dp = dot(v, do_i, contract_cols)
                ds = (dp * sg * (1.0 - sg)).astype(bf16)
                dq[at, lane[0]] += dot(ds, k, contract_rows)
                return dk + dot(ds, q), dv + dot(sg.astype(bf16), do_i)

            zero = jnp.zeros((block, HEAD_DIM), f32)
            dk, dv = lax.fori_loop(j, count, step, (zero, zero))
            dqkv[to, lane[1]] = turn_back(dk * score_scale, to).astype(bf16)
            dqkv[to, lane[2]] = dv.astype(bf16)

    @pl.loop(0, count)
    def _(i):
        at = pl.ds(pl.multiple_of(i * block, block), block)
        for h in range(hw // HEAD_DIM):
            lanes = slice(h * HEAD_DIM, (h + 1) * HEAD_DIM)
            dqkv[at, lanes] = turn_back(dq[at, lanes] * score_scale, at).astype(bf16)


def last_kernel(
    cn, dpn, do, g_gu, g_down, g_out, qkv, cosines, sines, q_info, k_info, an, w, dh1, x, gain,
    grad_in, term, gu_all, down_own, out_own, qkv_own,
    dq, dqkv, usem, local, *scratch,
):
    sum_refs, rings = scratch[:-9], (scratch[-9:-6], scratch[-6:-3], scratch[-3:])
    rows, width = x.shape
    hw = width // cn
    _, _, k, n, _ = place(cn)
    down_ring, out_ring, qkv_ring = (RingSum(dpn, *refs) for refs in rings)
    swap_gu = Swap(cn, g_gu, gu_all, usem, local.at[0])
    greet_ctx(cn)
    down_ring.ring.greet()
    pl.semaphore_wait(pltpu.get_barrier_semaphore(), cn - 1 + 2)
    swap_gu.start()
    fill_down = pltpu.make_async_copy(g_down, rings[0][0], local.at[1])
    fill_out = pltpu.make_async_copy(g_out, rings[1][0], local.at[2])
    fill_down.start()
    fill_out.start()
    fill_down.wait()
    down_ring.start()
    fill_out.wait()
    out_ring.start()
    m_qkv = rings[2][0].shape[1]
    order = qkv_ring.order()

    def grad_qkv(member):
        outer(an, dqkv, rings[2][0].at[member], pl.ds(pl.multiple_of(member * m_qkv, m_qkv), m_qkv))

    attend_back(qkv, do, cosines, sines, q_info, k_info, dq, dqkv, hw, 2 * rows)
    for i in range(down_ring.hops - 1):
        down_ring.forward(i + 1)
        out_ring.forward(i + 1)
    grad_qkv(order[0])
    qkv_ring.start()
    total = LineSum(cn, product(dqkv, w, contract_cols, rows, width), *sum_refs)

    def between(s):
        for i in range(qkv_ring.hops - 1):

            @pl.when(s == min(i, n - 2))
            def _():
                grad_qkv(order[1 + 2 * i])
                grad_qkv(order[2 + 2 * i])

            @pl.when(s == min(i + 1, n - 2))
            def _():
                qkv_ring.forward(i + 1)

    line_sums(cn, [total], between)
    grad_qkv(order[-1])
    dan = total.part[0, k]
    xf = x[...].astype(f32)
    r1 = rms(xf)
    xh1 = xf * r1
    term[...] = jnp.sum(dan * xh1, axis=0, keepdims=True)
    u1 = dan * gain[...]
    grad = dh1[...] + r1 * (u1 - xh1 * jnp.mean(u1 * xh1, axis=-1, keepdims=True))
    grad_in[...] = grad.astype(bf16)
    total.drain()
    down_ring.finish(down_own)
    out_ring.finish(out_own)
    qkv_ring.finish(qkv_own)
    swap_gu.finish()


def return_kernel(
    cn, dpn, qkv, out, tot, qkv_all, out_all, tot_out,
    tot_in, tot_sum, tot_last, qsem, tsem, dsem, osem, local,
):
    c, d = lax.axis_index("ctx"), lax.axis_index("dp")
    mine, goal = d * cn + c, c * dpn + d
    stays = mine == goal
    greet_ctx(cn)

    @pl.when(jnp.logical_not(stays))
    def _():
        greet({"dp": lax.rem(mine, dpn), "ctx": mine // dpn})

    hop = remote(
        out, out_all, osem.at[0], osem.at[1], {"dp": goal // cn, "ctx": lax.rem(goal, cn)}
    )
    keep = pltpu.make_async_copy(out, out_all, local.at[2])
    for s in range(1, dpn):
        greet({"dp": lax.rem(d + s, dpn)})
    pl.semaphore_wait(
        pltpu.get_barrier_semaphore(), cn - 1 + dpn - 1 + jnp.where(stays, 0, 1)
    )

    @pl.when(stays)
    def _():
        keep.start()

    @pl.when(jnp.logical_not(stays))
    def _():
        hop.start()

    totals = Swap(cn, tot, tot_in, tsem, local.at[0])
    totals.start()
    first = Swap(cn, qkv, qkv_all, qsem, local.at[1])
    first.start()
    totals.finish()
    tot_sum[...] = jnp.sum(tot_in[...], axis=0)

    def share(s):
        peer = lax.rem(d + s, dpn)
        return remote(
            tot_sum.at[peer], tot_last.at[d], dsem.at[0, s], dsem.at[1, s], {"dp": peer}
        )

    for s in range(1, dpn):
        share(s).start()
    tot_last[d] = tot_sum[d]
    for s in range(1, dpn):
        source = lax.rem(d - s + dpn, dpn)
        block = tot_last.at[source]
        remote(
            block, block, dsem.at[0, s], dsem.at[1, s], {"dp": source}
        ).wait_recv()
    for s in range(1, dpn):
        share(s).wait_send()
    tot_out[...] = jnp.sum(tot_last[...], axis=0)
    first.finish()

    @pl.when(stays)
    def _():
        keep.wait()

    @pl.when(jnp.logical_not(stays))
    def _():
        hop.wait_recv()
        hop.wait_send()


def spread_kernel(cn, dpn, qkv, gu, down, out, gq, gk, gv, go, gg, gu_out, gd):
    hw = qkv.shape[2] // 3
    ff_rows = gd.shape[0]
    ff = ff_rows * dpn
    gd[...] = down[...].astype(f32)
    go[...] = out[...].astype(f32)
    for c in range(cn):
        for i, ref in enumerate((gq, gk, gv)):
            ref[:, c * hw : (c + 1) * hw] = qkv[c, :, i * hw : (i + 1) * hw].astype(f32)
        for i, ref in enumerate((gg, gu_out)):
            for d in range(dpn):
                to = (d * cn + c) * ff_rows
                lo = i * ff + d * ff_rows
                ref[:, to : to + ff_rows] = gu[c, :, lo : lo + ff_rows].astype(f32)


def call(kernel, outs, ins, specs_in, specs_out, scratch, number, flops=0, moved=0):
    return pl.pallas_call(
        kernel,
        out_shape=outs,
        in_specs=specs_in,
        out_specs=specs_out,
        scratch_shapes=scratch,
        compiler_params=pltpu.CompilerParams(
            collective_id=number, has_side_effects=True, vmem_limit_bytes=60 * 2**20
        ),
        cost_estimate=pl.CostEstimate(flops=flops, bytes_accessed=moved, transcendentals=0),
    )(*ins)


def shape(dims, dtype=bf16):
    return jax.ShapeDtypeStruct(dims, dtype)


def rope_tables(positions):
    half_dim = HEAD_DIM // 2
    inverse = jnp.exp(
        jnp.arange(half_dim, dtype=f32) * (-2.0 * math.log(rope_base) / HEAD_DIM)
    )
    angles = positions[:, None] * inverse[None, :]
    return jnp.cos(angles), jnp.sin(angles)


def rotate(values, cosines, sines, sign):
    half = HEAD_DIM // 2
    parts = []
    for h in range(values.shape[1] // HEAD_DIM):
        a = values[:, h * HEAD_DIM : h * HEAD_DIM + half]
        b = values[:, h * HEAD_DIM + half : (h + 1) * HEAD_DIM]
        parts += [a * cosines - sign * b * sines, b * cosines + sign * a * sines]
    return jnp.concatenate(parts, axis=1)


def gather(v, axes, axis=0):
    return lax.all_gather(v, axes, axis=axis, tiled=True)


def scatter_sum(v, axes):
    return lax.psum_scatter(v, axes, scatter_dimension=0, tiled=True)


def shards(
    hidden_in,
    out_grad,
    seg_ids,
    valid_mask,
    w_query,
    w_key,
    w_value,
    w_output,
    w_gate,
    w_up,
    w_down,
    gain_attn,
    gain_mlp,
):
    dpn = lax.axis_size("dp")
    cn = lax.axis_size("ctx")
    n = cn // 2
    x_local = hidden_in[0]
    dy_local = out_grad[0]
    rows, width = x_local.shape
    seq = rows * cn
    dr = w_query.shape[0]
    hw = width // cn
    heads = hw // HEAD_DIM
    ff_rows = w_down.shape[0]
    ff = ff_rows * dpn
    dma = pltpu.SemaphoreType.DMA
    mib = 2**20

    code = (seg_ids[0] * 2 + valid_mask[0]).astype(bf16)
    x_ext = jnp.concatenate([x_local, jnp.broadcast_to(code[:, None], (rows, 128))], axis=1)
    lanes = jnp.arange(128)[None, :]
    gain_cols = jnp.where(lanes == 0, gain_attn[:, None], gain_mlp[:, None]).astype(bf16)
    qkv_pack = jnp.concatenate(
        [w.astype(bf16).reshape(dr, cn, hw) for w in (w_query, w_key, w_value)]
        + [jnp.broadcast_to(gain_cols[:, None, :], (dr, cn, 128))],
        axis=2,
    ).transpose(1, 0, 2)
    pw = 3 * hw + 128
    gate_pack, up_pack = (
        w.astype(bf16).reshape(dr, dpn, cn, ff_rows).transpose(2, 0, 1, 3).reshape(cn, dr, ff)
        for w in (w_gate, w_up)
    )
    ring_sem = dma((4, dpn // 2 + 1))
    x_all, qkv_full, down = call(
        functools.partial(front_kernel, cn, dpn),
        (shape((cn, rows, width + 128)), shape((dpn, cn, dr, pw)), shape((dpn, ff_rows, width))),
        (x_ext, qkv_pack, w_down.astype(bf16)),
        [ANY] * 3,
        (ANY, ANY, ANY),
        [dma((5, n)), dma((2, cn)), ring_sem, ring_sem, dma((3,))],
        1,
        moved=160 * mib,
    )
    down = down.reshape(ff, width)
    x_all, dy_own = lax.optimization_barrier((x_all, dy_local))
    dys = gather(dy_own, "ctx")
    qkv_full = qkv_full.reshape(width, pw)
    w_qkv = qkv_full
    gains = qkv_full[:, 3 * hw : 3 * hw + 2].astype(f32).T
    gain_one, gain_two = gains[0:1], gains[1:2]

    all_codes = x_all[:, :, width].reshape(seq).astype(jnp.int32)
    seg = all_codes // 2
    valid = all_codes % 2
    index = jnp.arange(seq, dtype=jnp.int32)
    starts = jnp.sum((seg[None, :] < seg[:, None]).astype(jnp.int32), axis=1)
    cosines, sines = rope_tables((index - starts).astype(f32))
    k_code = jnp.where(valid == 1, seg, -1)[None]
    q_info = jnp.stack([seg, valid], axis=1)
    cos_two = jnp.concatenate([cosines, cosines], axis=1)
    sin_two = jnp.concatenate([-sines, sines], axis=1)

    line_scratch = sum_scratch(cn, rows, width)
    an, proj, o, mass, w_gate_c, up_own, wo = call(
        functools.partial(attn_kernel, cn, dpn),
        (
            shape((seq, width)),
            shape((seq, 3 * hw)),
            shape((seq, hw)),
            shape((1, 2 * rows), f32),
            shape((dpn, cn, dr, ff)),
            shape((cn, dr, ff)),
            shape((dpn, dr, width)),
        ),
        (
            x_all, w_qkv, gain_one, cos_two, sin_two, q_info, k_code, gate_pack, up_pack,
            w_output.astype(bf16),
        ),
        [VMEM] * 7 + [ANY] * 3,
        (VMEM,) * 4 + (ANY,) * 3,
        [dma((2, 2, cn)), ring_sem, dma((2,)), ring_sem, dma((3,))],
        2,
        moved=160 * mib,
    )
    h1, bn, w_up_c = call(
        functools.partial(middle_kernel, cn, dpn),
        (
            shape((rows, width), f32),
            shape((cn, rows, width)),
            shape((dpn, cn, dr, ff)),
        ),
        (o, wo.reshape(hw, width), x_local, gain_two, up_own),
        [VMEM] * 4 + [ANY],
        (VMEM, ANY, ANY),
        [pltpu.VMEM((rows, width), bf16), dma((5, n)), ring_sem, dma((2,))] + line_scratch,
        3,
        moved=160 * mib,
    )
    wo = wo.reshape(hw, width)
    w_gate_c = w_gate_c.reshape(width, ff)
    w_up_c = w_up_c.reshape(width, ff)
    bn = bn.reshape(seq, width)
    gate = dot(bn, w_gate_c)
    up = dot(bn, w_up_c)
    sig = jax.nn.sigmoid(gate)
    silu = gate * sig
    hid = (silu * up).astype(bf16)
    dhid = dot(dys, down, contract_cols)
    dgate = (dhid * up * sig * (1.0 + gate * (1.0 - sig))).astype(bf16)
    dup = (dhid * silu).astype(bf16)
    dgu = jnp.concatenate([dgate, dup], axis=1)
    branch = dot(hid, down).astype(bf16)
    dgu, branch = lax.optimization_barrier((dgu, branch))
    branch = scatter_sum(branch, "ctx")
    result = (h1 + branch.astype(f32)).astype(bf16)
    dh1, dob, term_two, g_gu = call(
        functools.partial(back_kernel, cn, dpn),
        (
            shape((rows, width), f32),
            shape((cn, rows, width)),
            shape((1, width), f32),
            shape((cn, dr, 2 * ff)),
        ),
        (bn, dgu, w_gate_c, w_up_c, h1, dy_local, gain_two),
        [VMEM] * 7,
        (VMEM, ANY, VMEM, VMEM),
        [pltpu.VMEM((rows, width), bf16), dma((5, n)), dma]
        + line_scratch
        + ring_scratch(dpn, cn * dr, 2 * ff),
        4,
        moved=160 * mib,
    )
    dob = dob.reshape(seq, width)
    do = dot(dob, wo, contract_cols).astype(bf16)
    g_out = dot(o, dob, contract_rows).astype(bf16).reshape(dpn, dr, width)
    g_down = dot(hid, dys, contract_rows).astype(bf16).reshape(dpn, ff_rows, width)
    grad_input, term_one, gu_back, g_down, out_own, qkv_own = call(
        functools.partial(last_kernel, cn, dpn),
        (
            shape((rows, width)),
            shape((1, width), f32),
            shape((cn, dr, 2 * ff)),
            shape((ff_rows, width)),
            shape((dr, width)),
            shape((cn, dr, 3 * hw)),
        ),
        (
            do, g_gu, g_down, g_out, proj, cos_two, sin_two, seg[None], k_code.T, an, w_qkv,
            dh1, x_local, gain_one,
        ),
        [VMEM] + [ANY] * 3 + [VMEM] * 10,
        (VMEM, VMEM, ANY, VMEM, VMEM, VMEM),
        [
            pltpu.VMEM((seq, hw), f32),
            pltpu.VMEM((seq, 3 * hw), bf16),
            dma((2, cn)),
            dma((3,)),
        ]
        + line_scratch
        + ring_scratch(dpn, ff_rows, width)
        + ring_scratch(dpn, dr, width)
        + ring_scratch(dpn, cn * dr, 3 * hw),
        5,
        moved=160 * mib,
    )

    mass_part = jnp.sum(mass) / (heads * cn)
    pieces = [t.reshape(dpn, cn, dr).transpose(1, 0, 2) for t in (term_one, term_two)]
    pieces.append(jnp.broadcast_to(mass_part, (cn, dpn, dr)))
    tot = jnp.zeros((cn, dpn, 8, 128), f32).at[:, :, :3, :dr].set(jnp.stack(pieces, axis=2))
    q_all, g_out, totals = call(
        functools.partial(return_kernel, cn, dpn),
        (shape((cn, dr, 3 * hw)), shape((dr, width)), shape((8, 128), f32)),
        (qkv_own, out_own, tot),
        [ANY, ANY, VMEM],
        (ANY, ANY, VMEM),
        [
            pltpu.VMEM((cn, dpn, 8, 128), f32),
            pltpu.VMEM((dpn, 8, 128), f32),
            pltpu.VMEM((dpn, 8, 128), f32),
            dma((2, cn)),
            dma((2, cn)),
            dma((2, dpn)),
            dma((2,)),
            dma((3,)),
        ],
        6,
        moved=80 * mib,
    )
    g_q, g_k, g_v, g_o, g_gate, g_up, g_down = pl.pallas_call(
        functools.partial(spread_kernel, cn, dpn),
        out_shape=tuple(shape((dr, width), f32) for _ in range(4))
        + tuple(shape((dr, ff * cn), f32) for _ in range(2))
        + (shape((ff_rows, width), f32),),
        in_specs=[VMEM] * 4,
        out_specs=(VMEM,) * 7,
        compiler_params=pltpu.CompilerParams(vmem_limit_bytes=48 * 2**20),
    )(q_all, gu_back, g_down, g_out)
    mass_mean = totals[2, 0] / (dpn * seq)
    return (
        result[None],
        grad_input[None],
        g_q,
        g_k,
        g_v,
        g_o,
        g_gate,
        g_up,
        g_down,
        totals[0, :dr],
        totals[1, :dr],
        mass_mean,
    )


def solution(mesh):
    tok = P("dp", "ctx", None)
    ids = P("dp", "ctx")
    mat = P(("dp", "ctx"), None)
    vec = P(("dp", "ctx"))
    return jax.shard_map(
        shards,
        mesh=mesh,
        in_specs=(tok, tok, ids, ids) + (mat,) * 7 + (vec, vec),
        out_specs=(tok, tok) + (mat,) * 7 + (vec, vec, P()),
        check_vma=False,
    )
```

```python
import functools
import math

import jax
import jax.numpy as jnp
from jax import lax
from jax.experimental import pallas as pl
from jax.experimental.pallas import tpu as pltpu
from jax.sharding import PartitionSpec as P

HEAD_DIM = 128
norm_eps = 1e-05
rope_base = 10000.0
score_shift = math.log(4096.0)
score_scale = 1.0 / math.sqrt(HEAD_DIM)
contract_rows = (((0,), (0,)), ((), ()))
contract_cols = (((1,), (1,)), ((), ()))
plain = (((1,), (0,)), ((), ()))
f32 = jnp.float32
bf16 = jnp.bfloat16
MESH = pl.DeviceIdType.MESH
ANY = pl.BlockSpec(memory_space=pl.ANY)
VMEM = pl.BlockSpec(memory_space=pltpu.VMEM)


def dot(a, b, dims=plain):
    return lax.dot_general(a, b, dims, preferred_element_type=f32)


def remote(src, dst, send, recv, target):
    return pltpu.make_async_remote_copy(
        src_ref=src,
        dst_ref=dst,
        send_sem=send,
        recv_sem=recv,
        device_id=target,
        device_id_type=MESH,
    )


def greet(target):
    pl.semaphore_signal(
        pltpu.get_barrier_semaphore(), inc=1, device_id=target, device_id_type=MESH
    )


def by_rows(count, work, step=16):
    @pl.loop(0, count // step)
    def _(i):
        work(pl.ds(pl.multiple_of(i * step, step), step))


def place(cn):
    c = lax.axis_index("ctx")
    j, k = c // 2, c % 2
    return c, j, k, cn // 2, 2 * j + 1 - k


def greet_line(cn, ring):
    c, j, _, n, sib = place(cn)
    ring.greet()
    greet({"ctx": sib})

    @pl.when(j < n - 1)
    def _():
        greet({"ctx": c + 2})

    @pl.when(j > 0)
    def _():
        greet({"ctx": c - 2})

    inner = jnp.where(j > 0, 1, 0) + jnp.where(j < n - 1, 1, 0)
    pl.semaphore_wait(pltpu.get_barrier_semaphore(), 3 + inner)


def greet_ctx(cn):
    c = lax.axis_index("ctx")
    for s in range(1, cn):
        greet({"ctx": lax.rem(c + s, cn)})


class LineGather:
    def __init__(self, cn, own, full, sem):
        self.cn, self.own, self.full, self.sem = cn, own, full, sem

    def copy(self, src, origin, kind, target):
        _, _, k, _, _ = place(self.cn)
        sem = self.sem
        return remote(
            src,
            self.full.at[2 * origin + k],
            sem.at[kind, origin],
            sem.at[3 if kind < 2 else 4, origin],
            {"ctx": target},
        )

    def start(self):
        c, j, _, n, sib = place(self.cn)

        @pl.when(j < n - 1)
        def _():
            self.copy(self.own, j, 0, c + 2).start()

        @pl.when(j > 0)
        def _():
            self.copy(self.own, j, 1, c - 2).start()

        self.copy(self.own, j, 2, sib).start()

    def step(self, s):
        c, j, k, n, sib = place(self.cn)

        @pl.when(j - s >= 0)
        def _():
            o = j - s
            block = self.full.at[2 * o + k]
            self.copy(block, o, 0, sib).wait_recv()

            @pl.when(j < n - 1)
            def _():
                self.copy(block, o, 0, c + 2).start()

            self.copy(block, o, 2, sib).start()

        @pl.when(j + s <= n - 1)
        def _():
            o = j + s
            block = self.full.at[2 * o + k]
            self.copy(block, o, 1, sib).wait_recv()

            @pl.when(j > 0)
            def _():
                self.copy(block, o, 1, c - 2).start()

            self.copy(block, o, 2, sib).start()

    def forward(self, first=1, last=None):
        for s in range(first, self.cn // 2 if last is None else last + 1):
            self.step(s)

    def other(self, o):
        _, _, k, _, sib = place(self.cn)
        block = self.full.at[2 * o + 1 - k]
        remote(
            block, block, self.sem.at[2, o], self.sem.at[4, o], {"ctx": sib}
        ).wait_recv()

    def sent(self):
        c, j, k, n, sib = place(self.cn)
        for o in range(n):
            block = self.full.at[2 * o + k]

            @pl.when((j < n - 1) & (o <= j))
            def _():
                self.copy(block, o, 0, sib).wait_send()

            @pl.when((j > 0) & (o >= j))
            def _():
                self.copy(block, o, 1, sib).wait_send()

            self.copy(block, o, 2, sib).wait_send()

    def finish(self):
        for o in range(self.cn // 2):
            self.other(o)
        self.sent()


class Swap:
    def __init__(self, cn, src, dst, sem, local, pick=None):
        self.cn, self.sem, self.local = cn, sem, local
        self.src = pick or (lambda c: src.at[c])
        self.dst = dst if callable(dst) else lambda c: dst.at[c]

    def copy(self, s):
        c = lax.axis_index("ctx")
        peer = lax.rem(c + s, self.cn)
        return remote(
            self.src(peer),
            self.dst(c),
            self.sem.at[0, s],
            self.sem.at[1, s],
            {"ctx": peer},
        )

    def start(self):
        c = lax.axis_index("ctx")
        for s in range(1, self.cn):
            self.copy(s).start()
        pltpu.make_async_copy(self.src(c), self.dst(c), self.local).start()

    def receive(self, s):
        c = lax.axis_index("ctx")
        if s == 0:
            pltpu.make_async_copy(self.src(c), self.dst(c), self.local).wait()
            return c
        source = lax.rem(c - s + self.cn, self.cn)
        block = self.dst(source)
        remote(
            block, block, self.sem.at[0, s], self.sem.at[1, s], {"ctx": source}
        ).wait_recv()
        return source

    def sent(self):
        for s in range(1, self.cn):
            self.copy(s).wait_send()

    def finish(self):
        for s in range(self.cn):
            self.receive(s)
        self.sent()


class RingGather:
    def __init__(self, dpn, own, full, sem):
        self.dpn, self.own, self.full, self.sem = dpn, own, full, sem
        self.hops = dpn // 2
        d = lax.axis_index("dp")
        self.p = d // 2 * 2 + lax.rem(lax.rem(d, 2) + d // 2, 2)

    def member(self, step):
        p = lax.rem(self.p + step + self.dpn, self.dpn)
        return p // 2 * 2 + lax.rem(lax.rem(p, 2) + p // 2, 2)

    def half(self, ref, h, right):
        if h < self.hops:
            return ref
        m = self.full.shape[1] // 2
        if len(self.full.shape) == 3 and m % 16:
            m = self.full.shape[2] // 2
            return ref.at[:, pl.ds(0 if right else m, m)]
        return ref.at[pl.ds(0 if right else m, m)]

    def copy(self, h, right):
        way = 1 if right else -1
        origin = self.member(-way * (h - 1))
        src = self.own if h == 1 else self.full.at[origin]
        return remote(
            self.half(src, h, right),
            self.half(self.full.at[origin], h, right),
            self.sem.at[0 if right else 1, h],
            self.sem.at[2 if right else 3, h],
            {"dp": self.member(way)},
        )

    def arrival(self, h, right):
        way = 1 if right else -1
        block = self.half(self.full.at[self.member(-way * h)], h, right)
        return remote(
            block,
            block,
            self.sem.at[0 if right else 1, h],
            self.sem.at[2 if right else 3, h],
            {"dp": self.member(way)},
        )

    def greet(self):
        greet({"dp": self.member(1)})
        greet({"dp": self.member(-1)})

    def start(self):
        self.copy(1, True).start()
        self.copy(1, False).start()

    def forward(self):
        for h in range(1, self.hops):
            for right in (True, False):
                self.arrival(h, right).wait_recv()
                self.copy(h + 1, right).start()

    def finish(self):
        for right in (True, False):
            self.arrival(self.hops, right).wait_recv()
        for h in range(1, self.hops + 1):
            for right in (True, False):
                self.copy(h, right).wait_send()


class RingPieces(RingGather):
    def __init__(self, dpn, full, sem):
        super().__init__(dpn, None, full, sem)

    def piece(self, i, h, right, back):
        way = 1 if right else -1
        ref = self.full.at[self.member(-way * back), i]
        return remote(
            ref,
            ref,
            self.sem.at[0 if right else 1, h, i],
            self.sem.at[2 if right else 3, h, i],
            {"dp": self.member(way)},
        )

    def moves(self, i, h, right, act):
        if h < self.hops:
            act()
        else:
            first = i < self.full.shape[1] // 2
            pl.when(first if right else jnp.logical_not(first))(act)

    def start(self, i):
        for right in (True, False):
            self.moves(i, 1, right, lambda r=right: self.piece(i, 1, r, 0).start())

    def forward(self, i):
        for h in range(1, self.hops):
            for right in (True, False):
                self.piece(i, h, right, h).wait_recv()
                self.moves(
                    i, h + 1, right, lambda h=h, r=right: self.piece(i, h + 1, r, h).start()
                )

    def finish(self, i):
        for right in (True, False):
            h = self.hops
            self.moves(i, h, right, lambda r=right: self.piece(i, h, r, h).wait_recv())
        for h in range(1, self.hops + 1):
            for right in (True, False):
                self.moves(
                    i, h, right, lambda h=h, r=right: self.piece(i, h, r, h - 1).wait_send()
                )


class RingSum:
    def __init__(self, dpn, blocks, got, got_half, sem):
        self.dpn, self.blocks, self.sem = dpn, blocks, sem
        self.got, self.got_half = got, got_half
        self.ring = RingGather(dpn, None, blocks, sem)
        self.hops = dpn // 2

    def part(self, s, right):
        m, width = self.blocks.shape[1:]
        if s > 1:
            return 0, m, pl.ds(0, width)
        if (m // 2) % 16:
            return 0, m, pl.ds(0 if right else width // 2, width // 2)
        return 0 if right else m // 2, m // 2, pl.ds(0, width)

    def copy(self, s, right):
        way = 1 if right else -1
        target = self.ring.member(way * (self.hops - s + 1))
        start, size, lanes = self.part(s, right)
        return remote(
            self.blocks.at[target, pl.ds(start, size), lanes],
            self.arrived(s, right),
            self.sem.at[0 if right else 1, s],
            self.sem.at[2 if right else 3, s],
            {"dp": self.ring.member(way)},
        )

    def arrived(self, s, right):
        side = 0 if right else 1
        return self.got_half.at[side] if s == 1 else self.got.at[side, s - 2]

    def order(self):
        out = [self.ring.member(self.hops)]
        for s in range(self.hops - 1, 0, -1):
            out += [self.ring.member(s), self.ring.member(-s)]
        return out + [self.ring.member(0)]

    def start(self):
        self.copy(1, True).start()
        self.copy(1, False).start()

    def take(self, s, right, target):
        self.copy(s, right).wait_recv()
        start, size, lanes = self.part(s, right)
        block = self.blocks.at[target, pl.ds(start, size), lanes]
        came = self.arrived(s, right)

        def add(r):
            block[r, :] = (block[r, :].astype(f32) + came[r, :].astype(f32)).astype(bf16)

        by_rows(size, add)

    def forward(self, s):
        for right in (True, False):
            way = 1 if right else -1
            self.take(s, right, self.ring.member(way * (self.hops - s)))
            self.copy(s + 1, right).start()

    def finish(self, out):
        for right in (True, False):
            self.copy(self.hops, right).wait_recv()
        mine = self.ring.member(0)
        ends = [self.arrived(self.hops, right) for right in (True, False)]
        per = out.shape[-2]

        @pl.loop(0, self.blocks.shape[1] // 16)
        def _(i):
            r = pl.ds(pl.multiple_of(i * 16, 16), 16)
            total = self.blocks[mine, r, :].astype(f32)
            for end in ends:
                total = total + end[r, :].astype(f32)
            if len(out.shape) == 3:
                to = pl.ds(pl.multiple_of(lax.rem(i * 16, per), 16), 16)
                out[i * 16 // per, to, :] = total.astype(out.dtype)
            else:
                out[r, :] = total.astype(out.dtype)

        for s in range(1, self.hops + 1):
            for right in (True, False):
                self.copy(s, right).wait_send()


def ring_scratch(dpn, m, width):
    return [
        pltpu.VMEM((dpn, m, width), bf16),
        pltpu.VMEM((2, dpn // 2 - 1, m, width), bf16),
        pltpu.VMEM((2, m // 2, width) if m % 32 == 0 else (2, m, width // 2), bf16),
        pltpu.SemaphoreType.DMA((4, dpn // 2 + 1)),
    ]


def outer(a_ref, b_ref, out, at, tile=512):
    a = a_ref[:, at]
    width = out.shape[-1]
    for lo in range(0, width, tile):
        to = slice(lo, min(lo + tile, width))
        out[:, to] = dot(a, b_ref[:, to], contract_rows).astype(bf16)


def outer_all(a_ref, staged, halves, blocks, tile=512):
    count, m, width = blocks.shape
    many = max(1, 128 // m)
    for first in range(0, count, many):
        at = slice(first * m, (first + many) * m)
        for lo in range(0, width, tile):
            to = slice(lo, min(lo + tile, width))
            part = dot(a_ref[halves[0], at], staged(0, to), contract_rows)
            part = part + dot(a_ref[halves[1], at], staged(1, to), contract_rows)
            part = part.astype(bf16)
            for i in range(many):
                blocks[first + i, :, to] = part[i * m : (i + 1) * m]


class LineSum:
    def __init__(self, cn, compute, part, cross, cross_in, flow, arrived, sem):
        self.cn, self.compute, self.part = cn, compute, part
        self.cross, self.cross_in, self.flow = cross, cross_in, flow
        self.arrived, self.sem = arrived, sem

    def across(self, t):
        _, _, _, _, sib = place(self.cn)
        return remote(
            self.cross.at[t],
            self.cross_in.at[t],
            self.sem.at[0, t],
            self.sem.at[2, t],
            {"ctx": sib},
        )

    def along(self, t, slot, target):
        return remote(
            self.flow.at[t],
            self.arrived.at[slot],
            self.sem.at[1, t],
            self.sem.at[3, slot],
            {"ctx": target},
        )

    def produce(self, t, slot):
        _, _, k, _, _ = place(self.cn)
        part = self.part.at[slot]
        self.compute(t, part)

        def low(r):
            self.cross[t, r, :] = part[1 - k, r, :].astype(bf16)

        by_rows(self.cross.shape[1], low)
        self.across(t).start()

    def add(self, part, came):
        def more(r):
            part[r, :] += came[r, :].astype(f32)

        by_rows(part.shape[0], more)

    def collect(self, t, slot):
        _, j, k, n, sib = place(self.cn)
        part = self.part.at[slot, k]
        self.across(t).wait_recv()
        self.add(part, self.cross_in.at[t])

        @pl.when((j > 0) & (t >= j))
        def _():
            self.along(t, t, sib).wait_recv()
            self.add(part, self.arrived.at[t])

        @pl.when((j < n - 1) & (t <= j))
        def _():
            slot_in = jnp.where(t == j, n, t)
            self.along(t, slot_in, sib).wait_recv()
            self.add(part, self.arrived.at[slot_in])

    def send(self, t, slot, up):
        c, j, k, n, _ = place(self.cn)

        def low(r):
            self.flow[t, r, :] = self.part[slot, k, r, :].astype(bf16)

        by_rows(self.flow.shape[1], low)
        there = t if up else jnp.where(t == j - 1, n, t)
        self.along(t, there, c + 2 if up else c - 2).start()

    def drain(self):
        _, j, _, n, sib = place(self.cn)

        @pl.loop(0, n)
        def _(t):
            self.across(t).wait_send()

            @pl.when(t != j)
            def _():
                self.along(t, t, sib).wait_send()


class LineSumRows(LineSum):
    def __init__(self, cn, terms, stage, loads, *refs):
        super().__init__(cn, None, *refs)
        self.terms, self.stage, self.loads = terms, stage, loads

    def produce(self, t, slot):
        _, _, k, _, _ = place(self.cn)
        other = pltpu.make_async_copy(
            self.terms.at[2 * t + 1 - k], self.cross.at[t], self.loads.at[0]
        )
        own = pltpu.make_async_copy(self.terms.at[2 * t + k], self.stage, self.loads.at[1])
        other.start()
        own.start()
        other.wait()
        self.across(t).start()
        own.wait()

        def wide(r):
            self.part[slot, k, r, :] = self.stage[r, :].astype(f32)

        by_rows(self.stage.shape[0], wide)


def line_sums(cn, sums, between=None):
    _, j, _, n, _ = place(cn)

    @pl.loop(0, n - 1)
    def _(s):
        to_up, to_down = n - 1 - s + j, s - (n - 1 - j)
        for total in sums:

            @pl.when(s >= j)
            def _():
                total.produce(to_up, 0)

            @pl.when(s >= n - 1 - j)
            def _():
                total.produce(to_down, 1)

        for total in sums:

            @pl.when(s >= j)
            def _():
                total.collect(to_up, 0)
                total.send(to_up, 0, True)

            @pl.when(s >= n - 1 - j)
            def _():
                total.collect(to_down, 1)
                total.send(to_down, 1, False)

        if between is not None:
            between(s)

    for total in sums:
        total.produce(j, 0)
    for total in sums:
        total.collect(j, 0)


def sum_scratch(cn, rows, width):
    n = cn // 2
    return [
        pltpu.VMEM((2, 2, rows, width), f32),
        pltpu.VMEM((n, rows, width), bf16),
        pltpu.VMEM((n, rows, width), bf16),
        pltpu.VMEM((n, rows, width), bf16),
        pltpu.VMEM((n + 1, rows, width), bf16),
        pltpu.SemaphoreType.DMA((4, n + 1)),
    ]


def product(a_ref, b_ref, dims, rows, width):
    tile = min(512, width)

    def compute(t, out):
        a = a_ref[pl.ds(pl.multiple_of(t * 2 * rows, 2 * rows), 2 * rows), :]

        @pl.loop(0, width // tile)
        def _(i):
            at = pl.ds(pl.multiple_of(i * tile, tile), tile)
            b = b_ref[:, at] if dims == plain else b_ref[at, 0 : a_ref.shape[1]]
            out[:, :, at] = dot(a, b, dims).reshape(2, rows, tile)

    return compute


def rms(v):
    return lax.rsqrt(jnp.mean(v * v, axis=-1, keepdims=True) + norm_eps)


def front_kernel(
    cn, dpn, x, wq, wk, wv, gains, wo, gate_in, up_in, down_in,
    x_all, pack_all, gate, up, down_all, wo_low,
    pack, wide, tall, down, gsem, ssem, rsem, dsem, local,
):
    c, d = lax.axis_index("ctx"), lax.axis_index("dp")
    hw = wq.shape[1] // cn
    part = gate_in.shape[1] // (cn * dpn)
    mine = pack_all.at[d]
    swap = Swap(cn, pack, mine, ssem, local.at[0])
    gather = LineGather(cn, x, x_all, gsem)
    ring = RingPieces(dpn, pack_all, rsem)
    down_ring = RingGather(dpn, down, down_all, dsem)
    greet_ctx(cn)
    ring.greet()
    loads = [
        pltpu.make_async_copy(src, dst, local.at[i])
        for i, (src, dst) in enumerate(
            ((gate_in, wide.at[0]), (up_in, wide.at[1]), (down_in, tall)), 2
        )
    ]
    for load in loads:
        load.start()
    for to in range(cn):
        for i, w in enumerate((wq, wk, wv)):
            pack[to, :, i * hw : (i + 1) * hw] = w[:, to * hw : (to + 1) * hw].astype(bf16)
        pack[to, :, 3 * hw :] = gains[...]
    pl.semaphore_wait(pltpu.get_barrier_semaphore(), cn - 1 + 2)
    swap.start()
    gather.start()
    loads[2].wait()
    down[...] = tall[...].astype(bf16)
    down_ring.start()
    keep_down = pltpu.make_async_copy(down, down_all.at[d], local.at[5])
    keep_down.start()
    keep = pltpu.make_async_copy(x, x_all.at[c], local.at[1])
    keep.start()
    wo_low[...] = wo[...].astype(bf16)

    def lay(i, out):
        loads[i].wait()
        for to in range(cn):
            for row in range(dpn):
                lo = (row * cn + to) * part
                out[to, :, row * part : (row + 1) * part] = wide[i, :, lo : lo + part].astype(bf16)

    half = cn // 2
    sources = [swap.receive(0)]
    ring.start(sources[0])
    lay(0, gate)
    for s in range(1, half):
        sources.append(swap.receive(s))
        ring.start(sources[s])
    gather.forward(1, 1)
    lay(1, up)
    for s in range(half, cn):
        sources.append(swap.receive(s))
        ring.start(sources[s])
    down_ring.forward()
    gather.forward(2, 2)
    for source in sources:
        ring.forward(source)
    gather.forward(3)
    keep.wait()
    keep_down.wait()
    gather.finish()
    for source in sources:
        ring.finish(source)
    swap.sent()
    down_ring.finish()


def prepare(w, x_all, gains, info_rows, hw, block):
    width = w.shape[0]
    per = block // x_all.shape[1]

    @pl.loop(0, width // block)
    def _(i):
        at = pl.ds(pl.multiple_of(i * block, block), block)
        gains[:, at] = w[at, 3 * hw : 3 * hw + 128].astype(f32).T[0:8]

    @pl.loop(0, info_rows.shape[1] // block)
    def _(i):
        at = pl.ds(pl.multiple_of(i * block, block), block)
        codes = x_all[pl.ds(i * per, per), :, width:].reshape(block, 128).astype(f32).T[0:8]
        seg = jnp.floor(codes * 0.5)
        code = jnp.where(codes - 2.0 * seg == 1.0, seg, -1.0)
        first = lax.broadcasted_iota(jnp.int32, (8, block), 0) == 0
        info_rows[:, at] = jnp.where(first, seg, code)


def tables(x_all, inverse, info_rows, info_cols, cosines, sines, width, i, block):
    per = block // x_all.shape[1]
    at = pl.ds(pl.multiple_of(i * block, block), block)
    codes = x_all[pl.ds(i * per, per), :, width:].reshape(block, 128).astype(f32)
    seg = jnp.floor(codes * 0.5)
    valid = codes - 2.0 * seg
    lane = lax.broadcasted_iota(jnp.int32, (block, 128), 1)
    code = jnp.where(valid == 1.0, seg, -1.0)
    info_cols[at, :] = jnp.where(lane == 0, seg, jnp.where(lane == 1, valid, code))
    before = jnp.where(info_rows[0:1, :] < seg[:, 0:1], 1.0, 0.0)
    index = lax.broadcasted_iota(jnp.int32, (block, 128), 0) + i * block
    place_in = index.astype(f32) - jnp.sum(before, axis=1, keepdims=True)
    angles = place_in * inverse[...]
    cosines[at, :] = jnp.cos(angles)
    sines[at, :] = jnp.where(lane < HEAD_DIM // 2, -1.0, 1.0) * jnp.sin(angles)


def project(x_all, w, gain, inverse, rows_in, cols, cosines, sines, an, qkv, hw, block, hook):
    width = an.shape[1]
    per = block // x_all.shape[1]

    @pl.loop(0, an.shape[0] // block)
    def _(i):
        at = pl.ds(pl.multiple_of(i * block, block), block)
        tables(x_all, inverse, rows_in, cols, cosines, sines, width, i, block)
        x = x_all[pl.ds(i * per, per), :, 0:width].reshape(block, width).astype(f32)
        normed = (x * rms(x) * gain[...]).astype(bf16)
        an[at, :] = normed
        proj = dot(normed, w[:, 0 : 3 * hw])
        cos_b, sin_b = cosines[at, :], sines[at, :]
        for h in range(2 * hw // HEAD_DIM):
            lanes = slice(h * HEAD_DIM, (h + 1) * HEAD_DIM)
            v = proj[:, lanes]
            turned = v * cos_b + pltpu.roll(v, HEAD_DIM // 2, 1) * sin_b
            qkv[at, lanes] = turned.astype(bf16)
        qkv[at, 2 * hw :] = proj[:, 2 * hw :].astype(bf16)
        hook(i)


def mask_block(q_seg, k_code, i, j, block):
    rows = lax.broadcasted_iota(jnp.int32, (block, block), 0) + i * block
    cols = lax.broadcasted_iota(jnp.int32, (block, block), 1) + j * block
    return (q_seg == k_code) & (cols <= rows)


def attend(qkv, q_info, k_code, out, mass, hw, block, hook):
    mass[...] = jnp.zeros_like(mass)

    @pl.loop(0, qkv.shape[0] // block)
    def _(i):
        at = pl.ds(pl.multiple_of(i * block, block), block)
        q_seg, q_valid = q_info[at, 0:1], q_info[at, 1:2]
        for h in range(hw // HEAD_DIM):
            lane = [slice(t * hw + h * HEAD_DIM, t * hw + (h + 1) * HEAD_DIM) for t in range(3)]
            q = qkv[at, lane[0]]

            def step(j, acc):
                to = pl.ds(pl.multiple_of(j * block, block), block)
                s = dot(q, qkv[to, lane[1]], contract_cols) * score_scale - score_shift
                allowed = mask_block(q_seg, k_code[1:2, to], i, j, block)
                p = jnp.where(allowed, jax.nn.sigmoid(s), 0.0)
                mass[...] += jnp.sum(p * q_valid, axis=0, keepdims=True)
                return acc + dot(p.astype(bf16), qkv[to, lane[2]])

            acc = lax.fori_loop(0, i + 1, step, jnp.zeros((block, HEAD_DIM), f32))
            out[at, lane[0]] = acc.astype(bf16)
        hook(i)


def attn_kernel(
    cn, dpn, x_all, w, inverse, gate, up, wo,
    an, qkv, o, mass, gains, cosines, sines, cols, rows_in,
    gate_all, up_own, wo_all, ssem, rsem, hsem, wsem, local,
):
    c, d = lax.axis_index("ctx"), lax.axis_index("dp")
    mine, wanted = d * cn + c, c * dpn + d
    stays = mine == wanted
    hop = remote(
        wo,
        wo_all.at[lax.rem(mine, dpn)],
        hsem.at[0],
        hsem.at[1],
        {"dp": lax.rem(mine, dpn), "ctx": mine // dpn},
    )
    keep = pltpu.make_async_copy(wo, wo_all.at[d], local.at[2])
    wo_ring = RingGather(dpn, wo_all.at[d], wo_all, wsem)
    rows = x_all.shape[1]
    hw = qkv.shape[1] // 3
    swap_gate = Swap(cn, gate, gate_all.at[d], ssem.at[0], local.at[0])
    swap_up = Swap(cn, up, up_own, ssem.at[1], local.at[1])
    ring = RingPieces(dpn, gate_all, rsem)
    sources = [lax.rem(c - s + cn, cn) for s in range(cn)]
    greet_ctx(cn)
    ring.greet()

    @pl.when(jnp.logical_not(stays))
    def _():
        greet({"dp": wanted // cn, "ctx": lax.rem(wanted, cn)})

    pl.semaphore_wait(
        pltpu.get_barrier_semaphore(), cn - 1 + 2 + jnp.where(stays, 0, 1)
    )

    @pl.when(stays)
    def _():
        keep.start()
        keep.wait()

    @pl.when(jnp.logical_not(stays))
    def _():
        hop.start()

    swap_gate.start()

    def hop_done():
        @pl.when(jnp.logical_not(stays))
        def _():
            arrived = wo_all.at[d]
            remote(arrived, arrived, hsem.at[0], hsem.at[1], {"dp": d, "ctx": c}).wait_recv()

        wo_ring.start()

    def in_project(i):
        pl.when(i == 0)(hop_done)

        @pl.when(i == 1)
        def _():
            for s in range(cn // 2):
                ring.start(swap_gate.receive(s))

        @pl.when(i == 2)
        def _():
            for s in range(cn // 2, cn):
                ring.start(swap_gate.receive(s))
            swap_up.start()

    def in_attend(i):
        @pl.when(i == 1)
        def _():
            wo_ring.forward()

        @pl.when(i == 2)
        def _():
            for source in sources[: cn // 2]:
                ring.forward(source)

    prepare(w, x_all, gains, rows_in, hw, 2 * rows)
    project(
        x_all, w, gains.at[0:1], inverse, rows_in, cols, cosines, sines, an, qkv, hw, 2 * rows,
        in_project,
    )
    attend(qkv, cols, rows_in, o, mass, hw, 2 * rows, in_attend)
    for source in sources[cn // 2 :]:
        ring.forward(source)
    swap_up.finish()
    wo_ring.finish()
    for source in sources:
        ring.finish(source)
    swap_gate.sent()

    @pl.when(jnp.logical_not(stays))
    def _():
        hop.wait_send()


def middle_kernel(
    cn, dpn, o, wo, x, gain, dy, up, gate_all, down_all,
    h1, bn_all, up_all, hid, dgu, branch_all, dys_all,
    own, bn, dys, wg, wu, down, branch, gsem, ysem, rsem, local, *sum_refs,
):
    c, d = lax.axis_index("ctx"), lax.axis_index("dp")
    _, j, k, n, _ = place(cn)
    rows, width = x.shape
    ff = hid.shape[1]
    block = 2 * rows
    gather = LineGather(cn, own, bn, gsem)
    gather_dy = LineGather(cn, dy, dys, ysem)
    ring = RingGather(dpn, up, up_all, rsem)
    total = LineSum(cn, product(o, wo, plain, rows, width), *sum_refs)
    greet_line(cn, ring)
    ring.start()
    keep_up = pltpu.make_async_copy(up, up_all.at[d], local.at[0])
    loads = [
        pltpu.make_async_copy(src, dst, local.at[i])
        for i, (src, dst) in enumerate(((gate_all, wg), (down_all, down)), 2)
    ]
    keep_up.start()
    for load in loads:
        load.start()
    gather_dy.start()
    dys[c] = dy[...]

    def between(s):
        gather_dy.step(s + 1)

        @pl.when(s == n - 2)
        def _():
            ring.forward()

    line_sums(cn, [total], between)

    def norm(r):
        mid = x[r, :].astype(f32) + total.part[0, k, r, :]
        h1[r, :] = mid
        own[r, :] = (mid * rms(mid) * gain[1:2, :]).astype(bf16)

    by_rows(rows, norm)
    gather.start()
    bn[c] = own[...]
    gather_dy.finish()
    store_dy = pltpu.make_async_copy(dys, dys_all, local.at[4])
    store_dy.start()
    total.drain()
    keep_up.wait()
    for load in loads:
        load.wait()
    ring.finish()
    load_up = pltpu.make_async_copy(up_all, wu, local.at[0])
    load_up.start()
    load_up.wait()
    wgate, wup = wg, wu.reshape(width, ff)
    tile = min(512, ff)
    wide = min(512, width)

    def feed(t):
        gather.other(t)
        at = pl.ds(pl.multiple_of(t * block, block), block)
        pair = pl.ds(t * 2, 2)
        send = pltpu.make_async_copy(bn.at[pair], bn_all.at[pair], local.at[1])
        send.start()
        a = bn[pair].reshape(block, width)
        g_out = dys[pair].reshape(block, width)

        @pl.loop(0, ff // tile)
        def _(i):
            to = pl.ds(pl.multiple_of(i * tile, tile), tile)
            gate = dot(a, wgate[:, to])
            up_v = dot(a, wup[:, to])
            dhid = dot(g_out, down[to, :], contract_cols)
            sig = jax.nn.sigmoid(gate)
            silu = gate * sig
            hid[at, to] = (silu * up_v).astype(bf16)
            dgate = dhid * up_v * sig * (1.0 + gate * (1.0 - sig))
            dgu[at, to] = dgate.astype(bf16)
            dgu[at, pl.ds(pl.multiple_of(ff + i * tile, tile), tile)] = (dhid * silu).astype(bf16)

        h = hid[at, :]

        @pl.loop(0, width // wide)
        def _(i):
            to = pl.ds(pl.multiple_of(i * wide, wide), wide)
            branch[:, to] = dot(h, down[:, to]).astype(bf16)

        out = pltpu.make_async_copy(branch, branch_all.at[at], local.at[0])
        out.start()
        out.wait()
        send.wait()

    feed(j)

    @pl.loop(1, n)
    def _(s):
        gather.step(s)

        @pl.when(j - s >= 0)
        def _():
            feed(j - s)

        @pl.when(j + s <= n - 1)
        def _():
            feed(j + s)

    gather.sent()
    store_dy.wait()


def back_kernel(
    cn, dpn, bn, dgu, wg, wu, h1, dy, gain, branch_all, dh1, dob_all, term, g_own, result,
    own, branch, cross_in, arrived, bsem, gsem, loads, keep_sem, *scratch,
):
    sum_refs, ring_refs = scratch[:-4], scratch[-4:]
    rows, width = dy.shape
    ff = wg.shape[1]
    tile = min(512, width)
    c, _, k, n, _ = place(cn)

    def compute(t, out):
        at = pl.ds(pl.multiple_of(t * 2 * rows, 2 * rows), 2 * rows)

        @pl.loop(0, width // tile)
        def _(i):
            to = pl.ds(pl.multiple_of(i * tile, tile), tile)
            part = dot(dgu[at, 0:ff], wg[to, :], contract_cols)
            part = part + dot(dgu[at, ff:], wu[to, :], contract_cols)
            out[:, :, to] = part.reshape(2, rows, tile)

    total = LineSum(cn, compute, *sum_refs)
    ring = RingSum(dpn, *ring_refs)
    blocks = ring_refs[0]
    m = blocks.shape[1]
    greet_line(cn, ring.ring)
    order = ring.order()

    def weight_grad(member):
        outer(bn, dgu, blocks.at[member], pl.ds(pl.multiple_of(member * m, m), m))

    weight_grad(order[0])
    ring.start()

    def between(s):
        for i in range(ring.hops - 1):

            @pl.when(s == min(i, n - 2))
            def _():
                weight_grad(order[1 + 2 * i])
                weight_grad(order[2 + 2 * i])

            @pl.when(s == min(i + 1, n - 2))
            def _():
                ring.forward(i + 1)

    line_sums(cn, [total], between)
    term[...] = jnp.zeros_like(term)

    def norm_back(r):
        dbn = total.part[0, k, r, :]
        mid = h1[r, :]
        r2 = rms(mid)
        xh2 = mid * r2
        term[...] += jnp.sum(dbn * xh2, axis=0, keepdims=True)
        u2 = dbn * gain[1:2, :]
        mean = jnp.mean(u2 * xh2, axis=-1, keepdims=True)
        grad = dy[r, :].astype(f32) + r2 * (u2 - xh2 * mean)
        dh1[r, :] = grad
        own[r, :] = grad.astype(bf16)

    by_rows(rows, norm_back)
    gather = LineGather(cn, own, dob_all, gsem)
    gather.start()
    keep = pltpu.make_async_copy(own, dob_all.at[c], keep_sem)
    keep.start()
    total.drain()

    part, cross, _, flow, _, _ = sum_refs
    second = LineSumRows(
        cn, branch_all, branch, loads, part, cross, cross_in, flow, arrived, bsem
    )

    def pass_on(s):
        gather.step(s + 1)

        @pl.when(s == 0)
        def _():
            weight_grad(order[-1])

    line_sums(cn, [second], pass_on)

    def close(r):
        result[r, :] = (h1[r, :] + second.part[0, k, r, :]).astype(bf16)

    by_rows(rows, close)
    second.drain()
    keep.wait()
    gather.finish()
    ring.finish(g_own)


def attend_back(qkv, do, cosines, sines, q_info, k_info, dq, dqkv, hw, block):
    count = qkv.shape[0] // block
    dq[...] = jnp.zeros_like(dq)

    def turn_back(g, at):
        return g * cosines[at, :] - pltpu.roll(g, HEAD_DIM // 2, 1) * sines[at, :]

    @pl.loop(0, count)
    def _(j):
        to = pl.ds(pl.multiple_of(j * block, block), block)
        k_code = k_info[to, 2:3]
        for h in range(hw // HEAD_DIM):
            lane = [slice(t * hw + h * HEAD_DIM, t * hw + (h + 1) * HEAD_DIM) for t in range(3)]
            k, v = qkv[to, lane[1]], qkv[to, lane[2]]

            def step(i, carry):
                dk, dv = carry
                at = pl.ds(pl.multiple_of(i * block, block), block)
                q, do_i = qkv[at, lane[0]], do[at, lane[0]]
                s = dot(k, q, contract_cols) * score_scale - score_shift
                keys = lax.broadcasted_iota(jnp.int32, (block, block), 0) + j * block
                queries = lax.broadcasted_iota(jnp.int32, (block, block), 1) + i * block
                allowed = (k_code == q_info[0:1, at]) & (keys <= queries)
                sg = jnp.where(allowed, jax.nn.sigmoid(s), 0.0)
                dp = dot(v, do_i, contract_cols)
                ds = (dp * sg * (1.0 - sg)).astype(bf16)
                dq[at, lane[0]] += dot(ds, k, contract_rows)
                return dk + dot(ds, q), dv + dot(sg.astype(bf16), do_i)

            zero = jnp.zeros((block, HEAD_DIM), f32)
            dk, dv = lax.fori_loop(j, count, step, (zero, zero))
            dqkv[to, lane[1]] = turn_back(dk * score_scale, to).astype(bf16)
            dqkv[to, lane[2]] = dv.astype(bf16)

    @pl.loop(0, count)
    def _(i):
        at = pl.ds(pl.multiple_of(i * block, block), block)
        for h in range(hw // HEAD_DIM):
            lanes = slice(h * HEAD_DIM, (h + 1) * HEAD_DIM)
            dqkv[at, lanes] = turn_back(dq[at, lanes] * score_scale, at).astype(bf16)


def last_kernel(
    cn, dpn, g_gu, dob_all, dys_all, hid, o, wo, qkv, cosines, sines, q_info, k_info, an, w,
    dh1, x, gain, term_two, mass, grad_in, tot_out, gu_all, down_own, out_all, qkv_all,
    do, dq, dqkv, out_own, qkv_own, tot, tot_in, tot_sum, tot_last,
    usem, qsem, tsem, psem, osem, local, *scratch,
):
    sum_refs, rings = scratch[:-12], (scratch[-12:-8], scratch[-8:-4], scratch[-4:])
    rows, width = x.shape
    hw = width // cn
    _, _, k, n, _ = place(cn)
    down_ring, out_ring, qkv_ring = (RingSum(dpn, *refs) for refs in rings)
    swap_gu = Swap(cn, g_gu, gu_all, usem, local.at[0])
    swap_qkv = Swap(cn, qkv_own, qkv_all, qsem, local.at[4])
    totals = Swap(cn, None, tot_in, tsem, local.at[3], lambda i: tot)
    c, d = lax.axis_index("ctx"), lax.axis_index("dp")
    mine, goal = d * cn + c, c * dpn + d
    stays = mine == goal
    hop = remote(
        out_own, out_all, osem.at[0], osem.at[1], {"dp": goal // cn, "ctx": lax.rem(goal, cn)}
    )
    keep = pltpu.make_async_copy(out_own, out_all, local.at[5])

    def share(s):
        return remote(
            tot_sum, tot_last.at[d], psem.at[0, s], psem.at[1, s], {"dp": lax.rem(d + s, dpn)}
        )

    greet_ctx(cn)
    for s in range(1, dpn):
        greet({"dp": lax.rem(d + s, dpn)})

    @pl.when(jnp.logical_not(stays))
    def _():
        greet({"dp": lax.rem(mine, dpn), "ctx": mine // dpn})

    pl.semaphore_wait(
        pltpu.get_barrier_semaphore(), cn - 1 + dpn - 1 + jnp.where(stays, 0, 1)
    )
    swap_gu.start()
    seq = an.shape[0]
    stage = (sum_refs[1], sum_refs[3])
    halves = (slice(0, seq // 2), slice(seq // 2, seq))

    def fill(src):
        copies = [
            pltpu.make_async_copy(src.at[pl.ds(i * n, n)], stage[i], local.at[1 + i])
            for i in range(2)
        ]
        for copy in copies:
            copy.start()
        for copy in copies:
            copy.wait()

    def staged(i, to=slice(None)):
        return stage[i][:, :, to].reshape(seq // 2, -1)

    fill(dys_all)
    outer_all(hid, staged, halves, rings[0][0])
    down_ring.start()
    fill(dob_all)
    for i in range(2):
        do[halves[i], :] = dot(staged(i), wo[...], contract_cols).astype(bf16)
    outer_all(o, staged, halves, rings[1][0])
    out_ring.start()
    m_qkv = rings[2][0].shape[1]
    order = qkv_ring.order()

    def grad_qkv(member):
        outer(an, dqkv, rings[2][0].at[member], pl.ds(pl.multiple_of(member * m_qkv, m_qkv), m_qkv))

    attend_back(qkv, do, cosines, sines, q_info, k_info, dq, dqkv, hw, 2 * rows)
    for i in range(down_ring.hops - 1):
        down_ring.forward(i + 1)
        out_ring.forward(i + 1)
    grad_qkv(order[0])
    qkv_ring.start()
    total = LineSum(cn, product(dqkv, w, contract_cols, rows, width), *sum_refs)

    def between(s):
        for i in range(qkv_ring.hops - 1):

            @pl.when(s == min(i, n - 2))
            def _():
                grad_qkv(order[1 + 2 * i])
                grad_qkv(order[2 + 2 * i])

            @pl.when(s == min(i + 1, n - 2))
            def _():
                qkv_ring.forward(i + 1)

    line_sums(cn, [total], between)
    grad_qkv(order[-1])
    tot[0] = jnp.zeros((1, width), f32)

    def norm_back(r):
        dan = total.part[0, k, r, :]
        xf = x[r, :].astype(f32)
        r1 = rms(xf)
        xh1 = xf * r1
        tot[0] += jnp.sum(dan * xh1, axis=0, keepdims=True)
        u1 = dan * gain[0:1, :]
        mean = jnp.mean(u1 * xh1, axis=-1, keepdims=True)
        grad = dh1[r, :] + r1 * (u1 - xh1 * mean)
        grad_in[r, :] = grad.astype(bf16)

    by_rows(rows, norm_back)
    tot[1] = term_two[...]
    tot[2] = jnp.broadcast_to(jnp.sum(mass[...], axis=1, keepdims=True), (1, width))
    totals.start()
    qkv_ring.finish(qkv_own)
    swap_qkv.start()
    out_ring.finish(out_own)

    @pl.when(stays)
    def _():
        keep.start()

    @pl.when(jnp.logical_not(stays))
    def _():
        hop.start()

    totals.finish()
    tot_sum[...] = jnp.sum(tot_in[...], axis=0)
    for s in range(1, dpn):
        share(s).start()
    down_ring.finish(down_own)
    total.drain()
    swap_gu.finish()
    tot_last[d] = tot_sum[...]
    for s in range(1, dpn):
        source = lax.rem(d - s + dpn, dpn)
        block = tot_last.at[source]
        remote(block, block, psem.at[0, s], psem.at[1, s], {"dp": source}).wait_recv()
    for s in range(1, dpn):
        share(s).wait_send()
    tot_out[...] = jnp.sum(tot_last[...], axis=0)
    swap_qkv.finish()

    @pl.when(stays)
    def _():
        keep.wait()

    @pl.when(jnp.logical_not(stays))
    def _():
        hop.wait_recv()
        hop.wait_send()


def spread_kernel(
    cn, dpn, qkv_in, gu_in, down_in, out_in, gq, gk, gv, go, gg, gu_out, gd, qkv, gu, down, out, sem
):
    hw = qkv.shape[2] // 3
    ff_rows = gd.shape[0]
    ff = ff_rows * dpn
    pairs = ((down_in, down), (out_in, out), (qkv_in, qkv), (gu_in, gu))
    loads = [pltpu.make_async_copy(a, b, sem.at[i]) for i, (a, b) in enumerate(pairs)]
    for load in loads:
        load.start()
    for load in loads[:3]:
        load.wait()
    gd[...] = down[...].astype(f32)
    go[...] = out[...].astype(f32)
    for c in range(cn):
        for i, ref in enumerate((gq, gk, gv)):
            ref[:, c * hw : (c + 1) * hw] = qkv[c, :, i * hw : (i + 1) * hw].astype(f32)
    loads[3].wait()
    for c in range(cn):
        for i, ref in enumerate((gg, gu_out)):
            for d in range(dpn):
                to = (d * cn + c) * ff_rows
                lo = i * ff + d * ff_rows
                ref[:, to : to + ff_rows] = gu[c, :, lo : lo + ff_rows].astype(f32)


def call(kernel, outs, ins, specs_in, specs_out, scratch, number, flops=0, moved=0):
    return pl.pallas_call(
        kernel,
        out_shape=outs,
        in_specs=specs_in,
        out_specs=specs_out,
        scratch_shapes=scratch,
        compiler_params=pltpu.CompilerParams(
            collective_id=number, has_side_effects=True, vmem_limit_bytes=61 * 2**20
        ),
        cost_estimate=pl.CostEstimate(flops=flops, bytes_accessed=moved, transcendentals=0),
    )(*ins)


def shape(dims, dtype=bf16):
    return jax.ShapeDtypeStruct(dims, dtype)


def shards(
    hidden_in,
    out_grad,
    seg_ids,
    valid_mask,
    w_query,
    w_key,
    w_value,
    w_output,
    w_gate,
    w_up,
    w_down,
    gain_attn,
    gain_mlp,
):
    dpn = lax.axis_size("dp")
    cn = lax.axis_size("ctx")
    n = cn // 2
    x_local = hidden_in[0]
    dy_local = out_grad[0]
    rows, width = x_local.shape
    seq = rows * cn
    dr = w_query.shape[0]
    hw = width // cn
    heads = hw // HEAD_DIM
    ff_rows = w_down.shape[0]
    ff = ff_rows * dpn
    dma = pltpu.SemaphoreType.DMA
    mib = 2**20

    code = (seg_ids[0] * 2 + valid_mask[0]).astype(bf16)
    x_ext = jnp.concatenate([x_local, jnp.broadcast_to(code[:, None], (rows, 128))], axis=1)
    lanes = jnp.arange(128)[None, :]
    gain_cols = jnp.where(lanes == 0, gain_attn[:, None], gain_mlp[:, None]).astype(bf16)
    pw = 3 * hw + 128
    ring_sem = dma((4, dpn // 2 + 1))
    x_all, w_qkv, gate_pack, up_pack, down, wo_low = call(
        functools.partial(front_kernel, cn, dpn),
        (
            shape((cn, rows, width + 128)),
            shape((dpn, cn, dr, pw)),
            shape((cn, dr, ff)),
            shape((cn, dr, ff)),
            shape((dpn, ff_rows, width)),
            shape((dr, width)),
        ),
        (x_ext, w_query, w_key, w_value, gain_cols, w_output, w_gate, w_up, w_down),
        [ANY] + [VMEM] * 5 + [ANY] * 3,
        (ANY, ANY, VMEM, VMEM, ANY, VMEM),
        [
            pltpu.VMEM((cn, dr, pw), bf16),
            pltpu.VMEM((2, dr, ff * cn), f32),
            pltpu.VMEM((ff_rows, width), f32),
            pltpu.VMEM((ff_rows, width), bf16),
            dma((5, n)),
            dma((2, cn)),
            dma((4, dpn // 2 + 1, cn)),
            ring_sem,
            dma((6,)),
        ],
        1,
        moved=160 * mib,
    )
    w_qkv = w_qkv.reshape(width, pw)
    inverse = jnp.exp(
        jnp.arange(HEAD_DIM // 2, dtype=f32) * (-2.0 * math.log(rope_base) / HEAD_DIM)
    )
    inverse = jnp.concatenate([inverse, inverse])[None]

    line_scratch = sum_scratch(cn, rows, width)
    an, proj, o, mass, gains, cosines, sines, cols, infos, w_gate_c, up_own, wo = call(
        functools.partial(attn_kernel, cn, dpn),
        (
            shape((seq, width)),
            shape((seq, 3 * hw)),
            shape((seq, hw)),
            shape((1, 2 * rows), f32),
            shape((8, width), f32),
            shape((seq, HEAD_DIM), f32),
            shape((seq, HEAD_DIM), f32),
            shape((seq, 128), f32),
            shape((8, seq), f32),
            shape((dpn, cn, dr, ff)),
            shape((cn, dr, ff)),
            shape((dpn, dr, width)),
        ),
        (x_all, w_qkv, inverse, gate_pack, up_pack, wo_low),
        [VMEM] * 3 + [ANY] * 3,
        (VMEM,) * 9 + (ANY,) * 3,
        [dma((2, 2, cn)), dma((4, dpn // 2 + 1, cn)), dma((2,)), ring_sem, dma((3,))],
        2,
        moved=160 * mib,
    )
    down = down.reshape(ff, width)
    h1, bn, w_up_c, hid, dgu, branch, dys = call(
        functools.partial(middle_kernel, cn, dpn),
        (
            shape((rows, width), f32),
            shape((cn, rows, width)),
            shape((dpn, cn, dr, ff)),
            shape((seq, ff)),
            shape((seq, 2 * ff)),
            shape((seq, width)),
            shape((cn, rows, width)),
        ),
        (
            o, wo.reshape(hw, width), x_local, gains, dy_local, up_own,
            w_gate_c.reshape(width, ff), down,
        ),
        [VMEM] * 5 + [ANY] * 3,
        (VMEM, ANY, ANY, VMEM, VMEM, ANY, ANY),
        [
            pltpu.VMEM((rows, width), bf16),
            pltpu.VMEM((cn, rows, width), bf16),
            pltpu.VMEM((cn, rows, width), bf16),
            pltpu.VMEM((width, ff), bf16),
            pltpu.VMEM((dpn, cn, dr, ff), bf16),
            pltpu.VMEM((ff, width), bf16),
            pltpu.VMEM((2 * rows, width), bf16),
            dma((5, n)),
            dma((5, n)),
            ring_sem,
            dma((5,)),
        ]
        + line_scratch,
        3,
        moved=160 * mib,
    )
    wo = wo.reshape(hw, width)
    w_gate_c = w_gate_c.reshape(width, ff)
    w_up_c = w_up_c.reshape(width, ff)
    bn = bn.reshape(seq, width)
    dh1, dob, term_two, g_gu, result = call(
        functools.partial(back_kernel, cn, dpn),
        (
            shape((rows, width), f32),
            shape((cn, rows, width)),
            shape((1, width), f32),
            shape((cn, dr, 2 * ff)),
            shape((rows, width)),
        ),
        (bn, dgu, w_gate_c, w_up_c, h1, dy_local, gains, branch.reshape(cn, rows, width)),
        [VMEM] * 7 + [ANY],
        (VMEM, ANY, VMEM, VMEM, VMEM),
        [
            pltpu.VMEM((rows, width), bf16),
            pltpu.VMEM((rows, width), bf16),
            pltpu.VMEM((n, rows, width), bf16),
            pltpu.VMEM((n + 1, rows, width), bf16),
            dma((4, n + 1)),
            dma((5, n)),
            dma((2,)),
            dma,
        ]
        + line_scratch
        + ring_scratch(dpn, cn * dr, 2 * ff),
        4,
        moved=160 * mib,
    )
    grad_input, totals, gu_back, g_down, g_out, q_all = call(
        functools.partial(last_kernel, cn, dpn),
        (
            shape((rows, width)),
            shape((3, 1, width), f32),
            shape((cn, dr, 2 * ff)),
            shape((ff_rows, width)),
            shape((dr, width)),
            shape((cn, dr, 3 * hw)),
        ),
        (
            g_gu, dob, dys, hid, o, wo, proj, cosines, sines, infos, cols, an, w_qkv,
            dh1, x_local, gains, term_two, mass,
        ),
        [ANY] * 3 + [VMEM] * 15,
        (VMEM, VMEM, ANY, VMEM, ANY, ANY),
        [
            pltpu.VMEM((seq, hw), bf16),
            pltpu.VMEM((seq, hw), f32),
            pltpu.VMEM((seq, 3 * hw), bf16),
            pltpu.VMEM((dr, width), bf16),
            pltpu.VMEM((cn, dr, 3 * hw), bf16),
            pltpu.VMEM((3, 1, width), f32),
            pltpu.VMEM((cn, 3, 1, width), f32),
            pltpu.VMEM((3, 1, width), f32),
            pltpu.VMEM((dpn, 3, 1, width), f32),
            dma((2, cn)),
            dma((2, cn)),
            dma((2, cn)),
            dma((2, dpn)),
            dma((2,)),
            dma((6,)),
        ]
        + line_scratch
        + ring_scratch(dpn, ff_rows, width)
        + ring_scratch(dpn, dr, width)
        + ring_scratch(dpn, cn * dr, 3 * hw),
        5,
        moved=160 * mib,
    )

    g_q, g_k, g_v, g_o, g_gate, g_up, g_down = pl.pallas_call(
        functools.partial(spread_kernel, cn, dpn),
        out_shape=tuple(shape((dr, width), f32) for _ in range(4))
        + tuple(shape((dr, ff * cn), f32) for _ in range(2))
        + (shape((ff_rows, width), f32),),
        in_specs=[ANY] * 4,
        out_specs=(VMEM,) * 7,
        scratch_shapes=[
            pltpu.VMEM((cn, dr, 3 * hw), bf16),
            pltpu.VMEM((cn, dr, 2 * ff), bf16),
            pltpu.VMEM((ff_rows, width), bf16),
            pltpu.VMEM((dr, width), bf16),
            dma((4,)),
        ],
        compiler_params=pltpu.CompilerParams(vmem_limit_bytes=48 * 2**20),
    )(q_all, gu_back, g_down, g_out)
    mass_mean = totals[2, 0, 0] / (heads * cn * dpn * seq)
    owner = (lax.axis_index("dp") * cn + lax.axis_index("ctx")) * dr
    grad_gains = [lax.dynamic_slice_in_dim(totals[i, 0], owner, dr) for i in range(2)]
    return (
        result[None],
        grad_input[None],
        g_q,
        g_k,
        g_v,
        g_o,
        g_gate,
        g_up,
        g_down,
        grad_gains[0],
        grad_gains[1],
        mass_mean,
    )


def solution(mesh):
    tok = P("dp", "ctx", None)
    ids = P("dp", "ctx")
    mat = P(("dp", "ctx"), None)
    vec = P(("dp", "ctx"))
    return jax.shard_map(
        shards,
        mesh=mesh,
        in_specs=(tok, tok, ids, ids) + (mat,) * 7 + (vec, vec),
        out_specs=(tok, tok) + (mat,) * 7 + (vec, vec, P()),
        check_vma=False,
    )
```

```python
import functools
import math

import jax
import jax.numpy as jnp
from jax import lax
from jax.experimental import pallas as pl
from jax.experimental.pallas import tpu as pltpu
from jax.sharding import PartitionSpec as P

HEAD_DIM = 128
norm_eps = 1e-05
rope_base = 10000.0
score_shift = math.log(4096.0)
score_scale = 1.0 / math.sqrt(HEAD_DIM)
contract_rows = (((0,), (0,)), ((), ()))
contract_cols = (((1,), (1,)), ((), ()))
plain = (((1,), (0,)), ((), ()))
f32 = jnp.float32
bf16 = jnp.bfloat16
MESH = pl.DeviceIdType.MESH
ANY = pl.BlockSpec(memory_space=pl.ANY)
VMEM = pl.BlockSpec(memory_space=pltpu.VMEM)


def dot(a, b, dims=plain):
    return lax.dot_general(a, b, dims, preferred_element_type=f32)


def remote(src, dst, send, recv, target):
    return pltpu.make_async_remote_copy(
        src_ref=src,
        dst_ref=dst,
        send_sem=send,
        recv_sem=recv,
        device_id=target,
        device_id_type=MESH,
    )


def greet(target):
    pl.semaphore_signal(
        pltpu.get_barrier_semaphore(), inc=1, device_id=target, device_id_type=MESH
    )


def by_rows(count, work, step=16):
    @pl.loop(0, count // step)
    def _(i):
        work(pl.ds(pl.multiple_of(i * step, step), step))


def place(cn):
    c = lax.axis_index("ctx")
    j, k = c // 2, c % 2
    return c, j, k, cn // 2, 2 * j + 1 - k


def greet_line(cn, ring):
    c, j, _, n, sib = place(cn)
    ring.greet()
    greet({"ctx": sib})

    @pl.when(j < n - 1)
    def _():
        greet({"ctx": c + 2})

    @pl.when(j > 0)
    def _():
        greet({"ctx": c - 2})

    inner = jnp.where(j > 0, 1, 0) + jnp.where(j < n - 1, 1, 0)
    pl.semaphore_wait(pltpu.get_barrier_semaphore(), 3 + inner)


def greet_ctx(cn):
    c = lax.axis_index("ctx")
    for s in range(1, cn):
        greet({"ctx": lax.rem(c + s, cn)})


class LineGather:
    def __init__(self, cn, own, full, sem):
        self.cn, self.own, self.full, self.sem = cn, own, full, sem

    def copy(self, src, origin, kind, target):
        _, _, k, _, _ = place(self.cn)
        sem = self.sem
        return remote(
            src,
            self.full.at[2 * origin + k],
            sem.at[kind, origin],
            sem.at[3 if kind < 2 else 4, origin],
            {"ctx": target},
        )

    def start(self):
        c, j, _, n, sib = place(self.cn)

        @pl.when(j < n - 1)
        def _():
            self.copy(self.own, j, 0, c + 2).start()

        @pl.when(j > 0)
        def _():
            self.copy(self.own, j, 1, c - 2).start()

        self.copy(self.own, j, 2, sib).start()

    def step(self, s):
        c, j, k, n, sib = place(self.cn)

        @pl.when(j - s >= 0)
        def _():
            o = j - s
            block = self.full.at[2 * o + k]
            self.copy(block, o, 0, sib).wait_recv()

            @pl.when(j < n - 1)
            def _():
                self.copy(block, o, 0, c + 2).start()

            self.copy(block, o, 2, sib).start()

        @pl.when(j + s <= n - 1)
        def _():
            o = j + s
            block = self.full.at[2 * o + k]
            self.copy(block, o, 1, sib).wait_recv()

            @pl.when(j > 0)
            def _():
                self.copy(block, o, 1, c - 2).start()

            self.copy(block, o, 2, sib).start()

    def forward(self, first=1, last=None):
        for s in range(first, self.cn // 2 if last is None else last + 1):
            self.step(s)

    def other(self, o):
        _, _, k, _, sib = place(self.cn)
        block = self.full.at[2 * o + 1 - k]
        remote(
            block, block, self.sem.at[2, o], self.sem.at[4, o], {"ctx": sib}
        ).wait_recv()

    def sent(self):
        c, j, k, n, sib = place(self.cn)
        for o in range(n):
            block = self.full.at[2 * o + k]

            @pl.when((j < n - 1) & (o <= j))
            def _():
                self.copy(block, o, 0, sib).wait_send()

            @pl.when((j > 0) & (o >= j))
            def _():
                self.copy(block, o, 1, sib).wait_send()

            self.copy(block, o, 2, sib).wait_send()

    def finish(self):
        for o in range(self.cn // 2):
            self.other(o)
        self.sent()


class Swap:
    def __init__(self, cn, src, dst, sem, local, pick=None):
        self.cn, self.sem, self.local = cn, sem, local
        self.src = pick or (lambda c: src.at[c])
        self.dst = dst if callable(dst) else lambda c: dst.at[c]

    def copy(self, s):
        c = lax.axis_index("ctx")
        peer = lax.rem(c + s, self.cn)
        return remote(
            self.src(peer),
            self.dst(c),
            self.sem.at[0, s],
            self.sem.at[1, s],
            {"ctx": peer},
        )

    def start(self):
        c = lax.axis_index("ctx")
        for s in range(1, self.cn):
            self.copy(s).start()
        pltpu.make_async_copy(self.src(c), self.dst(c), self.local).start()

    def receive(self, s):
        c = lax.axis_index("ctx")
        if s == 0:
            pltpu.make_async_copy(self.src(c), self.dst(c), self.local).wait()
            return c
        source = lax.rem(c - s + self.cn, self.cn)
        block = self.dst(source)
        remote(
            block, block, self.sem.at[0, s], self.sem.at[1, s], {"ctx": source}
        ).wait_recv()
        return source

    def sent(self):
        for s in range(1, self.cn):
            self.copy(s).wait_send()

    def finish(self):
        for s in range(self.cn):
            self.receive(s)
        self.sent()


class RingGather:
    def __init__(self, dpn, own, full, sem):
        self.dpn, self.own, self.full, self.sem = dpn, own, full, sem
        self.hops = dpn // 2
        d = lax.axis_index("dp")
        self.p = d // 2 * 2 + lax.rem(lax.rem(d, 2) + d // 2, 2)

    def member(self, step):
        p = lax.rem(self.p + step + self.dpn, self.dpn)
        return p // 2 * 2 + lax.rem(lax.rem(p, 2) + p // 2, 2)

    def half(self, ref, h, right):
        if h < self.hops:
            return ref
        m = self.full.shape[1] // 2
        if len(self.full.shape) == 3 and m % 16:
            m = self.full.shape[2] // 2
            return ref.at[:, pl.ds(0 if right else m, m)]
        return ref.at[pl.ds(0 if right else m, m)]

    def copy(self, h, right):
        way = 1 if right else -1
        origin = self.member(-way * (h - 1))
        src = self.own if h == 1 else self.full.at[origin]
        return remote(
            self.half(src, h, right),
            self.half(self.full.at[origin], h, right),
            self.sem.at[0 if right else 1, h],
            self.sem.at[2 if right else 3, h],
            {"dp": self.member(way)},
        )

    def arrival(self, h, right):
        way = 1 if right else -1
        block = self.half(self.full.at[self.member(-way * h)], h, right)
        return remote(
            block,
            block,
            self.sem.at[0 if right else 1, h],
            self.sem.at[2 if right else 3, h],
            {"dp": self.member(way)},
        )

    def greet(self):
        greet({"dp": self.member(1)})
        greet({"dp": self.member(-1)})

    def start(self):
        self.copy(1, True).start()
        self.copy(1, False).start()

    def forward(self):
        for h in range(1, self.hops):
            for right in (True, False):
                self.arrival(h, right).wait_recv()
                self.copy(h + 1, right).start()

    def finish(self):
        for right in (True, False):
            self.arrival(self.hops, right).wait_recv()
        for h in range(1, self.hops + 1):
            for right in (True, False):
                self.copy(h, right).wait_send()


def head_of(cn, heads, c, i):
    return c // 2 + cn // 2 * (heads * (c % 2) + i)


class HeadRows:
    def __init__(self, cn, dpn, dr):
        self.cn, self.dpn = cn, dpn
        self.per = HEAD_DIM // dr
        self.heads = dpn // self.per
        self.c, self.d = lax.axis_index("ctx"), lax.axis_index("dp")
        mine = self.d * cn + self.c
        head, n = mine // self.per, cn // 2
        turn = head // n
        self.home = 2 * lax.rem(head, n) + turn // self.heads
        self.slot = lax.rem(turn, self.heads) * self.per + lax.rem(mine, self.per)
        self.links = dpn - jnp.where(self.home == self.c, 1, 0)

    def owner(self, r):
        i, q = r // self.per, r % self.per
        head = self.c // 2 + self.cn // 2 * (self.heads * lax.rem(self.c, 2) + i)
        g = head * self.per + q
        return {"dp": g // self.cn, "ctx": lax.rem(g, self.cn)}

    def from_here(self, r):
        at = self.owner(r)
        return (at["dp"] == self.d) & (at["ctx"] == self.c)

    def to_here(self, to):
        return (self.home == self.c) & (self.d == to)

    def greet_owners(self):
        for r in range(self.dpn):
            pl.when(jnp.logical_not(self.from_here(r)))(lambda r=r: greet(self.owner(r)))

    def greet_homes(self):
        for to in range(self.dpn):
            pl.when(jnp.logical_not(self.to_here(to)))(
                lambda to=to: greet({"dp": to, "ctx": self.home})
            )


class RowGather(HeadRows):
    def __init__(self, cn, dpn, rows, full, sem, local):
        super().__init__(cn, dpn, rows.shape[0])
        self.rows, self.full, self.sem = rows, full, sem
        self.keep = pltpu.make_async_copy(rows, full.at[self.slot], local)

    def copy(self, to):
        return remote(
            self.rows,
            self.full.at[self.slot],
            self.sem.at[0, to],
            self.sem.at[1, self.slot],
            {"dp": to, "ctx": self.home},
        )

    def start(self):
        for to in range(self.dpn):
            pl.when(jnp.logical_not(self.to_here(to)))(lambda to=to: self.copy(to).start())
            pl.when(self.to_here(to))(self.keep.start)

    def finish(self):
        for r in range(self.dpn):
            block = self.full.at[r]
            came = remote(block, block, self.sem.at[0, r], self.sem.at[1, r], self.owner(r))
            pl.when(jnp.logical_not(self.from_here(r)))(came.wait_recv)
            pl.when(self.from_here(r))(self.keep.wait)
        for to in range(self.dpn):
            pl.when(jnp.logical_not(self.to_here(to)))(lambda to=to: self.copy(to).wait_send())


class RowSum(HeadRows):
    def __init__(self, cn, dpn, parts, got, sem):
        super().__init__(cn, dpn, parts.shape[1])
        self.parts, self.got, self.sem = parts, got, sem

    def copy(self, r):
        return remote(
            self.parts.at[r],
            self.got.at[self.d],
            self.sem.at[0, r],
            self.sem.at[1, self.d],
            self.owner(r),
        )

    def start(self):
        for r in range(self.dpn):
            pl.when(jnp.logical_not(self.from_here(r)))(lambda r=r: self.copy(r).start())

            @pl.when(self.from_here(r))
            def _():
                self.got[self.d] = self.parts[r]

    def finish(self, out):
        for s in range(self.dpn):
            block = self.got.at[s]
            came = remote(
                block, block, self.sem.at[0, s], self.sem.at[1, s], {"dp": s, "ctx": self.home}
            )
            pl.when(jnp.logical_not(self.to_here(s)))(came.wait_recv)

        def add(r):
            total = self.got[0, r, :].astype(f32)
            for s in range(1, self.dpn):
                total = total + self.got[s, r, :].astype(f32)
            out[r, :] = total

        by_rows(out.shape[0], add)
        for r in range(self.dpn):
            pl.when(jnp.logical_not(self.from_here(r)))(lambda r=r: self.copy(r).wait_send())


class RingPieces(RingGather):
    def __init__(self, dpn, full, sem):
        super().__init__(dpn, None, full, sem)

    def piece(self, i, h, right, back):
        way = 1 if right else -1
        ref = self.full.at[self.member(-way * back), i]
        return remote(
            ref,
            ref,
            self.sem.at[0 if right else 1, h, i],
            self.sem.at[2 if right else 3, h, i],
            {"dp": self.member(way)},
        )

    def moves(self, i, h, right, act):
        if h < self.hops:
            act()
        else:
            first = i < self.full.shape[1] // 2
            pl.when(first if right else jnp.logical_not(first))(act)

    def start(self, i):
        for right in (True, False):
            self.moves(i, 1, right, lambda r=right: self.piece(i, 1, r, 0).start())

    def forward(self, i):
        for h in range(1, self.hops):
            for right in (True, False):
                self.piece(i, h, right, h).wait_recv()
                self.moves(
                    i, h + 1, right, lambda h=h, r=right: self.piece(i, h + 1, r, h).start()
                )

    def finish(self, i):
        for right in (True, False):
            h = self.hops
            self.moves(i, h, right, lambda r=right: self.piece(i, h, r, h).wait_recv())
        for h in range(1, self.hops + 1):
            for right in (True, False):
                self.moves(
                    i, h, right, lambda h=h, r=right: self.piece(i, h, r, h - 1).wait_send()
                )


class RingSum:
    def __init__(self, dpn, blocks, got, got_half, sem):
        self.dpn, self.blocks, self.sem = dpn, blocks, sem
        self.got, self.got_half = got, got_half
        self.ring = RingGather(dpn, None, blocks, sem)
        self.hops = dpn // 2

    def part(self, s, right):
        m, width = self.blocks.shape[1:]
        if s > 1:
            return 0, m, pl.ds(0, width)
        if (m // 2) % 16:
            return 0, m, pl.ds(0 if right else width // 2, width // 2)
        return 0 if right else m // 2, m // 2, pl.ds(0, width)

    def copy(self, s, right):
        way = 1 if right else -1
        target = self.ring.member(way * (self.hops - s + 1))
        start, size, lanes = self.part(s, right)
        return remote(
            self.blocks.at[target, pl.ds(start, size), lanes],
            self.arrived(s, right),
            self.sem.at[0 if right else 1, s],
            self.sem.at[2 if right else 3, s],
            {"dp": self.ring.member(way)},
        )

    def arrived(self, s, right):
        side = 0 if right else 1
        return self.got_half.at[side] if s == 1 else self.got.at[side, s - 2]

    def order(self):
        out = [self.ring.member(self.hops)]
        for s in range(self.hops - 1, 0, -1):
            out += [self.ring.member(s), self.ring.member(-s)]
        return out + [self.ring.member(0)]

    def start(self):
        self.copy(1, True).start()
        self.copy(1, False).start()

    def take(self, s, right, target):
        self.copy(s, right).wait_recv()
        start, size, lanes = self.part(s, right)
        block = self.blocks.at[target, pl.ds(start, size), lanes]
        came = self.arrived(s, right)

        def add(r):
            block[r, :] = (block[r, :].astype(f32) + came[r, :].astype(f32)).astype(bf16)

        by_rows(size, add)

    def forward(self, s):
        for right in (True, False):
            way = 1 if right else -1
            self.take(s, right, self.ring.member(way * (self.hops - s)))
            self.copy(s + 1, right).start()

    def finish(self, out):
        for right in (True, False):
            self.copy(self.hops, right).wait_recv()
        mine = self.ring.member(0)
        ends = [self.arrived(self.hops, right) for right in (True, False)]
        per = out.shape[-2]

        @pl.loop(0, self.blocks.shape[1] // 16)
        def _(i):
            r = pl.ds(pl.multiple_of(i * 16, 16), 16)
            total = self.blocks[mine, r, :].astype(f32)
            for end in ends:
                total = total + end[r, :].astype(f32)
            if len(out.shape) == 3:
                to = pl.ds(pl.multiple_of(lax.rem(i * 16, per), 16), 16)
                out[i * 16 // per, to, :] = total.astype(out.dtype)
            else:
                out[r, :] = total.astype(out.dtype)

        for s in range(1, self.hops + 1):
            for right in (True, False):
                self.copy(s, right).wait_send()


def ring_scratch(dpn, m, width):
    return [
        pltpu.VMEM((dpn, m, width), bf16),
        pltpu.VMEM((2, dpn // 2 - 1, m, width), bf16),
        pltpu.VMEM((2, m // 2, width) if m % 32 == 0 else (2, m, width // 2), bf16),
        pltpu.SemaphoreType.DMA((4, dpn // 2 + 1)),
    ]


def outer(a_ref, b_ref, out, at, tile=512):
    a = a_ref[:, at]
    width = out.shape[-1]
    for lo in range(0, width, tile):
        to = slice(lo, min(lo + tile, width))
        out[:, to] = dot(a, b_ref[:, to], contract_rows).astype(bf16)


def outer_all(a_ref, staged, halves, blocks, tile=512):
    count, m, width = blocks.shape
    many = max(1, 128 // m)
    for first in range(0, count, many):
        at = slice(first * m, (first + many) * m)
        for lo in range(0, width, tile):
            to = slice(lo, min(lo + tile, width))
            part = dot(a_ref[halves[0], at], staged(0, to), contract_rows)
            part = part + dot(a_ref[halves[1], at], staged(1, to), contract_rows)
            part = part.astype(bf16)
            for i in range(many):
                blocks[first + i, :, to] = part[i * m : (i + 1) * m]


class LineSum:
    def __init__(self, cn, compute, part, cross, cross_in, flow, arrived, sem):
        self.cn, self.compute, self.part = cn, compute, part
        self.cross, self.cross_in, self.flow = cross, cross_in, flow
        self.arrived, self.sem = arrived, sem

    def across(self, t):
        _, _, _, _, sib = place(self.cn)
        return remote(
            self.cross.at[t],
            self.cross_in.at[t],
            self.sem.at[0, t],
            self.sem.at[2, t],
            {"ctx": sib},
        )

    def along(self, t, slot, target):
        return remote(
            self.flow.at[t],
            self.arrived.at[slot],
            self.sem.at[1, t],
            self.sem.at[3, slot],
            {"ctx": target},
        )

    def produce(self, t, slot):
        _, _, k, _, _ = place(self.cn)
        part = self.part.at[slot]
        self.compute(t, part)

        def low(r):
            self.cross[t, r, :] = part[1 - k, r, :].astype(bf16)

        by_rows(self.cross.shape[1], low)
        self.across(t).start()

    def add(self, part, came):
        def more(r):
            part[r, :] += came[r, :].astype(f32)

        by_rows(part.shape[0], more)

    def collect(self, t, slot):
        _, j, k, n, sib = place(self.cn)
        part = self.part.at[slot, k]
        self.across(t).wait_recv()
        self.add(part, self.cross_in.at[t])

        @pl.when((j > 0) & (t >= j))
        def _():
            self.along(t, t, sib).wait_recv()
            self.add(part, self.arrived.at[t])

        @pl.when((j < n - 1) & (t <= j))
        def _():
            slot_in = jnp.where(t == j, n, t)
            self.along(t, slot_in, sib).wait_recv()
            self.add(part, self.arrived.at[slot_in])

    def send(self, t, slot, up):
        c, j, k, n, _ = place(self.cn)

        def low(r):
            self.flow[t, r, :] = self.part[slot, k, r, :].astype(bf16)

        by_rows(self.flow.shape[1], low)
        there = t if up else jnp.where(t == j - 1, n, t)
        self.along(t, there, c + 2 if up else c - 2).start()

    def drain(self):
        _, j, _, n, sib = place(self.cn)

        @pl.loop(0, n)
        def _(t):
            self.across(t).wait_send()

            @pl.when(t != j)
            def _():
                self.along(t, t, sib).wait_send()


class LineSumRows(LineSum):
    def __init__(self, cn, terms, stage, loads, *refs):
        super().__init__(cn, None, *refs)
        self.terms, self.stage, self.loads = terms, stage, loads

    def produce(self, t, slot):
        _, _, k, _, _ = place(self.cn)
        other = pltpu.make_async_copy(
            self.terms.at[2 * t + 1 - k], self.cross.at[t], self.loads.at[0]
        )
        own = pltpu.make_async_copy(self.terms.at[2 * t + k], self.stage, self.loads.at[1])
        other.start()
        own.start()
        other.wait()
        self.across(t).start()
        own.wait()

        def wide(r):
            self.part[slot, k, r, :] = self.stage[r, :].astype(f32)

        by_rows(self.stage.shape[0], wide)


def line_sums(cn, sums, between=None):
    _, j, _, n, _ = place(cn)

    @pl.loop(0, n - 1)
    def _(s):
        to_up, to_down = n - 1 - s + j, s - (n - 1 - j)
        for total in sums:

            @pl.when(s >= j)
            def _():
                total.produce(to_up, 0)

            @pl.when(s >= n - 1 - j)
            def _():
                total.produce(to_down, 1)

        for total in sums:

            @pl.when(s >= j)
            def _():
                total.collect(to_up, 0)
                total.send(to_up, 0, True)

            @pl.when(s >= n - 1 - j)
            def _():
                total.collect(to_down, 1)
                total.send(to_down, 1, False)

        if between is not None:
            between(s)

    for total in sums:
        total.produce(j, 0)
    for total in sums:
        total.collect(j, 0)


def sum_scratch(cn, rows, width):
    n = cn // 2
    return [
        pltpu.VMEM((2, 2, rows, width), f32),
        pltpu.VMEM((n, rows, width), bf16),
        pltpu.VMEM((n, rows, width), bf16),
        pltpu.VMEM((n, rows, width), bf16),
        pltpu.VMEM((n + 1, rows, width), bf16),
        pltpu.SemaphoreType.DMA((4, n + 1)),
    ]


def product(a_ref, b_ref, dims, rows, width):
    tile = min(512, width)

    def compute(t, out):
        a = a_ref[pl.ds(pl.multiple_of(t * 2 * rows, 2 * rows), 2 * rows), :]

        @pl.loop(0, width // tile)
        def _(i):
            at = pl.ds(pl.multiple_of(i * tile, tile), tile)
            b = b_ref[:, at] if dims == plain else b_ref[at, 0 : a_ref.shape[1]]
            out[:, :, at] = dot(a, b, dims).reshape(2, rows, tile)

    return compute


def rms(v):
    return lax.rsqrt(jnp.mean(v * v, axis=-1, keepdims=True) + norm_eps)


def front_kernel(
    cn, dpn, x, wq, wk, wv, gains, wo, gate_in, up_in, down_in,
    x_all, pack_all, gate, up, down_all, wo_low,
    pack, wide, tall, down, gsem, ssem, rsem, dsem, local,
):
    c, d = lax.axis_index("ctx"), lax.axis_index("dp")
    hw = wq.shape[1] // cn
    part = gate_in.shape[1] // (cn * dpn)
    mine = pack_all.at[d]
    swap = Swap(cn, pack, mine, ssem, local.at[0])
    gather = LineGather(cn, x, x_all, gsem)
    ring = RingPieces(dpn, pack_all, rsem)
    down_ring = RingGather(dpn, down, down_all, dsem)
    greet_ctx(cn)
    ring.greet()
    loads = [
        pltpu.make_async_copy(src, dst, local.at[i])
        for i, (src, dst) in enumerate(
            ((gate_in, wide.at[0]), (up_in, wide.at[1]), (down_in, tall)), 2
        )
    ]
    for load in loads:
        load.start()
    for to in range(cn):
        for i, w in enumerate((wq, wk, wv)):
            for t in range(hw // HEAD_DIM):
                lo, at = head_of(cn, hw // HEAD_DIM, to, t) * HEAD_DIM, i * hw + t * HEAD_DIM
                pack[to, :, at : at + HEAD_DIM] = w[:, lo : lo + HEAD_DIM].astype(bf16)
        pack[to, :, 3 * hw :] = gains[...]
    pl.semaphore_wait(pltpu.get_barrier_semaphore(), cn - 1 + 2)
    swap.start()
    gather.start()
    loads[2].wait()
    down[...] = tall[...].astype(bf16)
    down_ring.start()
    keep_down = pltpu.make_async_copy(down, down_all.at[d], local.at[5])
    keep_down.start()
    keep = pltpu.make_async_copy(x, x_all.at[c], local.at[1])
    keep.start()
    wo_low[...] = wo[...].astype(bf16)

    def lay(i, out):
        loads[i].wait()
        for to in range(cn):
            for row in range(dpn):
                lo = (row * cn + to) * part
                out[to, :, row * part : (row + 1) * part] = wide[i, :, lo : lo + part].astype(bf16)

    half = cn // 2
    sources = [swap.receive(0)]
    ring.start(sources[0])
    lay(0, gate)
    for s in range(1, half):
        sources.append(swap.receive(s))
        ring.start(sources[s])
    gather.forward(1, 1)
    lay(1, up)
    for s in range(half, cn):
        sources.append(swap.receive(s))
        ring.start(sources[s])
    down_ring.forward()
    gather.forward(2, 2)
    for source in sources:
        ring.forward(source)
    gather.forward(3)
    keep.wait()
    keep_down.wait()
    gather.finish()
    for source in sources:
        ring.finish(source)
    swap.sent()
    down_ring.finish()


def prepare(w, x_all, gains, info_rows, hw, block):
    width = w.shape[0]
    per = block // x_all.shape[1]

    @pl.loop(0, width // block)
    def _(i):
        at = pl.ds(pl.multiple_of(i * block, block), block)
        gains[:, at] = w[at, 3 * hw : 3 * hw + 128].astype(f32).T[0:8]

    @pl.loop(0, info_rows.shape[1] // block)
    def _(i):
        at = pl.ds(pl.multiple_of(i * block, block), block)
        codes = x_all[pl.ds(i * per, per), :, width:].reshape(block, 128).astype(f32).T[0:8]
        seg = jnp.floor(codes * 0.5)
        code = jnp.where(codes - 2.0 * seg == 1.0, seg, -1.0)
        first = lax.broadcasted_iota(jnp.int32, (8, block), 0) == 0
        info_rows[:, at] = jnp.where(first, seg, code)


def tables(x_all, inverse, info_rows, info_cols, cosines, sines, width, i, block):
    per = block // x_all.shape[1]
    at = pl.ds(pl.multiple_of(i * block, block), block)
    codes = x_all[pl.ds(i * per, per), :, width:].reshape(block, 128).astype(f32)
    seg = jnp.floor(codes * 0.5)
    valid = codes - 2.0 * seg
    lane = lax.broadcasted_iota(jnp.int32, (block, 128), 1)
    code = jnp.where(valid == 1.0, seg, -1.0)
    info_cols[at, :] = jnp.where(lane == 0, seg, jnp.where(lane == 1, valid, code))
    before = jnp.where(info_rows[0:1, :] < seg[:, 0:1], 1.0, 0.0)
    index = lax.broadcasted_iota(jnp.int32, (block, 128), 0) + i * block
    place_in = index.astype(f32) - jnp.sum(before, axis=1, keepdims=True)
    angles = place_in * inverse[...]
    cosines[at, :] = jnp.cos(angles)
    sines[at, :] = jnp.where(lane < HEAD_DIM // 2, -1.0, 1.0) * jnp.sin(angles)


def project(x_all, w, gain, inverse, rows_in, cols, cosines, sines, an, qkv, hw, block, hook):
    width = an.shape[1]
    per = block // x_all.shape[1]

    @pl.loop(0, an.shape[0] // block)
    def _(i):
        at = pl.ds(pl.multiple_of(i * block, block), block)
        tables(x_all, inverse, rows_in, cols, cosines, sines, width, i, block)
        x = x_all[pl.ds(i * per, per), :, 0:width].reshape(block, width).astype(f32)
        normed = (x * rms(x) * gain[...]).astype(bf16)
        an[at, :] = normed
        proj = dot(normed, w[:, 0 : 3 * hw])
        cos_b, sin_b = cosines[at, :], sines[at, :]
        for h in range(2 * hw // HEAD_DIM):
            lanes = slice(h * HEAD_DIM, (h + 1) * HEAD_DIM)
            v = proj[:, lanes]
            turned = v * cos_b + pltpu.roll(v, HEAD_DIM // 2, 1) * sin_b
            qkv[at, lanes] = turned.astype(bf16)
        qkv[at, 2 * hw :] = proj[:, 2 * hw :].astype(bf16)
        hook(i)


def mask_block(q_seg, k_code, i, j, block):
    rows = lax.broadcasted_iota(jnp.int32, (block, block), 0) + i * block
    cols = lax.broadcasted_iota(jnp.int32, (block, block), 1) + j * block
    return (q_seg == k_code) & (cols <= rows)


def attend(qkv, q_info, k_code, out, mass, hw, block, hook):
    mass[...] = jnp.zeros_like(mass)

    @pl.loop(0, qkv.shape[0] // block)
    def _(i):
        at = pl.ds(pl.multiple_of(i * block, block), block)
        q_seg, q_valid = q_info[at, 0:1], q_info[at, 1:2]
        for h in range(hw // HEAD_DIM):
            lane = [slice(t * hw + h * HEAD_DIM, t * hw + (h + 1) * HEAD_DIM) for t in range(3)]
            q = qkv[at, lane[0]]

            def step(j, acc):
                to = pl.ds(pl.multiple_of(j * block, block), block)
                s = dot(q, qkv[to, lane[1]], contract_cols) * score_scale - score_shift
                allowed = mask_block(q_seg, k_code[1:2, to], i, j, block)
                p = jnp.where(allowed, jax.nn.sigmoid(s), 0.0)
                mass[...] += jnp.sum(p * q_valid, axis=0, keepdims=True)
                return acc + dot(p.astype(bf16), qkv[to, lane[2]])

            acc = lax.fori_loop(0, i + 1, step, jnp.zeros((block, HEAD_DIM), f32))
            out[at, lane[0]] = acc.astype(bf16)
        hook(i)


def attn_kernel(
    cn, dpn, x_all, w, inverse, gate, up, wo,
    an, qkv, o, mass, gains, cosines, sines, cols, rows_in,
    gate_all, up_own, wo_all, ssem, rsem, wsem, local,
):
    c, d = lax.axis_index("ctx"), lax.axis_index("dp")
    wo_rows = RowGather(cn, dpn, wo, wo_all, wsem, local.at[2])
    rows = x_all.shape[1]
    hw = qkv.shape[1] // 3
    swap_gate = Swap(cn, gate, gate_all.at[d], ssem.at[0], local.at[0])
    swap_up = Swap(cn, up, up_own, ssem.at[1], local.at[1])
    ring = RingPieces(dpn, gate_all, rsem)
    sources = [lax.rem(c - s + cn, cn) for s in range(cn)]
    greet_ctx(cn)
    ring.greet()

    wo_rows.greet_owners()
    pl.semaphore_wait(pltpu.get_barrier_semaphore(), cn - 1 + 2 + wo_rows.links)
    wo_rows.start()
    swap_gate.start()

    def in_project(i):
        @pl.when(i == 1)
        def _():
            for s in range(cn // 2):
                ring.start(swap_gate.receive(s))

        @pl.when(i == 2)
        def _():
            for s in range(cn // 2, cn):
                ring.start(swap_gate.receive(s))
            swap_up.start()

    def in_attend(i):
        @pl.when(i == 2)
        def _():
            for source in sources[: cn // 2]:
                ring.forward(source)

    prepare(w, x_all, gains, rows_in, hw, 2 * rows)
    project(
        x_all, w, gains.at[0:1], inverse, rows_in, cols, cosines, sines, an, qkv, hw, 2 * rows,
        in_project,
    )
    attend(qkv, cols, rows_in, o, mass, hw, 2 * rows, in_attend)
    for source in sources[cn // 2 :]:
        ring.forward(source)
    swap_up.finish()
    wo_rows.finish()
    for source in sources:
        ring.finish(source)
    swap_gate.sent()


def middle_kernel(
    cn, dpn, o, wo, x, gain, dy, up, gate_all, down_all,
    h1, bn_all, up_all, hid, dgu, branch_all, dys_all,
    own, bn, dys, wg, wu, down, branch, gsem, ysem, rsem, local, *sum_refs,
):
    c, d = lax.axis_index("ctx"), lax.axis_index("dp")
    _, j, k, n, _ = place(cn)
    rows, width = x.shape
    ff = hid.shape[1]
    block = 2 * rows
    gather = LineGather(cn, own, bn, gsem)
    gather_dy = LineGather(cn, dy, dys, ysem)
    ring = RingGather(dpn, up, up_all, rsem)
    total = LineSum(cn, product(o, wo, plain, rows, width), *sum_refs)
    greet_line(cn, ring)
    ring.start()
    keep_up = pltpu.make_async_copy(up, up_all.at[d], local.at[0])
    loads = [
        pltpu.make_async_copy(src, dst, local.at[i])
        for i, (src, dst) in enumerate(((gate_all, wg), (down_all, down)), 2)
    ]
    keep_up.start()
    for load in loads:
        load.start()
    gather_dy.start()
    dys[c] = dy[...]

    def between(s):
        gather_dy.step(s + 1)

        @pl.when(s == n - 2)
        def _():
            ring.forward()

    line_sums(cn, [total], between)

    def norm(r):
        mid = x[r, :].astype(f32) + total.part[0, k, r, :]
        h1[r, :] = mid
        own[r, :] = (mid * rms(mid) * gain[1:2, :]).astype(bf16)

    by_rows(rows, norm)
    gather.start()
    bn[c] = own[...]
    gather_dy.finish()
    store_dy = pltpu.make_async_copy(dys, dys_all, local.at[4])
    store_dy.start()
    total.drain()
    keep_up.wait()
    for load in loads:
        load.wait()
    ring.finish()
    load_up = pltpu.make_async_copy(up_all, wu, local.at[0])
    load_up.start()
    load_up.wait()
    wgate, wup = wg, wu.reshape(width, ff)
    tile = min(512, ff)
    wide = min(512, width)

    def feed(t):
        gather.other(t)
        at = pl.ds(pl.multiple_of(t * block, block), block)
        pair = pl.ds(t * 2, 2)
        send = pltpu.make_async_copy(bn.at[pair], bn_all.at[pair], local.at[1])
        send.start()
        a = bn[pair].reshape(block, width)
        g_out = dys[pair].reshape(block, width)

        @pl.loop(0, ff // tile)
        def _(i):
            to = pl.ds(pl.multiple_of(i * tile, tile), tile)
            gate = dot(a, wgate[:, to])
            up_v = dot(a, wup[:, to])
            dhid = dot(g_out, down[to, :], contract_cols)
            sig = jax.nn.sigmoid(gate)
            silu = gate * sig
            hid[at, to] = (silu * up_v).astype(bf16)
            dgate = dhid * up_v * sig * (1.0 + gate * (1.0 - sig))
            dgu[at, to] = dgate.astype(bf16)
            dgu[at, pl.ds(pl.multiple_of(ff + i * tile, tile), tile)] = (dhid * silu).astype(bf16)

        h = hid[at, :]

        @pl.loop(0, width // wide)
        def _(i):
            to = pl.ds(pl.multiple_of(i * wide, wide), wide)
            branch[:, to] = dot(h, down[:, to]).astype(bf16)

        out = pltpu.make_async_copy(branch, branch_all.at[at], local.at[0])
        out.start()
        out.wait()
        send.wait()

    feed(j)

    @pl.loop(1, n)
    def _(s):
        gather.step(s)

        @pl.when(j - s >= 0)
        def _():
            feed(j - s)

        @pl.when(j + s <= n - 1)
        def _():
            feed(j + s)

    gather.sent()
    store_dy.wait()


def back_kernel(
    cn, dpn, bn, dgu, wg, wu, h1, dy, gain, branch_all, dh1, dob_all, term, g_own, result,
    own, branch, cross_in, arrived, bsem, gsem, loads, keep_sem, *scratch,
):
    sum_refs, ring_refs = scratch[:-4], scratch[-4:]
    rows, width = dy.shape
    ff = wg.shape[1]
    tile = min(512, width)
    c, _, k, n, _ = place(cn)

    def compute(t, out):
        at = pl.ds(pl.multiple_of(t * 2 * rows, 2 * rows), 2 * rows)

        @pl.loop(0, width // tile)
        def _(i):
            to = pl.ds(pl.multiple_of(i * tile, tile), tile)
            part = dot(dgu[at, 0:ff], wg[to, :], contract_cols)
            part = part + dot(dgu[at, ff:], wu[to, :], contract_cols)
            out[:, :, to] = part.reshape(2, rows, tile)

    total = LineSum(cn, compute, *sum_refs)
    ring = RingSum(dpn, *ring_refs)
    blocks = ring_refs[0]
    m = blocks.shape[1]
    greet_line(cn, ring.ring)
    order = ring.order()

    def weight_grad(member):
        outer(bn, dgu, blocks.at[member], pl.ds(pl.multiple_of(member * m, m), m))

    weight_grad(order[0])
    ring.start()

    def between(s):
        for i in range(ring.hops - 1):

            @pl.when(s == min(i, n - 2))
            def _():
                weight_grad(order[1 + 2 * i])
                weight_grad(order[2 + 2 * i])

            @pl.when(s == min(i + 1, n - 2))
            def _():
                ring.forward(i + 1)

    line_sums(cn, [total], between)
    term[...] = jnp.zeros_like(term)

    def norm_back(r):
        dbn = total.part[0, k, r, :]
        mid = h1[r, :]
        r2 = rms(mid)
        xh2 = mid * r2
        term[...] += jnp.sum(dbn * xh2, axis=0, keepdims=True)
        u2 = dbn * gain[1:2, :]
        mean = jnp.mean(u2 * xh2, axis=-1, keepdims=True)
        grad = dy[r, :].astype(f32) + r2 * (u2 - xh2 * mean)
        dh1[r, :] = grad
        own[r, :] = grad.astype(bf16)

    by_rows(rows, norm_back)
    gather = LineGather(cn, own, dob_all, gsem)
    gather.start()
    keep = pltpu.make_async_copy(own, dob_all.at[c], keep_sem)
    keep.start()
    total.drain()

    part, cross, _, flow, _, _ = sum_refs
    second = LineSumRows(
        cn, branch_all, branch, loads, part, cross, cross_in, flow, arrived, bsem
    )

    def pass_on(s):
        gather.step(s + 1)

        @pl.when(s == 0)
        def _():
            weight_grad(order[-1])

    line_sums(cn, [second], pass_on)

    def close(r):
        result[r, :] = (h1[r, :] + second.part[0, k, r, :]).astype(bf16)

    by_rows(rows, close)
    second.drain()
    keep.wait()
    gather.finish()
    ring.finish(g_own)


def attend_back(qkv, do, cosines, sines, q_info, k_info, dq, dqkv, hw, block):
    count = qkv.shape[0] // block
    dq[...] = jnp.zeros_like(dq)

    def turn_back(g, at):
        return g * cosines[at, :] - pltpu.roll(g, HEAD_DIM // 2, 1) * sines[at, :]

    @pl.loop(0, count)
    def _(j):
        to = pl.ds(pl.multiple_of(j * block, block), block)
        k_code = k_info[to, 2:3]
        for h in range(hw // HEAD_DIM):
            lane = [slice(t * hw + h * HEAD_DIM, t * hw + (h + 1) * HEAD_DIM) for t in range(3)]
            k, v = qkv[to, lane[1]], qkv[to, lane[2]]

            def step(i, carry):
                dk, dv = carry
                at = pl.ds(pl.multiple_of(i * block, block), block)
                q, do_i = qkv[at, lane[0]], do[at, lane[0]]
                s = dot(k, q, contract_cols) * score_scale - score_shift
                keys = lax.broadcasted_iota(jnp.int32, (block, block), 0) + j * block
                queries = lax.broadcasted_iota(jnp.int32, (block, block), 1) + i * block
                allowed = (k_code == q_info[0:1, at]) & (keys <= queries)
                sg = jnp.where(allowed, jax.nn.sigmoid(s), 0.0)
                dp = dot(v, do_i, contract_cols)
                ds = (dp * sg * (1.0 - sg)).astype(bf16)
                dq[at, lane[0]] += dot(ds, k, contract_rows)
                return dk + dot(ds, q), dv + dot(sg.astype(bf16), do_i)

            zero = jnp.zeros((block, HEAD_DIM), f32)
            dk, dv = lax.fori_loop(j, count, step, (zero, zero))
            dqkv[to, lane[1]] = turn_back(dk * score_scale, to).astype(bf16)
            dqkv[to, lane[2]] = dv.astype(bf16)

    @pl.loop(0, count)
    def _(i):
        at = pl.ds(pl.multiple_of(i * block, block), block)
        for h in range(hw // HEAD_DIM):
            lanes = slice(h * HEAD_DIM, (h + 1) * HEAD_DIM)
            dqkv[at, lanes] = turn_back(dq[at, lanes] * score_scale, at).astype(bf16)


def last_kernel(
    cn, dpn, g_gu, dob_all, dys_all, hid, o, wo, qkv, cosines, sines, q_info, k_info, an, w,
    dh1, x, gain, term_two, mass, grad_in, tot_out, gu_all, down_own, out_all, qkv_all,
    do, dq, dqkv, out_parts, out_got, qkv_own, tot, tot_in, tot_sum, tot_last,
    usem, qsem, tsem, psem, osem, local, *scratch,
):
    sum_refs, rings = scratch[:-8], (scratch[-8:-4], scratch[-4:])
    rows, width = x.shape
    hw = width // cn
    _, _, k, n, _ = place(cn)
    down_ring, qkv_ring = (RingSum(dpn, *refs) for refs in rings)
    rows_out = RowSum(cn, dpn, out_parts, out_got, osem)
    swap_gu = Swap(cn, g_gu, gu_all, usem, local.at[0])
    swap_qkv = Swap(cn, qkv_own, qkv_all, qsem, local.at[4])
    totals = Swap(cn, None, tot_in, tsem, local.at[3], lambda i: tot)
    c, d = lax.axis_index("ctx"), lax.axis_index("dp")
    def share(s):
        return remote(
            tot_sum, tot_last.at[d], psem.at[0, s], psem.at[1, s], {"dp": lax.rem(d + s, dpn)}
        )

    greet_ctx(cn)
    for s in range(1, dpn):
        greet({"dp": lax.rem(d + s, dpn)})

    rows_out.greet_homes()
    pl.semaphore_wait(
        pltpu.get_barrier_semaphore(), cn - 1 + dpn - 1 + rows_out.links
    )
    swap_gu.start()
    seq = an.shape[0]
    stage = (sum_refs[1], sum_refs[3])
    halves = (slice(0, seq // 2), slice(seq // 2, seq))

    def fill(src):
        copies = [
            pltpu.make_async_copy(src.at[pl.ds(i * n, n)], stage[i], local.at[1 + i])
            for i in range(2)
        ]
        for copy in copies:
            copy.start()
        for copy in copies:
            copy.wait()

    def staged(i, to=slice(None)):
        return stage[i][:, :, to].reshape(seq // 2, -1)

    fill(dys_all)
    outer_all(hid, staged, halves, rings[0][0])
    down_ring.start()
    fill(dob_all)
    for i in range(2):
        do[halves[i], :] = dot(staged(i), wo[...], contract_cols).astype(bf16)
    outer_all(o, staged, halves, out_parts)
    rows_out.start()
    m_qkv = rings[1][0].shape[1]
    order = qkv_ring.order()

    def grad_qkv(member):
        outer(an, dqkv, rings[1][0].at[member], pl.ds(pl.multiple_of(member * m_qkv, m_qkv), m_qkv))

    attend_back(qkv, do, cosines, sines, q_info, k_info, dq, dqkv, hw, 2 * rows)
    for i in range(down_ring.hops - 1):
        down_ring.forward(i + 1)
    grad_qkv(order[0])
    qkv_ring.start()
    total = LineSum(cn, product(dqkv, w, contract_cols, rows, width), *sum_refs)

    def between(s):
        for i in range(qkv_ring.hops - 1):

            @pl.when(s == min(i, n - 2))
            def _():
                grad_qkv(order[1 + 2 * i])
                grad_qkv(order[2 + 2 * i])

            @pl.when(s == min(i + 1, n - 2))
            def _():
                qkv_ring.forward(i + 1)

    line_sums(cn, [total], between)
    grad_qkv(order[-1])
    tot[0] = jnp.zeros((1, width), f32)

    def norm_back(r):
        dan = total.part[0, k, r, :]
        xf = x[r, :].astype(f32)
        r1 = rms(xf)
        xh1 = xf * r1
        tot[0] += jnp.sum(dan * xh1, axis=0, keepdims=True)
        u1 = dan * gain[0:1, :]
        mean = jnp.mean(u1 * xh1, axis=-1, keepdims=True)
        grad = dh1[r, :] + r1 * (u1 - xh1 * mean)
        grad_in[r, :] = grad.astype(bf16)

    by_rows(rows, norm_back)
    tot[1] = term_two[...]
    tot[2] = jnp.broadcast_to(jnp.sum(mass[...], axis=1, keepdims=True), (1, width))
    totals.start()
    qkv_ring.finish(qkv_own)
    swap_qkv.start()
    rows_out.finish(out_all)
    totals.finish()
    tot_sum[...] = jnp.sum(tot_in[...], axis=0)
    for s in range(1, dpn):
        share(s).start()
    down_ring.finish(down_own)
    total.drain()
    swap_gu.finish()
    tot_last[d] = tot_sum[...]
    for s in range(1, dpn):
        source = lax.rem(d - s + dpn, dpn)
        block = tot_last.at[source]
        remote(block, block, psem.at[0, s], psem.at[1, s], {"dp": source}).wait_recv()
    for s in range(1, dpn):
        share(s).wait_send()
    tot_out[...] = jnp.sum(tot_last[...], axis=0)
    swap_qkv.finish()


def spread_kernel(
    cn, dpn, qkv_in, gu_in, down_in, out_in, gq, gk, gv, go, gg, gu_out, gd, qkv, gu, down, out, sem
):
    hw = qkv.shape[2] // 3
    ff_rows = gd.shape[0]
    ff = ff_rows * dpn
    pairs = ((down_in, down), (out_in, out), (qkv_in, qkv), (gu_in, gu))
    loads = [pltpu.make_async_copy(a, b, sem.at[i]) for i, (a, b) in enumerate(pairs)]
    for load in loads:
        load.start()
    for load in loads[:3]:
        load.wait()
    gd[...] = down[...].astype(f32)
    go[...] = out[...]
    for c in range(cn):
        for i, ref in enumerate((gq, gk, gv)):
            for t in range(hw // HEAD_DIM):
                lo, at = head_of(cn, hw // HEAD_DIM, c, t) * HEAD_DIM, i * hw + t * HEAD_DIM
                ref[:, lo : lo + HEAD_DIM] = qkv[c, :, at : at + HEAD_DIM].astype(f32)
    loads[3].wait()
    for c in range(cn):
        for i, ref in enumerate((gg, gu_out)):
            for d in range(dpn):
                to = (d * cn + c) * ff_rows
                lo = i * ff + d * ff_rows
                ref[:, to : to + ff_rows] = gu[c, :, lo : lo + ff_rows].astype(f32)


def call(kernel, outs, ins, specs_in, specs_out, scratch, number, flops=0, moved=0):
    return pl.pallas_call(
        kernel,
        out_shape=outs,
        in_specs=specs_in,
        out_specs=specs_out,
        scratch_shapes=scratch,
        compiler_params=pltpu.CompilerParams(
            collective_id=number, has_side_effects=True, vmem_limit_bytes=61 * 2**20
        ),
        cost_estimate=pl.CostEstimate(flops=flops, bytes_accessed=moved, transcendentals=0),
    )(*ins)


def shape(dims, dtype=bf16):
    return jax.ShapeDtypeStruct(dims, dtype)


def shards(
    hidden_in,
    out_grad,
    seg_ids,
    valid_mask,
    w_query,
    w_key,
    w_value,
    w_output,
    w_gate,
    w_up,
    w_down,
    gain_attn,
    gain_mlp,
):
    dpn = lax.axis_size("dp")
    cn = lax.axis_size("ctx")
    n = cn // 2
    x_local = hidden_in[0]
    dy_local = out_grad[0]
    rows, width = x_local.shape
    seq = rows * cn
    dr = w_query.shape[0]
    hw = width // cn
    heads = hw // HEAD_DIM
    ff_rows = w_down.shape[0]
    ff = ff_rows * dpn
    dma = pltpu.SemaphoreType.DMA
    mib = 2**20

    code = (seg_ids[0] * 2 + valid_mask[0]).astype(bf16)
    x_ext = jnp.concatenate([x_local, jnp.broadcast_to(code[:, None], (rows, 128))], axis=1)
    lanes = jnp.arange(128)[None, :]
    gain_cols = jnp.where(lanes == 0, gain_attn[:, None], gain_mlp[:, None]).astype(bf16)
    pw = 3 * hw + 128
    ring_sem = dma((4, dpn // 2 + 1))
    x_all, w_qkv, gate_pack, up_pack, down, wo_low = call(
        functools.partial(front_kernel, cn, dpn),
        (
            shape((cn, rows, width + 128)),
            shape((dpn, cn, dr, pw)),
            shape((cn, dr, ff)),
            shape((cn, dr, ff)),
            shape((dpn, ff_rows, width)),
            shape((dr, width)),
        ),
        (x_ext, w_query, w_key, w_value, gain_cols, w_output, w_gate, w_up, w_down),
        [ANY] + [VMEM] * 5 + [ANY] * 3,
        (ANY, ANY, VMEM, VMEM, ANY, VMEM),
        [
            pltpu.VMEM((cn, dr, pw), bf16),
            pltpu.VMEM((2, dr, ff * cn), f32),
            pltpu.VMEM((ff_rows, width), f32),
            pltpu.VMEM((ff_rows, width), bf16),
            dma((5, n)),
            dma((2, cn)),
            dma((4, dpn // 2 + 1, cn)),
            ring_sem,
            dma((6,)),
        ],
        1,
        moved=160 * mib,
    )
    w_qkv = w_qkv.reshape(width, pw)
    inverse = jnp.exp(
        jnp.arange(HEAD_DIM // 2, dtype=f32) * (-2.0 * math.log(rope_base) / HEAD_DIM)
    )
    inverse = jnp.concatenate([inverse, inverse])[None]

    line_scratch = sum_scratch(cn, rows, width)
    an, proj, o, mass, gains, cosines, sines, cols, infos, w_gate_c, up_own, wo = call(
        functools.partial(attn_kernel, cn, dpn),
        (
            shape((seq, width)),
            shape((seq, 3 * hw)),
            shape((seq, hw)),
            shape((1, 2 * rows), f32),
            shape((8, width), f32),
            shape((seq, HEAD_DIM), f32),
            shape((seq, HEAD_DIM), f32),
            shape((seq, 128), f32),
            shape((8, seq), f32),
            shape((dpn, cn, dr, ff)),
            shape((cn, dr, ff)),
            shape((dpn, dr, width)),
        ),
        (x_all, w_qkv, inverse, gate_pack, up_pack, wo_low),
        [VMEM] * 3 + [ANY] * 3,
        (VMEM,) * 9 + (ANY,) * 3,
        [dma((2, 2, cn)), dma((4, dpn // 2 + 1, cn)), dma((2, dpn)), dma((3,))],
        2,
        moved=160 * mib,
    )
    down = down.reshape(ff, width)
    h1, bn, w_up_c, hid, dgu, branch, dys = call(
        functools.partial(middle_kernel, cn, dpn),
        (
            shape((rows, width), f32),
            shape((cn, rows, width)),
            shape((dpn, cn, dr, ff)),
            shape((seq, ff)),
            shape((seq, 2 * ff)),
            shape((seq, width)),
            shape((cn, rows, width)),
        ),
        (
            o, wo.reshape(hw, width), x_local, gains, dy_local, up_own,
            w_gate_c.reshape(width, ff), down,
        ),
        [VMEM] * 5 + [ANY] * 3,
        (VMEM, ANY, ANY, VMEM, VMEM, ANY, ANY),
        [
            pltpu.VMEM((rows, width), bf16),
            pltpu.VMEM((cn, rows, width), bf16),
            pltpu.VMEM((cn, rows, width), bf16),
            pltpu.VMEM((width, ff), bf16),
            pltpu.VMEM((dpn, cn, dr, ff), bf16),
            pltpu.VMEM((ff, width), bf16),
            pltpu.VMEM((2 * rows, width), bf16),
            dma((5, n)),
            dma((5, n)),
            ring_sem,
            dma((5,)),
        ]
        + line_scratch,
        3,
        moved=160 * mib,
    )
    wo = wo.reshape(hw, width)
    w_gate_c = w_gate_c.reshape(width, ff)
    w_up_c = w_up_c.reshape(width, ff)
    bn = bn.reshape(seq, width)
    dh1, dob, term_two, g_gu, result = call(
        functools.partial(back_kernel, cn, dpn),
        (
            shape((rows, width), f32),
            shape((cn, rows, width)),
            shape((1, width), f32),
            shape((cn, dr, 2 * ff)),
            shape((rows, width)),
        ),
        (bn, dgu, w_gate_c, w_up_c, h1, dy_local, gains, branch.reshape(cn, rows, width)),
        [VMEM] * 7 + [ANY],
        (VMEM, ANY, VMEM, VMEM, VMEM),
        [
            pltpu.VMEM((rows, width), bf16),
            pltpu.VMEM((rows, width), bf16),
            pltpu.VMEM((n, rows, width), bf16),
            pltpu.VMEM((n + 1, rows, width), bf16),
            dma((4, n + 1)),
            dma((5, n)),
            dma((2,)),
            dma,
        ]
        + line_scratch
        + ring_scratch(dpn, cn * dr, 2 * ff),
        4,
        moved=160 * mib,
    )
    grad_input, totals, gu_back, g_down, g_out, q_all = call(
        functools.partial(last_kernel, cn, dpn),
        (
            shape((rows, width)),
            shape((3, 1, width), f32),
            shape((cn, dr, 2 * ff)),
            shape((ff_rows, width)),
            shape((dr, width), f32),
            shape((cn, dr, 3 * hw)),
        ),
        (
            g_gu, dob, dys, hid, o, wo, proj, cosines, sines, infos, cols, an, w_qkv,
            dh1, x_local, gains, term_two, mass,
        ),
        [ANY] * 3 + [VMEM] * 15,
        (VMEM, VMEM, ANY, VMEM, VMEM, ANY),
        [
            pltpu.VMEM((seq, hw), bf16),
            pltpu.VMEM((seq, hw), f32),
            pltpu.VMEM((seq, 3 * hw), bf16),
            pltpu.VMEM((dpn, dr, width), bf16),
            pltpu.VMEM((dpn, dr, width), bf16),
            pltpu.VMEM((cn, dr, 3 * hw), bf16),
            pltpu.VMEM((3, 1, width), f32),
            pltpu.VMEM((cn, 3, 1, width), f32),
            pltpu.VMEM((3, 1, width), f32),
            pltpu.VMEM((dpn, 3, 1, width), f32),
            dma((2, cn)),
            dma((2, cn)),
            dma((2, cn)),
            dma((2, dpn)),
            dma((2, dpn)),
            dma((5,)),
        ]
        + line_scratch
        + ring_scratch(dpn, ff_rows, width)
        + ring_scratch(dpn, cn * dr, 3 * hw),
        5,
        moved=160 * mib,
    )

    g_q, g_k, g_v, g_o, g_gate, g_up, g_down = pl.pallas_call(
        functools.partial(spread_kernel, cn, dpn),
        out_shape=tuple(shape((dr, width), f32) for _ in range(4))
        + tuple(shape((dr, ff * cn), f32) for _ in range(2))
        + (shape((ff_rows, width), f32),),
        in_specs=[ANY] * 4,
        out_specs=(VMEM,) * 7,
        scratch_shapes=[
            pltpu.VMEM((cn, dr, 3 * hw), bf16),
            pltpu.VMEM((cn, dr, 2 * ff), bf16),
            pltpu.VMEM((ff_rows, width), bf16),
            pltpu.VMEM((dr, width), f32),
            dma((4,)),
        ],
        compiler_params=pltpu.CompilerParams(vmem_limit_bytes=48 * 2**20),
    )(q_all, gu_back, g_down, g_out)
    mass_mean = totals[2, 0, 0] / (heads * cn * dpn * seq)
    owner = (lax.axis_index("dp") * cn + lax.axis_index("ctx")) * dr
    grad_gains = [lax.dynamic_slice_in_dim(totals[i, 0], owner, dr) for i in range(2)]
    return (
        result[None],
        grad_input[None],
        g_q,
        g_k,
        g_v,
        g_o,
        g_gate,
        g_up,
        g_down,
        grad_gains[0],
        grad_gains[1],
        mass_mean,
    )


def solution(mesh):
    tok = P("dp", "ctx", None)
    ids = P("dp", "ctx")
    mat = P(("dp", "ctx"), None)
    vec = P(("dp", "ctx"))
    return jax.shard_map(
        shards,
        mesh=mesh,
        in_specs=(tok, tok, ids, ids) + (mat,) * 7 + (vec, vec),
        out_specs=(tok, tok) + (mat,) * 7 + (vec, vec, P()),
        check_vma=False,
    )
```

```python
import functools
import math

import jax
import jax.numpy as jnp
from jax import lax
from jax.experimental import pallas as pl
from jax.experimental.pallas import tpu as pltpu
from jax.sharding import PartitionSpec as P

HEAD_DIM = 128
norm_eps = 1e-05
rope_base = 10000.0
score_shift = math.log(4096.0)
score_scale = 1.0 / math.sqrt(HEAD_DIM)
contract_rows = (((0,), (0,)), ((), ()))
contract_cols = (((1,), (1,)), ((), ()))
plain = (((1,), (0,)), ((), ()))
f32 = jnp.float32
bf16 = jnp.bfloat16
MESH = pl.DeviceIdType.MESH
ANY = pl.BlockSpec(memory_space=pl.ANY)
VMEM = pl.BlockSpec(memory_space=pltpu.VMEM)


def dot(a, b, dims=plain):
    return lax.dot_general(a, b, dims, preferred_element_type=f32)


def remote(src, dst, send, recv, target):
    return pltpu.make_async_remote_copy(
        src_ref=src,
        dst_ref=dst,
        send_sem=send,
        recv_sem=recv,
        device_id=target,
        device_id_type=MESH,
    )


def greet(target):
    pl.semaphore_signal(
        pltpu.get_barrier_semaphore(), inc=1, device_id=target, device_id_type=MESH
    )


def by_rows(count, work, step=16):
    @pl.loop(0, count // step)
    def _(i):
        work(pl.ds(pl.multiple_of(i * step, step), step))


def place(cn):
    c = lax.axis_index("ctx")
    j, k = c // 2, c % 2
    return c, j, k, cn // 2, 2 * j + 1 - k


def greet_line(cn, ring):
    c, j, _, n, sib = place(cn)
    ring.greet()
    greet({"ctx": sib})

    @pl.when(j < n - 1)
    def _():
        greet({"ctx": c + 2})

    @pl.when(j > 0)
    def _():
        greet({"ctx": c - 2})

    inner = jnp.where(j > 0, 1, 0) + jnp.where(j < n - 1, 1, 0)
    pl.semaphore_wait(pltpu.get_barrier_semaphore(), 3 + inner)


def greet_ctx(cn):
    c = lax.axis_index("ctx")
    for s in range(1, cn):
        greet({"ctx": lax.rem(c + s, cn)})


class LineGather:
    def __init__(self, cn, own, full, sem):
        self.cn, self.own, self.full, self.sem = cn, own, full, sem

    def copy(self, src, origin, kind, target):
        _, _, k, _, _ = place(self.cn)
        sem = self.sem
        return remote(
            src,
            self.full.at[2 * origin + k],
            sem.at[kind, origin],
            sem.at[3 if kind < 2 else 4, origin],
            {"ctx": target},
        )

    def start(self):
        c, j, _, n, sib = place(self.cn)

        @pl.when(j < n - 1)
        def _():
            self.copy(self.own, j, 0, c + 2).start()

        @pl.when(j > 0)
        def _():
            self.copy(self.own, j, 1, c - 2).start()

        self.copy(self.own, j, 2, sib).start()

    def step(self, s):
        c, j, k, n, sib = place(self.cn)

        @pl.when(j - s >= 0)
        def _():
            o = j - s
            block = self.full.at[2 * o + k]
            self.copy(block, o, 0, sib).wait_recv()

            @pl.when(j < n - 1)
            def _():
                self.copy(block, o, 0, c + 2).start()

            self.copy(block, o, 2, sib).start()

        @pl.when(j + s <= n - 1)
        def _():
            o = j + s
            block = self.full.at[2 * o + k]
            self.copy(block, o, 1, sib).wait_recv()

            @pl.when(j > 0)
            def _():
                self.copy(block, o, 1, c - 2).start()

            self.copy(block, o, 2, sib).start()

    def forward(self, first=1, last=None):
        for s in range(first, self.cn // 2 if last is None else last + 1):
            self.step(s)

    def other(self, o):
        _, _, k, _, sib = place(self.cn)
        block = self.full.at[2 * o + 1 - k]
        remote(
            block, block, self.sem.at[2, o], self.sem.at[4, o], {"ctx": sib}
        ).wait_recv()

    def sent(self):
        c, j, k, n, sib = place(self.cn)
        for o in range(n):
            block = self.full.at[2 * o + k]

            @pl.when((j < n - 1) & (o <= j))
            def _():
                self.copy(block, o, 0, sib).wait_send()

            @pl.when((j > 0) & (o >= j))
            def _():
                self.copy(block, o, 1, sib).wait_send()

            self.copy(block, o, 2, sib).wait_send()

    def finish(self):
        for o in range(self.cn // 2):
            self.other(o)
        self.sent()


class Swap:
    def __init__(self, cn, src, dst, sem, local, pick=None):
        self.cn, self.sem, self.local = cn, sem, local
        self.src = pick or (lambda c: src.at[c])
        self.dst = dst if callable(dst) else lambda c: dst.at[c]

    def copy(self, s):
        c = lax.axis_index("ctx")
        peer = lax.rem(c + s, self.cn)
        return remote(
            self.src(peer),
            self.dst(c),
            self.sem.at[0, s],
            self.sem.at[1, s],
            {"ctx": peer},
        )

    def start(self):
        c = lax.axis_index("ctx")
        for s in range(1, self.cn):
            self.copy(s).start()
        pltpu.make_async_copy(self.src(c), self.dst(c), self.local).start()

    def receive(self, s):
        c = lax.axis_index("ctx")
        if s == 0:
            pltpu.make_async_copy(self.src(c), self.dst(c), self.local).wait()
            return c
        source = lax.rem(c - s + self.cn, self.cn)
        block = self.dst(source)
        remote(
            block, block, self.sem.at[0, s], self.sem.at[1, s], {"ctx": source}
        ).wait_recv()
        return source

    def sent(self):
        for s in range(1, self.cn):
            self.copy(s).wait_send()

    def finish(self):
        for s in range(self.cn):
            self.receive(s)
        self.sent()


class RingGather:
    def __init__(self, dpn, own, full, sem):
        self.dpn, self.own, self.full, self.sem = dpn, own, full, sem
        self.hops = dpn // 2
        d = lax.axis_index("dp")
        self.p = d // 2 * 2 + lax.rem(lax.rem(d, 2) + d // 2, 2)

    def member(self, step):
        p = lax.rem(self.p + step + self.dpn, self.dpn)
        return p // 2 * 2 + lax.rem(lax.rem(p, 2) + p // 2, 2)

    def half(self, ref, h, right):
        if h < self.hops:
            return ref
        m = self.full.shape[1] // 2
        if len(self.full.shape) == 3 and m % 16:
            m = self.full.shape[2] // 2
            return ref.at[:, pl.ds(0 if right else m, m)]
        return ref.at[pl.ds(0 if right else m, m)]

    def copy(self, h, right):
        way = 1 if right else -1
        origin = self.member(-way * (h - 1))
        src = self.own if h == 1 else self.full.at[origin]
        return remote(
            self.half(src, h, right),
            self.half(self.full.at[origin], h, right),
            self.sem.at[0 if right else 1, h],
            self.sem.at[2 if right else 3, h],
            {"dp": self.member(way)},
        )

    def arrival(self, h, right):
        way = 1 if right else -1
        block = self.half(self.full.at[self.member(-way * h)], h, right)
        return remote(
            block,
            block,
            self.sem.at[0 if right else 1, h],
            self.sem.at[2 if right else 3, h],
            {"dp": self.member(way)},
        )

    def greet(self):
        greet({"dp": self.member(1)})
        greet({"dp": self.member(-1)})

    def start(self):
        self.copy(1, True).start()
        self.copy(1, False).start()

    def forward(self):
        for h in range(1, self.hops):
            for right in (True, False):
                self.arrival(h, right).wait_recv()
                self.copy(h + 1, right).start()

    def finish(self):
        for right in (True, False):
            self.arrival(self.hops, right).wait_recv()
        for h in range(1, self.hops + 1):
            for right in (True, False):
                self.copy(h, right).wait_send()


def head_of(cn, heads, c, i):
    return c // 2 + cn // 2 * (heads * (c % 2) + i)


class HeadRows:
    def __init__(self, cn, dpn, dr):
        self.cn, self.dpn = cn, dpn
        self.per = HEAD_DIM // dr
        self.heads = dpn // self.per
        self.c, self.d = lax.axis_index("ctx"), lax.axis_index("dp")
        mine = self.d * cn + self.c
        head, n = mine // self.per, cn // 2
        turn = head // n
        self.home = 2 * lax.rem(head, n) + turn // self.heads
        self.slot = lax.rem(turn, self.heads) * self.per + lax.rem(mine, self.per)
        self.links = dpn - jnp.where(self.home == self.c, 1, 0)

    def owner(self, r):
        i, q = r // self.per, r % self.per
        head = self.c // 2 + self.cn // 2 * (self.heads * lax.rem(self.c, 2) + i)
        g = head * self.per + q
        return {"dp": g // self.cn, "ctx": lax.rem(g, self.cn)}

    def from_here(self, r):
        at = self.owner(r)
        return (at["dp"] == self.d) & (at["ctx"] == self.c)

    def to_here(self, to):
        return (self.home == self.c) & (self.d == to)

    def greet_owners(self):
        for r in range(self.dpn):
            pl.when(jnp.logical_not(self.from_here(r)))(lambda r=r: greet(self.owner(r)))

    def greet_homes(self):
        for to in range(self.dpn):
            pl.when(jnp.logical_not(self.to_here(to)))(
                lambda to=to: greet({"dp": to, "ctx": self.home})
            )


class RowGather(HeadRows):
    def __init__(self, cn, dpn, rows, full, sem, local):
        super().__init__(cn, dpn, rows.shape[0])
        self.rows, self.full, self.sem = rows, full, sem
        self.keep = pltpu.make_async_copy(rows, full.at[self.slot], local)

    def copy(self, to):
        return remote(
            self.rows,
            self.full.at[self.slot],
            self.sem.at[0, to],
            self.sem.at[1, self.slot],
            {"dp": to, "ctx": self.home},
        )

    def start(self):
        for to in range(self.dpn):
            pl.when(jnp.logical_not(self.to_here(to)))(lambda to=to: self.copy(to).start())
            pl.when(self.to_here(to))(self.keep.start)

    def finish(self):
        for r in range(self.dpn):
            block = self.full.at[r]
            came = remote(block, block, self.sem.at[0, r], self.sem.at[1, r], self.owner(r))
            pl.when(jnp.logical_not(self.from_here(r)))(came.wait_recv)
            pl.when(self.from_here(r))(self.keep.wait)
        for to in range(self.dpn):
            pl.when(jnp.logical_not(self.to_here(to)))(lambda to=to: self.copy(to).wait_send())


class RowSum(HeadRows):
    def __init__(self, cn, dpn, parts, got, sem):
        super().__init__(cn, dpn, parts.shape[1])
        self.parts, self.got, self.sem = parts, got, sem

    def copy(self, r):
        return remote(
            self.parts.at[r],
            self.got.at[self.d],
            self.sem.at[0, r],
            self.sem.at[1, self.d],
            self.owner(r),
        )

    def start(self):
        for r in range(self.dpn):
            pl.when(jnp.logical_not(self.from_here(r)))(lambda r=r: self.copy(r).start())

            @pl.when(self.from_here(r))
            def _():
                self.got[self.d] = self.parts[r]

    def finish(self, out):
        for s in range(self.dpn):
            block = self.got.at[s]
            came = remote(
                block, block, self.sem.at[0, s], self.sem.at[1, s], {"dp": s, "ctx": self.home}
            )
            pl.when(jnp.logical_not(self.to_here(s)))(came.wait_recv)

        def add(r):
            total = self.got[0, r, :].astype(f32)
            for s in range(1, self.dpn):
                total = total + self.got[s, r, :].astype(f32)
            out[r, :] = total

        by_rows(out.shape[0], add)
        for r in range(self.dpn):
            pl.when(jnp.logical_not(self.from_here(r)))(lambda r=r: self.copy(r).wait_send())


class RingPieces(RingGather):
    def __init__(self, dpn, full, sem):
        super().__init__(dpn, None, full, sem)

    def piece(self, i, h, right, back):
        way = 1 if right else -1
        ref = self.full.at[self.member(-way * back), i]
        return remote(
            ref,
            ref,
            self.sem.at[0 if right else 1, h, i],
            self.sem.at[2 if right else 3, h, i],
            {"dp": self.member(way)},
        )

    def moves(self, i, h, right, act):
        if h < self.hops:
            act()
        else:
            first = i < self.full.shape[1] // 2
            pl.when(first if right else jnp.logical_not(first))(act)

    def start(self, i):
        for right in (True, False):
            self.moves(i, 1, right, lambda r=right: self.piece(i, 1, r, 0).start())

    def forward(self, i):
        for h in range(1, self.hops):
            for right in (True, False):
                self.piece(i, h, right, h).wait_recv()
                self.moves(
                    i, h + 1, right, lambda h=h, r=right: self.piece(i, h + 1, r, h).start()
                )

    def finish(self, i):
        for right in (True, False):
            h = self.hops
            self.moves(i, h, right, lambda r=right: self.piece(i, h, r, h).wait_recv())
        for h in range(1, self.hops + 1):
            for right in (True, False):
                self.moves(
                    i, h, right, lambda h=h, r=right: self.piece(i, h, r, h - 1).wait_send()
                )


class RingSum:
    def __init__(self, dpn, blocks, got, got_half, sem):
        self.dpn, self.blocks, self.sem = dpn, blocks, sem
        self.got, self.got_half = got, got_half
        self.ring = RingGather(dpn, None, blocks, sem)
        self.hops = dpn // 2

    def part(self, s, right):
        m, width = self.blocks.shape[1:]
        if s > 1:
            return 0, m, pl.ds(0, width)
        if (m // 2) % 16:
            return 0, m, pl.ds(0 if right else width // 2, width // 2)
        return 0 if right else m // 2, m // 2, pl.ds(0, width)

    def copy(self, s, right):
        way = 1 if right else -1
        target = self.ring.member(way * (self.hops - s + 1))
        start, size, lanes = self.part(s, right)
        return remote(
            self.blocks.at[target, pl.ds(start, size), lanes],
            self.arrived(s, right),
            self.sem.at[0 if right else 1, s],
            self.sem.at[2 if right else 3, s],
            {"dp": self.ring.member(way)},
        )

    def arrived(self, s, right):
        side = 0 if right else 1
        return self.got_half.at[side] if s == 1 else self.got.at[side, s - 2]

    def order(self):
        out = [self.ring.member(self.hops)]
        for s in range(self.hops - 1, 0, -1):
            out += [self.ring.member(s), self.ring.member(-s)]
        return out + [self.ring.member(0)]

    def start(self):
        self.copy(1, True).start()
        self.copy(1, False).start()

    def take(self, s, right, target):
        self.copy(s, right).wait_recv()
        start, size, lanes = self.part(s, right)
        block = self.blocks.at[target, pl.ds(start, size), lanes]
        came = self.arrived(s, right)

        def add(r):
            block[r, :] = (block[r, :].astype(f32) + came[r, :].astype(f32)).astype(bf16)

        by_rows(size, add)

    def forward(self, s):
        for right in (True, False):
            way = 1 if right else -1
            self.take(s, right, self.ring.member(way * (self.hops - s)))
            self.copy(s + 1, right).start()

    def finish(self, out):
        for right in (True, False):
            self.copy(self.hops, right).wait_recv()
        mine = self.ring.member(0)
        ends = [self.arrived(self.hops, right) for right in (True, False)]
        per = out.shape[-2]

        @pl.loop(0, self.blocks.shape[1] // 16)
        def _(i):
            r = pl.ds(pl.multiple_of(i * 16, 16), 16)
            total = self.blocks[mine, r, :].astype(f32)
            for end in ends:
                total = total + end[r, :].astype(f32)
            if len(out.shape) == 3:
                to = pl.ds(pl.multiple_of(lax.rem(i * 16, per), 16), 16)
                out[i * 16 // per, to, :] = total.astype(out.dtype)
            else:
                out[r, :] = total.astype(out.dtype)

        for s in range(1, self.hops + 1):
            for right in (True, False):
                self.copy(s, right).wait_send()


def ring_scratch(dpn, m, width):
    return [
        pltpu.VMEM((dpn, m, width), bf16),
        pltpu.VMEM((2, dpn // 2 - 1, m, width), bf16),
        pltpu.VMEM((2, m // 2, width) if m % 32 == 0 else (2, m, width // 2), bf16),
        pltpu.SemaphoreType.DMA((4, dpn // 2 + 1)),
    ]


def outer(a_ref, b_ref, out, at, tile=512):
    a = a_ref[:, at]
    width = out.shape[-1]
    for lo in range(0, width, tile):
        to = slice(lo, min(lo + tile, width))
        out[:, to] = dot(a, b_ref[:, to], contract_rows).astype(bf16)


def outer_all(a_ref, staged, halves, blocks, tile=512):
    count, m, width = blocks.shape
    many = max(1, 128 // m)
    for first in range(0, count, many):
        at = slice(first * m, (first + many) * m)
        for lo in range(0, width, tile):
            to = slice(lo, min(lo + tile, width))
            part = dot(a_ref[halves[0], at], staged(0, to), contract_rows)
            part = part + dot(a_ref[halves[1], at], staged(1, to), contract_rows)
            part = part.astype(bf16)
            for i in range(many):
                blocks[first + i, :, to] = part[i * m : (i + 1) * m]


class LineSum:
    def __init__(self, cn, compute, part, cross, cross_in, flow, arrived, sem):
        self.cn, self.compute, self.part = cn, compute, part
        self.cross, self.cross_in, self.flow = cross, cross_in, flow
        self.arrived, self.sem = arrived, sem

    def across(self, t):
        _, _, _, _, sib = place(self.cn)
        return remote(
            self.cross.at[t],
            self.cross_in.at[t],
            self.sem.at[0, t],
            self.sem.at[2, t],
            {"ctx": sib},
        )

    def along(self, t, slot, target):
        return remote(
            self.flow.at[t],
            self.arrived.at[slot],
            self.sem.at[1, t],
            self.sem.at[3, slot],
            {"ctx": target},
        )

    def produce(self, t, slot):
        _, _, k, _, _ = place(self.cn)
        part = self.part.at[slot]
        self.compute(t, part)

        def low(r):
            self.cross[t, r, :] = part[1 - k, r, :].astype(bf16)

        by_rows(self.cross.shape[1], low)
        self.across(t).start()

    def add(self, part, came):
        def more(r):
            part[r, :] += came[r, :].astype(f32)

        by_rows(part.shape[0], more)

    def collect(self, t, slot):
        _, j, k, n, sib = place(self.cn)
        part = self.part.at[slot, k]
        self.across(t).wait_recv()
        self.add(part, self.cross_in.at[t])

        @pl.when((j > 0) & (t >= j))
        def _():
            self.along(t, t, sib).wait_recv()
            self.add(part, self.arrived.at[t])

        @pl.when((j < n - 1) & (t <= j))
        def _():
            slot_in = jnp.where(t == j, n, t)
            self.along(t, slot_in, sib).wait_recv()
            self.add(part, self.arrived.at[slot_in])

    def send(self, t, slot, up):
        c, j, k, n, _ = place(self.cn)

        def low(r):
            self.flow[t, r, :] = self.part[slot, k, r, :].astype(bf16)

        by_rows(self.flow.shape[1], low)
        there = t if up else jnp.where(t == j - 1, n, t)
        self.along(t, there, c + 2 if up else c - 2).start()

    def drain(self):
        _, j, _, n, sib = place(self.cn)

        @pl.loop(0, n)
        def _(t):
            self.across(t).wait_send()

            @pl.when(t != j)
            def _():
                self.along(t, t, sib).wait_send()


class LineSumRows(LineSum):
    def __init__(self, cn, terms, stage, loads, *refs):
        super().__init__(cn, None, *refs)
        self.terms, self.stage, self.loads = terms, stage, loads

    def produce(self, t, slot):
        _, _, k, _, _ = place(self.cn)
        other = pltpu.make_async_copy(
            self.terms.at[2 * t + 1 - k], self.cross.at[t], self.loads.at[0]
        )
        own = pltpu.make_async_copy(self.terms.at[2 * t + k], self.stage, self.loads.at[1])
        other.start()
        own.start()
        other.wait()
        self.across(t).start()
        own.wait()

        def wide(r):
            self.part[slot, k, r, :] = self.stage[r, :].astype(f32)

        by_rows(self.stage.shape[0], wide)


def line_sums(cn, sums, between=None):
    _, j, _, n, _ = place(cn)

    @pl.loop(0, n - 1)
    def _(s):
        to_up, to_down = n - 1 - s + j, s - (n - 1 - j)
        for total in sums:

            @pl.when(s >= j)
            def _():
                total.produce(to_up, 0)

            @pl.when(s >= n - 1 - j)
            def _():
                total.produce(to_down, 1)

        for total in sums:

            @pl.when(s >= j)
            def _():
                total.collect(to_up, 0)
                total.send(to_up, 0, True)

            @pl.when(s >= n - 1 - j)
            def _():
                total.collect(to_down, 1)
                total.send(to_down, 1, False)

        if between is not None:
            between(s)

    for total in sums:
        total.produce(j, 0)
    for total in sums:
        total.collect(j, 0)


def sum_scratch(cn, rows, width):
    n = cn // 2
    return [
        pltpu.VMEM((2, 2, rows, width), f32),
        pltpu.VMEM((n, rows, width), bf16),
        pltpu.VMEM((n, rows, width), bf16),
        pltpu.VMEM((n, rows, width), bf16),
        pltpu.VMEM((n + 1, rows, width), bf16),
        pltpu.SemaphoreType.DMA((4, n + 1)),
    ]


def product(a_ref, b_ref, dims, rows, width):
    tile = min(512, width)

    def compute(t, out):
        a = a_ref[pl.ds(pl.multiple_of(t * 2 * rows, 2 * rows), 2 * rows), :]

        @pl.loop(0, width // tile)
        def _(i):
            at = pl.ds(pl.multiple_of(i * tile, tile), tile)
            b = b_ref[:, at] if dims == plain else b_ref[at, 0 : a_ref.shape[1]]
            out[:, :, at] = dot(a, b, dims).reshape(2, rows, tile)

    return compute


def rms(v):
    return lax.rsqrt(jnp.mean(v * v, axis=-1, keepdims=True) + norm_eps)


def front_kernel(
    cn, dpn, x, wq, wk, wv, gains, wo, gate_in, up_in, down_in,
    x_all, pack_all, gate, up, down_all, wo_low,
    pack, wide, tall, down, gsem, ssem, rsem, dsem, local,
):
    c, d = lax.axis_index("ctx"), lax.axis_index("dp")
    hw = wq.shape[1] // cn
    part = gate_in.shape[1] // (cn * dpn)
    mine = pack_all.at[d]
    swap = Swap(cn, pack, mine, ssem, local.at[0])
    gather = LineGather(cn, x, x_all, gsem)
    ring = RingPieces(dpn, pack_all, rsem)
    down_ring = RingGather(dpn, down, down_all, dsem)
    greet_ctx(cn)
    ring.greet()
    loads = [
        pltpu.make_async_copy(src, dst, local.at[i])
        for i, (src, dst) in enumerate(
            ((gate_in, wide.at[0]), (up_in, wide.at[1]), (down_in, tall)), 2
        )
    ]
    for load in loads:
        load.start()
    pl.semaphore_wait(pltpu.get_barrier_semaphore(), cn - 1 + 2)
    gather.start()
    for to in range(cn):
        for i, w in enumerate((wq, wk, wv)):
            for t in range(hw // HEAD_DIM):
                lo, at = head_of(cn, hw // HEAD_DIM, to, t) * HEAD_DIM, i * hw + t * HEAD_DIM
                pack[to, :, at : at + HEAD_DIM] = w[:, lo : lo + HEAD_DIM].astype(bf16)
        pack[to, :, 3 * hw :] = gains[...]
    swap.start()
    loads[2].wait()
    down[...] = tall[...].astype(bf16)
    down_ring.start()
    keep_down = pltpu.make_async_copy(down, down_all.at[d], local.at[5])
    keep_down.start()
    keep = pltpu.make_async_copy(x, x_all.at[c], local.at[1])
    keep.start()
    wo_low[...] = wo[...].astype(bf16)

    def lay(i, out):
        loads[i].wait()
        for to in range(cn):
            for row in range(dpn):
                lo = (row * cn + to) * part
                out[to, :, row * part : (row + 1) * part] = wide[i, :, lo : lo + part].astype(bf16)

    half = cn // 2
    sources = [swap.receive(0)]
    ring.start(sources[0])
    lay(0, gate)
    for s in range(1, half):
        sources.append(swap.receive(s))
        ring.start(sources[s])
    gather.forward(1, 1)
    lay(1, up)
    for s in range(half, cn):
        sources.append(swap.receive(s))
        ring.start(sources[s])
    down_ring.forward()
    gather.forward(2, 2)
    for source in sources:
        ring.forward(source)
    gather.forward(3)
    keep.wait()
    keep_down.wait()
    gather.finish()
    for source in sources:
        ring.finish(source)
    swap.sent()
    down_ring.finish()


def prepare(w, x_all, gains, info_rows, hw, block):
    width = w.shape[0]
    per = block // x_all.shape[1]

    @pl.loop(0, width // block)
    def _(i):
        at = pl.ds(pl.multiple_of(i * block, block), block)
        gains[:, at] = w[at, 3 * hw : 3 * hw + 128].astype(f32).T[0:8]

    @pl.loop(0, info_rows.shape[1] // block)
    def _(i):
        at = pl.ds(pl.multiple_of(i * block, block), block)
        codes = x_all[pl.ds(i * per, per), :, width:].reshape(block, 128).astype(f32).T[0:8]
        seg = jnp.floor(codes * 0.5)
        code = jnp.where(codes - 2.0 * seg == 1.0, seg, -1.0)
        first = lax.broadcasted_iota(jnp.int32, (8, block), 0) == 0
        info_rows[:, at] = jnp.where(first, seg, code)


def tables(x_all, inverse, info_rows, info_cols, cosines, sines, width, i, block):
    per = block // x_all.shape[1]
    at = pl.ds(pl.multiple_of(i * block, block), block)
    codes = x_all[pl.ds(i * per, per), :, width:].reshape(block, 128).astype(f32)
    seg = jnp.floor(codes * 0.5)
    valid = codes - 2.0 * seg
    lane = lax.broadcasted_iota(jnp.int32, (block, 128), 1)
    code = jnp.where(valid == 1.0, seg, -1.0)
    info_cols[at, :] = jnp.where(lane == 0, seg, jnp.where(lane == 1, valid, code))
    before = jnp.where(info_rows[0:1, :] < seg[:, 0:1], 1.0, 0.0)
    index = lax.broadcasted_iota(jnp.int32, (block, 128), 0) + i * block
    place_in = index.astype(f32) - jnp.sum(before, axis=1, keepdims=True)
    angles = place_in * inverse[...]
    cosines[at, :] = jnp.cos(angles)
    sines[at, :] = jnp.where(lane < HEAD_DIM // 2, -1.0, 1.0) * jnp.sin(angles)


def project(x_all, w, gain, inverse, rows_in, cols, cosines, sines, an, qkv, hw, block, hook):
    width = an.shape[1]
    per = block // x_all.shape[1]

    @pl.loop(0, an.shape[0] // block)
    def _(i):
        at = pl.ds(pl.multiple_of(i * block, block), block)
        tables(x_all, inverse, rows_in, cols, cosines, sines, width, i, block)
        x = x_all[pl.ds(i * per, per), :, 0:width].reshape(block, width).astype(f32)
        normed = (x * rms(x) * gain[...]).astype(bf16)
        an[at, :] = normed
        proj = dot(normed, w[:, 0 : 3 * hw])
        cos_b, sin_b = cosines[at, :], sines[at, :]
        for h in range(2 * hw // HEAD_DIM):
            lanes = slice(h * HEAD_DIM, (h + 1) * HEAD_DIM)
            v = proj[:, lanes]
            turned = v * cos_b + pltpu.roll(v, HEAD_DIM // 2, 1) * sin_b
            qkv[at, lanes] = turned.astype(bf16)
        qkv[at, 2 * hw :] = proj[:, 2 * hw :].astype(bf16)
        hook(i)


def mask_block(q_seg, k_code, i, j, block):
    rows = lax.broadcasted_iota(jnp.int32, (block, block), 0) + i * block
    cols = lax.broadcasted_iota(jnp.int32, (block, block), 1) + j * block
    return (q_seg == k_code) & (cols <= rows)


def attend(qkv, q_info, k_code, out, mass, hw, block, hook):
    mass[...] = jnp.zeros_like(mass)

    @pl.loop(0, qkv.shape[0] // block)
    def _(i):
        at = pl.ds(pl.multiple_of(i * block, block), block)
        q_seg, q_valid = q_info[at, 0:1], q_info[at, 1:2]
        for h in range(hw // HEAD_DIM):
            lane = [slice(t * hw + h * HEAD_DIM, t * hw + (h + 1) * HEAD_DIM) for t in range(3)]
            q = qkv[at, lane[0]]

            def step(j, acc):
                to = pl.ds(pl.multiple_of(j * block, block), block)
                s = dot(q, qkv[to, lane[1]], contract_cols) * score_scale - score_shift
                allowed = mask_block(q_seg, k_code[1:2, to], i, j, block)
                p = jnp.where(allowed, jax.nn.sigmoid(s), 0.0)
                mass[...] += jnp.sum(p * q_valid, axis=0, keepdims=True)
                return acc + dot(p.astype(bf16), qkv[to, lane[2]])

            acc = lax.fori_loop(0, i + 1, step, jnp.zeros((block, HEAD_DIM), f32))
            out[at, lane[0]] = acc.astype(bf16)
        hook(i)


def attn_kernel(
    cn, dpn, x_all, w, inverse, gate, up, wo,
    an, qkv, o, mass, gains, cosines, sines, cols, rows_in,
    gate_all, up_own, wo_all, ssem, rsem, wsem, local,
):
    c, d = lax.axis_index("ctx"), lax.axis_index("dp")
    wo_rows = RowGather(cn, dpn, wo, wo_all, wsem, local.at[2])
    rows = x_all.shape[1]
    hw = qkv.shape[1] // 3
    swap_gate = Swap(cn, gate, gate_all.at[d], ssem.at[0], local.at[0])
    swap_up = Swap(cn, up, up_own, ssem.at[1], local.at[1])
    ring = RingPieces(dpn, gate_all, rsem)
    sources = [lax.rem(c - s + cn, cn) for s in range(cn)]
    greet_ctx(cn)
    ring.greet()

    wo_rows.greet_owners()
    pl.semaphore_wait(pltpu.get_barrier_semaphore(), cn - 1 + 2 + wo_rows.links)
    wo_rows.start()
    swap_gate.start()

    def in_project(i):
        @pl.when(i == 1)
        def _():
            for s in range(cn // 2):
                ring.start(swap_gate.receive(s))

        @pl.when(i == 2)
        def _():
            for s in range(cn // 2, cn):
                ring.start(swap_gate.receive(s))
            swap_up.start()

    def in_attend(i):
        @pl.when(i == 2)
        def _():
            for source in sources[: cn // 2]:
                ring.forward(source)

    prepare(w, x_all, gains, rows_in, hw, 2 * rows)
    project(
        x_all, w, gains.at[0:1], inverse, rows_in, cols, cosines, sines, an, qkv, hw, 2 * rows,
        in_project,
    )
    attend(qkv, cols, rows_in, o, mass, hw, 2 * rows, in_attend)
    for source in sources[cn // 2 :]:
        ring.forward(source)
    swap_up.finish()
    wo_rows.finish()
    for source in sources:
        ring.finish(source)
    swap_gate.sent()


def middle_kernel(
    cn, dpn, o, wo, x, gain, dy, up, gate_all, down_all,
    h1, bn_all, up_all, hid, dgu, branch_all, dys_all,
    own, bn, dys, wg, wu, down, branch, gsem, ysem, rsem, local, *sum_refs,
):
    c, d = lax.axis_index("ctx"), lax.axis_index("dp")
    _, j, k, n, _ = place(cn)
    rows, width = x.shape
    ff = hid.shape[1]
    block = 2 * rows
    gather = LineGather(cn, own, bn, gsem)
    gather_dy = LineGather(cn, dy, dys, ysem)
    ring = RingGather(dpn, up, up_all, rsem)
    total = LineSum(cn, product(o, wo, plain, rows, width), *sum_refs)
    greet_line(cn, ring)
    ring.start()
    keep_up = pltpu.make_async_copy(up, up_all.at[d], local.at[0])
    loads = [
        pltpu.make_async_copy(src, dst, local.at[i])
        for i, (src, dst) in enumerate(((gate_all, wg), (down_all, down)), 2)
    ]
    keep_up.start()
    for load in loads:
        load.start()
    gather_dy.start()
    dys[c] = dy[...]

    def between(s):
        gather_dy.step(s + 1)

        @pl.when(s == n - 2)
        def _():
            ring.forward()

    line_sums(cn, [total], between)

    def norm(r):
        mid = x[r, :].astype(f32) + total.part[0, k, r, :]
        h1[r, :] = mid
        own[r, :] = (mid * rms(mid) * gain[1:2, :]).astype(bf16)

    by_rows(rows, norm)
    gather.start()
    bn[c] = own[...]
    gather_dy.finish()
    store_dy = pltpu.make_async_copy(dys, dys_all, local.at[4])
    store_dy.start()
    total.drain()
    keep_up.wait()
    for load in loads:
        load.wait()
    ring.finish()
    load_up = pltpu.make_async_copy(up_all, wu, local.at[0])
    load_up.start()
    load_up.wait()
    wgate, wup = wg, wu.reshape(width, ff)
    tile = min(512, ff)
    wide = min(512, width)

    def feed(t):
        gather.other(t)
        at = pl.ds(pl.multiple_of(t * block, block), block)
        pair = pl.ds(t * 2, 2)
        send = pltpu.make_async_copy(bn.at[pair], bn_all.at[pair], local.at[1])
        send.start()
        a = bn[pair].reshape(block, width)
        g_out = dys[pair].reshape(block, width)

        @pl.loop(0, ff // tile)
        def _(i):
            to = pl.ds(pl.multiple_of(i * tile, tile), tile)
            gate = dot(a, wgate[:, to])
            up_v = dot(a, wup[:, to])
            dhid = dot(g_out, down[to, :], contract_cols)
            sig = jax.nn.sigmoid(gate)
            silu = gate * sig
            hid[at, to] = (silu * up_v).astype(bf16)
            dgate = dhid * up_v * sig * (1.0 + gate * (1.0 - sig))
            dgu[at, to] = dgate.astype(bf16)
            dgu[at, pl.ds(pl.multiple_of(ff + i * tile, tile), tile)] = (dhid * silu).astype(bf16)

        h = hid[at, :]

        @pl.loop(0, width // wide)
        def _(i):
            to = pl.ds(pl.multiple_of(i * wide, wide), wide)
            branch[:, to] = dot(h, down[:, to]).astype(bf16)

        out = pltpu.make_async_copy(branch, branch_all.at[at], local.at[0])
        out.start()
        out.wait()
        send.wait()

    feed(j)
    gather.step(1)

    @pl.loop(1, n)
    def _(s):
        both = (j - s >= 0) & (j + s <= n - 1)

        @pl.when(j - s >= 0)
        def _():
            feed(j - s)

        @pl.when(both & (s < n - 1))
        def _():
            gather.step(s + 1)

        @pl.when(j + s <= n - 1)
        def _():
            feed(j + s)

        @pl.when(jnp.logical_not(both) & (s < n - 1))
        def _():
            gather.step(s + 1)

    gather.sent()
    store_dy.wait()


def back_kernel(
    cn, dpn, bn, dgu, wg, wu, h1, dy, gain, branch_all, dh1, dob_all, term, g_own, result,
    own, branch, cross_in, arrived, bsem, gsem, loads, keep_sem, *scratch,
):
    sum_refs, ring_refs = scratch[:-4], scratch[-4:]
    rows, width = dy.shape
    ff = wg.shape[1]
    tile = min(512, width)
    c, _, k, n, _ = place(cn)

    def compute(t, out):
        at = pl.ds(pl.multiple_of(t * 2 * rows, 2 * rows), 2 * rows)

        @pl.loop(0, width // tile)
        def _(i):
            to = pl.ds(pl.multiple_of(i * tile, tile), tile)
            part = dot(dgu[at, 0:ff], wg[to, :], contract_cols)
            part = part + dot(dgu[at, ff:], wu[to, :], contract_cols)
            out[:, :, to] = part.reshape(2, rows, tile)

    total = LineSum(cn, compute, *sum_refs)
    ring = RingSum(dpn, *ring_refs)
    blocks = ring_refs[0]
    m = blocks.shape[1]
    greet_line(cn, ring.ring)
    order = ring.order()

    def weight_grad(member):
        outer(bn, dgu, blocks.at[member], pl.ds(pl.multiple_of(member * m, m), m))


    def between(s):
        @pl.when(s == 0)
        def _():
            weight_grad(order[0])
            ring.start()

        for i in range(ring.hops - 1):

            @pl.when(s == min(i, n - 2))
            def _():
                weight_grad(order[1 + 2 * i])
                weight_grad(order[2 + 2 * i])

            @pl.when(s == min(i + 2, n - 2))
            def _():
                ring.forward(i + 1)

    line_sums(cn, [total], between)
    term[...] = jnp.zeros_like(term)

    def norm_back(r):
        dbn = total.part[0, k, r, :]
        mid = h1[r, :]
        r2 = rms(mid)
        xh2 = mid * r2
        term[...] += jnp.sum(dbn * xh2, axis=0, keepdims=True)
        u2 = dbn * gain[1:2, :]
        mean = jnp.mean(u2 * xh2, axis=-1, keepdims=True)
        grad = dy[r, :].astype(f32) + r2 * (u2 - xh2 * mean)
        dh1[r, :] = grad
        own[r, :] = grad.astype(bf16)

    by_rows(rows, norm_back)
    gather = LineGather(cn, own, dob_all, gsem)
    gather.start()
    keep = pltpu.make_async_copy(own, dob_all.at[c], keep_sem)
    keep.start()
    total.drain()

    part, cross, _, flow, _, _ = sum_refs
    second = LineSumRows(
        cn, branch_all, branch, loads, part, cross, cross_in, flow, arrived, bsem
    )

    def pass_on(s):
        gather.step(s + 1)

        @pl.when(s == 0)
        def _():
            weight_grad(order[-1])

    line_sums(cn, [second], pass_on)

    def close(r):
        result[r, :] = (h1[r, :] + second.part[0, k, r, :]).astype(bf16)

    by_rows(rows, close)
    second.drain()
    keep.wait()
    gather.finish()
    ring.finish(g_own)


def attend_back(qkv, do, cosines, sines, q_info, k_info, dq, dqkv, hw, block):
    count = qkv.shape[0] // block
    dq[...] = jnp.zeros_like(dq)

    def turn_back(g, at):
        return g * cosines[at, :] - pltpu.roll(g, HEAD_DIM // 2, 1) * sines[at, :]

    @pl.loop(0, count)
    def _(j):
        to = pl.ds(pl.multiple_of(j * block, block), block)
        k_code = k_info[to, 2:3]
        for h in range(hw // HEAD_DIM):
            lane = [slice(t * hw + h * HEAD_DIM, t * hw + (h + 1) * HEAD_DIM) for t in range(3)]
            k, v = qkv[to, lane[1]], qkv[to, lane[2]]

            def step(i, carry):
                dk, dv = carry
                at = pl.ds(pl.multiple_of(i * block, block), block)
                q, do_i = qkv[at, lane[0]], do[at, lane[0]]
                s = dot(k, q, contract_cols) * score_scale - score_shift
                keys = lax.broadcasted_iota(jnp.int32, (block, block), 0) + j * block
                queries = lax.broadcasted_iota(jnp.int32, (block, block), 1) + i * block
                allowed = (k_code == q_info[0:1, at]) & (keys <= queries)
                sg = jnp.where(allowed, jax.nn.sigmoid(s), 0.0)
                dp = dot(v, do_i, contract_cols)
                ds = (dp * sg * (1.0 - sg)).astype(bf16)
                dq[at, lane[0]] += dot(ds, k, contract_rows)
                return dk + dot(ds, q), dv + dot(sg.astype(bf16), do_i)

            zero = jnp.zeros((block, HEAD_DIM), f32)
            dk, dv = lax.fori_loop(j, count, step, (zero, zero))
            dqkv[to, lane[1]] = turn_back(dk * score_scale, to).astype(bf16)
            dqkv[to, lane[2]] = dv.astype(bf16)

    @pl.loop(0, count)
    def _(i):
        at = pl.ds(pl.multiple_of(i * block, block), block)
        for h in range(hw // HEAD_DIM):
            lanes = slice(h * HEAD_DIM, (h + 1) * HEAD_DIM)
            dqkv[at, lanes] = turn_back(dq[at, lanes] * score_scale, at).astype(bf16)


def last_kernel(
    cn, dpn, g_gu, dob_all, dys_all, hid, o, wo, qkv, cosines, sines, q_info, k_info, an, w,
    dh1, x, gain, term_two, mass, grad_in, tot_out, gu_all, down_own, out_all, qkv_all,
    do, dq, dqkv, out_parts, out_got, qkv_own, tot, tot_in, tot_sum, tot_last,
    usem, qsem, tsem, psem, osem, local, *scratch,
):
    sum_refs, rings = scratch[:-8], (scratch[-8:-4], scratch[-4:])
    rows, width = x.shape
    hw = width // cn
    _, _, k, n, _ = place(cn)
    down_ring, qkv_ring = (RingSum(dpn, *refs) for refs in rings)
    rows_out = RowSum(cn, dpn, out_parts, out_got, osem)
    swap_gu = Swap(cn, g_gu, gu_all, usem, local.at[0])
    swap_qkv = Swap(cn, qkv_own, qkv_all, qsem, local.at[4])
    totals = Swap(cn, None, tot_in, tsem, local.at[3], lambda i: tot)
    c, d = lax.axis_index("ctx"), lax.axis_index("dp")
    def share(s):
        return remote(
            tot_sum, tot_last.at[d], psem.at[0, s], psem.at[1, s], {"dp": lax.rem(d + s, dpn)}
        )

    greet_ctx(cn)
    for s in range(1, dpn):
        greet({"dp": lax.rem(d + s, dpn)})

    rows_out.greet_homes()
    pl.semaphore_wait(
        pltpu.get_barrier_semaphore(), cn - 1 + dpn - 1 + rows_out.links
    )
    swap_gu.start()
    seq = an.shape[0]
    stage = (sum_refs[1], sum_refs[3])
    halves = (slice(0, seq // 2), slice(seq // 2, seq))

    def fill(src):
        copies = [
            pltpu.make_async_copy(src.at[pl.ds(i * n, n)], stage[i], local.at[1 + i])
            for i in range(2)
        ]
        for copy in copies:
            copy.start()
        for copy in copies:
            copy.wait()

    def staged(i, to=slice(None)):
        return stage[i][:, :, to].reshape(seq // 2, -1)

    fill(dob_all)
    outer_all(o, staged, halves, out_parts)
    rows_out.start()
    for i in range(2):
        do[halves[i], :] = dot(staged(i), wo[...], contract_cols).astype(bf16)
    fill(dys_all)
    outer_all(hid, staged, halves, rings[0][0])
    down_ring.start()
    m_qkv = rings[1][0].shape[1]
    order = qkv_ring.order()

    def grad_qkv(member):
        outer(an, dqkv, rings[1][0].at[member], pl.ds(pl.multiple_of(member * m_qkv, m_qkv), m_qkv))

    attend_back(qkv, do, cosines, sines, q_info, k_info, dq, dqkv, hw, 2 * rows)
    grad_qkv(order[0])
    qkv_ring.start()
    total = LineSum(cn, product(dqkv, w, contract_cols, rows, width), *sum_refs)

    def between(s):
        for i in range(qkv_ring.hops - 1):

            @pl.when(s == min(i, n - 2))
            def _():
                grad_qkv(order[1 + 2 * i])
                grad_qkv(order[2 + 2 * i])
                qkv_ring.forward(i + 1)

            @pl.when(s == min(i + 1, n - 2))
            def _():
                down_ring.forward(i + 1)

        @pl.when(s == n - 2)
        def _():
            grad_qkv(order[-1])
            qkv_ring.finish(qkv_own)
            swap_qkv.start()

    line_sums(cn, [total], between)
    tot[0] = jnp.zeros((1, width), f32)

    def norm_back(r):
        dan = total.part[0, k, r, :]
        xf = x[r, :].astype(f32)
        r1 = rms(xf)
        xh1 = xf * r1
        tot[0] += jnp.sum(dan * xh1, axis=0, keepdims=True)
        u1 = dan * gain[0:1, :]
        mean = jnp.mean(u1 * xh1, axis=-1, keepdims=True)
        grad = dh1[r, :] + r1 * (u1 - xh1 * mean)
        grad_in[r, :] = grad.astype(bf16)

    by_rows(rows, norm_back)
    tot[1] = term_two[...]
    tot[2] = jnp.broadcast_to(jnp.sum(mass[...], axis=1, keepdims=True), (1, width))
    totals.start()
    rows_out.finish(out_all)
    totals.finish()
    tot_sum[...] = jnp.sum(tot_in[...], axis=0)
    for s in range(1, dpn):
        share(s).start()
    down_ring.finish(down_own)
    total.drain()
    swap_gu.finish()
    tot_last[d] = tot_sum[...]
    for s in range(1, dpn):
        source = lax.rem(d - s + dpn, dpn)
        block = tot_last.at[source]
        remote(block, block, psem.at[0, s], psem.at[1, s], {"dp": source}).wait_recv()
    for s in range(1, dpn):
        share(s).wait_send()
    tot_out[...] = jnp.sum(tot_last[...], axis=0)
    swap_qkv.finish()


def spread_kernel(
    cn, dpn, qkv_in, gu_in, down_in, out_in, gq, gk, gv, go, gg, gu_out, gd, qkv, gu, down, out, sem
):
    hw = qkv.shape[2] // 3
    ff_rows = gd.shape[0]
    ff = ff_rows * dpn
    pairs = ((down_in, down), (out_in, out), (qkv_in, qkv), (gu_in, gu))
    loads = [pltpu.make_async_copy(a, b, sem.at[i]) for i, (a, b) in enumerate(pairs)]
    for load in loads:
        load.start()
    for load in loads[:3]:
        load.wait()
    gd[...] = down[...].astype(f32)
    go[...] = out[...]
    for c in range(cn):
        for i, ref in enumerate((gq, gk, gv)):
            for t in range(hw // HEAD_DIM):
                lo, at = head_of(cn, hw // HEAD_DIM, c, t) * HEAD_DIM, i * hw + t * HEAD_DIM
                ref[:, lo : lo + HEAD_DIM] = qkv[c, :, at : at + HEAD_DIM].astype(f32)
    loads[3].wait()
    for c in range(cn):
        for i, ref in enumerate((gg, gu_out)):
            for d in range(dpn):
                to = (d * cn + c) * ff_rows
                lo = i * ff + d * ff_rows
                ref[:, to : to + ff_rows] = gu[c, :, lo : lo + ff_rows].astype(f32)


def call(kernel, outs, ins, specs_in, specs_out, scratch, number, flops=0, moved=0):
    return pl.pallas_call(
        kernel,
        out_shape=outs,
        in_specs=specs_in,
        out_specs=specs_out,
        scratch_shapes=scratch,
        compiler_params=pltpu.CompilerParams(
            collective_id=number, has_side_effects=True, vmem_limit_bytes=61 * 2**20
        ),
        cost_estimate=pl.CostEstimate(flops=flops, bytes_accessed=moved, transcendentals=0),
    )(*ins)


def shape(dims, dtype=bf16):
    return jax.ShapeDtypeStruct(dims, dtype)


def shards(
    hidden_in,
    out_grad,
    seg_ids,
    valid_mask,
    w_query,
    w_key,
    w_value,
    w_output,
    w_gate,
    w_up,
    w_down,
    gain_attn,
    gain_mlp,
):
    dpn = lax.axis_size("dp")
    cn = lax.axis_size("ctx")
    n = cn // 2
    x_local = hidden_in[0]
    dy_local = out_grad[0]
    rows, width = x_local.shape
    seq = rows * cn
    dr = w_query.shape[0]
    hw = width // cn
    heads = hw // HEAD_DIM
    ff_rows = w_down.shape[0]
    ff = ff_rows * dpn
    dma = pltpu.SemaphoreType.DMA
    mib = 2**20

    code = (seg_ids[0] * 2 + valid_mask[0]).astype(bf16)
    x_ext = jnp.concatenate([x_local, jnp.broadcast_to(code[:, None], (rows, 128))], axis=1)
    lanes = jnp.arange(128)[None, :]
    gain_cols = jnp.where(lanes == 0, gain_attn[:, None], gain_mlp[:, None]).astype(bf16)
    pw = 3 * hw + 128
    ring_sem = dma((4, dpn // 2 + 1))
    x_all, w_qkv, gate_pack, up_pack, down, wo_low = call(
        functools.partial(front_kernel, cn, dpn),
        (
            shape((cn, rows, width + 128)),
            shape((dpn, cn, dr, pw)),
            shape((cn, dr, ff)),
            shape((cn, dr, ff)),
            shape((dpn, ff_rows, width)),
            shape((dr, width)),
        ),
        (x_ext, w_query, w_key, w_value, gain_cols, w_output, w_gate, w_up, w_down),
        [ANY] + [VMEM] * 5 + [ANY] * 3,
        (ANY, ANY, VMEM, VMEM, ANY, VMEM),
        [
            pltpu.VMEM((cn, dr, pw), bf16),
            pltpu.VMEM((2, dr, ff * cn), f32),
            pltpu.VMEM((ff_rows, width), f32),
            pltpu.VMEM((ff_rows, width), bf16),
            dma((5, n)),
            dma((2, cn)),
            dma((4, dpn // 2 + 1, cn)),
            ring_sem,
            dma((6,)),
        ],
        1,
        moved=160 * mib,
    )
    w_qkv = w_qkv.reshape(width, pw)
    inverse = jnp.exp(
        jnp.arange(HEAD_DIM // 2, dtype=f32) * (-2.0 * math.log(rope_base) / HEAD_DIM)
    )
    inverse = jnp.concatenate([inverse, inverse])[None]

    line_scratch = sum_scratch(cn, rows, width)
    an, proj, o, mass, gains, cosines, sines, cols, infos, w_gate_c, up_own, wo = call(
        functools.partial(attn_kernel, cn, dpn),
        (
            shape((seq, width)),
            shape((seq, 3 * hw)),
            shape((seq, hw)),
            shape((1, 2 * rows), f32),
            shape((8, width), f32),
            shape((seq, HEAD_DIM), f32),
            shape((seq, HEAD_DIM), f32),
            shape((seq, 128), f32),
            shape((8, seq), f32),
            shape((dpn, cn, dr, ff)),
            shape((cn, dr, ff)),
            shape((dpn, dr, width)),
        ),
        (x_all, w_qkv, inverse, gate_pack, up_pack, wo_low),
        [VMEM] * 3 + [ANY] * 3,
        (VMEM,) * 9 + (ANY,) * 3,
        [dma((2, 2, cn)), dma((4, dpn // 2 + 1, cn)), dma((2, dpn)), dma((3,))],
        2,
        moved=160 * mib,
    )
    down = down.reshape(ff, width)
    h1, bn, w_up_c, hid, dgu, branch, dys = call(
        functools.partial(middle_kernel, cn, dpn),
        (
            shape((rows, width), f32),
            shape((cn, rows, width)),
            shape((dpn, cn, dr, ff)),
            shape((seq, ff)),
            shape((seq, 2 * ff)),
            shape((seq, width)),
            shape((cn, rows, width)),
        ),
        (
            o, wo.reshape(hw, width), x_local, gains, dy_local, up_own,
            w_gate_c.reshape(width, ff), down,
        ),
        [VMEM] * 5 + [ANY] * 3,
        (VMEM, ANY, ANY, VMEM, VMEM, ANY, ANY),
        [
            pltpu.VMEM((rows, width), bf16),
            pltpu.VMEM((cn, rows, width), bf16),
            pltpu.VMEM((cn, rows, width), bf16),
            pltpu.VMEM((width, ff), bf16),
            pltpu.VMEM((dpn, cn, dr, ff), bf16),
            pltpu.VMEM((ff, width), bf16),
            pltpu.VMEM((2 * rows, width), bf16),
            dma((5, n)),
            dma((5, n)),
            ring_sem,
            dma((5,)),
        ]
        + line_scratch,
        3,
        moved=160 * mib,
    )
    wo = wo.reshape(hw, width)
    w_gate_c = w_gate_c.reshape(width, ff)
    w_up_c = w_up_c.reshape(width, ff)
    bn = bn.reshape(seq, width)
    dh1, dob, term_two, g_gu, result = call(
        functools.partial(back_kernel, cn, dpn),
        (
            shape((rows, width), f32),
            shape((cn, rows, width)),
            shape((1, width), f32),
            shape((cn, dr, 2 * ff)),
            shape((rows, width)),
        ),
        (bn, dgu, w_gate_c, w_up_c, h1, dy_local, gains, branch.reshape(cn, rows, width)),
        [VMEM] * 7 + [ANY],
        (VMEM, ANY, VMEM, VMEM, VMEM),
        [
            pltpu.VMEM((rows, width), bf16),
            pltpu.VMEM((rows, width), bf16),
            pltpu.VMEM((n, rows, width), bf16),
            pltpu.VMEM((n + 1, rows, width), bf16),
            dma((4, n + 1)),
            dma((5, n)),
            dma((2,)),
            dma,
        ]
        + line_scratch
        + ring_scratch(dpn, cn * dr, 2 * ff),
        4,
        moved=160 * mib,
    )
    grad_input, totals, gu_back, g_down, g_out, q_all = call(
        functools.partial(last_kernel, cn, dpn),
        (
            shape((rows, width)),
            shape((3, 1, width), f32),
            shape((cn, dr, 2 * ff)),
            shape((ff_rows, width)),
            shape((dr, width), f32),
            shape((cn, dr, 3 * hw)),
        ),
        (
            g_gu, dob, dys, hid, o, wo, proj, cosines, sines, infos, cols, an, w_qkv,
            dh1, x_local, gains, term_two, mass,
        ),
        [ANY] * 3 + [VMEM] * 15,
        (VMEM, VMEM, ANY, VMEM, VMEM, ANY),
        [
            pltpu.VMEM((seq, hw), bf16),
            pltpu.VMEM((seq, hw), f32),
            pltpu.VMEM((seq, 3 * hw), bf16),
            pltpu.VMEM((dpn, dr, width), bf16),
            pltpu.VMEM((dpn, dr, width), bf16),
            pltpu.VMEM((cn, dr, 3 * hw), bf16),
            pltpu.VMEM((3, 1, width), f32),
            pltpu.VMEM((cn, 3, 1, width), f32),
            pltpu.VMEM((3, 1, width), f32),
            pltpu.VMEM((dpn, 3, 1, width), f32),
            dma((2, cn)),
            dma((2, cn)),
            dma((2, cn)),
            dma((2, dpn)),
            dma((2, dpn)),
            dma((5,)),
        ]
        + line_scratch
        + ring_scratch(dpn, ff_rows, width)
        + ring_scratch(dpn, cn * dr, 3 * hw),
        5,
        moved=160 * mib,
    )

    g_q, g_k, g_v, g_o, g_gate, g_up, g_down = pl.pallas_call(
        functools.partial(spread_kernel, cn, dpn),
        out_shape=tuple(shape((dr, width), f32) for _ in range(4))
        + tuple(shape((dr, ff * cn), f32) for _ in range(2))
        + (shape((ff_rows, width), f32),),
        in_specs=[ANY] * 4,
        out_specs=(VMEM,) * 7,
        scratch_shapes=[
            pltpu.VMEM((cn, dr, 3 * hw), bf16),
            pltpu.VMEM((cn, dr, 2 * ff), bf16),
            pltpu.VMEM((ff_rows, width), bf16),
            pltpu.VMEM((dr, width), f32),
            dma((4,)),
        ],
        compiler_params=pltpu.CompilerParams(vmem_limit_bytes=61 * 2**20),
    )(q_all, gu_back, g_down, g_out)
    mass_mean = totals[2, 0, 0] / (heads * cn * dpn * seq)
    owner = (lax.axis_index("dp") * cn + lax.axis_index("ctx")) * dr
    grad_gains = [lax.dynamic_slice_in_dim(totals[i, 0], owner, dr) for i in range(2)]
    return (
        result[None],
        grad_input[None],
        g_q,
        g_k,
        g_v,
        g_o,
        g_gate,
        g_up,
        g_down,
        grad_gains[0],
        grad_gains[1],
        mass_mean,
    )


def solution(mesh):
    tok = P("dp", "ctx", None)
    ids = P("dp", "ctx")
    mat = P(("dp", "ctx"), None)
    vec = P(("dp", "ctx"))
    return jax.shard_map(
        shards,
        mesh=mesh,
        in_specs=(tok, tok, ids, ids) + (mat,) * 7 + (vec, vec),
        out_specs=(tok, tok) + (mat,) * 7 + (vec, vec, P()),
        check_vma=False,
    )
```

```python
import functools
import math

import jax
import jax.numpy as jnp
from jax import lax
from jax.experimental import pallas as pl
from jax.experimental.pallas import tpu as pltpu
from jax.sharding import PartitionSpec as P

HEAD_DIM = 128
norm_eps = 1e-05
rope_base = 10000.0
score_shift = math.log(4096.0)
score_scale = 1.0 / math.sqrt(HEAD_DIM)
contract_rows = (((0,), (0,)), ((), ()))
contract_cols = (((1,), (1,)), ((), ()))
plain = (((1,), (0,)), ((), ()))
f32 = jnp.float32
bf16 = jnp.bfloat16
MESH = pl.DeviceIdType.MESH
ANY = pl.BlockSpec(memory_space=pl.ANY)
VMEM = pl.BlockSpec(memory_space=pltpu.VMEM)


def dot(a, b, dims=plain):
    return lax.dot_general(a, b, dims, preferred_element_type=f32)


def remote(src, dst, send, recv, target):
    return pltpu.make_async_remote_copy(
        src_ref=src,
        dst_ref=dst,
        send_sem=send,
        recv_sem=recv,
        device_id=target,
        device_id_type=MESH,
    )


def greet(target):
    pl.semaphore_signal(
        pltpu.get_barrier_semaphore(), inc=1, device_id=target, device_id_type=MESH
    )


def by_rows(count, work, step=16):
    @pl.loop(0, count // step)
    def _(i):
        work(pl.ds(pl.multiple_of(i * step, step), step))


def place(cn):
    c = lax.axis_index("ctx")
    j, k = c // 2, c % 2
    return c, j, k, cn // 2, 2 * j + 1 - k


def greet_line(cn, ring):
    c, j, _, n, sib = place(cn)
    ring.greet()
    greet({"ctx": sib})

    @pl.when(j < n - 1)
    def _():
        greet({"ctx": c + 2})

    @pl.when(j > 0)
    def _():
        greet({"ctx": c - 2})

    inner = jnp.where(j > 0, 1, 0) + jnp.where(j < n - 1, 1, 0)
    pl.semaphore_wait(pltpu.get_barrier_semaphore(), 3 + inner)


def greet_ctx(cn):
    c = lax.axis_index("ctx")
    for s in range(1, cn):
        greet({"ctx": lax.rem(c + s, cn)})


class LineGather:
    def __init__(self, cn, own, full, sem):
        self.cn, self.own, self.full, self.sem = cn, own, full, sem

    def copy(self, src, origin, kind, target):
        _, _, k, _, _ = place(self.cn)
        sem = self.sem
        return remote(
            src,
            self.full.at[2 * origin + k],
            sem.at[kind, origin],
            sem.at[3 if kind < 2 else 4, origin],
            {"ctx": target},
        )

    def start(self):
        c, j, _, n, sib = place(self.cn)

        @pl.when(j < n - 1)
        def _():
            self.copy(self.own, j, 0, c + 2).start()

        @pl.when(j > 0)
        def _():
            self.copy(self.own, j, 1, c - 2).start()

        self.copy(self.own, j, 2, sib).start()

    def step(self, s):
        c, j, k, n, sib = place(self.cn)

        @pl.when(j - s >= 0)
        def _():
            o = j - s
            block = self.full.at[2 * o + k]
            self.copy(block, o, 0, sib).wait_recv()

            @pl.when(j < n - 1)
            def _():
                self.copy(block, o, 0, c + 2).start()

            self.copy(block, o, 2, sib).start()

        @pl.when(j + s <= n - 1)
        def _():
            o = j + s
            block = self.full.at[2 * o + k]
            self.copy(block, o, 1, sib).wait_recv()

            @pl.when(j > 0)
            def _():
                self.copy(block, o, 1, c - 2).start()

            self.copy(block, o, 2, sib).start()

    def forward(self, first=1, last=None):
        for s in range(first, self.cn // 2 if last is None else last + 1):
            self.step(s)

    def other(self, o):
        _, _, k, _, sib = place(self.cn)
        block = self.full.at[2 * o + 1 - k]
        remote(
            block, block, self.sem.at[2, o], self.sem.at[4, o], {"ctx": sib}
        ).wait_recv()

    def sent(self):
        c, j, k, n, sib = place(self.cn)
        for o in range(n):
            block = self.full.at[2 * o + k]

            @pl.when((j < n - 1) & (o <= j))
            def _():
                self.copy(block, o, 0, sib).wait_send()

            @pl.when((j > 0) & (o >= j))
            def _():
                self.copy(block, o, 1, sib).wait_send()

            self.copy(block, o, 2, sib).wait_send()

    def finish(self):
        for o in range(self.cn // 2):
            self.other(o)
        self.sent()


class Swap:
    def __init__(self, cn, src, dst, sem, local, pick=None):
        self.cn, self.sem, self.local = cn, sem, local
        self.src = pick or (lambda c: src.at[c])
        self.dst = dst if callable(dst) else lambda c: dst.at[c]

    def copy(self, s):
        c = lax.axis_index("ctx")
        peer = lax.rem(c + s, self.cn)
        return remote(
            self.src(peer),
            self.dst(c),
            self.sem.at[0, s],
            self.sem.at[1, s],
            {"ctx": peer},
        )

    def start(self):
        c = lax.axis_index("ctx")
        for s in range(1, self.cn):
            self.copy(s).start()
        pltpu.make_async_copy(self.src(c), self.dst(c), self.local).start()

    def receive(self, s):
        c = lax.axis_index("ctx")
        if s == 0:
            pltpu.make_async_copy(self.src(c), self.dst(c), self.local).wait()
            return c
        source = lax.rem(c - s + self.cn, self.cn)
        block = self.dst(source)
        remote(
            block, block, self.sem.at[0, s], self.sem.at[1, s], {"ctx": source}
        ).wait_recv()
        return source

    def sent(self):
        for s in range(1, self.cn):
            self.copy(s).wait_send()

    def finish(self):
        for s in range(self.cn):
            self.receive(s)
        self.sent()


class RingGather:
    def __init__(self, dpn, own, full, sem):
        self.dpn, self.own, self.full, self.sem = dpn, own, full, sem
        self.hops = dpn // 2
        d = lax.axis_index("dp")
        self.p = d // 2 * 2 + lax.rem(lax.rem(d, 2) + d // 2, 2)

    def member(self, step):
        p = lax.rem(self.p + step + self.dpn, self.dpn)
        return p // 2 * 2 + lax.rem(lax.rem(p, 2) + p // 2, 2)

    def half(self, ref, h, right):
        if h < self.hops:
            return ref
        m = self.full.shape[1] // 2
        if len(self.full.shape) == 3 and m % 16:
            m = self.full.shape[2] // 2
            return ref.at[:, pl.ds(0 if right else m, m)]
        return ref.at[pl.ds(0 if right else m, m)]

    def copy(self, h, right):
        way = 1 if right else -1
        origin = self.member(-way * (h - 1))
        src = self.own if h == 1 else self.full.at[origin]
        return remote(
            self.half(src, h, right),
            self.half(self.full.at[origin], h, right),
            self.sem.at[0 if right else 1, h],
            self.sem.at[2 if right else 3, h],
            {"dp": self.member(way)},
        )

    def arrival(self, h, right):
        way = 1 if right else -1
        block = self.half(self.full.at[self.member(-way * h)], h, right)
        return remote(
            block,
            block,
            self.sem.at[0 if right else 1, h],
            self.sem.at[2 if right else 3, h],
            {"dp": self.member(way)},
        )

    def greet(self):
        greet({"dp": self.member(1)})
        greet({"dp": self.member(-1)})

    def start(self):
        self.copy(1, True).start()
        self.copy(1, False).start()

    def forward(self):
        for h in range(1, self.hops):
            for right in (True, False):
                self.arrival(h, right).wait_recv()
                self.copy(h + 1, right).start()

    def finish(self):
        for right in (True, False):
            self.arrival(self.hops, right).wait_recv()
        for h in range(1, self.hops + 1):
            for right in (True, False):
                self.copy(h, right).wait_send()


def head_of(cn, heads, c, i):
    return c // 2 + cn // 2 * (heads * (c % 2) + i)


class HeadRows:
    def __init__(self, cn, dpn, dr):
        self.cn, self.dpn = cn, dpn
        self.per = HEAD_DIM // dr
        self.heads = dpn // self.per
        self.c, self.d = lax.axis_index("ctx"), lax.axis_index("dp")
        mine = self.d * cn + self.c
        head, n = mine // self.per, cn // 2
        turn = head // n
        self.home = 2 * lax.rem(head, n) + turn // self.heads
        self.slot = lax.rem(turn, self.heads) * self.per + lax.rem(mine, self.per)
        self.links = dpn - jnp.where(self.home == self.c, 1, 0)

    def owner(self, r):
        i, q = r // self.per, r % self.per
        head = self.c // 2 + self.cn // 2 * (self.heads * lax.rem(self.c, 2) + i)
        g = head * self.per + q
        return {"dp": g // self.cn, "ctx": lax.rem(g, self.cn)}

    def from_here(self, r):
        at = self.owner(r)
        return (at["dp"] == self.d) & (at["ctx"] == self.c)

    def to_here(self, to):
        return (self.home == self.c) & (self.d == to)

    def greet_owners(self):
        for r in range(self.dpn):
            pl.when(jnp.logical_not(self.from_here(r)))(lambda r=r: greet(self.owner(r)))

    def greet_homes(self):
        for to in range(self.dpn):
            pl.when(jnp.logical_not(self.to_here(to)))(
                lambda to=to: greet({"dp": to, "ctx": self.home})
            )


class RowGather(HeadRows):
    def __init__(self, cn, dpn, rows, full, sem, local):
        super().__init__(cn, dpn, rows.shape[0])
        self.rows, self.full, self.sem = rows, full, sem
        self.keep = pltpu.make_async_copy(rows, full.at[self.slot], local)

    def copy(self, to):
        return remote(
            self.rows,
            self.full.at[self.slot],
            self.sem.at[0, to],
            self.sem.at[1, self.slot],
            {"dp": to, "ctx": self.home},
        )

    def start(self):
        for to in range(self.dpn):
            pl.when(jnp.logical_not(self.to_here(to)))(lambda to=to: self.copy(to).start())
            pl.when(self.to_here(to))(self.keep.start)

    def finish(self):
        for r in range(self.dpn):
            block = self.full.at[r]
            came = remote(block, block, self.sem.at[0, r], self.sem.at[1, r], self.owner(r))
            pl.when(jnp.logical_not(self.from_here(r)))(came.wait_recv)
            pl.when(self.from_here(r))(self.keep.wait)
        for to in range(self.dpn):
            pl.when(jnp.logical_not(self.to_here(to)))(lambda to=to: self.copy(to).wait_send())


class RowSum(HeadRows):
    def __init__(self, cn, dpn, parts, got, sem):
        super().__init__(cn, dpn, parts.shape[1])
        self.parts, self.got, self.sem = parts, got, sem

    def copy(self, r):
        return remote(
            self.parts.at[r],
            self.got.at[self.d],
            self.sem.at[0, r],
            self.sem.at[1, self.d],
            self.owner(r),
        )

    def start(self):
        for r in range(self.dpn):
            pl.when(jnp.logical_not(self.from_here(r)))(lambda r=r: self.copy(r).start())

            @pl.when(self.from_here(r))
            def _():
                self.got[self.d] = self.parts[r]

    def finish(self, out):
        for s in range(self.dpn):
            block = self.got.at[s]
            came = remote(
                block, block, self.sem.at[0, s], self.sem.at[1, s], {"dp": s, "ctx": self.home}
            )
            pl.when(jnp.logical_not(self.to_here(s)))(came.wait_recv)

        def add(r):
            total = self.got[0, r, :].astype(f32)
            for s in range(1, self.dpn):
                total = total + self.got[s, r, :].astype(f32)
            out[r, :] = total

        by_rows(out.shape[0], add)
        for r in range(self.dpn):
            pl.when(jnp.logical_not(self.from_here(r)))(lambda r=r: self.copy(r).wait_send())


class RingPieces(RingGather):
    def __init__(self, dpn, full, sem):
        super().__init__(dpn, None, full, sem)

    def piece(self, i, h, right, back):
        way = 1 if right else -1
        ref = self.full.at[self.member(-way * back), i]
        return remote(
            ref,
            ref,
            self.sem.at[0 if right else 1, h, i],
            self.sem.at[2 if right else 3, h, i],
            {"dp": self.member(way)},
        )

    def moves(self, i, h, right, act):
        if h < self.hops:
            act()
        else:
            first = i < self.full.shape[1] // 2
            pl.when(first if right else jnp.logical_not(first))(act)

    def start(self, i):
        for right in (True, False):
            self.moves(i, 1, right, lambda r=right: self.piece(i, 1, r, 0).start())

    def forward(self, i):
        for h in range(1, self.hops):
            for right in (True, False):
                self.piece(i, h, right, h).wait_recv()
                self.moves(
                    i, h + 1, right, lambda h=h, r=right: self.piece(i, h + 1, r, h).start()
                )

    def finish(self, i):
        for right in (True, False):
            h = self.hops
            self.moves(i, h, right, lambda r=right: self.piece(i, h, r, h).wait_recv())
        for h in range(1, self.hops + 1):
            for right in (True, False):
                self.moves(
                    i, h, right, lambda h=h, r=right: self.piece(i, h, r, h - 1).wait_send()
                )


class RingSum:
    def __init__(self, dpn, blocks, got, got_half, sem):
        self.dpn, self.blocks, self.sem = dpn, blocks, sem
        self.got, self.got_half = got, got_half
        self.ring = RingGather(dpn, None, blocks, sem)
        self.hops = dpn // 2

    def part(self, s, right):
        m, width = self.blocks.shape[1:]
        if s > 1:
            return 0, m, pl.ds(0, width)
        if (m // 2) % 16:
            return 0, m, pl.ds(0 if right else width // 2, width // 2)
        return 0 if right else m // 2, m // 2, pl.ds(0, width)

    def copy(self, s, right):
        way = 1 if right else -1
        target = self.ring.member(way * (self.hops - s + 1))
        start, size, lanes = self.part(s, right)
        return remote(
            self.blocks.at[target, pl.ds(start, size), lanes],
            self.arrived(s, right),
            self.sem.at[0 if right else 1, s],
            self.sem.at[2 if right else 3, s],
            {"dp": self.ring.member(way)},
        )

    def arrived(self, s, right):
        side = 0 if right else 1
        return self.got_half.at[side] if s == 1 else self.got.at[side, s - 2]

    def order(self):
        out = [self.ring.member(self.hops)]
        for s in range(self.hops - 1, 0, -1):
            out += [self.ring.member(s), self.ring.member(-s)]
        return out + [self.ring.member(0)]

    def start(self):
        self.copy(1, True).start()
        self.copy(1, False).start()

    def take(self, s, right, target):
        self.copy(s, right).wait_recv()
        start, size, lanes = self.part(s, right)
        block = self.blocks.at[target, pl.ds(start, size), lanes]
        came = self.arrived(s, right)

        def add(r):
            block[r, :] = (block[r, :].astype(f32) + came[r, :].astype(f32)).astype(bf16)

        by_rows(size, add)

    def forward(self, s):
        for right in (True, False):
            way = 1 if right else -1
            self.take(s, right, self.ring.member(way * (self.hops - s)))
            self.copy(s + 1, right).start()

    def finish(self, out):
        for right in (True, False):
            self.copy(self.hops, right).wait_recv()
        mine = self.ring.member(0)
        ends = [self.arrived(self.hops, right) for right in (True, False)]
        per = out.shape[-2]

        @pl.loop(0, self.blocks.shape[1] // 16)
        def _(i):
            r = pl.ds(pl.multiple_of(i * 16, 16), 16)
            total = self.blocks[mine, r, :].astype(f32)
            for end in ends:
                total = total + end[r, :].astype(f32)
            if len(out.shape) == 3:
                to = pl.ds(pl.multiple_of(lax.rem(i * 16, per), 16), 16)
                out[i * 16 // per, to, :] = total.astype(out.dtype)
            else:
                out[r, :] = total.astype(out.dtype)

        for s in range(1, self.hops + 1):
            for right in (True, False):
                self.copy(s, right).wait_send()


def ring_scratch(dpn, m, width):
    return [
        pltpu.VMEM((dpn, m, width), bf16),
        pltpu.VMEM((2, dpn // 2 - 1, m, width), bf16),
        pltpu.VMEM((2, m // 2, width) if m % 32 == 0 else (2, m, width // 2), bf16),
        pltpu.SemaphoreType.DMA((4, dpn // 2 + 1)),
    ]


def outer(a_ref, b_ref, out, at, tile=512):
    a = a_ref[:, at]
    width = out.shape[-1]
    for lo in range(0, width, tile):
        to = slice(lo, min(lo + tile, width))
        out[:, to] = dot(a, b_ref[:, to], contract_rows).astype(bf16)


def outer_all(a_ref, staged, halves, blocks, tile=512):
    count, m, width = blocks.shape
    many = max(1, 128 // m)
    for first in range(0, count, many):
        at = slice(first * m, (first + many) * m)
        for lo in range(0, width, tile):
            to = slice(lo, min(lo + tile, width))
            part = dot(a_ref[halves[0], at], staged(0, to), contract_rows)
            part = part + dot(a_ref[halves[1], at], staged(1, to), contract_rows)
            part = part.astype(bf16)
            for i in range(many):
                blocks[first + i, :, to] = part[i * m : (i + 1) * m]


class LineSum:
    def __init__(self, cn, compute, part, cross, cross_in, flow, arrived, sem):
        self.cn, self.compute, self.part = cn, compute, part
        self.cross, self.cross_in, self.flow = cross, cross_in, flow
        self.arrived, self.sem = arrived, sem

    def across(self, t):
        _, _, _, _, sib = place(self.cn)
        return remote(
            self.cross.at[t],
            self.cross_in.at[t],
            self.sem.at[0, t],
            self.sem.at[2, t],
            {"ctx": sib},
        )

    def along(self, t, slot, target):
        return remote(
            self.flow.at[t],
            self.arrived.at[slot],
            self.sem.at[1, t],
            self.sem.at[3, slot],
            {"ctx": target},
        )

    def produce(self, t, slot):
        _, _, k, _, _ = place(self.cn)
        part = self.part.at[slot]
        self.compute(t, part)

        def low(r):
            self.cross[t, r, :] = part[1 - k, r, :].astype(bf16)

        by_rows(self.cross.shape[1], low)
        self.across(t).start()

    def add(self, part, came):
        def more(r):
            part[r, :] += came[r, :].astype(f32)

        by_rows(part.shape[0], more)

    def collect(self, t, slot):
        _, j, k, n, sib = place(self.cn)
        part = self.part.at[slot, k]
        self.across(t).wait_recv()
        self.add(part, self.cross_in.at[t])

        @pl.when((j > 0) & (t >= j))
        def _():
            self.along(t, t, sib).wait_recv()
            self.add(part, self.arrived.at[t])

        @pl.when((j < n - 1) & (t <= j))
        def _():
            slot_in = jnp.where(t == j, n, t)
            self.along(t, slot_in, sib).wait_recv()
            self.add(part, self.arrived.at[slot_in])

    def send(self, t, slot, up):
        c, j, k, n, _ = place(self.cn)

        def low(r):
            self.flow[t, r, :] = self.part[slot, k, r, :].astype(bf16)

        by_rows(self.flow.shape[1], low)
        there = t if up else jnp.where(t == j - 1, n, t)
        self.along(t, there, c + 2 if up else c - 2).start()

    def drain(self):
        _, j, _, n, sib = place(self.cn)

        @pl.loop(0, n)
        def _(t):
            self.across(t).wait_send()

            @pl.when(t != j)
            def _():
                self.along(t, t, sib).wait_send()


def line_sums(cn, sums, between=None):
    _, j, _, n, _ = place(cn)

    @pl.loop(0, n - 1)
    def _(s):
        to_up, to_down = n - 1 - s + j, s - (n - 1 - j)
        for total in sums:

            @pl.when(s >= j)
            def _():
                total.produce(to_up, 0)

            @pl.when(s >= n - 1 - j)
            def _():
                total.produce(to_down, 1)

        for total in sums:

            @pl.when(s >= j)
            def _():
                total.collect(to_up, 0)
                total.send(to_up, 0, True)

            @pl.when(s >= n - 1 - j)
            def _():
                total.collect(to_down, 1)
                total.send(to_down, 1, False)

        if between is not None:
            between(s)

    for total in sums:
        total.produce(j, 0)
    for total in sums:
        total.collect(j, 0)


def sum_scratch(cn, rows, width):
    n = cn // 2
    return [
        pltpu.VMEM((2, 2, rows, width), f32),
        pltpu.VMEM((n, rows, width), bf16),
        pltpu.VMEM((n, rows, width), bf16),
        pltpu.VMEM((n, rows, width), bf16),
        pltpu.VMEM((n + 1, rows, width), bf16),
        pltpu.SemaphoreType.DMA((4, n + 1)),
    ]


def product(a_ref, b_ref, dims, rows, width):
    tile = min(512, width)

    def compute(t, out):
        a = a_ref[pl.ds(pl.multiple_of(t * 2 * rows, 2 * rows), 2 * rows), :]

        @pl.loop(0, width // tile)
        def _(i):
            at = pl.ds(pl.multiple_of(i * tile, tile), tile)
            b = b_ref[:, at] if dims == plain else b_ref[at, 0 : a_ref.shape[1]]
            out[:, :, at] = dot(a, b, dims).reshape(2, rows, tile)

    return compute


def rms(v):
    return lax.rsqrt(jnp.mean(v * v, axis=-1, keepdims=True) + norm_eps)


def front_kernel(
    cn, dpn, x_in, seg, valid, gain_rows, wq, wk, wv, wo, gate_in, up_in, down_in,
    x_all, pack_all, gate, up, down_all, wo_low,
    x, pack, wide, tall, down, gsem, ssem, rsem, dsem, local,
):
    c, d = lax.axis_index("ctx"), lax.axis_index("dp")
    hw = wq.shape[1] // cn
    part = gate_in.shape[1] // (cn * dpn)
    mine = pack_all.at[d]
    swap = Swap(cn, pack, mine, ssem, local.at[0])
    gather = LineGather(cn, x, x_all, gsem)
    ring = RingPieces(dpn, pack_all, rsem)
    down_ring = RingGather(dpn, down, down_all, dsem)
    greet_ctx(cn)
    ring.greet()
    rows, width = x_in.shape
    load_x = pltpu.make_async_copy(x_in, x.at[:, 0:width], local.at[1])
    load_x.start()

    def column(row):
        return jnp.broadcast_to(row, (128, 128)).T

    code = (seg[...] * 2 + valid[...]).astype(f32)
    x[:, width:] = column(code).astype(bf16)
    lane = lax.broadcasted_iota(jnp.int32, (128, 128), 1)
    gains = jnp.where(lane == 0, column(gain_rows[0:1, :]), column(gain_rows[1:2, :]))
    gains = gains[0 : wq.shape[0]].astype(bf16)
    load_x.wait()
    loads = [
        pltpu.make_async_copy(src, dst, local.at[i])
        for i, (src, dst) in enumerate(
            ((gate_in, wide.at[0]), (up_in, wide.at[1]), (down_in, tall)), 2
        )
    ]
    for load in loads:
        load.start()
    pl.semaphore_wait(pltpu.get_barrier_semaphore(), cn - 1 + 2)
    gather.start()
    for to in range(cn):
        for i, w in enumerate((wq, wk, wv)):
            for t in range(hw // HEAD_DIM):
                lo, at = head_of(cn, hw // HEAD_DIM, to, t) * HEAD_DIM, i * hw + t * HEAD_DIM
                pack[to, :, at : at + HEAD_DIM] = w[:, lo : lo + HEAD_DIM].astype(bf16)
        pack[to, :, 3 * hw :] = gains
    swap.start()
    loads[2].wait()
    down[...] = tall[...].astype(bf16)
    down_ring.start()
    keep_down = pltpu.make_async_copy(down, down_all.at[d], local.at[5])
    keep_down.start()
    keep = pltpu.make_async_copy(x, x_all.at[c], local.at[1])
    keep.start()
    wo_low[...] = wo[...].astype(bf16)

    def lay(i, out):
        loads[i].wait()
        for to in range(cn):
            for row in range(dpn):
                lo = (row * cn + to) * part
                out[to, :, row * part : (row + 1) * part] = wide[i, :, lo : lo + part].astype(bf16)

    half = cn // 2
    sources = [swap.receive(0)]
    ring.start(sources[0])
    lay(0, gate)
    for s in range(1, half):
        sources.append(swap.receive(s))
        ring.start(sources[s])
    gather.forward(1, 1)
    lay(1, up)
    for s in range(half, cn):
        sources.append(swap.receive(s))
        ring.start(sources[s])
    down_ring.forward()
    gather.forward(2, 2)
    for source in sources:
        ring.forward(source)
    gather.forward(3)
    keep.wait()
    keep_down.wait()
    gather.finish()
    for source in sources:
        ring.finish(source)
    swap.sent()
    down_ring.finish()


def prepare(w, x_all, gains, info_rows, hw, block):
    width = w.shape[0]
    per = block // x_all.shape[1]

    @pl.loop(0, width // block)
    def _(i):
        at = pl.ds(pl.multiple_of(i * block, block), block)
        gains[:, at] = w[at, 3 * hw : 3 * hw + 128].astype(f32).T[0:8]

    @pl.loop(0, info_rows.shape[1] // block)
    def _(i):
        at = pl.ds(pl.multiple_of(i * block, block), block)
        codes = x_all[pl.ds(i * per, per), :, width:].reshape(block, 128).astype(f32).T[0:8]
        seg = jnp.floor(codes * 0.5)
        code = jnp.where(codes - 2.0 * seg == 1.0, seg, -1.0)
        first = lax.broadcasted_iota(jnp.int32, (8, block), 0) == 0
        info_rows[:, at] = jnp.where(first, seg, code)


def tables(x_all, inverse, info_rows, info_cols, cosines, sines, width, i, block):
    per = block // x_all.shape[1]
    at = pl.ds(pl.multiple_of(i * block, block), block)
    codes = x_all[pl.ds(i * per, per), :, width:].reshape(block, 128).astype(f32)
    seg = jnp.floor(codes * 0.5)
    valid = codes - 2.0 * seg
    lane = lax.broadcasted_iota(jnp.int32, (block, 128), 1)
    code = jnp.where(valid == 1.0, seg, -1.0)
    info_cols[at, :] = jnp.where(lane == 0, seg, jnp.where(lane == 1, valid, code))
    before = jnp.where(info_rows[0:1, :] < seg[:, 0:1], 1.0, 0.0)
    index = lax.broadcasted_iota(jnp.int32, (block, 128), 0) + i * block
    place_in = index.astype(f32) - jnp.sum(before, axis=1, keepdims=True)
    angles = place_in * inverse[...]
    cosines[at, :] = jnp.cos(angles)
    sines[at, :] = jnp.where(lane < HEAD_DIM // 2, -1.0, 1.0) * jnp.sin(angles)


def project(x_all, w, gain, inverse, rows_in, cols, cosines, sines, an, qkv, hw, block, hook):
    width = an.shape[1]
    per = block // x_all.shape[1]

    @pl.loop(0, an.shape[0] // block)
    def _(i):
        at = pl.ds(pl.multiple_of(i * block, block), block)
        tables(x_all, inverse, rows_in, cols, cosines, sines, width, i, block)
        x = x_all[pl.ds(i * per, per), :, 0:width].reshape(block, width).astype(f32)
        normed = (x * rms(x) * gain[...]).astype(bf16)
        an[at, :] = normed
        proj = dot(normed, w[:, 0 : 3 * hw])
        cos_b, sin_b = cosines[at, :], sines[at, :]
        for h in range(2 * hw // HEAD_DIM):
            lanes = slice(h * HEAD_DIM, (h + 1) * HEAD_DIM)
            v = proj[:, lanes]
            turned = v * cos_b + pltpu.roll(v, HEAD_DIM // 2, 1) * sin_b
            qkv[at, lanes] = turned.astype(bf16)
        qkv[at, 2 * hw :] = proj[:, 2 * hw :].astype(bf16)
        hook(i)


def mask_block(q_seg, k_code, i, j, block):
    rows = lax.broadcasted_iota(jnp.int32, (block, block), 0) + i * block
    cols = lax.broadcasted_iota(jnp.int32, (block, block), 1) + j * block
    return (q_seg == k_code) & (cols <= rows)


def attend(qkv, q_info, k_code, out, mass, hw, block, hook):
    mass[...] = jnp.zeros_like(mass)

    @pl.loop(0, qkv.shape[0] // block)
    def _(i):
        at = pl.ds(pl.multiple_of(i * block, block), block)
        q_seg, q_valid = q_info[at, 0:1], q_info[at, 1:2]
        for h in range(hw // HEAD_DIM):
            lane = [slice(t * hw + h * HEAD_DIM, t * hw + (h + 1) * HEAD_DIM) for t in range(3)]
            q = qkv[at, lane[0]]

            def step(j, acc):
                to = pl.ds(pl.multiple_of(j * block, block), block)
                s = dot(q, qkv[to, lane[1]], contract_cols) * score_scale - score_shift
                allowed = mask_block(q_seg, k_code[1:2, to], i, j, block)
                p = jnp.where(allowed, jax.nn.sigmoid(s), 0.0)
                mass[...] += jnp.sum(p * q_valid, axis=0, keepdims=True)
                return acc + dot(p.astype(bf16), qkv[to, lane[2]])

            acc = lax.fori_loop(0, i + 1, step, jnp.zeros((block, HEAD_DIM), f32))
            out[at, lane[0]] = acc.astype(bf16)
        hook(i)


def attn_kernel(
    cn, dpn, x_all, w, inverse, gate, up, wo,
    an, qkv, o, mass, gains, cosines, sines, cols, rows_in,
    gate_all, up_own, wo_all, ssem, rsem, wsem, local,
):
    c, d = lax.axis_index("ctx"), lax.axis_index("dp")
    wo_rows = RowGather(cn, dpn, wo, wo_all, wsem, local.at[2])
    rows = x_all.shape[1]
    hw = qkv.shape[1] // 3
    swap_gate = Swap(cn, gate, gate_all.at[d], ssem.at[0], local.at[0])
    swap_up = Swap(cn, up, up_own, ssem.at[1], local.at[1])
    ring = RingPieces(dpn, gate_all, rsem)
    sources = [lax.rem(c - s + cn, cn) for s in range(cn)]
    greet_ctx(cn)
    ring.greet()

    wo_rows.greet_owners()
    pl.semaphore_wait(pltpu.get_barrier_semaphore(), cn - 1 + 2 + wo_rows.links)
    wo_rows.start()
    swap_gate.start()

    def in_project(i):
        @pl.when(i == 1)
        def _():
            for s in range(cn // 2):
                ring.start(swap_gate.receive(s))

        @pl.when(i == 2)
        def _():
            for s in range(cn // 2, cn):
                ring.start(swap_gate.receive(s))
            swap_up.start()

    def in_attend(i):
        @pl.when(i == 2)
        def _():
            for source in sources[: cn // 2]:
                ring.forward(source)

    prepare(w, x_all, gains, rows_in, hw, 2 * rows)
    project(
        x_all, w, gains.at[0:1], inverse, rows_in, cols, cosines, sines, an, qkv, hw, 2 * rows,
        in_project,
    )
    attend(qkv, cols, rows_in, o, mass, hw, 2 * rows, in_attend)
    for source in sources[cn // 2 :]:
        ring.forward(source)
    swap_up.finish()
    wo_rows.finish()
    for source in sources:
        ring.finish(source)
    swap_gate.sent()


def middle_kernel(
    cn, dpn, o, wo, x, gain, dy, up, gate_all, down_all,
    h1, bn_all, up_all, hid, dgu, dys_all,
    own, bn, dys, wg, wu, down, gsem, ysem, rsem, local, *sum_refs,
):
    c, d = lax.axis_index("ctx"), lax.axis_index("dp")
    _, j, k, n, _ = place(cn)
    rows, width = x.shape
    ff = hid.shape[1]
    block = 2 * rows
    gather = LineGather(cn, own, bn, gsem)
    gather_dy = LineGather(cn, dy, dys, ysem)
    ring = RingGather(dpn, up, up_all, rsem)
    total = LineSum(cn, product(o, wo, plain, rows, width), *sum_refs)
    greet_line(cn, ring)
    ring.start()
    keep_up = pltpu.make_async_copy(up, up_all.at[d], local.at[0])
    loads = [
        pltpu.make_async_copy(src, dst, local.at[i])
        for i, (src, dst) in enumerate(((gate_all, wg), (down_all, down)), 2)
    ]
    keep_up.start()
    for load in loads:
        load.start()
    gather_dy.start()
    dys[c] = dy[...]

    def between(s):
        gather_dy.step(s + 1)

        @pl.when(s == n - 2)
        def _():
            ring.forward()

    line_sums(cn, [total], between)

    def norm(r):
        mid = x[r, :].astype(f32) + total.part[0, k, r, :]
        h1[r, :] = mid
        own[r, :] = (mid * rms(mid) * gain[1:2, :]).astype(bf16)

    by_rows(rows, norm)
    gather.start()
    bn[c] = own[...]
    gather_dy.finish()
    store_dy = pltpu.make_async_copy(dys, dys_all, local.at[4])
    store_dy.start()
    total.drain()
    keep_up.wait()
    for load in loads:
        load.wait()
    ring.finish()
    load_up = pltpu.make_async_copy(up_all, wu, local.at[0])
    load_up.start()
    load_up.wait()
    wgate, wup = wg, wu.reshape(width, ff)
    tile = min(512, ff)

    def feed(t):
        gather.other(t)
        at = pl.ds(pl.multiple_of(t * block, block), block)
        pair = pl.ds(t * 2, 2)
        send = pltpu.make_async_copy(bn.at[pair], bn_all.at[pair], local.at[1])
        send.start()
        a = bn[pair].reshape(block, width)
        g_out = dys[pair].reshape(block, width)

        @pl.loop(0, ff // tile)
        def _(i):
            to = pl.ds(pl.multiple_of(i * tile, tile), tile)
            gate = dot(a, wgate[:, to])
            up_v = dot(a, wup[:, to])
            dhid = dot(g_out, down[to, :], contract_cols)
            sig = jax.nn.sigmoid(gate)
            silu = gate * sig
            hid[at, to] = (silu * up_v).astype(bf16)
            dgate = dhid * up_v * sig * (1.0 + gate * (1.0 - sig))
            dgu[at, to] = dgate.astype(bf16)
            dgu[at, pl.ds(pl.multiple_of(ff + i * tile, tile), tile)] = (dhid * silu).astype(bf16)

        send.wait()

    feed(j)
    gather.step(1)

    @pl.loop(1, n)
    def _(s):
        both = (j - s >= 0) & (j + s <= n - 1)

        @pl.when(j - s >= 0)
        def _():
            feed(j - s)

        @pl.when(both & (s < n - 1))
        def _():
            gather.step(s + 1)

        @pl.when(j + s <= n - 1)
        def _():
            feed(j + s)

        @pl.when(jnp.logical_not(both) & (s < n - 1))
        def _():
            gather.step(s + 1)

    gather.sent()
    store_dy.wait()


def back_kernel(
    cn, dpn, bn_in, dgu_in, hid, down, wg, wu, h1, dy, gain, dh1, dob_all, term, g_own, result,
    own, bn, dgu, cross_in, arrived, bsem, gsem, loads, keep_sem, *scratch,
):
    sum_refs, ring_refs = scratch[:-4], scratch[-4:]
    rows, width = dy.shape
    ff = wg.shape[1]
    tile = min(512, width)
    c, _, k, n, _ = place(cn)

    def compute(t, out):
        at = pl.ds(pl.multiple_of(t * 2 * rows, 2 * rows), 2 * rows)

        @pl.loop(0, width // tile)
        def _(i):
            to = pl.ds(pl.multiple_of(i * tile, tile), tile)
            part = dot(dgu[at, 0:ff], wg[to, :], contract_cols)
            part = part + dot(dgu[at, ff:], wu[to, :], contract_cols)
            out[:, :, to] = part.reshape(2, rows, tile)

    total = LineSum(cn, compute, *sum_refs)
    ring = RingSum(dpn, *ring_refs)
    blocks = ring_refs[0]
    m = blocks.shape[1]
    load_dgu = pltpu.make_async_copy(dgu_in, dgu, loads.at[0])
    load_bn = pltpu.make_async_copy(bn_in, bn, loads.at[1])
    load_dgu.start()
    load_bn.start()
    greet_line(cn, ring.ring)
    order = ring.order()
    load_dgu.wait()

    def weight_grad(member):
        outer(bn, dgu, blocks.at[member], pl.ds(pl.multiple_of(member * m, m), m))


    def between(s):
        @pl.when(s == 0)
        def _():
            load_bn.wait()
            weight_grad(order[0])
            ring.start()

        for i in range(ring.hops - 1):

            @pl.when(s == min(i, n - 2))
            def _():
                weight_grad(order[1 + 2 * i])
                weight_grad(order[2 + 2 * i])

            @pl.when(s == min(i + 2, n - 2))
            def _():
                ring.forward(i + 1)

        @pl.when(s == n - 2)
        def _():
            weight_grad(order[-1])

    line_sums(cn, [total], between)
    load_hid = pltpu.make_async_copy(hid, dgu.at[:, 0:ff], loads.at[0])
    load_down = pltpu.make_async_copy(down, bn.at[0:ff], loads.at[1])
    load_hid.start()
    load_down.start()
    term[...] = jnp.zeros_like(term)

    def norm_back(r):
        dbn = total.part[0, k, r, :]
        mid = h1[r, :]
        r2 = rms(mid)
        xh2 = mid * r2
        term[...] += jnp.sum(dbn * xh2, axis=0, keepdims=True)
        u2 = dbn * gain[1:2, :]
        mean = jnp.mean(u2 * xh2, axis=-1, keepdims=True)
        grad = dy[r, :].astype(f32) + r2 * (u2 - xh2 * mean)
        dh1[r, :] = grad
        own[r, :] = grad.astype(bf16)

    by_rows(rows, norm_back)
    gather = LineGather(cn, own, dob_all, gsem)
    gather.start()
    keep = pltpu.make_async_copy(own, dob_all.at[c], keep_sem)
    keep.start()
    total.drain()

    part, cross, _, flow, _, _ = sum_refs
    second = LineSum(
        cn,
        product(dgu.at[:, 0:ff], bn.at[0:ff], plain, rows, width),
        part, cross, cross_in, flow, arrived, bsem,
    )
    load_hid.wait()
    load_down.wait()

    def pass_on(s):
        gather.step(s + 1)

    line_sums(cn, [second], pass_on)

    def close(r):
        result[r, :] = (h1[r, :] + second.part[0, k, r, :]).astype(bf16)

    by_rows(rows, close)
    second.drain()
    keep.wait()
    gather.finish()
    ring.finish(g_own)


def attend_back(qkv, do, cosines, sines, q_info, k_info, dq, dqkv, hw, block):
    count = qkv.shape[0] // block
    dq[...] = jnp.zeros_like(dq)

    def turn_back(g, at):
        return g * cosines[at, :] - pltpu.roll(g, HEAD_DIM // 2, 1) * sines[at, :]

    @pl.loop(0, count)
    def _(j):
        to = pl.ds(pl.multiple_of(j * block, block), block)
        k_code = k_info[to, 2:3]
        for h in range(hw // HEAD_DIM):
            lane = [slice(t * hw + h * HEAD_DIM, t * hw + (h + 1) * HEAD_DIM) for t in range(3)]
            k, v = qkv[to, lane[1]], qkv[to, lane[2]]

            def step(i, carry):
                dk, dv = carry
                at = pl.ds(pl.multiple_of(i * block, block), block)
                q, do_i = qkv[at, lane[0]], do[at, lane[0]]
                s = dot(k, q, contract_cols) * score_scale - score_shift
                keys = lax.broadcasted_iota(jnp.int32, (block, block), 0) + j * block
                queries = lax.broadcasted_iota(jnp.int32, (block, block), 1) + i * block
                allowed = (k_code == q_info[0:1, at]) & (keys <= queries)
                sg = jnp.where(allowed, jax.nn.sigmoid(s), 0.0)
                dp = dot(v, do_i, contract_cols)
                ds = (dp * sg * (1.0 - sg)).astype(bf16)
                dq[at, lane[0]] += dot(ds, k, contract_rows)
                return dk + dot(ds, q), dv + dot(sg.astype(bf16), do_i)

            zero = jnp.zeros((block, HEAD_DIM), f32)
            dk, dv = lax.fori_loop(j, count, step, (zero, zero))
            dqkv[to, lane[1]] = turn_back(dk * score_scale, to).astype(bf16)
            dqkv[to, lane[2]] = dv.astype(bf16)

    @pl.loop(0, count)
    def _(i):
        at = pl.ds(pl.multiple_of(i * block, block), block)
        for h in range(hw // HEAD_DIM):
            lanes = slice(h * HEAD_DIM, (h + 1) * HEAD_DIM)
            dqkv[at, lanes] = turn_back(dq[at, lanes] * score_scale, at).astype(bf16)


def last_kernel(
    cn, dpn, g_gu, dob_all, dys_all, hid, o, wo, qkv, cosines, sines, q_info, k_info, an, w,
    dh1, x, gain, term_two, mass, grad_in, tot_out, gu_all, down_own, out_all, qkv_all,
    do, dq, dqkv, out_parts, out_got, qkv_own, tot, tot_in, tot_sum, tot_last,
    usem, qsem, tsem, psem, osem, local, *scratch,
):
    sum_refs, rings = scratch[:-8], (scratch[-8:-4], scratch[-4:])
    rows, width = x.shape
    hw = width // cn
    _, _, k, n, _ = place(cn)
    down_ring, qkv_ring = (RingSum(dpn, *refs) for refs in rings)
    rows_out = RowSum(cn, dpn, out_parts, out_got, osem)
    swap_gu = Swap(cn, g_gu, gu_all, usem, local.at[0])
    swap_qkv = Swap(cn, qkv_own, qkv_all, qsem, local.at[4])
    totals = Swap(cn, None, tot_in, tsem, local.at[3], lambda i: tot)
    c, d = lax.axis_index("ctx"), lax.axis_index("dp")
    def share(s):
        return remote(
            tot_sum, tot_last.at[d], psem.at[0, s], psem.at[1, s], {"dp": lax.rem(d + s, dpn)}
        )

    greet_ctx(cn)
    for s in range(1, dpn):
        greet({"dp": lax.rem(d + s, dpn)})

    rows_out.greet_homes()
    pl.semaphore_wait(
        pltpu.get_barrier_semaphore(), cn - 1 + dpn - 1 + rows_out.links
    )
    swap_gu.start()
    seq = an.shape[0]
    stage = (sum_refs[1], sum_refs[3])
    halves = (slice(0, seq // 2), slice(seq // 2, seq))

    def fill(src):
        copies = [
            pltpu.make_async_copy(src.at[pl.ds(i * n, n)], stage[i], local.at[1 + i])
            for i in range(2)
        ]
        for copy in copies:
            copy.start()
        for copy in copies:
            copy.wait()

    def staged(i, to=slice(None)):
        return stage[i][:, :, to].reshape(seq // 2, -1)

    fill(dob_all)
    outer_all(o, staged, halves, out_parts)
    rows_out.start()
    for i in range(2):
        do[halves[i], :] = dot(staged(i), wo[...], contract_cols).astype(bf16)
    fill(dys_all)
    outer_all(hid, staged, halves, rings[0][0])
    down_ring.start()
    m_qkv = rings[1][0].shape[1]
    order = qkv_ring.order()

    def grad_qkv(member):
        outer(an, dqkv, rings[1][0].at[member], pl.ds(pl.multiple_of(member * m_qkv, m_qkv), m_qkv))

    attend_back(qkv, do, cosines, sines, q_info, k_info, dq, dqkv, hw, 2 * rows)
    grad_qkv(order[0])
    qkv_ring.start()
    total = LineSum(cn, product(dqkv, w, contract_cols, rows, width), *sum_refs)

    def between(s):
        for i in range(qkv_ring.hops - 1):

            @pl.when(s == min(i, n - 2))
            def _():
                grad_qkv(order[1 + 2 * i])
                grad_qkv(order[2 + 2 * i])
                qkv_ring.forward(i + 1)

            @pl.when(s == min(i + 1, n - 2))
            def _():
                down_ring.forward(i + 1)

        @pl.when(s == n - 2)
        def _():
            grad_qkv(order[-1])
            qkv_ring.finish(qkv_own)
            swap_qkv.start()

    line_sums(cn, [total], between)
    tot[0] = jnp.zeros((1, width), f32)

    def norm_back(r):
        dan = total.part[0, k, r, :]
        xf = x[r, :].astype(f32)
        r1 = rms(xf)
        xh1 = xf * r1
        tot[0] += jnp.sum(dan * xh1, axis=0, keepdims=True)
        u1 = dan * gain[0:1, :]
        mean = jnp.mean(u1 * xh1, axis=-1, keepdims=True)
        grad = dh1[r, :] + r1 * (u1 - xh1 * mean)
        grad_in[r, :] = grad.astype(bf16)

    by_rows(rows, norm_back)
    tot[1] = term_two[...]
    tot[2] = jnp.broadcast_to(jnp.sum(mass[...], axis=1, keepdims=True), (1, width))
    totals.start()
    rows_out.finish(out_all)
    totals.finish()
    tot_sum[...] = jnp.sum(tot_in[...], axis=0)
    for s in range(1, dpn):
        share(s).start()
    down_ring.finish(down_own)
    total.drain()
    swap_gu.finish()
    tot_last[d] = tot_sum[...]
    for s in range(1, dpn):
        source = lax.rem(d - s + dpn, dpn)
        block = tot_last.at[source]
        remote(block, block, psem.at[0, s], psem.at[1, s], {"dp": source}).wait_recv()
    for s in range(1, dpn):
        share(s).wait_send()
    tot_out[...] = jnp.sum(tot_last[...], axis=0)
    swap_qkv.finish()


def spread_kernel(
    cn, dpn, qkv_in, gu_in, down_in, out_in, gq, gk, gv, go, gg, gu_out, gd, qkv, gu, down, out, sem
):
    hw = qkv.shape[2] // 3
    ff_rows = gd.shape[0]
    ff = ff_rows * dpn
    pairs = ((down_in, down), (out_in, out), (qkv_in, qkv), (gu_in, gu))
    loads = [pltpu.make_async_copy(a, b, sem.at[i]) for i, (a, b) in enumerate(pairs)]
    for load in loads:
        load.start()
    for load in loads[:3]:
        load.wait()
    gd[...] = down[...].astype(f32)
    go[...] = out[...]
    for c in range(cn):
        for i, ref in enumerate((gq, gk, gv)):
            for t in range(hw // HEAD_DIM):
                lo, at = head_of(cn, hw // HEAD_DIM, c, t) * HEAD_DIM, i * hw + t * HEAD_DIM
                ref[:, lo : lo + HEAD_DIM] = qkv[c, :, at : at + HEAD_DIM].astype(f32)
    loads[3].wait()
    for c in range(cn):
        for i, ref in enumerate((gg, gu_out)):
            for d in range(dpn):
                to = (d * cn + c) * ff_rows
                lo = i * ff + d * ff_rows
                ref[:, to : to + ff_rows] = gu[c, :, lo : lo + ff_rows].astype(f32)


def call(kernel, outs, ins, specs_in, specs_out, scratch, number, flops=0, moved=0):
    return pl.pallas_call(
        kernel,
        out_shape=outs,
        in_specs=specs_in,
        out_specs=specs_out,
        scratch_shapes=scratch,
        compiler_params=pltpu.CompilerParams(
            collective_id=number, has_side_effects=True, vmem_limit_bytes=61 * 2**20
        ),
        cost_estimate=pl.CostEstimate(flops=flops, bytes_accessed=moved, transcendentals=0),
    )(*ins)


def shape(dims, dtype=bf16):
    return jax.ShapeDtypeStruct(dims, dtype)


def shards(
    hidden_in,
    out_grad,
    seg_ids,
    valid_mask,
    w_query,
    w_key,
    w_value,
    w_output,
    w_gate,
    w_up,
    w_down,
    gain_attn,
    gain_mlp,
):
    dpn = lax.axis_size("dp")
    cn = lax.axis_size("ctx")
    n = cn // 2
    x_local = hidden_in[0]
    dy_local = out_grad[0]
    rows, width = x_local.shape
    seq = rows * cn
    dr = w_query.shape[0]
    hw = width // cn
    heads = hw // HEAD_DIM
    ff_rows = w_down.shape[0]
    ff = ff_rows * dpn
    dma = pltpu.SemaphoreType.DMA
    mib = 2**20

    gain_rows = jnp.pad(jnp.stack([gain_attn, gain_mlp]), ((0, 0), (0, 128 - dr)))
    pw = 3 * hw + 128
    ring_sem = dma((4, dpn // 2 + 1))
    x_all, w_qkv, gate_pack, up_pack, down, wo_low = call(
        functools.partial(front_kernel, cn, dpn),
        (
            shape((cn, rows, width + 128)),
            shape((dpn, cn, dr, pw)),
            shape((cn, dr, ff)),
            shape((cn, dr, ff)),
            shape((dpn, ff_rows, width)),
            shape((dr, width)),
        ),
        (
            x_local, seg_ids, valid_mask, gain_rows, w_query, w_key, w_value, w_output,
            w_gate, w_up, w_down,
        ),
        [ANY] + [VMEM] * 7 + [ANY] * 3,
        (ANY, ANY, VMEM, VMEM, ANY, VMEM),
        [
            pltpu.VMEM((rows, width + 128), bf16),
            pltpu.VMEM((cn, dr, pw), bf16),
            pltpu.VMEM((2, dr, ff * cn), f32),
            pltpu.VMEM((ff_rows, width), f32),
            pltpu.VMEM((ff_rows, width), bf16),
            dma((5, n)),
            dma((2, cn)),
            dma((4, dpn // 2 + 1, cn)),
            ring_sem,
            dma((6,)),
        ],
        1,
        moved=160 * mib,
    )
    w_qkv = w_qkv.reshape(width, pw)
    inverse = jnp.exp(
        jnp.arange(HEAD_DIM // 2, dtype=f32) * (-2.0 * math.log(rope_base) / HEAD_DIM)
    )
    inverse = jnp.concatenate([inverse, inverse])[None]

    line_scratch = sum_scratch(cn, rows, width)
    an, proj, o, mass, gains, cosines, sines, cols, infos, w_gate_c, up_own, wo = call(
        functools.partial(attn_kernel, cn, dpn),
        (
            shape((seq, width)),
            shape((seq, 3 * hw)),
            shape((seq, hw)),
            shape((1, 2 * rows), f32),
            shape((8, width), f32),
            shape((seq, HEAD_DIM), f32),
            shape((seq, HEAD_DIM), f32),
            shape((seq, 128), f32),
            shape((8, seq), f32),
            shape((dpn, cn, dr, ff)),
            shape((cn, dr, ff)),
            shape((dpn, dr, width)),
        ),
        (x_all, w_qkv, inverse, gate_pack, up_pack, wo_low),
        [VMEM] * 3 + [ANY] * 3,
        (VMEM,) * 9 + (ANY,) * 3,
        [dma((2, 2, cn)), dma((4, dpn // 2 + 1, cn)), dma((2, dpn)), dma((3,))],
        2,
        moved=160 * mib,
    )
    down = down.reshape(ff, width)
    h1, bn, w_up_c, hid, dgu, dys = call(
        functools.partial(middle_kernel, cn, dpn),
        (
            shape((rows, width), f32),
            shape((cn, rows, width)),
            shape((dpn, cn, dr, ff)),
            shape((seq, ff)),
            shape((seq, 2 * ff)),
            shape((cn, rows, width)),
        ),
        (
            o, wo.reshape(hw, width), x_local, gains, dy_local, up_own,
            w_gate_c.reshape(width, ff), down,
        ),
        [VMEM] * 5 + [ANY] * 3,
        (VMEM, ANY, ANY, VMEM, VMEM, ANY),
        [
            pltpu.VMEM((rows, width), bf16),
            pltpu.VMEM((cn, rows, width), bf16),
            pltpu.VMEM((cn, rows, width), bf16),
            pltpu.VMEM((width, ff), bf16),
            pltpu.VMEM((dpn, cn, dr, ff), bf16),
            pltpu.VMEM((ff, width), bf16),
            dma((5, n)),
            dma((5, n)),
            ring_sem,
            dma((5,)),
        ]
        + line_scratch,
        3,
        moved=160 * mib,
    )
    wo = wo.reshape(hw, width)
    w_gate_c = w_gate_c.reshape(width, ff)
    w_up_c = w_up_c.reshape(width, ff)
    bn = bn.reshape(seq, width)
    dh1, dob, term_two, g_gu, result = call(
        functools.partial(back_kernel, cn, dpn),
        (
            shape((rows, width), f32),
            shape((cn, rows, width)),
            shape((1, width), f32),
            shape((cn, dr, 2 * ff)),
            shape((rows, width)),
        ),
        (bn, dgu, hid, down, w_gate_c, w_up_c, h1, dy_local, gains),
        [ANY] * 4 + [VMEM] * 5,
        (VMEM, ANY, VMEM, VMEM, VMEM),
        [
            pltpu.VMEM((rows, width), bf16),
            pltpu.VMEM((seq, width), bf16),
            pltpu.VMEM((seq, 2 * ff), bf16),
            pltpu.VMEM((n, rows, width), bf16),
            pltpu.VMEM((n + 1, rows, width), bf16),
            dma((4, n + 1)),
            dma((5, n)),
            dma((2,)),
            dma,
        ]
        + line_scratch
        + ring_scratch(dpn, cn * dr, 2 * ff),
        4,
        moved=160 * mib,
    )
    grad_input, totals, gu_back, g_down, g_out, q_all = call(
        functools.partial(last_kernel, cn, dpn),
        (
            shape((rows, width)),
            shape((3, 1, width), f32),
            shape((cn, dr, 2 * ff)),
            shape((ff_rows, width)),
            shape((dr, width), f32),
            shape((cn, dr, 3 * hw)),
        ),
        (
            g_gu, dob, dys, hid, o, wo, proj, cosines, sines, infos, cols, an, w_qkv,
            dh1, x_local, gains, term_two, mass,
        ),
        [ANY] * 3 + [VMEM] * 15,
        (VMEM, VMEM, ANY, VMEM, VMEM, ANY),
        [
            pltpu.VMEM((seq, hw), bf16),
            pltpu.VMEM((seq, hw), f32),
            pltpu.VMEM((seq, 3 * hw), bf16),
            pltpu.VMEM((dpn, dr, width), bf16),
            pltpu.VMEM((dpn, dr, width), bf16),
            pltpu.VMEM((cn, dr, 3 * hw), bf16),
            pltpu.VMEM((3, 1, width), f32),
            pltpu.VMEM((cn, 3, 1, width), f32),
            pltpu.VMEM((3, 1, width), f32),
            pltpu.VMEM((dpn, 3, 1, width), f32),
            dma((2, cn)),
            dma((2, cn)),
            dma((2, cn)),
            dma((2, dpn)),
            dma((2, dpn)),
            dma((5,)),
        ]
        + line_scratch
        + ring_scratch(dpn, ff_rows, width)
        + ring_scratch(dpn, cn * dr, 3 * hw),
        5,
        moved=160 * mib,
    )

    g_q, g_k, g_v, g_o, g_gate, g_up, g_down = pl.pallas_call(
        functools.partial(spread_kernel, cn, dpn),
        out_shape=tuple(shape((dr, width), f32) for _ in range(4))
        + tuple(shape((dr, ff * cn), f32) for _ in range(2))
        + (shape((ff_rows, width), f32),),
        in_specs=[ANY] * 4,
        out_specs=(VMEM,) * 7,
        scratch_shapes=[
            pltpu.VMEM((cn, dr, 3 * hw), bf16),
            pltpu.VMEM((cn, dr, 2 * ff), bf16),
            pltpu.VMEM((ff_rows, width), bf16),
            pltpu.VMEM((dr, width), f32),
            dma((4,)),
        ],
        compiler_params=pltpu.CompilerParams(vmem_limit_bytes=61 * 2**20),
    )(q_all, gu_back, g_down, g_out)
    mass_mean = totals[2, 0, 0] / (heads * cn * dpn * seq)
    owner = (lax.axis_index("dp") * cn + lax.axis_index("ctx")) * dr
    grad_gains = [lax.dynamic_slice_in_dim(totals[i, 0], owner, dr) for i in range(2)]
    return (
        result[None],
        grad_input[None],
        g_q,
        g_k,
        g_v,
        g_o,
        g_gate,
        g_up,
        g_down,
        grad_gains[0],
        grad_gains[1],
        mass_mean,
    )


def solution(mesh):
    tok = P("dp", "ctx", None)
    ids = P("dp", "ctx")
    mat = P(("dp", "ctx"), None)
    vec = P(("dp", "ctx"))
    return jax.shard_map(
        shards,
        mesh=mesh,
        in_specs=(tok, tok, ids, ids) + (mat,) * 7 + (vec, vec),
        out_specs=(tok, tok) + (mat,) * 7 + (vec, vec, P()),
        check_vma=False,
    )
```

```python
import functools
import math

import jax
import jax.numpy as jnp
from jax import lax
from jax.experimental import pallas as pl
from jax.experimental.pallas import tpu as pltpu
from jax.sharding import PartitionSpec as P

HEAD_DIM = 128
norm_eps = 1e-05
rope_base = 10000.0
score_shift = math.log(4096.0)
score_scale = 1.0 / math.sqrt(HEAD_DIM)
contract_rows = (((0,), (0,)), ((), ()))
contract_cols = (((1,), (1,)), ((), ()))
plain = (((1,), (0,)), ((), ()))
f32 = jnp.float32
bf16 = jnp.bfloat16
MESH = pl.DeviceIdType.MESH
ANY = pl.BlockSpec(memory_space=pl.ANY)
VMEM = pl.BlockSpec(memory_space=pltpu.VMEM)


def dot(a, b, dims=plain):
    return lax.dot_general(a, b, dims, preferred_element_type=f32)


def remote(src, dst, send, recv, target):
    return pltpu.make_async_remote_copy(
        src_ref=src,
        dst_ref=dst,
        send_sem=send,
        recv_sem=recv,
        device_id=target,
        device_id_type=MESH,
    )


def greet(target):
    pl.semaphore_signal(
        pltpu.get_barrier_semaphore(), inc=1, device_id=target, device_id_type=MESH
    )


def by_rows(count, work, step=16):
    @pl.loop(0, count // step)
    def _(i):
        work(pl.ds(pl.multiple_of(i * step, step), step))


def place(cn):
    c = lax.axis_index("ctx")
    j, k = c // 2, c % 2
    return c, j, k, cn // 2, 2 * j + 1 - k


def greet_line(cn, ring):
    c, j, _, n, sib = place(cn)
    ring.greet()
    greet({"ctx": sib})

    @pl.when(j < n - 1)
    def _():
        greet({"ctx": c + 2})

    @pl.when(j > 0)
    def _():
        greet({"ctx": c - 2})

    inner = jnp.where(j > 0, 1, 0) + jnp.where(j < n - 1, 1, 0)
    pl.semaphore_wait(pltpu.get_barrier_semaphore(), 3 + inner)


def greet_ctx(cn):
    c = lax.axis_index("ctx")
    for s in range(1, cn):
        greet({"ctx": lax.rem(c + s, cn)})


class LineGather:
    def __init__(self, cn, own, full, sem):
        self.cn, self.own, self.full, self.sem = cn, own, full, sem

    def copy(self, src, origin, kind, target):
        _, _, k, _, _ = place(self.cn)
        sem = self.sem
        return remote(
            src,
            self.full.at[2 * origin + k],
            sem.at[kind, origin],
            sem.at[3 if kind < 2 else 4, origin],
            {"ctx": target},
        )

    def start(self):
        c, j, _, n, sib = place(self.cn)

        @pl.when(j < n - 1)
        def _():
            self.copy(self.own, j, 0, c + 2).start()

        @pl.when(j > 0)
        def _():
            self.copy(self.own, j, 1, c - 2).start()

        self.copy(self.own, j, 2, sib).start()

    def step(self, s):
        c, j, k, n, sib = place(self.cn)

        @pl.when(j - s >= 0)
        def _():
            o = j - s
            block = self.full.at[2 * o + k]
            self.copy(block, o, 0, sib).wait_recv()

            @pl.when(j < n - 1)
            def _():
                self.copy(block, o, 0, c + 2).start()

            self.copy(block, o, 2, sib).start()

        @pl.when(j + s <= n - 1)
        def _():
            o = j + s
            block = self.full.at[2 * o + k]
            self.copy(block, o, 1, sib).wait_recv()

            @pl.when(j > 0)
            def _():
                self.copy(block, o, 1, c - 2).start()

            self.copy(block, o, 2, sib).start()

    def forward(self, first=1, last=None):
        for s in range(first, self.cn // 2 if last is None else last + 1):
            self.step(s)

    def other(self, o):
        _, _, k, _, sib = place(self.cn)
        block = self.full.at[2 * o + 1 - k]
        remote(
            block, block, self.sem.at[2, o], self.sem.at[4, o], {"ctx": sib}
        ).wait_recv()

    def sent(self):
        c, j, k, n, sib = place(self.cn)
        for o in range(n):
            block = self.full.at[2 * o + k]

            @pl.when((j < n - 1) & (o <= j))
            def _():
                self.copy(block, o, 0, sib).wait_send()

            @pl.when((j > 0) & (o >= j))
            def _():
                self.copy(block, o, 1, sib).wait_send()

            self.copy(block, o, 2, sib).wait_send()

    def finish(self):
        for o in range(self.cn // 2):
            self.other(o)
        self.sent()


class Swap:
    def __init__(self, cn, src, dst, sem, local, pick=None):
        self.cn, self.sem, self.local = cn, sem, local
        self.src = pick or (lambda c: src.at[c])
        self.dst = dst if callable(dst) else lambda c: dst.at[c]

    def copy(self, s):
        c = lax.axis_index("ctx")
        peer = lax.rem(c + s, self.cn)
        return remote(
            self.src(peer),
            self.dst(c),
            self.sem.at[0, s],
            self.sem.at[1, s],
            {"ctx": peer},
        )

    def start(self):
        c = lax.axis_index("ctx")
        for s in range(1, self.cn):
            self.copy(s).start()
        pltpu.make_async_copy(self.src(c), self.dst(c), self.local).start()

    def receive(self, s):
        c = lax.axis_index("ctx")
        if s == 0:
            pltpu.make_async_copy(self.src(c), self.dst(c), self.local).wait()
            return c
        source = lax.rem(c - s + self.cn, self.cn)
        block = self.dst(source)
        remote(
            block, block, self.sem.at[0, s], self.sem.at[1, s], {"ctx": source}
        ).wait_recv()
        return source

    def sent(self):
        for s in range(1, self.cn):
            self.copy(s).wait_send()

    def finish(self):
        for s in range(self.cn):
            self.receive(s)
        self.sent()


class RingGather:
    def __init__(self, dpn, own, full, sem):
        self.dpn, self.own, self.full, self.sem = dpn, own, full, sem
        self.hops = dpn // 2
        d = lax.axis_index("dp")
        self.p = d // 2 * 2 + lax.rem(lax.rem(d, 2) + d // 2, 2)

    def member(self, step):
        p = lax.rem(self.p + step + self.dpn, self.dpn)
        return p // 2 * 2 + lax.rem(lax.rem(p, 2) + p // 2, 2)

    def half(self, ref, h, right):
        if h < self.hops:
            return ref
        m = self.full.shape[1] // 2
        if len(self.full.shape) == 3 and m % 16:
            m = self.full.shape[2] // 2
            return ref.at[:, pl.ds(0 if right else m, m)]
        return ref.at[pl.ds(0 if right else m, m)]

    def copy(self, h, right):
        way = 1 if right else -1
        origin = self.member(-way * (h - 1))
        src = self.own if h == 1 else self.full.at[origin]
        return remote(
            self.half(src, h, right),
            self.half(self.full.at[origin], h, right),
            self.sem.at[0 if right else 1, h],
            self.sem.at[2 if right else 3, h],
            {"dp": self.member(way)},
        )

    def arrival(self, h, right):
        way = 1 if right else -1
        block = self.half(self.full.at[self.member(-way * h)], h, right)
        return remote(
            block,
            block,
            self.sem.at[0 if right else 1, h],
            self.sem.at[2 if right else 3, h],
            {"dp": self.member(way)},
        )

    def greet(self):
        greet({"dp": self.member(1)})
        greet({"dp": self.member(-1)})

    def start(self):
        self.copy(1, True).start()
        self.copy(1, False).start()

    def forward(self):
        for h in range(1, self.hops):
            for right in (True, False):
                self.arrival(h, right).wait_recv()
                self.copy(h + 1, right).start()

    def finish(self):
        for right in (True, False):
            self.arrival(self.hops, right).wait_recv()
        for h in range(1, self.hops + 1):
            for right in (True, False):
                self.copy(h, right).wait_send()


def head_of(cn, heads, c, i):
    return c // 2 + cn // 2 * (heads * (c % 2) + i)


class HeadRows:
    def __init__(self, cn, dpn, dr):
        self.cn, self.dpn = cn, dpn
        self.per = HEAD_DIM // dr
        self.heads = dpn // self.per
        self.c, self.d = lax.axis_index("ctx"), lax.axis_index("dp")
        mine = self.d * cn + self.c
        head, n = mine // self.per, cn // 2
        turn = head // n
        self.home = 2 * lax.rem(head, n) + turn // self.heads
        self.slot = lax.rem(turn, self.heads) * self.per + lax.rem(mine, self.per)
        self.links = dpn - jnp.where(self.home == self.c, 1, 0)

    def owner(self, r):
        i, q = r // self.per, r % self.per
        head = self.c // 2 + self.cn // 2 * (self.heads * lax.rem(self.c, 2) + i)
        g = head * self.per + q
        return {"dp": g // self.cn, "ctx": lax.rem(g, self.cn)}

    def from_here(self, r):
        at = self.owner(r)
        return (at["dp"] == self.d) & (at["ctx"] == self.c)

    def to_here(self, to):
        return (self.home == self.c) & (self.d == to)

    def greet_owners(self):
        for r in range(self.dpn):
            pl.when(jnp.logical_not(self.from_here(r)))(lambda r=r: greet(self.owner(r)))

    def greet_homes(self):
        for to in range(self.dpn):
            pl.when(jnp.logical_not(self.to_here(to)))(
                lambda to=to: greet({"dp": to, "ctx": self.home})
            )


class RowGather(HeadRows):
    def __init__(self, cn, dpn, rows, full, sem, local):
        super().__init__(cn, dpn, rows.shape[0])
        self.rows, self.full, self.sem = rows, full, sem
        self.keep = pltpu.make_async_copy(rows, full.at[self.slot], local)

    def copy(self, to):
        return remote(
            self.rows,
            self.full.at[self.slot],
            self.sem.at[0, to],
            self.sem.at[1, self.slot],
            {"dp": to, "ctx": self.home},
        )

    def start(self):
        for to in range(self.dpn):
            pl.when(jnp.logical_not(self.to_here(to)))(lambda to=to: self.copy(to).start())
            pl.when(self.to_here(to))(self.keep.start)

    def finish(self):
        for r in range(self.dpn):
            block = self.full.at[r]
            came = remote(block, block, self.sem.at[0, r], self.sem.at[1, r], self.owner(r))
            pl.when(jnp.logical_not(self.from_here(r)))(came.wait_recv)
            pl.when(self.from_here(r))(self.keep.wait)
        for to in range(self.dpn):
            pl.when(jnp.logical_not(self.to_here(to)))(lambda to=to: self.copy(to).wait_send())


class RowSum(HeadRows):
    def __init__(self, cn, dpn, parts, got, sem):
        super().__init__(cn, dpn, parts.shape[1])
        self.parts, self.got, self.sem = parts, got, sem

    def copy(self, r):
        return remote(
            self.parts.at[r],
            self.got.at[self.d],
            self.sem.at[0, r],
            self.sem.at[1, self.d],
            self.owner(r),
        )

    def start(self):
        for r in range(self.dpn):
            pl.when(jnp.logical_not(self.from_here(r)))(lambda r=r: self.copy(r).start())

            @pl.when(self.from_here(r))
            def _():
                self.got[self.d] = self.parts[r]

    def finish(self, out):
        for s in range(self.dpn):
            block = self.got.at[s]
            came = remote(
                block, block, self.sem.at[0, s], self.sem.at[1, s], {"dp": s, "ctx": self.home}
            )
            pl.when(jnp.logical_not(self.to_here(s)))(came.wait_recv)

        def add(r):
            total = self.got[0, r, :].astype(f32)
            for s in range(1, self.dpn):
                total = total + self.got[s, r, :].astype(f32)
            out[r, :] = total

        by_rows(out.shape[0], add)
        for r in range(self.dpn):
            pl.when(jnp.logical_not(self.from_here(r)))(lambda r=r: self.copy(r).wait_send())


class RingPieces(RingGather):
    def __init__(self, dpn, full, sem):
        super().__init__(dpn, None, full, sem)

    def piece(self, i, h, right, back):
        way = 1 if right else -1
        ref = self.full.at[self.member(-way * back), i]
        return remote(
            ref,
            ref,
            self.sem.at[0 if right else 1, h, i],
            self.sem.at[2 if right else 3, h, i],
            {"dp": self.member(way)},
        )

    def moves(self, i, h, right, act):
        if h < self.hops:
            act()
        else:
            first = i < self.full.shape[1] // 2
            pl.when(first if right else jnp.logical_not(first))(act)

    def start(self, i):
        for right in (True, False):
            self.moves(i, 1, right, lambda r=right: self.piece(i, 1, r, 0).start())

    def forward(self, i):
        for h in range(1, self.hops):
            for right in (True, False):
                self.piece(i, h, right, h).wait_recv()
                self.moves(
                    i, h + 1, right, lambda h=h, r=right: self.piece(i, h + 1, r, h).start()
                )

    def finish(self, i):
        for right in (True, False):
            h = self.hops
            self.moves(i, h, right, lambda r=right: self.piece(i, h, r, h).wait_recv())
        for h in range(1, self.hops + 1):
            for right in (True, False):
                self.moves(
                    i, h, right, lambda h=h, r=right: self.piece(i, h, r, h - 1).wait_send()
                )


class RingSum:
    def __init__(self, dpn, blocks, got, got_half, sem):
        self.dpn, self.blocks, self.sem = dpn, blocks, sem
        self.got, self.got_half = got, got_half
        self.ring = RingGather(dpn, None, blocks, sem)
        self.hops = dpn // 2

    def part(self, s, right):
        m, width = self.blocks.shape[1:]
        if s > 1:
            return 0, m, pl.ds(0, width)
        if (m // 2) % 16:
            return 0, m, pl.ds(0 if right else width // 2, width // 2)
        return 0 if right else m // 2, m // 2, pl.ds(0, width)

    def copy(self, s, right):
        way = 1 if right else -1
        target = self.ring.member(way * (self.hops - s + 1))
        start, size, lanes = self.part(s, right)
        return remote(
            self.blocks.at[target, pl.ds(start, size), lanes],
            self.arrived(s, right),
            self.sem.at[0 if right else 1, s],
            self.sem.at[2 if right else 3, s],
            {"dp": self.ring.member(way)},
        )

    def arrived(self, s, right):
        side = 0 if right else 1
        return self.got_half.at[side] if s == 1 else self.got.at[side, s - 2]

    def order(self):
        out = [self.ring.member(self.hops)]
        for s in range(self.hops - 1, 0, -1):
            out += [self.ring.member(s), self.ring.member(-s)]
        return out + [self.ring.member(0)]

    def start(self):
        self.copy(1, True).start()
        self.copy(1, False).start()

    def take(self, s, right, target):
        self.copy(s, right).wait_recv()
        start, size, lanes = self.part(s, right)
        block = self.blocks.at[target, pl.ds(start, size), lanes]
        came = self.arrived(s, right)

        def add(r):
            block[r, :] = (block[r, :].astype(f32) + came[r, :].astype(f32)).astype(bf16)

        by_rows(size, add)

    def forward(self, s):
        for right in (True, False):
            way = 1 if right else -1
            self.take(s, right, self.ring.member(way * (self.hops - s)))
            self.copy(s + 1, right).start()

    def finish(self, out):
        for right in (True, False):
            self.copy(self.hops, right).wait_recv()
        mine = self.ring.member(0)
        ends = [self.arrived(self.hops, right) for right in (True, False)]
        per = out.shape[-2]

        @pl.loop(0, self.blocks.shape[1] // 16)
        def _(i):
            r = pl.ds(pl.multiple_of(i * 16, 16), 16)
            total = self.blocks[mine, r, :].astype(f32)
            for end in ends:
                total = total + end[r, :].astype(f32)
            if len(out.shape) == 3:
                to = pl.ds(pl.multiple_of(lax.rem(i * 16, per), 16), 16)
                out[i * 16 // per, to, :] = total.astype(out.dtype)
            else:
                out[r, :] = total.astype(out.dtype)

        for s in range(1, self.hops + 1):
            for right in (True, False):
                self.copy(s, right).wait_send()


def ring_scratch(dpn, m, width):
    return [
        pltpu.VMEM((dpn, m, width), bf16),
        pltpu.VMEM((2, dpn // 2 - 1, m, width), bf16),
        pltpu.VMEM((2, m // 2, width) if m % 32 == 0 else (2, m, width // 2), bf16),
        pltpu.SemaphoreType.DMA((4, dpn // 2 + 1)),
    ]


def outer(a_ref, b_ref, out, at, tile=512):
    a = a_ref[:, at]
    width = out.shape[-1]
    for lo in range(0, width, tile):
        to = slice(lo, min(lo + tile, width))
        out[:, to] = dot(a, b_ref[:, to], contract_rows).astype(bf16)


def outer_all(a_ref, staged, halves, blocks, tile=512):
    count, m, width = blocks.shape
    many = max(1, 128 // m)
    for first in range(0, count, many):
        at = slice(first * m, (first + many) * m)
        for lo in range(0, width, tile):
            to = slice(lo, min(lo + tile, width))
            part = dot(a_ref[halves[0], at], staged(0, to), contract_rows)
            part = part + dot(a_ref[halves[1], at], staged(1, to), contract_rows)
            part = part.astype(bf16)
            for i in range(many):
                blocks[first + i, :, to] = part[i * m : (i + 1) * m]


class LineSum:
    def __init__(self, cn, compute, part, cross, cross_in, flow, arrived, sem):
        self.cn, self.compute, self.part = cn, compute, part
        self.cross, self.cross_in, self.flow = cross, cross_in, flow
        self.arrived, self.sem = arrived, sem

    def across(self, t):
        _, _, _, _, sib = place(self.cn)
        return remote(
            self.cross.at[t],
            self.cross_in.at[t],
            self.sem.at[0, t],
            self.sem.at[2, t],
            {"ctx": sib},
        )

    def along(self, t, slot, target):
        return remote(
            self.flow.at[t],
            self.arrived.at[slot],
            self.sem.at[1, t],
            self.sem.at[3, slot],
            {"ctx": target},
        )

    def produce(self, t, slot):
        _, _, k, _, _ = place(self.cn)
        part = self.part.at[slot]
        self.compute(t, part)

        def low(r):
            self.cross[t, r, :] = part[1 - k, r, :].astype(bf16)

        by_rows(self.cross.shape[1], low)
        self.across(t).start()

    def add(self, part, came):
        def more(r):
            part[r, :] += came[r, :].astype(f32)

        by_rows(part.shape[0], more)

    def collect(self, t, slot):
        _, j, k, n, sib = place(self.cn)
        part = self.part.at[slot, k]
        self.across(t).wait_recv()
        self.add(part, self.cross_in.at[t])

        @pl.when((j > 0) & (t >= j))
        def _():
            self.along(t, t, sib).wait_recv()
            self.add(part, self.arrived.at[t])

        @pl.when((j < n - 1) & (t <= j))
        def _():
            slot_in = jnp.where(t == j, n, t)
            self.along(t, slot_in, sib).wait_recv()
            self.add(part, self.arrived.at[slot_in])

    def send(self, t, slot, up):
        c, j, k, n, _ = place(self.cn)

        def low(r):
            self.flow[t, r, :] = self.part[slot, k, r, :].astype(bf16)

        by_rows(self.flow.shape[1], low)
        there = t if up else jnp.where(t == j - 1, n, t)
        self.along(t, there, c + 2 if up else c - 2).start()

    def drain(self):
        _, j, _, n, sib = place(self.cn)

        @pl.loop(0, n)
        def _(t):
            self.across(t).wait_send()

            @pl.when(t != j)
            def _():
                self.along(t, t, sib).wait_send()


def line_sums(cn, sums, between=None):
    _, j, _, n, _ = place(cn)

    @pl.loop(0, n - 1)
    def _(s):
        to_up, to_down = n - 1 - s + j, s - (n - 1 - j)
        for total in sums:

            @pl.when(s >= j)
            def _():
                total.produce(to_up, 0)

            @pl.when(s >= n - 1 - j)
            def _():
                total.produce(to_down, 1)

        for total in sums:

            @pl.when(s >= j)
            def _():
                total.collect(to_up, 0)
                total.send(to_up, 0, True)

            @pl.when(s >= n - 1 - j)
            def _():
                total.collect(to_down, 1)
                total.send(to_down, 1, False)

        if between is not None:
            between(s)

    for total in sums:
        total.produce(j, 0)
    for total in sums:
        total.collect(j, 0)


def sum_scratch(cn, rows, width):
    n = cn // 2
    return [
        pltpu.VMEM((2, 2, rows, width), f32),
        pltpu.VMEM((n, rows, width), bf16),
        pltpu.VMEM((n, rows, width), bf16),
        pltpu.VMEM((n, rows, width), bf16),
        pltpu.VMEM((n + 1, rows, width), bf16),
        pltpu.SemaphoreType.DMA((4, n + 1)),
    ]


def product(a_ref, b_ref, dims, rows, width):
    tile = min(512, width)

    def compute(t, out):
        a = a_ref[pl.ds(pl.multiple_of(t * 2 * rows, 2 * rows), 2 * rows), :]

        @pl.loop(0, width // tile)
        def _(i):
            at = pl.ds(pl.multiple_of(i * tile, tile), tile)
            b = b_ref[:, at] if dims == plain else b_ref[at, 0 : a_ref.shape[1]]
            out[:, :, at] = dot(a, b, dims).reshape(2, rows, tile)

    return compute


def rms(v):
    return lax.rsqrt(jnp.mean(v * v, axis=-1, keepdims=True) + norm_eps)


def front_kernel(
    cn, dpn, x_in, seg, valid, gain_rows, wq, wk, wv, wo, gate_in, up_in, down_in,
    x_all, pack_all, gate, up, down_all, wo_low, down_rest,
    x, pack, wide, tall, down, gsem, ssem, rsem, dsem, local,
):
    c, d = lax.axis_index("ctx"), lax.axis_index("dp")
    hw = wq.shape[1] // cn
    part = gate_in.shape[1] // (cn * dpn)
    mine = pack_all.at[d]
    swap = Swap(cn, pack, mine, ssem, local.at[0])
    gather = LineGather(cn, x, x_all, gsem)
    ring = RingPieces(dpn, pack_all, rsem)
    down_ring = RingGather(dpn, down, down_all, dsem)
    greet_ctx(cn)
    ring.greet()
    rows, width = x_in.shape
    load_x = pltpu.make_async_copy(x_in, x.at[:, 0:width], local.at[1])
    load_x.start()

    def column(row):
        return jnp.broadcast_to(row, (128, 128)).T

    code = (seg[...] * 2 + valid[...]).astype(f32)
    x[:, width:] = column(code).astype(bf16)
    lane = lax.broadcasted_iota(jnp.int32, (128, 128), 1)
    gains = jnp.where(lane == 0, column(gain_rows[0:1, :]), column(gain_rows[1:2, :]))
    gains = gains[0 : wq.shape[0]].astype(bf16)
    load_x.wait()
    loads = [
        pltpu.make_async_copy(src, dst, local.at[i])
        for i, (src, dst) in enumerate(
            ((gate_in, wide.at[0]), (up_in, wide.at[1]), (down_in, tall)), 2
        )
    ]
    for load in loads:
        load.start()
    pl.semaphore_wait(pltpu.get_barrier_semaphore(), cn - 1 + 2)
    gather.start()
    for to in range(cn):
        for i, w in enumerate((wq, wk, wv)):
            for t in range(hw // HEAD_DIM):
                lo, at = head_of(cn, hw // HEAD_DIM, to, t) * HEAD_DIM, i * hw + t * HEAD_DIM
                pack[to, :, at : at + HEAD_DIM] = w[:, lo : lo + HEAD_DIM].astype(bf16)
        pack[to, :, 3 * hw :] = gains
    swap.start()
    loads[2].wait()
    split = down.shape[0]
    down[...] = tall[0:split, :].astype(bf16)
    down_rest[...] = tall[split:, :].astype(bf16)
    down_ring.start()
    keep_down = pltpu.make_async_copy(down, down_all.at[d], local.at[5])
    keep_down.start()
    keep = pltpu.make_async_copy(x, x_all.at[c], local.at[1])
    keep.start()
    wo_low[...] = wo[...].astype(bf16)

    def lay(i, out):
        loads[i].wait()
        for to in range(cn):
            for row in range(dpn):
                lo = (row * cn + to) * part
                out[to, :, row * part : (row + 1) * part] = wide[i, :, lo : lo + part].astype(bf16)

    half = cn // 2
    sources = [swap.receive(0)]
    ring.start(sources[0])
    lay(0, gate)
    for s in range(1, half):
        sources.append(swap.receive(s))
        ring.start(sources[s])
    gather.forward(1, 1)
    lay(1, up)
    for s in range(half, cn):
        sources.append(swap.receive(s))
        ring.start(sources[s])
    down_ring.forward()
    gather.forward(2, 2)
    for source in sources:
        ring.forward(source)
    gather.forward(3)
    keep.wait()
    keep_down.wait()
    gather.finish()
    for source in sources:
        ring.finish(source)
    swap.sent()
    down_ring.finish()


def prepare(w, x_all, gains, info_rows, hw, block):
    width = w.shape[0]
    per = block // x_all.shape[1]

    @pl.loop(0, width // block)
    def _(i):
        at = pl.ds(pl.multiple_of(i * block, block), block)
        gains[:, at] = w[at, 3 * hw : 3 * hw + 128].astype(f32).T[0:8]

    @pl.loop(0, info_rows.shape[1] // block)
    def _(i):
        at = pl.ds(pl.multiple_of(i * block, block), block)
        codes = x_all[pl.ds(i * per, per), :, width:].reshape(block, 128).astype(f32).T[0:8]
        seg = jnp.floor(codes * 0.5)
        code = jnp.where(codes - 2.0 * seg == 1.0, seg, -1.0)
        first = lax.broadcasted_iota(jnp.int32, (8, block), 0) == 0
        info_rows[:, at] = jnp.where(first, seg, code)


def tables(x_all, inverse, info_rows, info_cols, cosines, sines, width, i, block):
    per = block // x_all.shape[1]
    at = pl.ds(pl.multiple_of(i * block, block), block)
    codes = x_all[pl.ds(i * per, per), :, width:].reshape(block, 128).astype(f32)
    seg = jnp.floor(codes * 0.5)
    valid = codes - 2.0 * seg
    lane = lax.broadcasted_iota(jnp.int32, (block, 128), 1)
    code = jnp.where(valid == 1.0, seg, -1.0)
    info_cols[at, :] = jnp.where(lane == 0, seg, jnp.where(lane == 1, valid, code))
    before = jnp.where(info_rows[0:1, :] < seg[:, 0:1], 1.0, 0.0)
    index = lax.broadcasted_iota(jnp.int32, (block, 128), 0) + i * block
    place_in = index.astype(f32) - jnp.sum(before, axis=1, keepdims=True)
    angles = place_in * inverse[...]
    cosines[at, :] = jnp.cos(angles)
    sines[at, :] = jnp.where(lane < HEAD_DIM // 2, -1.0, 1.0) * jnp.sin(angles)


def project(x_all, w, gain, inverse, rows_in, cols, cosines, sines, an, qkv, hw, block, hook):
    width = an.shape[1]
    per = block // x_all.shape[1]

    @pl.loop(0, an.shape[0] // block)
    def _(i):
        at = pl.ds(pl.multiple_of(i * block, block), block)
        tables(x_all, inverse, rows_in, cols, cosines, sines, width, i, block)
        x = x_all[pl.ds(i * per, per), :, 0:width].reshape(block, width).astype(f32)
        normed = (x * rms(x) * gain[...]).astype(bf16)
        an[at, :] = normed
        proj = dot(normed, w[:, 0 : 3 * hw])
        cos_b, sin_b = cosines[at, :], sines[at, :]
        for h in range(2 * hw // HEAD_DIM):
            lanes = slice(h * HEAD_DIM, (h + 1) * HEAD_DIM)
            v = proj[:, lanes]
            turned = v * cos_b + pltpu.roll(v, HEAD_DIM // 2, 1) * sin_b
            qkv[at, lanes] = turned.astype(bf16)
        qkv[at, 2 * hw :] = proj[:, 2 * hw :].astype(bf16)
        hook(i)


def mask_block(q_seg, k_code, i, j, block):
    rows = lax.broadcasted_iota(jnp.int32, (block, block), 0) + i * block
    cols = lax.broadcasted_iota(jnp.int32, (block, block), 1) + j * block
    return (q_seg == k_code) & (cols <= rows)


def attend(qkv, q_info, k_code, out, mass, hw, block, hook):
    mass[...] = jnp.zeros_like(mass)

    @pl.loop(0, qkv.shape[0] // block)
    def _(i):
        at = pl.ds(pl.multiple_of(i * block, block), block)
        q_seg, q_valid = q_info[at, 0:1], q_info[at, 1:2]
        for h in range(hw // HEAD_DIM):
            lane = [slice(t * hw + h * HEAD_DIM, t * hw + (h + 1) * HEAD_DIM) for t in range(3)]
            q = qkv[at, lane[0]]

            def step(j, acc):
                to = pl.ds(pl.multiple_of(j * block, block), block)
                s = dot(q, qkv[to, lane[1]], contract_cols) * score_scale - score_shift
                allowed = mask_block(q_seg, k_code[1:2, to], i, j, block)
                p = jnp.where(allowed, jax.nn.sigmoid(s), 0.0)
                mass[...] += jnp.sum(p * q_valid, axis=0, keepdims=True)
                return acc + dot(p.astype(bf16), qkv[to, lane[2]])

            acc = lax.fori_loop(0, i + 1, step, jnp.zeros((block, HEAD_DIM), f32))
            out[at, lane[0]] = acc.astype(bf16)
        hook(i)


def attn_kernel(
    cn, dpn, x_all, w, inverse, gate, up, wo,
    an, qkv, o, mass, gains, cosines, sines, cols, rows_in,
    gate_all, up_own, wo_all, ssem, rsem, wsem, local,
):
    c, d = lax.axis_index("ctx"), lax.axis_index("dp")
    wo_rows = RowGather(cn, dpn, wo, wo_all, wsem, local.at[2])
    rows = x_all.shape[1]
    hw = qkv.shape[1] // 3
    swap_gate = Swap(cn, gate, gate_all.at[d], ssem.at[0], local.at[0])
    swap_up = Swap(cn, up, up_own, ssem.at[1], local.at[1])
    ring = RingPieces(dpn, gate_all, rsem)
    sources = [lax.rem(c - s + cn, cn) for s in range(cn)]
    greet_ctx(cn)
    ring.greet()

    wo_rows.greet_owners()
    pl.semaphore_wait(pltpu.get_barrier_semaphore(), cn - 1 + 2 + wo_rows.links)
    wo_rows.start()
    swap_gate.start()

    def in_project(i):
        @pl.when(i == 1)
        def _():
            for s in range(cn // 2):
                ring.start(swap_gate.receive(s))

        @pl.when(i == 2)
        def _():
            for s in range(cn // 2, cn):
                ring.start(swap_gate.receive(s))
            swap_up.start()

    def in_attend(i):
        @pl.when(i == 2)
        def _():
            for source in sources[: cn // 2]:
                ring.forward(source)

    prepare(w, x_all, gains, rows_in, hw, 2 * rows)
    project(
        x_all, w, gains.at[0:1], inverse, rows_in, cols, cosines, sines, an, qkv, hw, 2 * rows,
        in_project,
    )
    attend(qkv, cols, rows_in, o, mass, hw, 2 * rows, in_attend)
    for source in sources[cn // 2 :]:
        ring.forward(source)
    swap_up.finish()
    wo_rows.finish()
    for source in sources:
        ring.finish(source)
    swap_gate.sent()


def middle_kernel(
    cn, dpn, o, wo, x, gain, dy, up, gate_all, down_half, down_rest,
    h1, bn_all, up_all, hid, dgu, dys_all, down_all,
    own, bn, dys, wg, wu, down_by, gsem, ysem, rsem, dsem, local, *sum_refs,
):
    c, d = lax.axis_index("ctx"), lax.axis_index("dp")
    _, j, k, n, _ = place(cn)
    rows, width = x.shape
    ff = hid.shape[1]
    block = 2 * rows
    gather = LineGather(cn, own, bn, gsem)
    gather_dy = LineGather(cn, dy, dys, ysem)
    ring = RingGather(dpn, up, up_all, rsem)
    split = down_rest.shape[0]
    rest_ring = RingGather(dpn, down_rest, down_by.at[:, pl.ds(split, split)], dsem)
    keep_rest = pltpu.make_async_copy(
        down_rest, down_by.at[d, pl.ds(split, split)], local.at[5]
    )
    total = LineSum(cn, product(o, wo, plain, rows, width), *sum_refs)
    greet_line(cn, ring)
    ring.start()
    rest_ring.start()
    keep_rest.start()
    keep_up = pltpu.make_async_copy(up, up_all.at[d], local.at[0])
    loads = [
        pltpu.make_async_copy(src, dst, local.at[i])
        for i, (src, dst) in enumerate(((gate_all, wg), (down_half, down_by.at[:, pl.ds(0, split)])), 2)
    ]
    keep_up.start()
    for load in loads:
        load.start()
    gather_dy.start()
    dys[c] = dy[...]

    def between(s):
        gather_dy.step(s + 1)

        @pl.when(s == n - 2)
        def _():
            ring.forward()
            rest_ring.forward()

    line_sums(cn, [total], between)

    def norm(r):
        mid = x[r, :].astype(f32) + total.part[0, k, r, :]
        h1[r, :] = mid
        own[r, :] = (mid * rms(mid) * gain[1:2, :]).astype(bf16)

    by_rows(rows, norm)
    gather.start()
    bn[c] = own[...]
    gather_dy.finish()
    store_dy = pltpu.make_async_copy(dys, dys_all, local.at[4])
    store_dy.start()
    total.drain()
    keep_up.wait()
    for load in loads:
        load.wait()
    rest_ring.finish()
    keep_rest.wait()
    store_down = pltpu.make_async_copy(down_by, down_all, local.at[6])
    store_down.start()
    ring.finish()
    load_up = pltpu.make_async_copy(up_all, wu, local.at[0])
    load_up.start()
    load_up.wait()
    wgate, wup, down = wg, wu.reshape(width, ff), down_by.reshape(ff, width)
    tile = min(512, ff)

    def feed(t):
        gather.other(t)
        at = pl.ds(pl.multiple_of(t * block, block), block)
        pair = pl.ds(t * 2, 2)
        send = pltpu.make_async_copy(bn.at[pair], bn_all.at[pair], local.at[1])
        send.start()
        a = bn[pair].reshape(block, width)
        g_out = dys[pair].reshape(block, width)

        @pl.loop(0, ff // tile)
        def _(i):
            to = pl.ds(pl.multiple_of(i * tile, tile), tile)
            gate = dot(a, wgate[:, to])
            up_v = dot(a, wup[:, to])
            dhid = dot(g_out, down[to, :], contract_cols)
            sig = jax.nn.sigmoid(gate)
            silu = gate * sig
            hid[at, to] = (silu * up_v).astype(bf16)
            dgate = dhid * up_v * sig * (1.0 + gate * (1.0 - sig))
            dgu[at, to] = dgate.astype(bf16)
            dgu[at, pl.ds(pl.multiple_of(ff + i * tile, tile), tile)] = (dhid * silu).astype(bf16)

        send.wait()

    feed(j)
    gather.step(1)

    @pl.loop(1, n)
    def _(s):
        both = (j - s >= 0) & (j + s <= n - 1)

        @pl.when(j - s >= 0)
        def _():
            feed(j - s)

        @pl.when(both & (s < n - 1))
        def _():
            gather.step(s + 1)

        @pl.when(j + s <= n - 1)
        def _():
            feed(j + s)

        @pl.when(jnp.logical_not(both) & (s < n - 1))
        def _():
            gather.step(s + 1)

    gather.sent()
    store_dy.wait()
    store_down.wait()


def back_kernel(
    cn, dpn, bn_in, dgu_in, hid, down, wg, wu, h1, dy, gain, dh1, dob_all, term, g_own, result,
    own, bn, dgu, cross_in, arrived, bsem, gsem, loads, keep_sem, *scratch,
):
    sum_refs, ring_refs = scratch[:-4], scratch[-4:]
    rows, width = dy.shape
    ff = wg.shape[1]
    tile = min(512, width)
    c, _, k, n, _ = place(cn)

    def compute(t, out):
        at = pl.ds(pl.multiple_of(t * 2 * rows, 2 * rows), 2 * rows)

        @pl.loop(0, width // tile)
        def _(i):
            to = pl.ds(pl.multiple_of(i * tile, tile), tile)
            part = dot(dgu[at, 0:ff], wg[to, :], contract_cols)
            part = part + dot(dgu[at, ff:], wu[to, :], contract_cols)
            out[:, :, to] = part.reshape(2, rows, tile)

    total = LineSum(cn, compute, *sum_refs)
    ring = RingSum(dpn, *ring_refs)
    blocks = ring_refs[0]
    m = blocks.shape[1]
    load_dgu = pltpu.make_async_copy(dgu_in, dgu, loads.at[0])
    load_bn = pltpu.make_async_copy(bn_in, bn, loads.at[1])
    load_dgu.start()
    load_bn.start()
    greet_line(cn, ring.ring)
    order = ring.order()
    load_dgu.wait()

    def weight_grad(member):
        outer(bn, dgu, blocks.at[member], pl.ds(pl.multiple_of(member * m, m), m))


    def between(s):
        @pl.when(s == 0)
        def _():
            load_bn.wait()
            weight_grad(order[0])
            ring.start()

        for i in range(ring.hops - 1):

            @pl.when(s == min(i, n - 2))
            def _():
                weight_grad(order[1 + 2 * i])
                weight_grad(order[2 + 2 * i])

            @pl.when(s == min(i + 2, n - 2))
            def _():
                ring.forward(i + 1)

        @pl.when(s == n - 2)
        def _():
            weight_grad(order[-1])

    line_sums(cn, [total], between)
    load_hid = pltpu.make_async_copy(hid, dgu.at[:, 0:ff], loads.at[0])
    load_down = pltpu.make_async_copy(down, bn.at[0:ff], loads.at[1])
    load_hid.start()
    load_down.start()
    term[...] = jnp.zeros_like(term)

    def norm_back(r):
        dbn = total.part[0, k, r, :]
        mid = h1[r, :]
        r2 = rms(mid)
        xh2 = mid * r2
        term[...] += jnp.sum(dbn * xh2, axis=0, keepdims=True)
        u2 = dbn * gain[1:2, :]
        mean = jnp.mean(u2 * xh2, axis=-1, keepdims=True)
        grad = dy[r, :].astype(f32) + r2 * (u2 - xh2 * mean)
        dh1[r, :] = grad
        own[r, :] = grad.astype(bf16)

    by_rows(rows, norm_back)
    gather = LineGather(cn, own, dob_all, gsem)
    gather.start()
    keep = pltpu.make_async_copy(own, dob_all.at[c], keep_sem)
    keep.start()
    total.drain()

    part, cross, _, flow, _, _ = sum_refs
    second = LineSum(
        cn,
        product(dgu.at[:, 0:ff], bn.at[0:ff], plain, rows, width),
        part, cross, cross_in, flow, arrived, bsem,
    )
    load_hid.wait()
    load_down.wait()

    def pass_on(s):
        gather.step(s + 1)

    line_sums(cn, [second], pass_on)

    def close(r):
        result[r, :] = (h1[r, :] + second.part[0, k, r, :]).astype(bf16)

    by_rows(rows, close)
    second.drain()
    keep.wait()
    gather.finish()
    ring.finish(g_own)


def attend_back(qkv, do, cosines, sines, q_info, k_info, dq, dqkv, hw, block):
    count = qkv.shape[0] // block
    dq[...] = jnp.zeros_like(dq)

    def turn_back(g, at):
        return g * cosines[at, :] - pltpu.roll(g, HEAD_DIM // 2, 1) * sines[at, :]

    @pl.loop(0, count)
    def _(j):
        to = pl.ds(pl.multiple_of(j * block, block), block)
        k_code = k_info[to, 2:3]
        for h in range(hw // HEAD_DIM):
            lane = [slice(t * hw + h * HEAD_DIM, t * hw + (h + 1) * HEAD_DIM) for t in range(3)]
            k, v = qkv[to, lane[1]], qkv[to, lane[2]]

            def step(i, carry):
                dk, dv = carry
                at = pl.ds(pl.multiple_of(i * block, block), block)
                q, do_i = qkv[at, lane[0]], do[at, lane[0]]
                s = dot(k, q, contract_cols) * score_scale - score_shift
                keys = lax.broadcasted_iota(jnp.int32, (block, block), 0) + j * block
                queries = lax.broadcasted_iota(jnp.int32, (block, block), 1) + i * block
                allowed = (k_code == q_info[0:1, at]) & (keys <= queries)
                sg = jnp.where(allowed, jax.nn.sigmoid(s), 0.0)
                dp = dot(v, do_i, contract_cols)
                ds = (dp * sg * (1.0 - sg)).astype(bf16)
                dq[at, lane[0]] += dot(ds, k, contract_rows)
                return dk + dot(ds, q), dv + dot(sg.astype(bf16), do_i)

            zero = jnp.zeros((block, HEAD_DIM), f32)
            dk, dv = lax.fori_loop(j, count, step, (zero, zero))
            dqkv[to, lane[1]] = turn_back(dk * score_scale, to).astype(bf16)
            dqkv[to, lane[2]] = dv.astype(bf16)

    @pl.loop(0, count)
    def _(i):
        at = pl.ds(pl.multiple_of(i * block, block), block)
        for h in range(hw // HEAD_DIM):
            lanes = slice(h * HEAD_DIM, (h + 1) * HEAD_DIM)
            dqkv[at, lanes] = turn_back(dq[at, lanes] * score_scale, at).astype(bf16)


def last_kernel(
    cn, dpn, g_gu, dob_all, dys_all, hid, o, wo, qkv, cosines, sines, q_info, k_info, an, w,
    dh1, x, gain, term_two, mass, grad_in, tot_out, gu_all, down_own, out_all, qkv_all,
    do, dq, dqkv, out_parts, out_got, qkv_own, tot, tot_in, tot_sum, tot_last,
    usem, qsem, tsem, psem, osem, local, *scratch,
):
    sum_refs, rings = scratch[:-8], (scratch[-8:-4], scratch[-4:])
    rows, width = x.shape
    hw = width // cn
    _, _, k, n, _ = place(cn)
    down_ring, qkv_ring = (RingSum(dpn, *refs) for refs in rings)
    rows_out = RowSum(cn, dpn, out_parts, out_got, osem)
    swap_gu = Swap(cn, g_gu, gu_all, usem, local.at[0])
    swap_qkv = Swap(cn, qkv_own, qkv_all, qsem, local.at[4])
    totals = Swap(cn, None, tot_in, tsem, local.at[3], lambda i: tot)
    c, d = lax.axis_index("ctx"), lax.axis_index("dp")
    def share(s):
        return remote(
            tot_sum, tot_last.at[d], psem.at[0, s], psem.at[1, s], {"dp": lax.rem(d + s, dpn)}
        )

    greet_ctx(cn)
    for s in range(1, dpn):
        greet({"dp": lax.rem(d + s, dpn)})

    rows_out.greet_homes()
    pl.semaphore_wait(
        pltpu.get_barrier_semaphore(), cn - 1 + dpn - 1 + rows_out.links
    )
    swap_gu.start()
    seq = an.shape[0]
    stage = (sum_refs[1], sum_refs[3])
    halves = (slice(0, seq // 2), slice(seq // 2, seq))

    def fill(src):
        copies = [
            pltpu.make_async_copy(src.at[pl.ds(i * n, n)], stage[i], local.at[1 + i])
            for i in range(2)
        ]
        for copy in copies:
            copy.start()
        for copy in copies:
            copy.wait()

    def staged(i, to=slice(None)):
        return stage[i][:, :, to].reshape(seq // 2, -1)

    fill(dob_all)
    outer_all(o, staged, halves, out_parts)
    rows_out.start()
    for i in range(2):
        do[halves[i], :] = dot(staged(i), wo[...], contract_cols).astype(bf16)
    fill(dys_all)
    outer_all(hid, staged, halves, rings[0][0])
    down_ring.start()
    m_qkv = rings[1][0].shape[1]
    order = qkv_ring.order()

    def grad_qkv(member):
        outer(an, dqkv, rings[1][0].at[member], pl.ds(pl.multiple_of(member * m_qkv, m_qkv), m_qkv))

    attend_back(qkv, do, cosines, sines, q_info, k_info, dq, dqkv, hw, 2 * rows)
    grad_qkv(order[0])
    qkv_ring.start()
    total = LineSum(cn, product(dqkv, w, contract_cols, rows, width), *sum_refs)

    def between(s):
        for i in range(qkv_ring.hops - 1):

            @pl.when(s == min(i, n - 2))
            def _():
                grad_qkv(order[1 + 2 * i])
                grad_qkv(order[2 + 2 * i])
                qkv_ring.forward(i + 1)

            @pl.when(s == min(i + 1, n - 2))
            def _():
                down_ring.forward(i + 1)

        @pl.when(s == n - 2)
        def _():
            grad_qkv(order[-1])
            qkv_ring.finish(qkv_own)
            swap_qkv.start()

    line_sums(cn, [total], between)
    tot[0] = jnp.zeros((1, width), f32)

    def norm_back(r):
        dan = total.part[0, k, r, :]
        xf = x[r, :].astype(f32)
        r1 = rms(xf)
        xh1 = xf * r1
        tot[0] += jnp.sum(dan * xh1, axis=0, keepdims=True)
        u1 = dan * gain[0:1, :]
        mean = jnp.mean(u1 * xh1, axis=-1, keepdims=True)
        grad = dh1[r, :] + r1 * (u1 - xh1 * mean)
        grad_in[r, :] = grad.astype(bf16)

    by_rows(rows, norm_back)
    tot[1] = term_two[...]
    tot[2] = jnp.broadcast_to(jnp.sum(mass[...], axis=1, keepdims=True), (1, width))
    totals.start()
    rows_out.finish(out_all)
    totals.finish()
    tot_sum[...] = jnp.sum(tot_in[...], axis=0)
    for s in range(1, dpn):
        share(s).start()
    down_ring.finish(down_own)
    total.drain()
    swap_gu.finish()
    tot_last[d] = tot_sum[...]
    for s in range(1, dpn):
        source = lax.rem(d - s + dpn, dpn)
        block = tot_last.at[source]
        remote(block, block, psem.at[0, s], psem.at[1, s], {"dp": source}).wait_recv()
    for s in range(1, dpn):
        share(s).wait_send()
    tot_out[...] = jnp.sum(tot_last[...], axis=0)
    swap_qkv.finish()


def spread_kernel(
    cn, dpn, qkv_in, gu_in, down_in, out_in, gq, gk, gv, go, gg, gu_out, gd, qkv, gu, down, out, sem
):
    hw = qkv.shape[2] // 3
    ff_rows = gd.shape[0]
    ff = ff_rows * dpn
    pairs = ((down_in, down), (out_in, out), (qkv_in, qkv), (gu_in, gu))
    loads = [pltpu.make_async_copy(a, b, sem.at[i]) for i, (a, b) in enumerate(pairs)]
    for load in loads:
        load.start()
    for load in loads[:3]:
        load.wait()
    gd[...] = down[...].astype(f32)
    go[...] = out[...]
    for c in range(cn):
        for i, ref in enumerate((gq, gk, gv)):
            for t in range(hw // HEAD_DIM):
                lo, at = head_of(cn, hw // HEAD_DIM, c, t) * HEAD_DIM, i * hw + t * HEAD_DIM
                ref[:, lo : lo + HEAD_DIM] = qkv[c, :, at : at + HEAD_DIM].astype(f32)
    loads[3].wait()
    for c in range(cn):
        for i, ref in enumerate((gg, gu_out)):
            for d in range(dpn):
                to = (d * cn + c) * ff_rows
                lo = i * ff + d * ff_rows
                ref[:, to : to + ff_rows] = gu[c, :, lo : lo + ff_rows].astype(f32)


def call(kernel, outs, ins, specs_in, specs_out, scratch, number, flops=0, moved=0):
    return pl.pallas_call(
        kernel,
        out_shape=outs,
        in_specs=specs_in,
        out_specs=specs_out,
        scratch_shapes=scratch,
        compiler_params=pltpu.CompilerParams(
            collective_id=number, has_side_effects=True, vmem_limit_bytes=61 * 2**20
        ),
        cost_estimate=pl.CostEstimate(flops=flops, bytes_accessed=moved, transcendentals=0),
    )(*ins)


def shape(dims, dtype=bf16):
    return jax.ShapeDtypeStruct(dims, dtype)


def shards(
    hidden_in,
    out_grad,
    seg_ids,
    valid_mask,
    w_query,
    w_key,
    w_value,
    w_output,
    w_gate,
    w_up,
    w_down,
    gain_attn,
    gain_mlp,
):
    dpn = lax.axis_size("dp")
    cn = lax.axis_size("ctx")
    n = cn // 2
    x_local = hidden_in[0]
    dy_local = out_grad[0]
    rows, width = x_local.shape
    seq = rows * cn
    dr = w_query.shape[0]
    hw = width // cn
    heads = hw // HEAD_DIM
    ff_rows = w_down.shape[0]
    ff = ff_rows * dpn
    dma = pltpu.SemaphoreType.DMA
    mib = 2**20

    gain_rows = jnp.pad(jnp.stack([gain_attn, gain_mlp]), ((0, 0), (0, 128 - dr)))
    pw = 3 * hw + 128
    ring_sem = dma((4, dpn // 2 + 1))
    x_all, w_qkv, gate_pack, up_pack, down_half, wo_low, down_rest = call(
        functools.partial(front_kernel, cn, dpn),
        (
            shape((cn, rows, width + 128)),
            shape((dpn, cn, dr, pw)),
            shape((cn, dr, ff)),
            shape((cn, dr, ff)),
            shape((dpn, ff_rows // 2, width)),
            shape((dr, width)),
            shape((ff_rows // 2, width)),
        ),
        (
            x_local, seg_ids, valid_mask, gain_rows, w_query, w_key, w_value, w_output,
            w_gate, w_up, w_down,
        ),
        [ANY] + [VMEM] * 7 + [ANY] * 3,
        (ANY, ANY, VMEM, VMEM, ANY, VMEM, VMEM),
        [
            pltpu.VMEM((rows, width + 128), bf16),
            pltpu.VMEM((cn, dr, pw), bf16),
            pltpu.VMEM((2, dr, ff * cn), f32),
            pltpu.VMEM((ff_rows, width), f32),
            pltpu.VMEM((ff_rows // 2, width), bf16),
            dma((5, n)),
            dma((2, cn)),
            dma((4, dpn // 2 + 1, cn)),
            ring_sem,
            dma((6,)),
        ],
        1,
        moved=160 * mib,
    )
    w_qkv = w_qkv.reshape(width, pw)
    inverse = jnp.exp(
        jnp.arange(HEAD_DIM // 2, dtype=f32) * (-2.0 * math.log(rope_base) / HEAD_DIM)
    )
    inverse = jnp.concatenate([inverse, inverse])[None]

    line_scratch = sum_scratch(cn, rows, width)
    an, proj, o, mass, gains, cosines, sines, cols, infos, w_gate_c, up_own, wo = call(
        functools.partial(attn_kernel, cn, dpn),
        (
            shape((seq, width)),
            shape((seq, 3 * hw)),
            shape((seq, hw)),
            shape((1, 2 * rows), f32),
            shape((8, width), f32),
            shape((seq, HEAD_DIM), f32),
            shape((seq, HEAD_DIM), f32),
            shape((seq, 128), f32),
            shape((8, seq), f32),
            shape((dpn, cn, dr, ff)),
            shape((cn, dr, ff)),
            shape((dpn, dr, width)),
        ),
        (x_all, w_qkv, inverse, gate_pack, up_pack, wo_low),
        [VMEM] * 3 + [ANY] * 3,
        (VMEM,) * 9 + (ANY,) * 3,
        [dma((2, 2, cn)), dma((4, dpn // 2 + 1, cn)), dma((2, dpn)), dma((3,))],
        2,
        moved=160 * mib,
    )
    h1, bn, w_up_c, hid, dgu, dys, down = call(
        functools.partial(middle_kernel, cn, dpn),
        (
            shape((rows, width), f32),
            shape((cn, rows, width)),
            shape((dpn, cn, dr, ff)),
            shape((seq, ff)),
            shape((seq, 2 * ff)),
            shape((cn, rows, width)),
            shape((dpn, ff_rows, width)),
        ),
        (
            o, wo.reshape(hw, width), x_local, gains, dy_local, up_own,
            w_gate_c.reshape(width, ff), down_half, down_rest,
        ),
        [VMEM] * 5 + [ANY] * 4,
        (VMEM, ANY, ANY, VMEM, VMEM, ANY, ANY),
        [
            pltpu.VMEM((rows, width), bf16),
            pltpu.VMEM((cn, rows, width), bf16),
            pltpu.VMEM((cn, rows, width), bf16),
            pltpu.VMEM((width, ff), bf16),
            pltpu.VMEM((dpn, cn, dr, ff), bf16),
            pltpu.VMEM((dpn, ff_rows, width), bf16),
            dma((5, n)),
            dma((5, n)),
            ring_sem,
            ring_sem,
            dma((7,)),
        ]
        + line_scratch,
        3,
        moved=160 * mib,
    )
    wo = wo.reshape(hw, width)
    w_gate_c = w_gate_c.reshape(width, ff)
    w_up_c = w_up_c.reshape(width, ff)
    bn = bn.reshape(seq, width)
    dh1, dob, term_two, g_gu, result = call(
        functools.partial(back_kernel, cn, dpn),
        (
            shape((rows, width), f32),
            shape((cn, rows, width)),
            shape((1, width), f32),
            shape((cn, dr, 2 * ff)),
            shape((rows, width)),
        ),
        (bn, dgu, hid, down.reshape(ff, width), w_gate_c, w_up_c, h1, dy_local, gains),
        [ANY] * 4 + [VMEM] * 5,
        (VMEM, ANY, VMEM, VMEM, VMEM),
        [
            pltpu.VMEM((rows, width), bf16),
            pltpu.VMEM((seq, width), bf16),
            pltpu.VMEM((seq, 2 * ff), bf16),
            pltpu.VMEM((n, rows, width), bf16),
            pltpu.VMEM((n + 1, rows, width), bf16),
            dma((4, n + 1)),
            dma((5, n)),
            dma((2,)),
            dma,
        ]
        + line_scratch
        + ring_scratch(dpn, cn * dr, 2 * ff),
        4,
        moved=160 * mib,
    )
    grad_input, totals, gu_back, g_down, g_out, q_all = call(
        functools.partial(last_kernel, cn, dpn),
        (
            shape((rows, width)),
            shape((3, 1, width), f32),
            shape((cn, dr, 2 * ff)),
            shape((ff_rows, width)),
            shape((dr, width), f32),
            shape((cn, dr, 3 * hw)),
        ),
        (
            g_gu, dob, dys, hid, o, wo, proj, cosines, sines, infos, cols, an, w_qkv,
            dh1, x_local, gains, term_two, mass,
        ),
        [ANY] * 3 + [VMEM] * 15,
        (VMEM, VMEM, ANY, VMEM, VMEM, ANY),
        [
            pltpu.VMEM((seq, hw), bf16),
            pltpu.VMEM((seq, hw), f32),
            pltpu.VMEM((seq, 3 * hw), bf16),
            pltpu.VMEM((dpn, dr, width), bf16),
            pltpu.VMEM((dpn, dr, width), bf16),
            pltpu.VMEM((cn, dr, 3 * hw), bf16),
            pltpu.VMEM((3, 1, width), f32),
            pltpu.VMEM((cn, 3, 1, width), f32),
            pltpu.VMEM((3, 1, width), f32),
            pltpu.VMEM((dpn, 3, 1, width), f32),
            dma((2, cn)),
            dma((2, cn)),
            dma((2, cn)),
            dma((2, dpn)),
            dma((2, dpn)),
            dma((5,)),
        ]
        + line_scratch
        + ring_scratch(dpn, ff_rows, width)
        + ring_scratch(dpn, cn * dr, 3 * hw),
        5,
        moved=160 * mib,
    )

    g_q, g_k, g_v, g_o, g_gate, g_up, g_down = pl.pallas_call(
        functools.partial(spread_kernel, cn, dpn),
        out_shape=tuple(shape((dr, width), f32) for _ in range(4))
        + tuple(shape((dr, ff * cn), f32) for _ in range(2))
        + (shape((ff_rows, width), f32),),
        in_specs=[ANY] * 4,
        out_specs=(VMEM,) * 7,
        scratch_shapes=[
            pltpu.VMEM((cn, dr, 3 * hw), bf16),
            pltpu.VMEM((cn, dr, 2 * ff), bf16),
            pltpu.VMEM((ff_rows, width), bf16),
            pltpu.VMEM((dr, width), f32),
            dma((4,)),
        ],
        compiler_params=pltpu.CompilerParams(vmem_limit_bytes=61 * 2**20),
    )(q_all, gu_back, g_down, g_out)
    mass_mean = totals[2, 0, 0] / (heads * cn * dpn * seq)
    owner = (lax.axis_index("dp") * cn + lax.axis_index("ctx")) * dr
    grad_gains = [lax.dynamic_slice_in_dim(totals[i, 0], owner, dr) for i in range(2)]
    return (
        result[None],
        grad_input[None],
        g_q,
        g_k,
        g_v,
        g_o,
        g_gate,
        g_up,
        g_down,
        grad_gains[0],
        grad_gains[1],
        mass_mean,
    )


def solution(mesh):
    tok = P("dp", "ctx", None)
    ids = P("dp", "ctx")
    mat = P(("dp", "ctx"), None)
    vec = P(("dp", "ctx"))
    return jax.shard_map(
        shards,
        mesh=mesh,
        in_specs=(tok, tok, ids, ids) + (mat,) * 7 + (vec, vec),
        out_specs=(tok, tok) + (mat,) * 7 + (vec, vec, P()),
        check_vma=False,
    )
```

```python
import functools
import math

import jax
import jax.numpy as jnp
from jax import lax
from jax.experimental import pallas as pl
from jax.experimental.pallas import tpu as pltpu
from jax.sharding import PartitionSpec as P

HEAD_DIM = 128
norm_eps = 1e-05
rope_base = 10000.0
score_shift = math.log(4096.0)
score_scale = 1.0 / math.sqrt(HEAD_DIM)
contract_rows = (((0,), (0,)), ((), ()))
contract_cols = (((1,), (1,)), ((), ()))
plain = (((1,), (0,)), ((), ()))
f32 = jnp.float32
bf16 = jnp.bfloat16
MESH = pl.DeviceIdType.MESH
ANY = pl.BlockSpec(memory_space=pl.ANY)
VMEM = pl.BlockSpec(memory_space=pltpu.VMEM)


def dot(a, b, dims=plain):
    return lax.dot_general(a, b, dims, preferred_element_type=f32)


def remote(src, dst, send, recv, target):
    return pltpu.make_async_remote_copy(
        src_ref=src,
        dst_ref=dst,
        send_sem=send,
        recv_sem=recv,
        device_id=target,
        device_id_type=MESH,
    )


def greet(target):
    pl.semaphore_signal(
        pltpu.get_barrier_semaphore(), inc=1, device_id=target, device_id_type=MESH
    )


def by_rows(count, work, step=16, start=0):
    @pl.loop(0, count // step)
    def _(i):
        work(pl.ds(pl.multiple_of(start + i * step, step), step))


def place(cn):
    c = lax.axis_index("ctx")
    j, k = c // 2, c % 2
    return c, j, k, cn // 2, 2 * j + 1 - k


def greet_line(cn, ring):
    c, j, _, n, sib = place(cn)
    ring.greet()
    greet({"ctx": sib})

    @pl.when(j < n - 1)
    def _():
        greet({"ctx": c + 2})

    @pl.when(j > 0)
    def _():
        greet({"ctx": c - 2})

    inner = jnp.where(j > 0, 1, 0) + jnp.where(j < n - 1, 1, 0)
    pl.semaphore_wait(pltpu.get_barrier_semaphore(), 3 + inner)


def greet_ctx(cn):
    c = lax.axis_index("ctx")
    for s in range(1, cn):
        greet({"ctx": lax.rem(c + s, cn)})


class LineGather:
    def __init__(self, cn, own, full, sem):
        self.cn, self.own, self.full, self.sem = cn, own, full, sem

    def copy(self, src, origin, kind, target):
        _, _, k, _, _ = place(self.cn)
        sem = self.sem
        return remote(
            src,
            self.full.at[2 * origin + k],
            sem.at[kind, origin],
            sem.at[3 if kind < 2 else 4, origin],
            {"ctx": target},
        )

    def start(self):
        c, j, _, n, sib = place(self.cn)

        @pl.when(j < n - 1)
        def _():
            self.copy(self.own, j, 0, c + 2).start()

        @pl.when(j > 0)
        def _():
            self.copy(self.own, j, 1, c - 2).start()

        self.copy(self.own, j, 2, sib).start()

    def step(self, s):
        c, j, k, n, sib = place(self.cn)

        @pl.when(j - s >= 0)
        def _():
            o = j - s
            block = self.full.at[2 * o + k]
            self.copy(block, o, 0, sib).wait_recv()

            @pl.when(j < n - 1)
            def _():
                self.copy(block, o, 0, c + 2).start()

            self.copy(block, o, 2, sib).start()

        @pl.when(j + s <= n - 1)
        def _():
            o = j + s
            block = self.full.at[2 * o + k]
            self.copy(block, o, 1, sib).wait_recv()

            @pl.when(j > 0)
            def _():
                self.copy(block, o, 1, c - 2).start()

            self.copy(block, o, 2, sib).start()

    def forward(self, first=1, last=None):
        for s in range(first, self.cn // 2 if last is None else last + 1):
            self.step(s)

    def other(self, o):
        _, _, k, _, sib = place(self.cn)
        block = self.full.at[2 * o + 1 - k]
        remote(
            block, block, self.sem.at[2, o], self.sem.at[4, o], {"ctx": sib}
        ).wait_recv()

    def sent(self):
        c, j, k, n, sib = place(self.cn)
        for o in range(n):
            block = self.full.at[2 * o + k]

            @pl.when((j < n - 1) & (o <= j))
            def _():
                self.copy(block, o, 0, sib).wait_send()

            @pl.when((j > 0) & (o >= j))
            def _():
                self.copy(block, o, 1, sib).wait_send()

            self.copy(block, o, 2, sib).wait_send()

    def finish(self):
        for o in range(self.cn // 2):
            self.other(o)
        self.sent()


class PairGather:
    def __init__(self, cn, own, full, sem):
        self.cn, half = cn, own.shape[0] // 2
        self.parts = []
        for i in range(2):
            at = pl.ds(i * half, half)
            self.parts.append(LineGather(cn, own.at[at], full.at[:, at], sem.at[i]))

    def start(self):
        for part in self.parts:
            part.start()

    def step(self, s):
        for part in self.parts:
            part.step(s)

    def forward(self, first=1, last=None):
        for s in range(first, self.cn // 2 if last is None else last + 1):
            self.step(s)

    def other(self, o):
        for part in self.parts:
            part.other(o)

    def sent(self):
        for part in self.parts:
            part.sent()

    def finish(self):
        for part in self.parts:
            part.finish()


class Swap:
    def __init__(self, cn, src, dst, sem, local, pick=None):
        self.cn, self.sem, self.local = cn, sem, local
        self.src = pick or (lambda c: src.at[c])
        self.dst = dst if callable(dst) else lambda c: dst.at[c]

    def copy(self, s):
        c = lax.axis_index("ctx")
        peer = lax.rem(c + s, self.cn)
        return remote(
            self.src(peer),
            self.dst(c),
            self.sem.at[0, s],
            self.sem.at[1, s],
            {"ctx": peer},
        )

    def start(self):
        c = lax.axis_index("ctx")
        for s in range(1, self.cn):
            self.copy(s).start()
        pltpu.make_async_copy(self.src(c), self.dst(c), self.local).start()

    def receive(self, s):
        c = lax.axis_index("ctx")
        if s == 0:
            pltpu.make_async_copy(self.src(c), self.dst(c), self.local).wait()
            return c
        source = lax.rem(c - s + self.cn, self.cn)
        block = self.dst(source)
        remote(
            block, block, self.sem.at[0, s], self.sem.at[1, s], {"ctx": source}
        ).wait_recv()
        return source

    def sent(self):
        for s in range(1, self.cn):
            self.copy(s).wait_send()

    def finish(self):
        for s in range(self.cn):
            self.receive(s)
        self.sent()


class RingGather:
    def __init__(self, dpn, own, full, sem):
        self.dpn, self.own, self.full, self.sem = dpn, own, full, sem
        self.hops = dpn // 2
        d = lax.axis_index("dp")
        self.p = d // 2 * 2 + lax.rem(lax.rem(d, 2) + d // 2, 2)

    def member(self, step):
        p = lax.rem(self.p + step + self.dpn, self.dpn)
        return p // 2 * 2 + lax.rem(lax.rem(p, 2) + p // 2, 2)

    def half(self, ref, h, right):
        if h < self.hops:
            return ref
        m = self.full.shape[1] // 2
        if len(self.full.shape) == 3 and m % 16:
            m = self.full.shape[2] // 2
            return ref.at[:, pl.ds(0 if right else m, m)]
        return ref.at[pl.ds(0 if right else m, m)]

    def copy(self, h, right):
        way = 1 if right else -1
        origin = self.member(-way * (h - 1))
        src = self.own if h == 1 else self.full.at[origin]
        return remote(
            self.half(src, h, right),
            self.half(self.full.at[origin], h, right),
            self.sem.at[0 if right else 1, h],
            self.sem.at[2 if right else 3, h],
            {"dp": self.member(way)},
        )

    def arrival(self, h, right):
        way = 1 if right else -1
        block = self.half(self.full.at[self.member(-way * h)], h, right)
        return remote(
            block,
            block,
            self.sem.at[0 if right else 1, h],
            self.sem.at[2 if right else 3, h],
            {"dp": self.member(way)},
        )

    def greet(self):
        greet({"dp": self.member(1)})
        greet({"dp": self.member(-1)})

    def start(self):
        self.copy(1, True).start()
        self.copy(1, False).start()

    def forward(self):
        for h in range(1, self.hops):
            for right in (True, False):
                self.arrival(h, right).wait_recv()
                self.copy(h + 1, right).start()

    def finish(self):
        for right in (True, False):
            self.arrival(self.hops, right).wait_recv()
        for h in range(1, self.hops + 1):
            for right in (True, False):
                self.copy(h, right).wait_send()


def head_of(cn, heads, c, i):
    return c // 2 + cn // 2 * (heads * (c % 2) + i)


class HeadRows:
    def __init__(self, cn, dpn, dr):
        self.cn, self.dpn = cn, dpn
        self.per = HEAD_DIM // dr
        self.heads = dpn // self.per
        self.c, self.d = lax.axis_index("ctx"), lax.axis_index("dp")
        mine = self.d * cn + self.c
        head, n = mine // self.per, cn // 2
        turn = head // n
        self.home = 2 * lax.rem(head, n) + turn // self.heads
        self.slot = lax.rem(turn, self.heads) * self.per + lax.rem(mine, self.per)
        self.links = dpn - jnp.where(self.home == self.c, 1, 0)

    def owner(self, r):
        i, q = r // self.per, r % self.per
        head = self.c // 2 + self.cn // 2 * (self.heads * lax.rem(self.c, 2) + i)
        g = head * self.per + q
        return {"dp": g // self.cn, "ctx": lax.rem(g, self.cn)}

    def from_here(self, r):
        at = self.owner(r)
        return (at["dp"] == self.d) & (at["ctx"] == self.c)

    def to_here(self, to):
        return (self.home == self.c) & (self.d == to)

    def greet_owners(self):
        for r in range(self.dpn):
            pl.when(jnp.logical_not(self.from_here(r)))(lambda r=r: greet(self.owner(r)))

    def greet_homes(self):
        for to in range(self.dpn):
            pl.when(jnp.logical_not(self.to_here(to)))(
                lambda to=to: greet({"dp": to, "ctx": self.home})
            )


class RowGather(HeadRows):
    def __init__(self, cn, dpn, rows, full, sem, local):
        super().__init__(cn, dpn, rows.shape[0])
        self.rows, self.full, self.sem = rows, full, sem
        self.keep = pltpu.make_async_copy(rows, full.at[self.slot], local)

    def copy(self, to):
        return remote(
            self.rows,
            self.full.at[self.slot],
            self.sem.at[0, to],
            self.sem.at[1, self.slot],
            {"dp": to, "ctx": self.home},
        )

    def start(self):
        for to in range(self.dpn):
            pl.when(jnp.logical_not(self.to_here(to)))(lambda to=to: self.copy(to).start())
            pl.when(self.to_here(to))(self.keep.start)

    def finish(self):
        for r in range(self.dpn):
            block = self.full.at[r]
            came = remote(block, block, self.sem.at[0, r], self.sem.at[1, r], self.owner(r))
            pl.when(jnp.logical_not(self.from_here(r)))(came.wait_recv)
            pl.when(self.from_here(r))(self.keep.wait)
        for to in range(self.dpn):
            pl.when(jnp.logical_not(self.to_here(to)))(lambda to=to: self.copy(to).wait_send())


class RowSum(HeadRows):
    def __init__(self, cn, dpn, parts, got, sem):
        super().__init__(cn, dpn, parts.shape[1])
        self.parts, self.got, self.sem = parts, got, sem

    def copy(self, r):
        return remote(
            self.parts.at[r],
            self.got.at[self.d],
            self.sem.at[0, r],
            self.sem.at[1, self.d],
            self.owner(r),
        )

    def start(self):
        for r in range(self.dpn):
            pl.when(jnp.logical_not(self.from_here(r)))(lambda r=r: self.copy(r).start())

            @pl.when(self.from_here(r))
            def _():
                self.got[self.d] = self.parts[r]

    def finish(self, out):
        for s in range(self.dpn):
            block = self.got.at[s]
            came = remote(
                block, block, self.sem.at[0, s], self.sem.at[1, s], {"dp": s, "ctx": self.home}
            )
            pl.when(jnp.logical_not(self.to_here(s)))(came.wait_recv)

        def add(r):
            total = self.got[0, r, :].astype(f32)
            for s in range(1, self.dpn):
                total = total + self.got[s, r, :].astype(f32)
            out[r, :] = total

        by_rows(out.shape[0], add)
        for r in range(self.dpn):
            pl.when(jnp.logical_not(self.from_here(r)))(lambda r=r: self.copy(r).wait_send())


class RingPieces(RingGather):
    def __init__(self, dpn, full, sem):
        super().__init__(dpn, None, full, sem)

    def piece(self, i, h, right, back):
        way = 1 if right else -1
        ref = self.full.at[self.member(-way * back), i]
        return remote(
            ref,
            ref,
            self.sem.at[0 if right else 1, h, i],
            self.sem.at[2 if right else 3, h, i],
            {"dp": self.member(way)},
        )

    def moves(self, i, h, right, act):
        if h < self.hops:
            act()
        else:
            first = i < self.full.shape[1] // 2
            pl.when(first if right else jnp.logical_not(first))(act)

    def start(self, i):
        for right in (True, False):
            self.moves(i, 1, right, lambda r=right: self.piece(i, 1, r, 0).start())

    def forward(self, i):
        for h in range(1, self.hops):
            for right in (True, False):
                self.piece(i, h, right, h).wait_recv()
                self.moves(
                    i, h + 1, right, lambda h=h, r=right: self.piece(i, h + 1, r, h).start()
                )

    def finish(self, i):
        for right in (True, False):
            h = self.hops
            self.moves(i, h, right, lambda r=right: self.piece(i, h, r, h).wait_recv())
        for h in range(1, self.hops + 1):
            for right in (True, False):
                self.moves(
                    i, h, right, lambda h=h, r=right: self.piece(i, h, r, h - 1).wait_send()
                )


class RingSum:
    def __init__(self, dpn, blocks, got, got_half, sem):
        self.dpn, self.blocks, self.sem = dpn, blocks, sem
        self.got, self.got_half = got, got_half
        self.ring = RingGather(dpn, None, blocks, sem)
        self.hops = dpn // 2

    def part(self, s, right):
        m, width = self.blocks.shape[1:]
        if s > 1:
            return 0, m, pl.ds(0, width)
        if (m // 2) % 16:
            return 0, m, pl.ds(0 if right else width // 2, width // 2)
        return 0 if right else m // 2, m // 2, pl.ds(0, width)

    def copy(self, s, right):
        way = 1 if right else -1
        target = self.ring.member(way * (self.hops - s + 1))
        start, size, lanes = self.part(s, right)
        return remote(
            self.blocks.at[target, pl.ds(start, size), lanes],
            self.arrived(s, right),
            self.sem.at[0 if right else 1, s],
            self.sem.at[2 if right else 3, s],
            {"dp": self.ring.member(way)},
        )

    def arrived(self, s, right):
        side = 0 if right else 1
        return self.got_half.at[side] if s == 1 else self.got.at[side, s - 2]

    def order(self):
        out = [self.ring.member(self.hops)]
        for s in range(self.hops - 1, 0, -1):
            out += [self.ring.member(s), self.ring.member(-s)]
        return out + [self.ring.member(0)]

    def start(self):
        self.copy(1, True).start()
        self.copy(1, False).start()

    def take(self, s, right, target):
        self.copy(s, right).wait_recv()
        start, size, lanes = self.part(s, right)
        block = self.blocks.at[target, pl.ds(start, size), lanes]
        came = self.arrived(s, right)

        def add(r):
            block[r, :] = (block[r, :].astype(f32) + came[r, :].astype(f32)).astype(bf16)

        by_rows(size, add)

    def forward(self, s):
        for right in (True, False):
            way = 1 if right else -1
            self.take(s, right, self.ring.member(way * (self.hops - s)))
            self.copy(s + 1, right).start()

    def finish(self, out):
        for right in (True, False):
            self.copy(self.hops, right).wait_recv()
        mine = self.ring.member(0)
        ends = [self.arrived(self.hops, right) for right in (True, False)]
        per = out.shape[-2]

        @pl.loop(0, self.blocks.shape[1] // 16)
        def _(i):
            r = pl.ds(pl.multiple_of(i * 16, 16), 16)
            total = self.blocks[mine, r, :].astype(f32)
            for end in ends:
                total = total + end[r, :].astype(f32)
            if len(out.shape) == 3:
                to = pl.ds(pl.multiple_of(lax.rem(i * 16, per), 16), 16)
                out[i * 16 // per, to, :] = total.astype(out.dtype)
            else:
                out[r, :] = total.astype(out.dtype)

        for s in range(1, self.hops + 1):
            for right in (True, False):
                self.copy(s, right).wait_send()


def ring_scratch(dpn, m, width):
    return [
        pltpu.VMEM((dpn, m, width), bf16),
        pltpu.VMEM((2, dpn // 2 - 1, m, width), bf16),
        pltpu.VMEM((2, m // 2, width) if m % 32 == 0 else (2, m, width // 2), bf16),
        pltpu.SemaphoreType.DMA((4, dpn // 2 + 1)),
    ]


def outer(a_ref, b_ref, out, at, tile=512):
    a = a_ref[:, at]
    width = out.shape[-1]
    for lo in range(0, width, tile):
        to = slice(lo, min(lo + tile, width))
        out[:, to] = dot(a, b_ref[:, to], contract_rows).astype(bf16)


def outer_all(a_ref, staged, halves, blocks, tile=512):
    count, m, width = blocks.shape
    many = max(1, 128 // m)
    for first in range(0, count, many):
        at = slice(first * m, (first + many) * m)
        for lo in range(0, width, tile):
            to = slice(lo, min(lo + tile, width))
            part = dot(a_ref[halves[0], at], staged(0, to), contract_rows)
            part = part + dot(a_ref[halves[1], at], staged(1, to), contract_rows)
            part = part.astype(bf16)
            for i in range(many):
                blocks[first + i, :, to] = part[i * m : (i + 1) * m]


class LineSum:
    def __init__(self, cn, compute, part, cross, cross_in, flow, arrived, sem):
        self.cn, self.compute, self.part = cn, compute, part
        self.cross, self.cross_in, self.flow = cross, cross_in, flow
        self.arrived, self.sem = arrived, sem

    def half(self, h):
        count = self.cross.shape[1] // 2
        return pl.ds(h * count, count)

    def across(self, t, h):
        _, _, _, _, sib = place(self.cn)
        return remote(
            self.cross.at[t, self.half(h)],
            self.cross_in.at[t, self.half(h)],
            self.sem.at[0, t, h],
            self.sem.at[2, t, h],
            {"ctx": sib},
        )

    def along(self, t, slot, target, h):
        return remote(
            self.flow.at[t, self.half(h)],
            self.arrived.at[slot, self.half(h)],
            self.sem.at[1, t, h],
            self.sem.at[3, slot, h],
            {"ctx": target},
        )

    def rows(self, h, work):
        count = self.cross.shape[1] // 2
        by_rows(count, work, min(16, count), h * count)

    def produce(self, t, slot):
        _, _, k, _, _ = place(self.cn)
        part = self.part.at[slot]
        self.compute(t, part)

        def low(r):
            self.cross[t, r, :] = part[1 - k, r, :].astype(bf16)

        for h in range(2):
            self.rows(h, low)
            self.across(t, h).start()

    def add(self, part, came, h):
        def more(r):
            part[r, :] += came[r, :].astype(f32)

        self.rows(h, more)

    def collect(self, t, slot, h):
        _, j, k, n, sib = place(self.cn)
        part = self.part.at[slot, k]
        self.across(t, h).wait_recv()
        self.add(part, self.cross_in.at[t], h)

        @pl.when((j > 0) & (t >= j))
        def _():
            self.along(t, t, sib, h).wait_recv()
            self.add(part, self.arrived.at[t], h)

        @pl.when((j < n - 1) & (t <= j))
        def _():
            slot_in = jnp.where(t == j, n, t)
            self.along(t, slot_in, sib, h).wait_recv()
            self.add(part, self.arrived.at[slot_in], h)

    def send(self, t, slot, up, h):
        c, j, k, n, _ = place(self.cn)

        def low(r):
            self.flow[t, r, :] = self.part[slot, k, r, :].astype(bf16)

        self.rows(h, low)
        there = t if up else jnp.where(t == j - 1, n, t)
        self.along(t, there, c + 2 if up else c - 2, h).start()

    def pass_on(self, t, slot, up):
        for h in range(2):
            self.collect(t, slot, h)
            self.send(t, slot, up, h)

    def drain(self):
        _, j, _, n, sib = place(self.cn)

        @pl.loop(0, n)
        def _(t):
            for h in range(2):
                self.across(t, h).wait_send()

            @pl.when(t != j)
            def _():
                for h in range(2):
                    self.along(t, t, sib, h).wait_send()


def line_sums(cn, sums, between=None):
    _, j, _, n, _ = place(cn)

    @pl.loop(0, n - 1)
    def _(s):
        to_up, to_down = n - 1 - s + j, s - (n - 1 - j)
        for total in sums:

            @pl.when(s >= j)
            def _():
                total.produce(to_up, 0)

            @pl.when(s >= n - 1 - j)
            def _():
                total.produce(to_down, 1)

        for total in sums:

            @pl.when(s >= j)
            def _():
                total.pass_on(to_up, 0, True)

            @pl.when(s >= n - 1 - j)
            def _():
                total.pass_on(to_down, 1, False)

        if between is not None:
            between(s)

    for total in sums:
        total.produce(j, 0)
    for total in sums:
        for h in range(2):
            total.collect(j, 0, h)


def sum_scratch(cn, rows, width):
    n = cn // 2
    return [
        pltpu.VMEM((2, 2, rows, width), f32),
        pltpu.VMEM((n, rows, width), bf16),
        pltpu.VMEM((n, rows, width), bf16),
        pltpu.VMEM((n, rows, width), bf16),
        pltpu.VMEM((n + 1, rows, width), bf16),
        pltpu.SemaphoreType.DMA((4, n + 1, 2)),
    ]


def product(a_ref, b_ref, dims, rows, width):
    tile = min(512, width)

    def compute(t, out):
        a = a_ref[pl.ds(pl.multiple_of(t * 2 * rows, 2 * rows), 2 * rows), :]

        @pl.loop(0, width // tile)
        def _(i):
            at = pl.ds(pl.multiple_of(i * tile, tile), tile)
            b = b_ref[:, at] if dims == plain else b_ref[at, 0 : a_ref.shape[1]]
            out[:, :, at] = dot(a, b, dims).reshape(2, rows, tile)

    return compute


def rms(v):
    return lax.rsqrt(jnp.mean(v * v, axis=-1, keepdims=True) + norm_eps)


def front_kernel(
    cn, dpn, x_in, seg, valid, gain_rows, wq, wk, wv, wo, gate_in, up_in, down_in,
    x_all, pack_all, gate, up, down_all, wo_low, down_rest,
    x, pack, wide, tall, down, gsem, ssem, rsem, dsem, local,
):
    c, d = lax.axis_index("ctx"), lax.axis_index("dp")
    hw = wq.shape[1] // cn
    part = gate_in.shape[1] // (cn * dpn)
    mine = pack_all.at[d]
    swap = Swap(cn, pack, mine, ssem, local.at[0])
    gather = PairGather(cn, x, x_all, gsem)
    ring = RingPieces(dpn, pack_all, rsem)
    down_ring = RingGather(dpn, down, down_all, dsem)
    greet_ctx(cn)
    ring.greet()
    rows, width = x_in.shape
    load_x = pltpu.make_async_copy(x_in, x.at[:, 0:width], local.at[1])
    load_x.start()

    def column(row):
        return jnp.broadcast_to(row, (128, 128)).T

    code = (seg[...] * 2 + valid[...]).astype(f32)
    x[:, width:] = column(code).astype(bf16)
    lane = lax.broadcasted_iota(jnp.int32, (128, 128), 1)
    gains = jnp.where(lane == 0, column(gain_rows[0:1, :]), column(gain_rows[1:2, :]))
    gains = gains[0 : wq.shape[0]].astype(bf16)
    load_x.wait()
    loads = [
        pltpu.make_async_copy(src, dst, local.at[i])
        for i, (src, dst) in enumerate(
            ((gate_in, wide.at[0]), (up_in, wide.at[1]), (down_in, tall)), 2
        )
    ]
    for load in loads:
        load.start()
    pl.semaphore_wait(pltpu.get_barrier_semaphore(), cn - 1 + 2)
    gather.start()
    for to in range(cn):
        for i, w in enumerate((wq, wk, wv)):
            for t in range(hw // HEAD_DIM):
                lo, at = head_of(cn, hw // HEAD_DIM, to, t) * HEAD_DIM, i * hw + t * HEAD_DIM
                pack[to, :, at : at + HEAD_DIM] = w[:, lo : lo + HEAD_DIM].astype(bf16)
        pack[to, :, 3 * hw :] = gains
    swap.start()
    loads[2].wait()
    split = down.shape[0]
    down[...] = tall[0:split, :].astype(bf16)
    down_rest[...] = tall[split:, :].astype(bf16)
    down_ring.start()
    keep_down = pltpu.make_async_copy(down, down_all.at[d], local.at[5])
    keep_down.start()
    keep = pltpu.make_async_copy(x, x_all.at[c], local.at[1])
    keep.start()
    wo_low[...] = wo[...].astype(bf16)

    def lay(i, out):
        loads[i].wait()
        for to in range(cn):
            for row in range(dpn):
                lo = (row * cn + to) * part
                out[to, :, row * part : (row + 1) * part] = wide[i, :, lo : lo + part].astype(bf16)

    half = cn // 2
    sources = [swap.receive(0)]
    ring.start(sources[0])
    lay(0, gate)
    for s in range(1, half):
        sources.append(swap.receive(s))
        ring.start(sources[s])
    gather.forward(1, 1)
    lay(1, up)
    for s in range(half, cn):
        sources.append(swap.receive(s))
        ring.start(sources[s])
    down_ring.forward()
    gather.forward(2, 2)
    for source in sources:
        ring.forward(source)
    gather.forward(3)
    keep.wait()
    keep_down.wait()
    gather.finish()
    for source in sources:
        ring.finish(source)
    swap.sent()
    down_ring.finish()


def prepare(w, x_all, gains, info_rows, hw, block):
    width = w.shape[0]
    per = block // x_all.shape[1]

    @pl.loop(0, width // block)
    def _(i):
        at = pl.ds(pl.multiple_of(i * block, block), block)
        gains[:, at] = w[at, 3 * hw : 3 * hw + 128].astype(f32).T[0:8]

    @pl.loop(0, info_rows.shape[1] // block)
    def _(i):
        at = pl.ds(pl.multiple_of(i * block, block), block)
        codes = x_all[pl.ds(i * per, per), :, width:].reshape(block, 128).astype(f32).T[0:8]
        seg = jnp.floor(codes * 0.5)
        code = jnp.where(codes - 2.0 * seg == 1.0, seg, -1.0)
        first = lax.broadcasted_iota(jnp.int32, (8, block), 0) == 0
        info_rows[:, at] = jnp.where(first, seg, code)


def tables(x_all, inverse, info_rows, info_cols, cosines, sines, width, i, block):
    per = block // x_all.shape[1]
    at = pl.ds(pl.multiple_of(i * block, block), block)
    codes = x_all[pl.ds(i * per, per), :, width:].reshape(block, 128).astype(f32)
    seg = jnp.floor(codes * 0.5)
    valid = codes - 2.0 * seg
    lane = lax.broadcasted_iota(jnp.int32, (block, 128), 1)
    code = jnp.where(valid == 1.0, seg, -1.0)
    info_cols[at, :] = jnp.where(lane == 0, seg, jnp.where(lane == 1, valid, code))
    before = jnp.where(info_rows[0:1, :] < seg[:, 0:1], 1.0, 0.0)
    index = lax.broadcasted_iota(jnp.int32, (block, 128), 0) + i * block
    place_in = index.astype(f32) - jnp.sum(before, axis=1, keepdims=True)
    angles = place_in * inverse[...]
    cosines[at, :] = jnp.cos(angles)
    sines[at, :] = jnp.where(lane < HEAD_DIM // 2, -1.0, 1.0) * jnp.sin(angles)


def project(x_all, w, gain, inverse, rows_in, cols, cosines, sines, an, qkv, hw, block, hook):
    width = an.shape[1]
    per = block // x_all.shape[1]

    @pl.loop(0, an.shape[0] // block)
    def _(i):
        at = pl.ds(pl.multiple_of(i * block, block), block)
        tables(x_all, inverse, rows_in, cols, cosines, sines, width, i, block)
        x = x_all[pl.ds(i * per, per), :, 0:width].reshape(block, width).astype(f32)
        normed = (x * rms(x) * gain[...]).astype(bf16)
        an[at, :] = normed
        proj = dot(normed, w[:, 0 : 3 * hw])
        cos_b, sin_b = cosines[at, :], sines[at, :]
        for h in range(2 * hw // HEAD_DIM):
            lanes = slice(h * HEAD_DIM, (h + 1) * HEAD_DIM)
            v = proj[:, lanes]
            turned = v * cos_b + pltpu.roll(v, HEAD_DIM // 2, 1) * sin_b
            qkv[at, lanes] = turned.astype(bf16)
        qkv[at, 2 * hw :] = proj[:, 2 * hw :].astype(bf16)
        hook(i)


def mask_block(q_seg, k_code, i, j, block):
    rows = lax.broadcasted_iota(jnp.int32, (block, block), 0) + i * block
    cols = lax.broadcasted_iota(jnp.int32, (block, block), 1) + j * block
    return (q_seg == k_code) & (cols <= rows)


def attend(qkv, q_info, k_code, out, mass, hw, block, hook):
    mass[...] = jnp.zeros_like(mass)

    @pl.loop(0, qkv.shape[0] // block)
    def _(i):
        at = pl.ds(pl.multiple_of(i * block, block), block)
        q_seg, q_valid = q_info[at, 0:1], q_info[at, 1:2]
        for h in range(hw // HEAD_DIM):
            lane = [slice(t * hw + h * HEAD_DIM, t * hw + (h + 1) * HEAD_DIM) for t in range(3)]
            q = qkv[at, lane[0]]

            def step(j, acc):
                to = pl.ds(pl.multiple_of(j * block, block), block)
                s = dot(q, qkv[to, lane[1]], contract_cols) * score_scale - score_shift
                allowed = mask_block(q_seg, k_code[1:2, to], i, j, block)
                p = jnp.where(allowed, jax.nn.sigmoid(s), 0.0)
                mass[...] += jnp.sum(p * q_valid, axis=0, keepdims=True)
                return acc + dot(p.astype(bf16), qkv[to, lane[2]])

            acc = lax.fori_loop(0, i + 1, step, jnp.zeros((block, HEAD_DIM), f32))
            out[at, lane[0]] = acc.astype(bf16)
        hook(i)


def attn_kernel(
    cn, dpn, x_all, w, inverse, gate, up, wo,
    an, qkv, o, mass, gains, cosines, sines, cols, rows_in,
    gate_all, up_own, wo_all, ssem, rsem, wsem, local,
):
    c, d = lax.axis_index("ctx"), lax.axis_index("dp")
    wo_rows = RowGather(cn, dpn, wo, wo_all, wsem, local.at[2])
    rows = x_all.shape[1]
    hw = qkv.shape[1] // 3
    swap_gate = Swap(cn, gate, gate_all.at[d], ssem.at[0], local.at[0])
    swap_up = Swap(cn, up, up_own, ssem.at[1], local.at[1])
    ring = RingPieces(dpn, gate_all, rsem)
    sources = [lax.rem(c - s + cn, cn) for s in range(cn)]
    greet_ctx(cn)
    ring.greet()

    wo_rows.greet_owners()
    pl.semaphore_wait(pltpu.get_barrier_semaphore(), cn - 1 + 2 + wo_rows.links)
    wo_rows.start()
    swap_gate.start()

    def in_project(i):
        @pl.when(i == 1)
        def _():
            for s in range(cn // 2):
                ring.start(swap_gate.receive(s))

        @pl.when(i == 2)
        def _():
            for s in range(cn // 2, cn):
                ring.start(swap_gate.receive(s))
            swap_up.start()

    def in_attend(i):
        @pl.when(i == 2)
        def _():
            for source in sources[: cn // 2]:
                ring.forward(source)

    prepare(w, x_all, gains, rows_in, hw, 2 * rows)
    project(
        x_all, w, gains.at[0:1], inverse, rows_in, cols, cosines, sines, an, qkv, hw, 2 * rows,
        in_project,
    )
    attend(qkv, cols, rows_in, o, mass, hw, 2 * rows, in_attend)
    for source in sources[cn // 2 :]:
        ring.forward(source)
    swap_up.finish()
    wo_rows.finish()
    for source in sources:
        ring.finish(source)
    swap_gate.sent()


def middle_kernel(
    cn, dpn, o, wo, x, gain, dy, up, gate_all, down_half, down_rest,
    h1, bn_all, up_all, hid, dgu, dys_all, down_all,
    own, bn, dys, wg, wu, down_by, gsem, ysem, rsem, dsem, local, *sum_refs,
):
    c, d = lax.axis_index("ctx"), lax.axis_index("dp")
    _, j, k, n, _ = place(cn)
    rows, width = x.shape
    ff = hid.shape[1]
    block = 2 * rows
    gather = PairGather(cn, own, bn, gsem)
    gather_dy = PairGather(cn, dy, dys, ysem)
    ring = RingGather(dpn, up, up_all, rsem)
    split = down_rest.shape[0]
    rest_ring = RingGather(dpn, down_rest, down_by.at[:, pl.ds(split, split)], dsem)
    keep_rest = pltpu.make_async_copy(
        down_rest, down_by.at[d, pl.ds(split, split)], local.at[5]
    )
    total = LineSum(cn, product(o, wo, plain, rows, width), *sum_refs)
    greet_line(cn, ring)
    ring.start()
    rest_ring.start()
    keep_rest.start()
    keep_up = pltpu.make_async_copy(up, up_all.at[d], local.at[0])
    loads = [
        pltpu.make_async_copy(src, dst, local.at[i])
        for i, (src, dst) in enumerate(((gate_all, wg), (down_half, down_by.at[:, pl.ds(0, split)])), 2)
    ]
    keep_up.start()
    for load in loads:
        load.start()
    gather_dy.start()
    dys[c] = dy[...]

    def between(s):
        gather_dy.step(s + 1)

        @pl.when(s == n - 2)
        def _():
            ring.forward()
            rest_ring.forward()

    line_sums(cn, [total], between)

    def norm(r):
        mid = x[r, :].astype(f32) + total.part[0, k, r, :]
        h1[r, :] = mid
        own[r, :] = (mid * rms(mid) * gain[1:2, :]).astype(bf16)

    by_rows(rows, norm)
    gather.start()
    bn[c] = own[...]
    gather_dy.finish()
    store_dy = pltpu.make_async_copy(dys, dys_all, local.at[4])
    store_dy.start()
    total.drain()
    keep_up.wait()
    for load in loads:
        load.wait()
    rest_ring.finish()
    keep_rest.wait()
    store_down = pltpu.make_async_copy(down_by, down_all, local.at[6])
    store_down.start()
    ring.finish()
    load_up = pltpu.make_async_copy(up_all, wu, local.at[0])
    load_up.start()
    load_up.wait()
    wgate, wup, down = wg, wu.reshape(width, ff), down_by.reshape(ff, width)
    tile = min(512, ff)

    def feed(t):
        gather.other(t)
        at = pl.ds(pl.multiple_of(t * block, block), block)
        pair = pl.ds(t * 2, 2)
        send = pltpu.make_async_copy(bn.at[pair], bn_all.at[pair], local.at[1])
        send.start()
        a = bn[pair].reshape(block, width)
        g_out = dys[pair].reshape(block, width)

        @pl.loop(0, ff // tile)
        def _(i):
            to = pl.ds(pl.multiple_of(i * tile, tile), tile)
            gate = dot(a, wgate[:, to])
            up_v = dot(a, wup[:, to])
            dhid = dot(g_out, down[to, :], contract_cols)
            sig = jax.nn.sigmoid(gate)
            silu = gate * sig
            hid[at, to] = (silu * up_v).astype(bf16)
            dgate = dhid * up_v * sig * (1.0 + gate * (1.0 - sig))
            dgu[at, to] = dgate.astype(bf16)
            dgu[at, pl.ds(pl.multiple_of(ff + i * tile, tile), tile)] = (dhid * silu).astype(bf16)

        send.wait()

    feed(j)
    gather.step(1)

    @pl.loop(1, n)
    def _(s):
        both = (j - s >= 0) & (j + s <= n - 1)

        @pl.when(j - s >= 0)
        def _():
            feed(j - s)

        @pl.when(both & (s < n - 1))
        def _():
            gather.step(s + 1)

        @pl.when(j + s <= n - 1)
        def _():
            feed(j + s)

        @pl.when(jnp.logical_not(both) & (s < n - 1))
        def _():
            gather.step(s + 1)

    gather.sent()
    store_dy.wait()
    store_down.wait()


def back_kernel(
    cn, dpn, bn_in, dgu_in, hid, down, wg, wu, h1, dy, gain, dh1, dob_all, term, g_own, result,
    own, bn, dgu, cross_in, arrived, bsem, gsem, loads, keep_sem, *scratch,
):
    sum_refs, ring_refs = scratch[:-4], scratch[-4:]
    rows, width = dy.shape
    ff = wg.shape[1]
    tile = min(512, width)
    c, _, k, n, _ = place(cn)

    def compute(t, out):
        at = pl.ds(pl.multiple_of(t * 2 * rows, 2 * rows), 2 * rows)

        @pl.loop(0, width // tile)
        def _(i):
            to = pl.ds(pl.multiple_of(i * tile, tile), tile)
            part = dot(dgu[at, 0:ff], wg[to, :], contract_cols)
            part = part + dot(dgu[at, ff:], wu[to, :], contract_cols)
            out[:, :, to] = part.reshape(2, rows, tile)

    total = LineSum(cn, compute, *sum_refs)
    ring = RingSum(dpn, *ring_refs)
    blocks = ring_refs[0]
    m = blocks.shape[1]
    load_dgu = pltpu.make_async_copy(dgu_in, dgu, loads.at[0])
    load_bn = pltpu.make_async_copy(bn_in, bn, loads.at[1])
    load_dgu.start()
    load_bn.start()
    greet_line(cn, ring.ring)
    order = ring.order()
    load_dgu.wait()

    def weight_grad(member):
        outer(bn, dgu, blocks.at[member], pl.ds(pl.multiple_of(member * m, m), m))


    def between(s):
        @pl.when(s == 0)
        def _():
            load_bn.wait()
            weight_grad(order[0])
            ring.start()

        for i in range(ring.hops - 1):

            @pl.when(s == min(i, n - 2))
            def _():
                weight_grad(order[1 + 2 * i])
                weight_grad(order[2 + 2 * i])

            @pl.when(s == min(i + 2, n - 2))
            def _():
                ring.forward(i + 1)

        @pl.when(s == n - 2)
        def _():
            weight_grad(order[-1])

    line_sums(cn, [total], between)
    load_hid = pltpu.make_async_copy(hid, dgu.at[:, 0:ff], loads.at[0])
    load_down = pltpu.make_async_copy(down, bn.at[0:ff], loads.at[1])
    load_hid.start()
    load_down.start()
    term[...] = jnp.zeros_like(term)

    def norm_back(r):
        dbn = total.part[0, k, r, :]
        mid = h1[r, :]
        r2 = rms(mid)
        xh2 = mid * r2
        term[...] += jnp.sum(dbn * xh2, axis=0, keepdims=True)
        u2 = dbn * gain[1:2, :]
        mean = jnp.mean(u2 * xh2, axis=-1, keepdims=True)
        grad = dy[r, :].astype(f32) + r2 * (u2 - xh2 * mean)
        dh1[r, :] = grad
        own[r, :] = grad.astype(bf16)

    by_rows(rows, norm_back)
    gather = PairGather(cn, own, dob_all, gsem)
    gather.start()
    keep = pltpu.make_async_copy(own, dob_all.at[c], keep_sem)
    keep.start()
    total.drain()

    part, cross, _, flow, _, _ = sum_refs
    second = LineSum(
        cn,
        product(dgu.at[:, 0:ff], bn.at[0:ff], plain, rows, width),
        part, cross, cross_in, flow, arrived, bsem,
    )
    load_hid.wait()
    load_down.wait()

    def pass_on(s):
        gather.step(s + 1)

    line_sums(cn, [second], pass_on)

    def close(r):
        result[r, :] = (h1[r, :] + second.part[0, k, r, :]).astype(bf16)

    by_rows(rows, close)
    second.drain()
    keep.wait()
    gather.finish()
    ring.finish(g_own)


def attend_back(qkv, do, cosines, sines, q_info, k_info, dq, dqkv, hw, block):
    count = qkv.shape[0] // block
    dq[...] = jnp.zeros_like(dq)

    def turn_back(g, at):
        return g * cosines[at, :] - pltpu.roll(g, HEAD_DIM // 2, 1) * sines[at, :]

    @pl.loop(0, count)
    def _(j):
        to = pl.ds(pl.multiple_of(j * block, block), block)
        k_code = k_info[to, 2:3]
        for h in range(hw // HEAD_DIM):
            lane = [slice(t * hw + h * HEAD_DIM, t * hw + (h + 1) * HEAD_DIM) for t in range(3)]
            k, v = qkv[to, lane[1]], qkv[to, lane[2]]

            def step(i, carry):
                dk, dv = carry
                at = pl.ds(pl.multiple_of(i * block, block), block)
                q, do_i = qkv[at, lane[0]], do[at, lane[0]]
                s = dot(k, q, contract_cols) * score_scale - score_shift
                keys = lax.broadcasted_iota(jnp.int32, (block, block), 0) + j * block
                queries = lax.broadcasted_iota(jnp.int32, (block, block), 1) + i * block
                allowed = (k_code == q_info[0:1, at]) & (keys <= queries)
                sg = jnp.where(allowed, jax.nn.sigmoid(s), 0.0)
                dp = dot(v, do_i, contract_cols)
                ds = (dp * sg * (1.0 - sg)).astype(bf16)
                dq[at, lane[0]] += dot(ds, k, contract_rows)
                return dk + dot(ds, q), dv + dot(sg.astype(bf16), do_i)

            zero = jnp.zeros((block, HEAD_DIM), f32)
            dk, dv = lax.fori_loop(j, count, step, (zero, zero))
            dqkv[to, lane[1]] = turn_back(dk * score_scale, to).astype(bf16)
            dqkv[to, lane[2]] = dv.astype(bf16)

    @pl.loop(0, count)
    def _(i):
        at = pl.ds(pl.multiple_of(i * block, block), block)
        for h in range(hw // HEAD_DIM):
            lanes = slice(h * HEAD_DIM, (h + 1) * HEAD_DIM)
            dqkv[at, lanes] = turn_back(dq[at, lanes] * score_scale, at).astype(bf16)


def last_kernel(
    cn, dpn, g_gu, dob_all, dys_all, hid, o, wo, qkv, cosines, sines, q_info, k_info, an, w,
    dh1, x, gain, term_two, mass, grad_in, tot_out, gu_all, down_own, out_all, qkv_all,
    do, dq, dqkv, out_parts, out_got, qkv_own, tot, tot_in, tot_sum, tot_last,
    usem, qsem, tsem, psem, osem, local, *scratch,
):
    sum_refs, rings = scratch[:-8], (scratch[-8:-4], scratch[-4:])
    rows, width = x.shape
    hw = width // cn
    _, _, k, n, _ = place(cn)
    down_ring, qkv_ring = (RingSum(dpn, *refs) for refs in rings)
    rows_out = RowSum(cn, dpn, out_parts, out_got, osem)
    swap_gu = Swap(cn, g_gu, gu_all, usem, local.at[0])
    swap_qkv = Swap(cn, qkv_own, qkv_all, qsem, local.at[4])
    totals = Swap(cn, None, tot_in, tsem, local.at[3], lambda i: tot)
    c, d = lax.axis_index("ctx"), lax.axis_index("dp")
    def share(s):
        return remote(
            tot_sum, tot_last.at[d], psem.at[0, s], psem.at[1, s], {"dp": lax.rem(d + s, dpn)}
        )

    greet_ctx(cn)
    for s in range(1, dpn):
        greet({"dp": lax.rem(d + s, dpn)})

    rows_out.greet_homes()
    pl.semaphore_wait(
        pltpu.get_barrier_semaphore(), cn - 1 + dpn - 1 + rows_out.links
    )
    swap_gu.start()
    seq = an.shape[0]
    stage = (sum_refs[1], sum_refs[3])
    halves = (slice(0, seq // 2), slice(seq // 2, seq))

    def fill(src):
        copies = [
            pltpu.make_async_copy(src.at[pl.ds(i * n, n)], stage[i], local.at[1 + i])
            for i in range(2)
        ]
        for copy in copies:
            copy.start()
        for copy in copies:
            copy.wait()

    def staged(i, to=slice(None)):
        return stage[i][:, :, to].reshape(seq // 2, -1)

    fill(dob_all)
    outer_all(o, staged, halves, out_parts)
    rows_out.start()
    for i in range(2):
        do[halves[i], :] = dot(staged(i), wo[...], contract_cols).astype(bf16)
    fill(dys_all)
    outer_all(hid, staged, halves, rings[0][0])
    down_ring.start()
    m_qkv = rings[1][0].shape[1]
    order = qkv_ring.order()

    def grad_qkv(member):
        outer(an, dqkv, rings[1][0].at[member], pl.ds(pl.multiple_of(member * m_qkv, m_qkv), m_qkv))

    attend_back(qkv, do, cosines, sines, q_info, k_info, dq, dqkv, hw, 2 * rows)
    grad_qkv(order[0])
    qkv_ring.start()
    total = LineSum(cn, product(dqkv, w, contract_cols, rows, width), *sum_refs)

    def between(s):
        for i in range(qkv_ring.hops - 1):

            @pl.when(s == min(i, n - 2))
            def _():
                grad_qkv(order[1 + 2 * i])
                grad_qkv(order[2 + 2 * i])
                qkv_ring.forward(i + 1)

            @pl.when(s == min(i + 1, n - 2))
            def _():
                down_ring.forward(i + 1)

        @pl.when(s == n - 2)
        def _():
            grad_qkv(order[-1])
            qkv_ring.finish(qkv_own)
            swap_qkv.start()

    line_sums(cn, [total], between)
    tot[0] = jnp.zeros((1, width), f32)

    def norm_back(r):
        dan = total.part[0, k, r, :]
        xf = x[r, :].astype(f32)
        r1 = rms(xf)
        xh1 = xf * r1
        tot[0] += jnp.sum(dan * xh1, axis=0, keepdims=True)
        u1 = dan * gain[0:1, :]
        mean = jnp.mean(u1 * xh1, axis=-1, keepdims=True)
        grad = dh1[r, :] + r1 * (u1 - xh1 * mean)
        grad_in[r, :] = grad.astype(bf16)

    by_rows(rows, norm_back)
    tot[1] = term_two[...]
    tot[2] = jnp.broadcast_to(jnp.sum(mass[...], axis=1, keepdims=True), (1, width))
    totals.start()
    rows_out.finish(out_all)
    totals.finish()
    tot_sum[...] = jnp.sum(tot_in[...], axis=0)
    for s in range(1, dpn):
        share(s).start()
    down_ring.finish(down_own)
    total.drain()
    swap_gu.finish()
    tot_last[d] = tot_sum[...]
    for s in range(1, dpn):
        source = lax.rem(d - s + dpn, dpn)
        block = tot_last.at[source]
        remote(block, block, psem.at[0, s], psem.at[1, s], {"dp": source}).wait_recv()
    for s in range(1, dpn):
        share(s).wait_send()
    tot_out[...] = jnp.sum(tot_last[...], axis=0)
    swap_qkv.finish()


def spread_kernel(
    cn, dpn, qkv_in, gu_in, down_in, out_in, gq, gk, gv, go, gg, gu_out, gd, qkv, gu, down, out, sem
):
    hw = qkv.shape[2] // 3
    ff_rows = gd.shape[0]
    ff = ff_rows * dpn
    pairs = ((down_in, down), (out_in, out), (qkv_in, qkv), (gu_in, gu))
    loads = [pltpu.make_async_copy(a, b, sem.at[i]) for i, (a, b) in enumerate(pairs)]
    for load in loads:
        load.start()
    for load in loads[:3]:
        load.wait()
    gd[...] = down[...].astype(f32)
    go[...] = out[...]
    for c in range(cn):
        for i, ref in enumerate((gq, gk, gv)):
            for t in range(hw // HEAD_DIM):
                lo, at = head_of(cn, hw // HEAD_DIM, c, t) * HEAD_DIM, i * hw + t * HEAD_DIM
                ref[:, lo : lo + HEAD_DIM] = qkv[c, :, at : at + HEAD_DIM].astype(f32)
    loads[3].wait()
    for c in range(cn):
        for i, ref in enumerate((gg, gu_out)):
            for d in range(dpn):
                to = (d * cn + c) * ff_rows
                lo = i * ff + d * ff_rows
                ref[:, to : to + ff_rows] = gu[c, :, lo : lo + ff_rows].astype(f32)


def call(kernel, outs, ins, specs_in, specs_out, scratch, number, flops=0, moved=0):
    return pl.pallas_call(
        kernel,
        out_shape=outs,
        in_specs=specs_in,
        out_specs=specs_out,
        scratch_shapes=scratch,
        compiler_params=pltpu.CompilerParams(
            collective_id=number, has_side_effects=True, vmem_limit_bytes=61 * 2**20
        ),
        cost_estimate=pl.CostEstimate(flops=flops, bytes_accessed=moved, transcendentals=0),
    )(*ins)


def shape(dims, dtype=bf16):
    return jax.ShapeDtypeStruct(dims, dtype)


def shards(
    hidden_in,
    out_grad,
    seg_ids,
    valid_mask,
    w_query,
    w_key,
    w_value,
    w_output,
    w_gate,
    w_up,
    w_down,
    gain_attn,
    gain_mlp,
):
    dpn = lax.axis_size("dp")
    cn = lax.axis_size("ctx")
    n = cn // 2
    x_local = hidden_in[0]
    dy_local = out_grad[0]
    rows, width = x_local.shape
    seq = rows * cn
    dr = w_query.shape[0]
    hw = width // cn
    heads = hw // HEAD_DIM
    ff_rows = w_down.shape[0]
    ff = ff_rows * dpn
    dma = pltpu.SemaphoreType.DMA
    mib = 2**20

    gain_rows = jnp.pad(jnp.stack([gain_attn, gain_mlp]), ((0, 0), (0, 128 - dr)))
    pw = 3 * hw + 128
    ring_sem = dma((4, dpn // 2 + 1))
    x_all, w_qkv, gate_pack, up_pack, down_half, wo_low, down_rest = call(
        functools.partial(front_kernel, cn, dpn),
        (
            shape((cn, rows, width + 128)),
            shape((dpn, cn, dr, pw)),
            shape((cn, dr, ff)),
            shape((cn, dr, ff)),
            shape((dpn, ff_rows // 2, width)),
            shape((dr, width)),
            shape((ff_rows // 2, width)),
        ),
        (
            x_local, seg_ids, valid_mask, gain_rows, w_query, w_key, w_value, w_output,
            w_gate, w_up, w_down,
        ),
        [ANY] + [VMEM] * 7 + [ANY] * 3,
        (ANY, ANY, VMEM, VMEM, ANY, VMEM, VMEM),
        [
            pltpu.VMEM((rows, width + 128), bf16),
            pltpu.VMEM((cn, dr, pw), bf16),
            pltpu.VMEM((2, dr, ff * cn), f32),
            pltpu.VMEM((ff_rows, width), f32),
            pltpu.VMEM((ff_rows // 2, width), bf16),
            dma((2, 5, n)),
            dma((2, cn)),
            dma((4, dpn // 2 + 1, cn)),
            ring_sem,
            dma((6,)),
        ],
        1,
        moved=160 * mib,
    )
    w_qkv = w_qkv.reshape(width, pw)
    inverse = jnp.exp(
        jnp.arange(HEAD_DIM // 2, dtype=f32) * (-2.0 * math.log(rope_base) / HEAD_DIM)
    )
    inverse = jnp.concatenate([inverse, inverse])[None]

    line_scratch = sum_scratch(cn, rows, width)
    an, proj, o, mass, gains, cosines, sines, cols, infos, w_gate_c, up_own, wo = call(
        functools.partial(attn_kernel, cn, dpn),
        (
            shape((seq, width)),
            shape((seq, 3 * hw)),
            shape((seq, hw)),
            shape((1, 2 * rows), f32),
            shape((8, width), f32),
            shape((seq, HEAD_DIM), f32),
            shape((seq, HEAD_DIM), f32),
            shape((seq, 128), f32),
            shape((8, seq), f32),
            shape((dpn, cn, dr, ff)),
            shape((cn, dr, ff)),
            shape((dpn, dr, width)),
        ),
        (x_all, w_qkv, inverse, gate_pack, up_pack, wo_low),
        [VMEM] * 3 + [ANY] * 3,
        (VMEM,) * 9 + (ANY,) * 3,
        [dma((2, 2, cn)), dma((4, dpn // 2 + 1, cn)), dma((2, dpn)), dma((3,))],
        2,
        moved=160 * mib,
    )
    h1, bn, w_up_c, hid, dgu, dys, down = call(
        functools.partial(middle_kernel, cn, dpn),
        (
            shape((rows, width), f32),
            shape((cn, rows, width)),
            shape((dpn, cn, dr, ff)),
            shape((seq, ff)),
            shape((seq, 2 * ff)),
            shape((cn, rows, width)),
            shape((dpn, ff_rows, width)),
        ),
        (
            o, wo.reshape(hw, width), x_local, gains, dy_local, up_own,
            w_gate_c.reshape(width, ff), down_half, down_rest,
        ),
        [VMEM] * 5 + [ANY] * 4,
        (VMEM, ANY, ANY, VMEM, VMEM, ANY, ANY),
        [
            pltpu.VMEM((rows, width), bf16),
            pltpu.VMEM((cn, rows, width), bf16),
            pltpu.VMEM((cn, rows, width), bf16),
            pltpu.VMEM((width, ff), bf16),
            pltpu.VMEM((dpn, cn, dr, ff), bf16),
            pltpu.VMEM((dpn, ff_rows, width), bf16),
            dma((2, 5, n)),
            dma((2, 5, n)),
            ring_sem,
            ring_sem,
            dma((7,)),
        ]
        + line_scratch,
        3,
        moved=160 * mib,
    )
    wo = wo.reshape(hw, width)
    w_gate_c = w_gate_c.reshape(width, ff)
    w_up_c = w_up_c.reshape(width, ff)
    bn = bn.reshape(seq, width)
    dh1, dob, term_two, g_gu, result = call(
        functools.partial(back_kernel, cn, dpn),
        (
            shape((rows, width), f32),
            shape((cn, rows, width)),
            shape((1, width), f32),
            shape((cn, dr, 2 * ff)),
            shape((rows, width)),
        ),
        (bn, dgu, hid, down.reshape(ff, width), w_gate_c, w_up_c, h1, dy_local, gains),
        [ANY] * 4 + [VMEM] * 5,
        (VMEM, ANY, VMEM, VMEM, VMEM),
        [
            pltpu.VMEM((rows, width), bf16),
            pltpu.VMEM((seq, width), bf16),
            pltpu.VMEM((seq, 2 * ff), bf16),
            pltpu.VMEM((n, rows, width), bf16),
            pltpu.VMEM((n + 1, rows, width), bf16),
            dma((4, n + 1, 2)),
            dma((2, 5, n)),
            dma((2,)),
            dma,
        ]
        + line_scratch
        + ring_scratch(dpn, cn * dr, 2 * ff),
        4,
        moved=160 * mib,
    )
    grad_input, totals, gu_back, g_down, g_out, q_all = call(
        functools.partial(last_kernel, cn, dpn),
        (
            shape((rows, width)),
            shape((3, 1, width), f32),
            shape((cn, dr, 2 * ff)),
            shape((ff_rows, width)),
            shape((dr, width), f32),
            shape((cn, dr, 3 * hw)),
        ),
        (
            g_gu, dob, dys, hid, o, wo, proj, cosines, sines, infos, cols, an, w_qkv,
            dh1, x_local, gains, term_two, mass,
        ),
        [ANY] * 3 + [VMEM] * 15,
        (VMEM, VMEM, ANY, VMEM, VMEM, ANY),
        [
            pltpu.VMEM((seq, hw), bf16),
            pltpu.VMEM((seq, hw), f32),
            pltpu.VMEM((seq, 3 * hw), bf16),
            pltpu.VMEM((dpn, dr, width), bf16),
            pltpu.VMEM((dpn, dr, width), bf16),
            pltpu.VMEM((cn, dr, 3 * hw), bf16),
            pltpu.VMEM((3, 1, width), f32),
            pltpu.VMEM((cn, 3, 1, width), f32),
            pltpu.VMEM((3, 1, width), f32),
            pltpu.VMEM((dpn, 3, 1, width), f32),
            dma((2, cn)),
            dma((2, cn)),
            dma((2, cn)),
            dma((2, dpn)),
            dma((2, dpn)),
            dma((5,)),
        ]
        + line_scratch
        + ring_scratch(dpn, ff_rows, width)
        + ring_scratch(dpn, cn * dr, 3 * hw),
        5,
        moved=160 * mib,
    )

    g_q, g_k, g_v, g_o, g_gate, g_up, g_down = pl.pallas_call(
        functools.partial(spread_kernel, cn, dpn),
        out_shape=tuple(shape((dr, width), f32) for _ in range(4))
        + tuple(shape((dr, ff * cn), f32) for _ in range(2))
        + (shape((ff_rows, width), f32),),
        in_specs=[ANY] * 4,
        out_specs=(VMEM,) * 7,
        scratch_shapes=[
            pltpu.VMEM((cn, dr, 3 * hw), bf16),
            pltpu.VMEM((cn, dr, 2 * ff), bf16),
            pltpu.VMEM((ff_rows, width), bf16),
            pltpu.VMEM((dr, width), f32),
            dma((4,)),
        ],
        compiler_params=pltpu.CompilerParams(vmem_limit_bytes=61 * 2**20),
    )(q_all, gu_back, g_down, g_out)
    mass_mean = totals[2, 0, 0] / (heads * cn * dpn * seq)
    owner = (lax.axis_index("dp") * cn + lax.axis_index("ctx")) * dr
    grad_gains = [lax.dynamic_slice_in_dim(totals[i, 0], owner, dr) for i in range(2)]
    return (
        result[None],
        grad_input[None],
        g_q,
        g_k,
        g_v,
        g_o,
        g_gate,
        g_up,
        g_down,
        grad_gains[0],
        grad_gains[1],
        mass_mean,
    )


def solution(mesh):
    tok = P("dp", "ctx", None)
    ids = P("dp", "ctx")
    mat = P(("dp", "ctx"), None)
    vec = P(("dp", "ctx"))
    return jax.shard_map(
        shards,
        mesh=mesh,
        in_specs=(tok, tok, ids, ids) + (mat,) * 7 + (vec, vec),
        out_specs=(tok, tok) + (mat,) * 7 + (vec, vec, P()),
        check_vma=False,
    )
```

```python
import functools
import math

import jax
import jax.numpy as jnp
from jax import lax
from jax.experimental import pallas as pl
from jax.experimental.pallas import tpu as pltpu
from jax.sharding import PartitionSpec as P

HEAD_DIM = 128
norm_eps = 1e-05
rope_base = 10000.0
score_shift = math.log(4096.0)
score_scale = 1.0 / math.sqrt(HEAD_DIM)
contract_rows = (((0,), (0,)), ((), ()))
contract_cols = (((1,), (1,)), ((), ()))
plain = (((1,), (0,)), ((), ()))
f32 = jnp.float32
bf16 = jnp.bfloat16
MESH = pl.DeviceIdType.MESH
ANY = pl.BlockSpec(memory_space=pl.ANY)
VMEM = pl.BlockSpec(memory_space=pltpu.VMEM)


def dot(a, b, dims=plain):
    return lax.dot_general(a, b, dims, preferred_element_type=f32)


def remote(src, dst, send, recv, target):
    return pltpu.make_async_remote_copy(
        src_ref=src,
        dst_ref=dst,
        send_sem=send,
        recv_sem=recv,
        device_id=target,
        device_id_type=MESH,
    )


def greet(target):
    pl.semaphore_signal(
        pltpu.get_barrier_semaphore(), inc=1, device_id=target, device_id_type=MESH
    )


def by_rows(count, work, step=16):
    @pl.loop(0, count // step)
    def _(i):
        work(pl.ds(pl.multiple_of(i * step, step), step))


def place(cn):
    c = lax.axis_index("ctx")
    j, k = c // 2, c % 2
    return c, j, k, cn // 2, 2 * j + 1 - k


def greet_line(cn, ring):
    c, j, _, n, sib = place(cn)
    ring.greet()
    greet({"ctx": sib})

    @pl.when(j < n - 1)
    def _():
        greet({"ctx": c + 2})

    @pl.when(j > 0)
    def _():
        greet({"ctx": c - 2})

    inner = jnp.where(j > 0, 1, 0) + jnp.where(j < n - 1, 1, 0)
    pl.semaphore_wait(pltpu.get_barrier_semaphore(), 3 + inner)


def greet_ctx(cn):
    c = lax.axis_index("ctx")
    for s in range(1, cn):
        greet({"ctx": lax.rem(c + s, cn)})


class LineGather:
    def __init__(self, cn, own, full, sem):
        self.cn, self.own, self.full, self.sem = cn, own, full, sem

    def copy(self, src, origin, kind, target):
        _, _, k, _, _ = place(self.cn)
        sem = self.sem
        return remote(
            src,
            self.full.at[2 * origin + k],
            sem.at[kind, origin],
            sem.at[3 if kind < 2 else 4, origin],
            {"ctx": target},
        )

    def start(self):
        c, j, _, n, sib = place(self.cn)

        @pl.when(j < n - 1)
        def _():
            self.copy(self.own, j, 0, c + 2).start()

        @pl.when(j > 0)
        def _():
            self.copy(self.own, j, 1, c - 2).start()

        self.copy(self.own, j, 2, sib).start()

    def step(self, s):
        c, j, k, n, sib = place(self.cn)

        @pl.when(j - s >= 0)
        def _():
            o = j - s
            block = self.full.at[2 * o + k]
            self.copy(block, o, 0, sib).wait_recv()

            @pl.when(j < n - 1)
            def _():
                self.copy(block, o, 0, c + 2).start()

            self.copy(block, o, 2, sib).start()

        @pl.when(j + s <= n - 1)
        def _():
            o = j + s
            block = self.full.at[2 * o + k]
            self.copy(block, o, 1, sib).wait_recv()

            @pl.when(j > 0)
            def _():
                self.copy(block, o, 1, c - 2).start()

            self.copy(block, o, 2, sib).start()

    def forward(self, first=1, last=None):
        for s in range(first, self.cn // 2 if last is None else last + 1):
            self.step(s)

    def other(self, o):
        _, _, k, _, sib = place(self.cn)
        block = self.full.at[2 * o + 1 - k]
        remote(
            block, block, self.sem.at[2, o], self.sem.at[4, o], {"ctx": sib}
        ).wait_recv()

    def sent(self):
        c, j, k, n, sib = place(self.cn)
        for o in range(n):
            block = self.full.at[2 * o + k]

            @pl.when((j < n - 1) & (o <= j))
            def _():
                self.copy(block, o, 0, sib).wait_send()

            @pl.when((j > 0) & (o >= j))
            def _():
                self.copy(block, o, 1, sib).wait_send()

            self.copy(block, o, 2, sib).wait_send()

    def finish(self):
        for o in range(self.cn // 2):
            self.other(o)
        self.sent()


class PairGather:
    def __init__(self, cn, own, full, sem):
        self.cn, half = cn, own.shape[0] // 2
        self.parts = []
        for i in range(2):
            at = pl.ds(i * half, half)
            self.parts.append(LineGather(cn, own.at[at], full.at[:, at], sem.at[i]))

    def start(self):
        for part in self.parts:
            part.start()

    def step(self, s):
        for part in self.parts:
            part.step(s)

    def forward(self, first=1, last=None):
        for s in range(first, self.cn // 2 if last is None else last + 1):
            self.step(s)

    def other(self, o):
        for part in self.parts:
            part.other(o)

    def sent(self):
        for part in self.parts:
            part.sent()

    def finish(self):
        for part in self.parts:
            part.finish()


class Swap:
    def __init__(self, cn, src, dst, sem, local, pick=None):
        self.cn, self.sem, self.local = cn, sem, local
        self.src = pick or (lambda c: src.at[c])
        self.dst = dst if callable(dst) else lambda c: dst.at[c]

    def copy(self, s):
        c = lax.axis_index("ctx")
        peer = lax.rem(c + s, self.cn)
        return remote(
            self.src(peer),
            self.dst(c),
            self.sem.at[0, s],
            self.sem.at[1, s],
            {"ctx": peer},
        )

    def start(self):
        c = lax.axis_index("ctx")
        for s in range(1, self.cn):
            self.copy(s).start()
        pltpu.make_async_copy(self.src(c), self.dst(c), self.local).start()

    def receive(self, s):
        c = lax.axis_index("ctx")
        if s == 0:
            pltpu.make_async_copy(self.src(c), self.dst(c), self.local).wait()
            return c
        source = lax.rem(c - s + self.cn, self.cn)
        block = self.dst(source)
        remote(
            block, block, self.sem.at[0, s], self.sem.at[1, s], {"ctx": source}
        ).wait_recv()
        return source

    def sent(self):
        for s in range(1, self.cn):
            self.copy(s).wait_send()

    def finish(self):
        for s in range(self.cn):
            self.receive(s)
        self.sent()


class RingGather:
    def __init__(self, dpn, own, full, sem):
        self.dpn, self.own, self.full, self.sem = dpn, own, full, sem
        self.hops = dpn // 2
        d = lax.axis_index("dp")
        self.p = d // 2 * 2 + lax.rem(lax.rem(d, 2) + d // 2, 2)

    def member(self, step):
        p = lax.rem(self.p + step + self.dpn, self.dpn)
        return p // 2 * 2 + lax.rem(lax.rem(p, 2) + p // 2, 2)

    def half(self, ref, h, right):
        if h < self.hops:
            return ref
        m = self.full.shape[1] // 2
        if len(self.full.shape) == 3 and m % 16:
            m = self.full.shape[2] // 2
            return ref.at[:, pl.ds(0 if right else m, m)]
        return ref.at[pl.ds(0 if right else m, m)]

    def copy(self, h, right):
        way = 1 if right else -1
        origin = self.member(-way * (h - 1))
        src = self.own if h == 1 else self.full.at[origin]
        return remote(
            self.half(src, h, right),
            self.half(self.full.at[origin], h, right),
            self.sem.at[0 if right else 1, h],
            self.sem.at[2 if right else 3, h],
            {"dp": self.member(way)},
        )

    def arrival(self, h, right):
        way = 1 if right else -1
        block = self.half(self.full.at[self.member(-way * h)], h, right)
        return remote(
            block,
            block,
            self.sem.at[0 if right else 1, h],
            self.sem.at[2 if right else 3, h],
            {"dp": self.member(way)},
        )

    def greet(self):
        greet({"dp": self.member(1)})
        greet({"dp": self.member(-1)})

    def start(self):
        self.copy(1, True).start()
        self.copy(1, False).start()

    def forward(self):
        for h in range(1, self.hops):
            for right in (True, False):
                self.arrival(h, right).wait_recv()
                self.copy(h + 1, right).start()

    def finish(self):
        for right in (True, False):
            self.arrival(self.hops, right).wait_recv()
        for h in range(1, self.hops + 1):
            for right in (True, False):
                self.copy(h, right).wait_send()


def head_of(cn, heads, c, i):
    return c // 2 + cn // 2 * (heads * (c % 2) + i)


class HeadRows:
    def __init__(self, cn, dpn, dr):
        self.cn, self.dpn = cn, dpn
        self.per = HEAD_DIM // dr
        self.heads = dpn // self.per
        self.c, self.d = lax.axis_index("ctx"), lax.axis_index("dp")
        mine = self.d * cn + self.c
        head, n = mine // self.per, cn // 2
        turn = head // n
        self.home = 2 * lax.rem(head, n) + turn // self.heads
        self.slot = lax.rem(turn, self.heads) * self.per + lax.rem(mine, self.per)
        self.links = dpn - jnp.where(self.home == self.c, 1, 0)

    def owner(self, r):
        i, q = r // self.per, r % self.per
        head = self.c // 2 + self.cn // 2 * (self.heads * lax.rem(self.c, 2) + i)
        g = head * self.per + q
        return {"dp": g // self.cn, "ctx": lax.rem(g, self.cn)}

    def from_here(self, r):
        at = self.owner(r)
        return (at["dp"] == self.d) & (at["ctx"] == self.c)

    def to_here(self, to):
        return (self.home == self.c) & (self.d == to)

    def greet_owners(self):
        for r in range(self.dpn):
            pl.when(jnp.logical_not(self.from_here(r)))(lambda r=r: greet(self.owner(r)))

    def greet_homes(self):
        for to in range(self.dpn):
            pl.when(jnp.logical_not(self.to_here(to)))(
                lambda to=to: greet({"dp": to, "ctx": self.home})
            )


class RowGather(HeadRows):
    def __init__(self, cn, dpn, rows, full, sem, local):
        super().__init__(cn, dpn, rows.shape[0])
        self.rows, self.full, self.sem = rows, full, sem
        self.keep = pltpu.make_async_copy(rows, full.at[self.slot], local)

    def copy(self, to):
        return remote(
            self.rows,
            self.full.at[self.slot],
            self.sem.at[0, to],
            self.sem.at[1, self.slot],
            {"dp": to, "ctx": self.home},
        )

    def start(self):
        for to in range(self.dpn):
            pl.when(jnp.logical_not(self.to_here(to)))(lambda to=to: self.copy(to).start())
            pl.when(self.to_here(to))(self.keep.start)

    def finish(self):
        for r in range(self.dpn):
            block = self.full.at[r]
            came = remote(block, block, self.sem.at[0, r], self.sem.at[1, r], self.owner(r))
            pl.when(jnp.logical_not(self.from_here(r)))(came.wait_recv)
            pl.when(self.from_here(r))(self.keep.wait)
        for to in range(self.dpn):
            pl.when(jnp.logical_not(self.to_here(to)))(lambda to=to: self.copy(to).wait_send())


class RowSum(HeadRows):
    def __init__(self, cn, dpn, parts, got, sem):
        super().__init__(cn, dpn, parts.shape[1])
        self.parts, self.got, self.sem = parts, got, sem

    def copy(self, r):
        return remote(
            self.parts.at[r],
            self.got.at[self.d],
            self.sem.at[0, r],
            self.sem.at[1, self.d],
            self.owner(r),
        )

    def start(self):
        for r in range(self.dpn):
            pl.when(jnp.logical_not(self.from_here(r)))(lambda r=r: self.copy(r).start())

            @pl.when(self.from_here(r))
            def _():
                self.got[self.d] = self.parts[r]

    def finish(self, out):
        for s in range(self.dpn):
            block = self.got.at[s]
            came = remote(
                block, block, self.sem.at[0, s], self.sem.at[1, s], {"dp": s, "ctx": self.home}
            )
            pl.when(jnp.logical_not(self.to_here(s)))(came.wait_recv)

        def add(r):
            total = self.got[0, r, :].astype(f32)
            for s in range(1, self.dpn):
                total = total + self.got[s, r, :].astype(f32)
            out[r, :] = total

        by_rows(out.shape[0], add)
        for r in range(self.dpn):
            pl.when(jnp.logical_not(self.from_here(r)))(lambda r=r: self.copy(r).wait_send())


class RingPieces(RingGather):
    def __init__(self, dpn, full, sem):
        super().__init__(dpn, None, full, sem)

    def piece(self, i, h, right, back):
        way = 1 if right else -1
        ref = self.full.at[self.member(-way * back), i]
        return remote(
            ref,
            ref,
            self.sem.at[0 if right else 1, h, i],
            self.sem.at[2 if right else 3, h, i],
            {"dp": self.member(way)},
        )

    def moves(self, i, h, right, act):
        if h < self.hops:
            act()
        else:
            first = i < self.full.shape[1] // 2
            pl.when(first if right else jnp.logical_not(first))(act)

    def start(self, i):
        for right in (True, False):
            self.moves(i, 1, right, lambda r=right: self.piece(i, 1, r, 0).start())

    def forward(self, i):
        for h in range(1, self.hops):
            for right in (True, False):
                self.piece(i, h, right, h).wait_recv()
                self.moves(
                    i, h + 1, right, lambda h=h, r=right: self.piece(i, h + 1, r, h).start()
                )

    def finish(self, i):
        for right in (True, False):
            h = self.hops
            self.moves(i, h, right, lambda r=right: self.piece(i, h, r, h).wait_recv())
        for h in range(1, self.hops + 1):
            for right in (True, False):
                self.moves(
                    i, h, right, lambda h=h, r=right: self.piece(i, h, r, h - 1).wait_send()
                )


class RingSum:
    def __init__(self, dpn, blocks, got, got_half, sem):
        self.dpn, self.blocks, self.sem = dpn, blocks, sem
        self.got, self.got_half = got, got_half
        self.ring = RingGather(dpn, None, blocks, sem)
        self.hops = dpn // 2

    def part(self, s, right):
        m, width = self.blocks.shape[1:]
        if s > 1:
            return 0, m, pl.ds(0, width)
        if (m // 2) % 16:
            return 0, m, pl.ds(0 if right else width // 2, width // 2)
        return 0 if right else m // 2, m // 2, pl.ds(0, width)

    def copy(self, s, right):
        way = 1 if right else -1
        target = self.ring.member(way * (self.hops - s + 1))
        start, size, lanes = self.part(s, right)
        return remote(
            self.blocks.at[target, pl.ds(start, size), lanes],
            self.arrived(s, right),
            self.sem.at[0 if right else 1, s],
            self.sem.at[2 if right else 3, s],
            {"dp": self.ring.member(way)},
        )

    def arrived(self, s, right):
        side = 0 if right else 1
        return self.got_half.at[side] if s == 1 else self.got.at[side, s - 2]

    def order(self):
        out = [self.ring.member(self.hops)]
        for s in range(self.hops - 1, 0, -1):
            out += [self.ring.member(s), self.ring.member(-s)]
        return out + [self.ring.member(0)]

    def start(self):
        self.copy(1, True).start()
        self.copy(1, False).start()

    def take(self, s, right, target):
        self.copy(s, right).wait_recv()
        start, size, lanes = self.part(s, right)
        block = self.blocks.at[target, pl.ds(start, size), lanes]
        came = self.arrived(s, right)

        def add(r):
            block[r, :] = (block[r, :].astype(f32) + came[r, :].astype(f32)).astype(bf16)

        by_rows(size, add)

    def forward(self, s):
        for right in (True, False):
            way = 1 if right else -1
            self.take(s, right, self.ring.member(way * (self.hops - s)))
            self.copy(s + 1, right).start()

    def finish(self, out):
        for right in (True, False):
            self.copy(self.hops, right).wait_recv()
        mine = self.ring.member(0)
        ends = [self.arrived(self.hops, right) for right in (True, False)]
        per = out.shape[-2]

        @pl.loop(0, self.blocks.shape[1] // 16)
        def _(i):
            r = pl.ds(pl.multiple_of(i * 16, 16), 16)
            total = self.blocks[mine, r, :].astype(f32)
            for end in ends:
                total = total + end[r, :].astype(f32)
            if len(out.shape) == 3:
                to = pl.ds(pl.multiple_of(lax.rem(i * 16, per), 16), 16)
                out[i * 16 // per, to, :] = total.astype(out.dtype)
            else:
                out[r, :] = total.astype(out.dtype)

        for s in range(1, self.hops + 1):
            for right in (True, False):
                self.copy(s, right).wait_send()


def ring_scratch(dpn, m, width):
    return [
        pltpu.VMEM((dpn, m, width), bf16),
        pltpu.VMEM((2, dpn // 2 - 1, m, width), bf16),
        pltpu.VMEM((2, m // 2, width) if m % 32 == 0 else (2, m, width // 2), bf16),
        pltpu.SemaphoreType.DMA((4, dpn // 2 + 1)),
    ]


def outer(a_ref, b_ref, out, at, tile=512):
    a = a_ref[:, at]
    width = out.shape[-1]
    for lo in range(0, width, tile):
        to = slice(lo, min(lo + tile, width))
        out[:, to] = dot(a, b_ref[:, to], contract_rows).astype(bf16)


def outer_all(a_ref, staged, halves, blocks, tile=512):
    count, m, width = blocks.shape
    many = max(1, 128 // m)
    for first in range(0, count, many):
        at = slice(first * m, (first + many) * m)
        for lo in range(0, width, tile):
            to = slice(lo, min(lo + tile, width))
            part = dot(a_ref[halves[0], at], staged(0, to), contract_rows)
            part = part + dot(a_ref[halves[1], at], staged(1, to), contract_rows)
            part = part.astype(bf16)
            for i in range(many):
                blocks[first + i, :, to] = part[i * m : (i + 1) * m]


class LineSum:
    def __init__(self, cn, compute, part, cross, cross_in, flow, arrived, sem):
        self.cn, self.compute, self.part = cn, compute, part
        self.cross, self.cross_in, self.flow = cross, cross_in, flow
        self.arrived, self.sem = arrived, sem

    def across(self, t):
        _, _, _, _, sib = place(self.cn)
        return remote(
            self.cross.at[t],
            self.cross_in.at[t],
            self.sem.at[0, t],
            self.sem.at[2, t],
            {"ctx": sib},
        )

    def along(self, t, slot, target):
        return remote(
            self.flow.at[t],
            self.arrived.at[slot],
            self.sem.at[1, t],
            self.sem.at[3, slot],
            {"ctx": target},
        )

    def produce(self, t, slot):
        _, _, k, _, _ = place(self.cn)
        part = self.part.at[slot]
        self.compute(t, part)

        def low(r):
            self.cross[t, r, :] = part[1 - k, r, :].astype(bf16)

        by_rows(self.cross.shape[1], low)
        self.across(t).start()

    def add(self, part, came):
        def more(r):
            part[r, :] += came[r, :].astype(f32)

        by_rows(part.shape[0], more)

    def collect(self, t, slot):
        _, j, k, n, sib = place(self.cn)
        part = self.part.at[slot, k]
        self.across(t).wait_recv()
        self.add(part, self.cross_in.at[t])

        @pl.when((j > 0) & (t >= j))
        def _():
            self.along(t, t, sib).wait_recv()
            self.add(part, self.arrived.at[t])

        @pl.when((j < n - 1) & (t <= j))
        def _():
            slot_in = jnp.where(t == j, n, t)
            self.along(t, slot_in, sib).wait_recv()
            self.add(part, self.arrived.at[slot_in])

    def send(self, t, slot, up):
        c, j, k, n, _ = place(self.cn)

        def low(r):
            self.flow[t, r, :] = self.part[slot, k, r, :].astype(bf16)

        by_rows(self.flow.shape[1], low)
        there = t if up else jnp.where(t == j - 1, n, t)
        self.along(t, there, c + 2 if up else c - 2).start()

    def drain(self):
        _, j, _, n, sib = place(self.cn)

        @pl.loop(0, n)
        def _(t):
            self.across(t).wait_send()

            @pl.when(t != j)
            def _():
                self.along(t, t, sib).wait_send()


def line_sums(cn, sums, between=None):
    _, j, _, n, _ = place(cn)

    @pl.loop(0, n - 1)
    def _(s):
        to_up, to_down = n - 1 - s + j, s - (n - 1 - j)
        for total in sums:

            @pl.when(s >= j)
            def _():
                total.produce(to_up, 0)

            @pl.when(s >= n - 1 - j)
            def _():
                total.produce(to_down, 1)

        for total in sums:

            @pl.when(s >= j)
            def _():
                total.collect(to_up, 0)
                total.send(to_up, 0, True)

            @pl.when(s >= n - 1 - j)
            def _():
                total.collect(to_down, 1)
                total.send(to_down, 1, False)

        if between is not None:
            between(s)

    for total in sums:
        total.produce(j, 0)
    for total in sums:
        total.collect(j, 0)


def sum_scratch(cn, rows, width):
    n = cn // 2
    return [
        pltpu.VMEM((2, 2, rows, width), f32),
        pltpu.VMEM((n, rows, width), bf16),
        pltpu.VMEM((n, rows, width), bf16),
        pltpu.VMEM((n, rows, width), bf16),
        pltpu.VMEM((n + 1, rows, width), bf16),
        pltpu.SemaphoreType.DMA((4, n + 1)),
    ]


def product(a_ref, b_ref, dims, rows, width):
    tile = min(512, width)

    def compute(t, out):
        a = a_ref[pl.ds(pl.multiple_of(t * 2 * rows, 2 * rows), 2 * rows), :]

        @pl.loop(0, width // tile)
        def _(i):
            at = pl.ds(pl.multiple_of(i * tile, tile), tile)
            b = b_ref[:, at] if dims == plain else b_ref[at, 0 : a_ref.shape[1]]
            out[:, :, at] = dot(a, b, dims).reshape(2, rows, tile)

    return compute


def rms(v):
    return lax.rsqrt(jnp.mean(v * v, axis=-1, keepdims=True) + norm_eps)


def front_kernel(
    cn, dpn, x_in, seg, valid, gain_rows, wq, wk, wv, wo, gate_in, up_in, down_in,
    x_all, pack_all, gate, up, down_all, wo_low, down_rest,
    x, pack, wide, tall, down, gsem, ssem, rsem, dsem, local,
):
    c, d = lax.axis_index("ctx"), lax.axis_index("dp")
    hw = wq.shape[1] // cn
    part = gate_in.shape[1] // (cn * dpn)
    mine = pack_all.at[d]
    swap = Swap(cn, pack, mine, ssem, local.at[0])
    gather = PairGather(cn, x, x_all, gsem)
    ring = RingPieces(dpn, pack_all, rsem)
    down_ring = RingGather(dpn, down, down_all, dsem)
    greet_ctx(cn)
    ring.greet()
    rows, width = x_in.shape
    load_x = pltpu.make_async_copy(x_in, x.at[:, 0:width], local.at[1])
    load_x.start()

    def column(row):
        return jnp.broadcast_to(row, (128, 128)).T

    code = (seg[...] * 2 + valid[...]).astype(f32)
    x[:, width:] = column(code).astype(bf16)
    lane = lax.broadcasted_iota(jnp.int32, (128, 128), 1)
    gains = jnp.where(lane == 0, column(gain_rows[0:1, :]), column(gain_rows[1:2, :]))
    gains = gains[0 : wq.shape[0]].astype(bf16)
    load_x.wait()
    loads = [
        pltpu.make_async_copy(src, dst, local.at[i])
        for i, (src, dst) in enumerate(
            ((gate_in, wide.at[0]), (up_in, wide.at[1]), (down_in, tall)), 2
        )
    ]
    for load in loads:
        load.start()
    pl.semaphore_wait(pltpu.get_barrier_semaphore(), cn - 1 + 2)
    gather.start()
    for to in range(cn):
        for i, w in enumerate((wq, wk, wv)):
            for t in range(hw // HEAD_DIM):
                lo, at = head_of(cn, hw // HEAD_DIM, to, t) * HEAD_DIM, i * hw + t * HEAD_DIM
                pack[to, :, at : at + HEAD_DIM] = w[:, lo : lo + HEAD_DIM].astype(bf16)
        pack[to, :, 3 * hw :] = gains
    swap.start()
    loads[2].wait()
    split = down.shape[0]
    down[...] = tall[0:split, :].astype(bf16)
    down_rest[...] = tall[split:, :].astype(bf16)
    down_ring.start()
    keep_down = pltpu.make_async_copy(down, down_all.at[d], local.at[5])
    keep_down.start()
    keep = pltpu.make_async_copy(x, x_all.at[c], local.at[1])
    keep.start()
    wo_low[...] = wo[...].astype(bf16)

    def lay(i, out):
        loads[i].wait()
        for to in range(cn):
            for row in range(dpn):
                lo = (row * cn + to) * part
                out[to, :, row * part : (row + 1) * part] = wide[i, :, lo : lo + part].astype(bf16)

    half = cn // 2
    sources = [swap.receive(0)]
    ring.start(sources[0])
    lay(0, gate)
    for s in range(1, half):
        sources.append(swap.receive(s))
        ring.start(sources[s])
    gather.forward(1, 1)
    lay(1, up)
    for s in range(half, cn):
        sources.append(swap.receive(s))
        ring.start(sources[s])
    down_ring.forward()
    gather.forward(2, 2)
    for source in sources:
        ring.forward(source)
    gather.forward(3)
    keep.wait()
    keep_down.wait()
    gather.finish()
    for source in sources:
        ring.finish(source)
    swap.sent()
    down_ring.finish()


def prepare(w, x_all, gains, info_rows, hw, block):
    width = w.shape[0]
    per = block // x_all.shape[1]

    @pl.loop(0, width // block)
    def _(i):
        at = pl.ds(pl.multiple_of(i * block, block), block)
        gains[:, at] = w[at, 3 * hw : 3 * hw + 128].astype(f32).T[0:8]

    @pl.loop(0, info_rows.shape[1] // block)
    def _(i):
        at = pl.ds(pl.multiple_of(i * block, block), block)
        codes = x_all[pl.ds(i * per, per), :, width:].reshape(block, 128).astype(f32).T[0:8]
        seg = jnp.floor(codes * 0.5)
        code = jnp.where(codes - 2.0 * seg == 1.0, seg, -1.0)
        first = lax.broadcasted_iota(jnp.int32, (8, block), 0) == 0
        info_rows[:, at] = jnp.where(first, seg, code)


def tables(x_all, inverse, info_rows, info_cols, cosines, sines, width, i, block):
    per = block // x_all.shape[1]
    at = pl.ds(pl.multiple_of(i * block, block), block)
    codes = x_all[pl.ds(i * per, per), :, width:].reshape(block, 128).astype(f32)
    seg = jnp.floor(codes * 0.5)
    valid = codes - 2.0 * seg
    lane = lax.broadcasted_iota(jnp.int32, (block, 128), 1)
    code = jnp.where(valid == 1.0, seg, -1.0)
    info_cols[at, :] = jnp.where(lane == 0, seg, jnp.where(lane == 1, valid, code))
    before = jnp.where(info_rows[0:1, :] < seg[:, 0:1], 1.0, 0.0)
    index = lax.broadcasted_iota(jnp.int32, (block, 128), 0) + i * block
    place_in = index.astype(f32) - jnp.sum(before, axis=1, keepdims=True)
    angles = place_in * inverse[...]
    cosines[at, :] = jnp.cos(angles)
    sines[at, :] = jnp.where(lane < HEAD_DIM // 2, -1.0, 1.0) * jnp.sin(angles)


def project(x_all, w, gain, inverse, rows_in, cols, cosines, sines, an, qkv, hw, block, hook):
    width = an.shape[1]
    per = block // x_all.shape[1]

    @pl.loop(0, an.shape[0] // block)
    def _(i):
        at = pl.ds(pl.multiple_of(i * block, block), block)
        tables(x_all, inverse, rows_in, cols, cosines, sines, width, i, block)
        x = x_all[pl.ds(i * per, per), :, 0:width].reshape(block, width).astype(f32)
        normed = (x * rms(x) * gain[...]).astype(bf16)
        an[at, :] = normed
        proj = dot(normed, w[:, 0 : 3 * hw])
        cos_b, sin_b = cosines[at, :], sines[at, :]
        for h in range(2 * hw // HEAD_DIM):
            lanes = slice(h * HEAD_DIM, (h + 1) * HEAD_DIM)
            v = proj[:, lanes]
            turned = v * cos_b + pltpu.roll(v, HEAD_DIM // 2, 1) * sin_b
            qkv[at, lanes] = turned.astype(bf16)
        qkv[at, 2 * hw :] = proj[:, 2 * hw :].astype(bf16)
        hook(i)


def mask_block(q_seg, k_code, i, j, block):
    rows = lax.broadcasted_iota(jnp.int32, (block, block), 0) + i * block
    cols = lax.broadcasted_iota(jnp.int32, (block, block), 1) + j * block
    return (q_seg == k_code) & (cols <= rows)


def attend(qkv, q_info, k_code, out, mass, hw, block, hook):
    mass[...] = jnp.zeros_like(mass)

    @pl.loop(0, qkv.shape[0] // block)
    def _(i):
        at = pl.ds(pl.multiple_of(i * block, block), block)
        q_seg, q_valid = q_info[at, 0:1], q_info[at, 1:2]
        for h in range(hw // HEAD_DIM):
            lane = [slice(t * hw + h * HEAD_DIM, t * hw + (h + 1) * HEAD_DIM) for t in range(3)]
            q = qkv[at, lane[0]]

            def step(j, acc):
                to = pl.ds(pl.multiple_of(j * block, block), block)
                s = dot(q, qkv[to, lane[1]], contract_cols) * score_scale - score_shift
                allowed = mask_block(q_seg, k_code[1:2, to], i, j, block)
                p = jnp.where(allowed, jax.nn.sigmoid(s), 0.0)
                mass[...] += jnp.sum(p * q_valid, axis=0, keepdims=True)
                return acc + dot(p.astype(bf16), qkv[to, lane[2]])

            acc = lax.fori_loop(0, i + 1, step, jnp.zeros((block, HEAD_DIM), f32))
            out[at, lane[0]] = acc.astype(bf16)
        hook(i)


def attn_kernel(
    cn, dpn, x_all, w, inverse, gate, up, wo,
    an, qkv, o, mass, gains, cosines, sines, cols, rows_in,
    gate_all, up_own, wo_all, ssem, rsem, wsem, local,
):
    c, d = lax.axis_index("ctx"), lax.axis_index("dp")
    wo_rows = RowGather(cn, dpn, wo, wo_all, wsem, local.at[2])
    rows = x_all.shape[1]
    hw = qkv.shape[1] // 3
    swap_gate = Swap(cn, gate, gate_all.at[d], ssem.at[0], local.at[0])
    swap_up = Swap(cn, up, up_own, ssem.at[1], local.at[1])
    ring = RingPieces(dpn, gate_all, rsem)
    sources = [lax.rem(c - s + cn, cn) for s in range(cn)]
    greet_ctx(cn)
    ring.greet()

    wo_rows.greet_owners()
    pl.semaphore_wait(pltpu.get_barrier_semaphore(), cn - 1 + 2 + wo_rows.links)
    wo_rows.start()
    swap_gate.start()

    def in_project(i):
        @pl.when(i == 1)
        def _():
            for s in range(cn // 2):
                ring.start(swap_gate.receive(s))

        @pl.when(i == 2)
        def _():
            for s in range(cn // 2, cn):
                ring.start(swap_gate.receive(s))
            swap_up.start()

    def in_attend(i):
        @pl.when(i == 2)
        def _():
            for source in sources[: cn // 2]:
                ring.forward(source)

    prepare(w, x_all, gains, rows_in, hw, 2 * rows)
    project(
        x_all, w, gains.at[0:1], inverse, rows_in, cols, cosines, sines, an, qkv, hw, 2 * rows,
        in_project,
    )
    attend(qkv, cols, rows_in, o, mass, hw, 2 * rows, in_attend)
    for source in sources[cn // 2 :]:
        ring.forward(source)
    swap_up.finish()
    wo_rows.finish()
    for source in sources:
        ring.finish(source)
    swap_gate.sent()


def middle_kernel(
    cn, dpn, o, wo, x, gain, dy, up, gate_all, down_half, down_rest,
    h1, bn_all, up_all, hid, dgu, dys_all, down_all,
    own, bn, dys, wg, wu, down_by, gsem, ysem, rsem, dsem, local, *sum_refs,
):
    c, d = lax.axis_index("ctx"), lax.axis_index("dp")
    _, j, k, n, _ = place(cn)
    rows, width = x.shape
    ff = hid.shape[1]
    block = 2 * rows
    gather = PairGather(cn, own, bn, gsem)
    gather_dy = PairGather(cn, dy, dys, ysem)
    ring = RingGather(dpn, up, up_all, rsem)
    split = down_rest.shape[0]
    rest_ring = RingGather(dpn, down_rest, down_by.at[:, pl.ds(split, split)], dsem)
    keep_rest = pltpu.make_async_copy(
        down_rest, down_by.at[d, pl.ds(split, split)], local.at[5]
    )
    total = LineSum(cn, product(o, wo, plain, rows, width), *sum_refs)
    greet_line(cn, ring)
    ring.start()
    rest_ring.start()
    keep_rest.start()
    keep_up = pltpu.make_async_copy(up, up_all.at[d], local.at[0])
    loads = [
        pltpu.make_async_copy(src, dst, local.at[i])
        for i, (src, dst) in enumerate(((gate_all, wg), (down_half, down_by.at[:, pl.ds(0, split)])), 2)
    ]
    keep_up.start()
    for load in loads:
        load.start()
    gather_dy.start()
    dys[c] = dy[...]

    def between(s):
        gather_dy.step(s + 1)

        @pl.when(s == n - 2)
        def _():
            ring.forward()
            rest_ring.forward()

    line_sums(cn, [total], between)

    def norm(r):
        mid = x[r, :].astype(f32) + total.part[0, k, r, :]
        h1[r, :] = mid
        own[r, :] = (mid * rms(mid) * gain[1:2, :]).astype(bf16)

    by_rows(rows, norm)
    gather.start()
    bn[c] = own[...]
    gather_dy.finish()
    store_dy = pltpu.make_async_copy(dys, dys_all, local.at[4])
    store_dy.start()
    total.drain()
    keep_up.wait()
    for load in loads:
        load.wait()
    rest_ring.finish()
    keep_rest.wait()
    store_down = pltpu.make_async_copy(down_by, down_all, local.at[6])
    store_down.start()
    ring.finish()
    load_up = pltpu.make_async_copy(up_all, wu, local.at[0])
    load_up.start()
    load_up.wait()
    wgate, wup, down = wg, wu.reshape(width, ff), down_by.reshape(ff, width)
    tile = min(512, ff)

    def feed(t):
        gather.other(t)
        at = pl.ds(pl.multiple_of(t * block, block), block)
        pair = pl.ds(t * 2, 2)
        send = pltpu.make_async_copy(bn.at[pair], bn_all.at[pair], local.at[1])
        send.start()
        a = bn[pair].reshape(block, width)
        g_out = dys[pair].reshape(block, width)

        @pl.loop(0, ff // tile)
        def _(i):
            to = pl.ds(pl.multiple_of(i * tile, tile), tile)
            gate = dot(a, wgate[:, to])
            up_v = dot(a, wup[:, to])
            dhid = dot(g_out, down[to, :], contract_cols)
            sig = jax.nn.sigmoid(gate)
            silu = gate * sig
            hid[at, to] = (silu * up_v).astype(bf16)
            dgate = dhid * up_v * sig * (1.0 + gate * (1.0 - sig))
            dgu[at, to] = dgate.astype(bf16)
            dgu[at, pl.ds(pl.multiple_of(ff + i * tile, tile), tile)] = (dhid * silu).astype(bf16)

        send.wait()

    feed(j)
    gather.step(1)

    @pl.loop(1, n)
    def _(s):
        both = (j - s >= 0) & (j + s <= n - 1)

        @pl.when(j - s >= 0)
        def _():
            feed(j - s)

        @pl.when(both & (s < n - 1))
        def _():
            gather.step(s + 1)

        @pl.when(j + s <= n - 1)
        def _():
            feed(j + s)

        @pl.when(jnp.logical_not(both) & (s < n - 1))
        def _():
            gather.step(s + 1)

    gather.sent()
    store_dy.wait()
    store_down.wait()


def back_kernel(
    cn, dpn, bn_in, dgu_in, hid, down, wg, wu, h1, dy, gain, dh1, dob_all, term, g_own, result,
    own, bn, dgu, cross_in, arrived, bsem, gsem, loads, keep_sem, *scratch,
):
    sum_refs, ring_refs = scratch[:-4], scratch[-4:]
    rows, width = dy.shape
    ff = wg.shape[1]
    tile = min(512, width)
    c, _, k, n, _ = place(cn)

    def compute(t, out):
        at = pl.ds(pl.multiple_of(t * 2 * rows, 2 * rows), 2 * rows)

        @pl.loop(0, width // tile)
        def _(i):
            to = pl.ds(pl.multiple_of(i * tile, tile), tile)
            part = dot(dgu[at, 0:ff], wg[to, :], contract_cols)
            part = part + dot(dgu[at, ff:], wu[to, :], contract_cols)
            out[:, :, to] = part.reshape(2, rows, tile)

    total = LineSum(cn, compute, *sum_refs)
    ring = RingSum(dpn, *ring_refs)
    blocks = ring_refs[0]
    m = blocks.shape[1]
    load_dgu = pltpu.make_async_copy(dgu_in, dgu, loads.at[0])
    load_bn = pltpu.make_async_copy(bn_in, bn, loads.at[1])
    load_dgu.start()
    load_bn.start()
    greet_line(cn, ring.ring)
    order = ring.order()
    load_dgu.wait()

    def weight_grad(member):
        outer(bn, dgu, blocks.at[member], pl.ds(pl.multiple_of(member * m, m), m))


    def between(s):
        @pl.when(s == 0)
        def _():
            load_bn.wait()
            weight_grad(order[0])
            ring.start()

        for i in range(ring.hops - 1):

            @pl.when(s == min(i, n - 2))
            def _():
                weight_grad(order[1 + 2 * i])
                weight_grad(order[2 + 2 * i])

            @pl.when(s == min(i + 2, n - 2))
            def _():
                ring.forward(i + 1)

        @pl.when(s == n - 2)
        def _():
            weight_grad(order[-1])

    line_sums(cn, [total], between)
    load_hid = pltpu.make_async_copy(hid, dgu.at[:, 0:ff], loads.at[0])
    load_down = pltpu.make_async_copy(down, bn.at[0:ff], loads.at[1])
    load_hid.start()
    load_down.start()
    term[...] = jnp.zeros_like(term)

    def norm_back(r):
        dbn = total.part[0, k, r, :]
        mid = h1[r, :]
        r2 = rms(mid)
        xh2 = mid * r2
        term[...] += jnp.sum(dbn * xh2, axis=0, keepdims=True)
        u2 = dbn * gain[1:2, :]
        mean = jnp.mean(u2 * xh2, axis=-1, keepdims=True)
        grad = dy[r, :].astype(f32) + r2 * (u2 - xh2 * mean)
        dh1[r, :] = grad
        own[r, :] = grad.astype(bf16)

    by_rows(rows, norm_back)
    gather = PairGather(cn, own, dob_all, gsem)
    gather.start()
    keep = pltpu.make_async_copy(own, dob_all.at[c], keep_sem)
    keep.start()
    total.drain()

    part, cross, _, flow, _, _ = sum_refs
    second = LineSum(
        cn,
        product(dgu.at[:, 0:ff], bn.at[0:ff], plain, rows, width),
        part, cross, cross_in, flow, arrived, bsem,
    )
    load_hid.wait()
    load_down.wait()

    def pass_on(s):
        gather.step(s + 1)

    line_sums(cn, [second], pass_on)

    def close(r):
        result[r, :] = (h1[r, :] + second.part[0, k, r, :]).astype(bf16)

    by_rows(rows, close)
    second.drain()
    keep.wait()
    gather.finish()
    ring.finish(g_own)


def attend_back(qkv, do, cosines, sines, q_info, k_info, dq, dqkv, hw, block):
    count = qkv.shape[0] // block
    dq[...] = jnp.zeros_like(dq)

    def turn_back(g, at):
        return g * cosines[at, :] - pltpu.roll(g, HEAD_DIM // 2, 1) * sines[at, :]

    @pl.loop(0, count)
    def _(j):
        to = pl.ds(pl.multiple_of(j * block, block), block)
        k_code = k_info[to, 2:3]
        for h in range(hw // HEAD_DIM):
            lane = [slice(t * hw + h * HEAD_DIM, t * hw + (h + 1) * HEAD_DIM) for t in range(3)]
            k, v = qkv[to, lane[1]], qkv[to, lane[2]]

            def step(i, carry):
                dk, dv = carry
                at = pl.ds(pl.multiple_of(i * block, block), block)
                q, do_i = qkv[at, lane[0]], do[at, lane[0]]
                s = dot(k, q, contract_cols) * score_scale - score_shift
                keys = lax.broadcasted_iota(jnp.int32, (block, block), 0) + j * block
                queries = lax.broadcasted_iota(jnp.int32, (block, block), 1) + i * block
                allowed = (k_code == q_info[0:1, at]) & (keys <= queries)
                sg = jnp.where(allowed, jax.nn.sigmoid(s), 0.0)
                dp = dot(v, do_i, contract_cols)
                ds = (dp * sg * (1.0 - sg)).astype(bf16)
                dq[at, lane[0]] += dot(ds, k, contract_rows)
                return dk + dot(ds, q), dv + dot(sg.astype(bf16), do_i)

            zero = jnp.zeros((block, HEAD_DIM), f32)
            dk, dv = lax.fori_loop(j, count, step, (zero, zero))
            dqkv[to, lane[1]] = turn_back(dk * score_scale, to).astype(bf16)
            dqkv[to, lane[2]] = dv.astype(bf16)

    @pl.loop(0, count)
    def _(i):
        at = pl.ds(pl.multiple_of(i * block, block), block)
        for h in range(hw // HEAD_DIM):
            lanes = slice(h * HEAD_DIM, (h + 1) * HEAD_DIM)
            dqkv[at, lanes] = turn_back(dq[at, lanes] * score_scale, at).astype(bf16)


def last_kernel(
    cn, dpn, g_gu, dob_all, dys_all, hid, o, wo, qkv, cosines, sines, q_info, k_info, an, w,
    dh1, x, gain, term_two, mass, grad_in, tot_out, gu_all, down_own, out_all, qkv_all,
    do, dq, dqkv, out_parts, out_got, qkv_own, tot, tot_in, tot_sum, tot_last,
    usem, qsem, tsem, psem, osem, local, *scratch,
):
    sum_refs, rings = scratch[:-8], (scratch[-8:-4], scratch[-4:])
    rows, width = x.shape
    hw = width // cn
    _, _, k, n, _ = place(cn)
    down_ring, qkv_ring = (RingSum(dpn, *refs) for refs in rings)
    rows_out = RowSum(cn, dpn, out_parts, out_got, osem)
    swap_gu = Swap(cn, g_gu, gu_all, usem, local.at[0])
    swap_qkv = Swap(cn, qkv_own, qkv_all, qsem, local.at[4])
    totals = Swap(cn, None, tot_in, tsem, local.at[3], lambda i: tot)
    c, d = lax.axis_index("ctx"), lax.axis_index("dp")
    def share(s):
        return remote(
            tot_sum, tot_last.at[d], psem.at[0, s], psem.at[1, s], {"dp": lax.rem(d + s, dpn)}
        )

    greet_ctx(cn)
    for s in range(1, dpn):
        greet({"dp": lax.rem(d + s, dpn)})

    rows_out.greet_homes()
    pl.semaphore_wait(
        pltpu.get_barrier_semaphore(), cn - 1 + dpn - 1 + rows_out.links
    )
    swap_gu.start()
    seq = an.shape[0]
    stage = (sum_refs[1], sum_refs[3])
    halves = (slice(0, seq // 2), slice(seq // 2, seq))

    def fill(src):
        copies = [
            pltpu.make_async_copy(src.at[pl.ds(i * n, n)], stage[i], local.at[1 + i])
            for i in range(2)
        ]
        for copy in copies:
            copy.start()
        for copy in copies:
            copy.wait()

    def staged(i, to=slice(None)):
        return stage[i][:, :, to].reshape(seq // 2, -1)

    fill(dob_all)
    outer_all(o, staged, halves, out_parts)
    rows_out.start()
    for i in range(2):
        do[halves[i], :] = dot(staged(i), wo[...], contract_cols).astype(bf16)
    fill(dys_all)
    outer_all(hid, staged, halves, rings[0][0])
    down_ring.start()
    m_qkv = rings[1][0].shape[1]
    order = qkv_ring.order()

    def grad_qkv(member):
        outer(an, dqkv, rings[1][0].at[member], pl.ds(pl.multiple_of(member * m_qkv, m_qkv), m_qkv))

    attend_back(qkv, do, cosines, sines, q_info, k_info, dq, dqkv, hw, 2 * rows)
    grad_qkv(order[0])
    qkv_ring.start()
    total = LineSum(cn, product(dqkv, w, contract_cols, rows, width), *sum_refs)

    def between(s):
        for i in range(qkv_ring.hops - 1):

            @pl.when(s == min(i, n - 2))
            def _():
                grad_qkv(order[1 + 2 * i])
                grad_qkv(order[2 + 2 * i])
                qkv_ring.forward(i + 1)

            @pl.when(s == min(i + 1, n - 2))
            def _():
                down_ring.forward(i + 1)

        @pl.when(s == n - 2)
        def _():
            grad_qkv(order[-1])
            qkv_ring.finish(qkv_own)
            swap_qkv.start()

    line_sums(cn, [total], between)
    tot[0] = jnp.zeros((1, width), f32)

    def norm_back(r):
        dan = total.part[0, k, r, :]
        xf = x[r, :].astype(f32)
        r1 = rms(xf)
        xh1 = xf * r1
        tot[0] += jnp.sum(dan * xh1, axis=0, keepdims=True)
        u1 = dan * gain[0:1, :]
        mean = jnp.mean(u1 * xh1, axis=-1, keepdims=True)
        grad = dh1[r, :] + r1 * (u1 - xh1 * mean)
        grad_in[r, :] = grad.astype(bf16)

    by_rows(rows, norm_back)
    tot[1] = term_two[...]
    tot[2] = jnp.broadcast_to(jnp.sum(mass[...], axis=1, keepdims=True), (1, width))
    totals.start()
    rows_out.finish(out_all)
    totals.finish()
    tot_sum[...] = jnp.sum(tot_in[...], axis=0)
    for s in range(1, dpn):
        share(s).start()
    down_ring.finish(down_own)
    total.drain()
    swap_gu.finish()
    tot_last[d] = tot_sum[...]
    for s in range(1, dpn):
        source = lax.rem(d - s + dpn, dpn)
        block = tot_last.at[source]
        remote(block, block, psem.at[0, s], psem.at[1, s], {"dp": source}).wait_recv()
    for s in range(1, dpn):
        share(s).wait_send()
    tot_out[...] = jnp.sum(tot_last[...], axis=0)
    swap_qkv.finish()


def spread_kernel(
    cn, dpn, qkv_in, gu_in, down_in, out_in, gq, gk, gv, go, gg, gu_out, gd, qkv, gu, down, out, sem
):
    hw = qkv.shape[2] // 3
    ff_rows = gd.shape[0]
    ff = ff_rows * dpn
    pairs = ((down_in, down), (out_in, out), (qkv_in, qkv), (gu_in, gu))
    loads = [pltpu.make_async_copy(a, b, sem.at[i]) for i, (a, b) in enumerate(pairs)]
    for load in loads:
        load.start()
    for load in loads[:3]:
        load.wait()
    gd[...] = down[...].astype(f32)
    go[...] = out[...]
    for c in range(cn):
        for i, ref in enumerate((gq, gk, gv)):
            for t in range(hw // HEAD_DIM):
                lo, at = head_of(cn, hw // HEAD_DIM, c, t) * HEAD_DIM, i * hw + t * HEAD_DIM
                ref[:, lo : lo + HEAD_DIM] = qkv[c, :, at : at + HEAD_DIM].astype(f32)
    loads[3].wait()
    for c in range(cn):
        for i, ref in enumerate((gg, gu_out)):
            for d in range(dpn):
                to = (d * cn + c) * ff_rows
                lo = i * ff + d * ff_rows
                ref[:, to : to + ff_rows] = gu[c, :, lo : lo + ff_rows].astype(f32)


def call(kernel, outs, ins, specs_in, specs_out, scratch, number, flops=0, moved=0):
    return pl.pallas_call(
        kernel,
        out_shape=outs,
        in_specs=specs_in,
        out_specs=specs_out,
        scratch_shapes=scratch,
        compiler_params=pltpu.CompilerParams(
            collective_id=number, has_side_effects=True, vmem_limit_bytes=61 * 2**20
        ),
        cost_estimate=pl.CostEstimate(flops=flops, bytes_accessed=moved, transcendentals=0),
    )(*ins)


def shape(dims, dtype=bf16):
    return jax.ShapeDtypeStruct(dims, dtype)


def shards(
    hidden_in,
    out_grad,
    seg_ids,
    valid_mask,
    w_query,
    w_key,
    w_value,
    w_output,
    w_gate,
    w_up,
    w_down,
    gain_attn,
    gain_mlp,
):
    dpn = lax.axis_size("dp")
    cn = lax.axis_size("ctx")
    n = cn // 2
    x_local = hidden_in[0]
    dy_local = out_grad[0]
    rows, width = x_local.shape
    seq = rows * cn
    dr = w_query.shape[0]
    hw = width // cn
    heads = hw // HEAD_DIM
    ff_rows = w_down.shape[0]
    ff = ff_rows * dpn
    dma = pltpu.SemaphoreType.DMA
    mib = 2**20

    gain_rows = jnp.pad(jnp.stack([gain_attn, gain_mlp]), ((0, 0), (0, 128 - dr)))
    pw = 3 * hw + 128
    ring_sem = dma((4, dpn // 2 + 1))
    x_all, w_qkv, gate_pack, up_pack, down_half, wo_low, down_rest = call(
        functools.partial(front_kernel, cn, dpn),
        (
            shape((cn, rows, width + 128)),
            shape((dpn, cn, dr, pw)),
            shape((cn, dr, ff)),
            shape((cn, dr, ff)),
            shape((dpn, ff_rows // 2, width)),
            shape((dr, width)),
            shape((ff_rows // 2, width)),
        ),
        (
            x_local, seg_ids, valid_mask, gain_rows, w_query, w_key, w_value, w_output,
            w_gate, w_up, w_down,
        ),
        [ANY] + [VMEM] * 7 + [ANY] * 3,
        (ANY, ANY, VMEM, VMEM, ANY, VMEM, VMEM),
        [
            pltpu.VMEM((rows, width + 128), bf16),
            pltpu.VMEM((cn, dr, pw), bf16),
            pltpu.VMEM((2, dr, ff * cn), f32),
            pltpu.VMEM((ff_rows, width), f32),
            pltpu.VMEM((ff_rows // 2, width), bf16),
            dma((2, 5, n)),
            dma((2, cn)),
            dma((4, dpn // 2 + 1, cn)),
            ring_sem,
            dma((6,)),
        ],
        1,
        moved=160 * mib,
    )
    w_qkv = w_qkv.reshape(width, pw)
    inverse = jnp.exp(
        jnp.arange(HEAD_DIM // 2, dtype=f32) * (-2.0 * math.log(rope_base) / HEAD_DIM)
    )
    inverse = jnp.concatenate([inverse, inverse])[None]

    line_scratch = sum_scratch(cn, rows, width)
    an, proj, o, mass, gains, cosines, sines, cols, infos, w_gate_c, up_own, wo = call(
        functools.partial(attn_kernel, cn, dpn),
        (
            shape((seq, width)),
            shape((seq, 3 * hw)),
            shape((seq, hw)),
            shape((1, 2 * rows), f32),
            shape((8, width), f32),
            shape((seq, HEAD_DIM), f32),
            shape((seq, HEAD_DIM), f32),
            shape((seq, 128), f32),
            shape((8, seq), f32),
            shape((dpn, cn, dr, ff)),
            shape((cn, dr, ff)),
            shape((dpn, dr, width)),
        ),
        (x_all, w_qkv, inverse, gate_pack, up_pack, wo_low),
        [VMEM] * 3 + [ANY] * 3,
        (VMEM,) * 9 + (ANY,) * 3,
        [dma((2, 2, cn)), dma((4, dpn // 2 + 1, cn)), dma((2, dpn)), dma((3,))],
        2,
        moved=160 * mib,
    )
    h1, bn, w_up_c, hid, dgu, dys, down = call(
        functools.partial(middle_kernel, cn, dpn),
        (
            shape((rows, width), f32),
            shape((cn, rows, width)),
            shape((dpn, cn, dr, ff)),
            shape((seq, ff)),
            shape((seq, 2 * ff)),
            shape((cn, rows, width)),
            shape((dpn, ff_rows, width)),
        ),
        (
            o, wo.reshape(hw, width), x_local, gains, dy_local, up_own,
            w_gate_c.reshape(width, ff), down_half, down_rest,
        ),
        [VMEM] * 5 + [ANY] * 4,
        (VMEM, ANY, ANY, VMEM, VMEM, ANY, ANY),
        [
            pltpu.VMEM((rows, width), bf16),
            pltpu.VMEM((cn, rows, width), bf16),
            pltpu.VMEM((cn, rows, width), bf16),
            pltpu.VMEM((width, ff), bf16),
            pltpu.VMEM((dpn, cn, dr, ff), bf16),
            pltpu.VMEM((dpn, ff_rows, width), bf16),
            dma((2, 5, n)),
            dma((2, 5, n)),
            ring_sem,
            ring_sem,
            dma((7,)),
        ]
        + line_scratch,
        3,
        moved=160 * mib,
    )
    wo = wo.reshape(hw, width)
    w_gate_c = w_gate_c.reshape(width, ff)
    w_up_c = w_up_c.reshape(width, ff)
    bn = bn.reshape(seq, width)
    dh1, dob, term_two, g_gu, result = call(
        functools.partial(back_kernel, cn, dpn),
        (
            shape((rows, width), f32),
            shape((cn, rows, width)),
            shape((1, width), f32),
            shape((cn, dr, 2 * ff)),
            shape((rows, width)),
        ),
        (bn, dgu, hid, down.reshape(ff, width), w_gate_c, w_up_c, h1, dy_local, gains),
        [ANY] * 4 + [VMEM] * 5,
        (VMEM, ANY, VMEM, VMEM, VMEM),
        [
            pltpu.VMEM((rows, width), bf16),
            pltpu.VMEM((seq, width), bf16),
            pltpu.VMEM((seq, 2 * ff), bf16),
            pltpu.VMEM((n, rows, width), bf16),
            pltpu.VMEM((n + 1, rows, width), bf16),
            dma((4, n + 1)),
            dma((2, 5, n)),
            dma((2,)),
            dma,
        ]
        + line_scratch
        + ring_scratch(dpn, cn * dr, 2 * ff),
        4,
        moved=160 * mib,
    )
    grad_input, totals, gu_back, g_down, g_out, q_all = call(
        functools.partial(last_kernel, cn, dpn),
        (
            shape((rows, width)),
            shape((3, 1, width), f32),
            shape((cn, dr, 2 * ff)),
            shape((ff_rows, width)),
            shape((dr, width), f32),
            shape((cn, dr, 3 * hw)),
        ),
        (
            g_gu, dob, dys, hid, o, wo, proj, cosines, sines, infos, cols, an, w_qkv,
            dh1, x_local, gains, term_two, mass,
        ),
        [ANY] * 3 + [VMEM] * 15,
        (VMEM, VMEM, ANY, VMEM, VMEM, ANY),
        [
            pltpu.VMEM((seq, hw), bf16),
            pltpu.VMEM((seq, hw), f32),
            pltpu.VMEM((seq, 3 * hw), bf16),
            pltpu.VMEM((dpn, dr, width), bf16),
            pltpu.VMEM((dpn, dr, width), bf16),
            pltpu.VMEM((cn, dr, 3 * hw), bf16),
            pltpu.VMEM((3, 1, width), f32),
            pltpu.VMEM((cn, 3, 1, width), f32),
            pltpu.VMEM((3, 1, width), f32),
            pltpu.VMEM((dpn, 3, 1, width), f32),
            dma((2, cn)),
            dma((2, cn)),
            dma((2, cn)),
            dma((2, dpn)),
            dma((2, dpn)),
            dma((5,)),
        ]
        + line_scratch
        + ring_scratch(dpn, ff_rows, width)
        + ring_scratch(dpn, cn * dr, 3 * hw),
        5,
        moved=160 * mib,
    )

    g_q, g_k, g_v, g_o, g_gate, g_up, g_down = pl.pallas_call(
        functools.partial(spread_kernel, cn, dpn),
        out_shape=tuple(shape((dr, width), f32) for _ in range(4))
        + tuple(shape((dr, ff * cn), f32) for _ in range(2))
        + (shape((ff_rows, width), f32),),
        in_specs=[ANY] * 4,
        out_specs=(VMEM,) * 7,
        scratch_shapes=[
            pltpu.VMEM((cn, dr, 3 * hw), bf16),
            pltpu.VMEM((cn, dr, 2 * ff), bf16),
            pltpu.VMEM((ff_rows, width), bf16),
            pltpu.VMEM((dr, width), f32),
            dma((4,)),
        ],
        compiler_params=pltpu.CompilerParams(vmem_limit_bytes=61 * 2**20),
    )(q_all, gu_back, g_down, g_out)
    mass_mean = totals[2, 0, 0] / (heads * cn * dpn * seq)
    owner = (lax.axis_index("dp") * cn + lax.axis_index("ctx")) * dr
    grad_gains = [lax.dynamic_slice_in_dim(totals[i, 0], owner, dr) for i in range(2)]
    return (
        result[None],
        grad_input[None],
        g_q,
        g_k,
        g_v,
        g_o,
        g_gate,
        g_up,
        g_down,
        grad_gains[0],
        grad_gains[1],
        mass_mean,
    )


def solution(mesh):
    tok = P("dp", "ctx", None)
    ids = P("dp", "ctx")
    mat = P(("dp", "ctx"), None)
    vec = P(("dp", "ctx"))
    return jax.shard_map(
        shards,
        mesh=mesh,
        in_specs=(tok, tok, ids, ids) + (mat,) * 7 + (vec, vec),
        out_specs=(tok, tok) + (mat,) * 7 + (vec, vec, P()),
        check_vma=False,
    )
```
